32 devices in a mesh: stream: 2 (over y), batch: 16 (over z, x, core).
Axes of the slice: x: 2, y: 2, z: 4, core: 2. Of those that a mesh axis runs over, the one named last changes fastest.
Arguments:
- layer_input: bfloat16 [2, 16, 1024, 768], P('stream', 'batch'), may hold values from -6 to 6
- out_cotangent: bfloat16 [2, 16, 1024, 768], P('stream', 'batch'), may hold values from -6 to 6
- block_size: int32 [16], P('batch'), may hold values from 4 to 16, as said below
- norm1_gain: float32 [768], replicated, may hold values from 0.5 to 1.5
- norm1_bias: float32 [768], replicated, may hold values from -1 to 1
- qkv_weight: bfloat16 [768, 2304], replicated, may hold values from -0.21875 to 0.21875
- qkv_bias: float32 [2304], replicated, may hold values from -1 to 1
- proj_weight: bfloat16 [768, 768], replicated, may hold values from -0.875 to 0.875
- proj_bias: float32 [768], replicated, may hold values from -1 to 1
- norm2_gain: float32 [768], replicated, may hold values from 0.5 to 1.5
- norm2_bias: float32 [768], replicated, may hold values from -1 to 1
- up_weight: bfloat16 [768, 3072], replicated, may hold values from -0.21875 to 0.21875
- up_bias: float32 [3072], replicated, may hold values from -1 to 1
- down_weight: bfloat16 [3072, 768], replicated, may hold values from -0.109375 to 0.109375
- down_bias: float32 [768], replicated, may hold values from -1 to 1
Outputs:
- layer_output: bfloat16 [2, 16, 1024, 768], P('stream', 'batch')
- input_grad: float32 [2, 16, 1024, 768], P('stream', 'batch')
- gain1_grad: float32 [768], P('batch')
- bias1_grad: float32 [768], P('batch')
- qkvw_grad: float32 [768, 2304], P('batch')
- qkvb_grad: float32 [2304], P('batch')
- projw_grad: float32 [768, 768], P('batch')
- projb_grad: float32 [768], P('batch')
- gain2_grad: float32 [768], P('batch')
- bias2_grad: float32 [768], P('batch')
- upw_grad: float32 [768, 3072], P('batch')
- upb_grad: float32 [3072], P('batch')
- downw_grad: float32 [3072, 768], P('batch')
- downb_grad: float32 [768], P('batch')
The draws below stay inside these ranges and needn't reach their ends.
Inputs may be any that keep to these rules, and one draw needn't show every extreme that they name: `block_size`: each sequence's block size is 4, 8 or 16.
All inputs are finite; a program needn't handle non-finite values.
Results may differ from the reference program's by a relative error of at most 0.014.
Values may be sent and summed in bfloat16 or wider, within the bound.
No kernel may reach another device: no remote copies, remote signals or barrier semaphores. Data moves between devices by JAX's collectives and lax.ppermute only.
A program may use at most 384 MiB of HBM per device.

```python
import math
import jax
import jax.numpy as jnp
from jax import lax

D = 768
HEADS = 12
HEAD = 64
FF = 3072
LEN = 1024
SEQS = 16


def draw_block_size(key, part):
    picked = jax.random.randint(key, (SEQS,), 0, 3)
    return jnp.where(picked == 0, 4, jnp.where(picked == 1, 8, 16)).astype(jnp.int32)


def level_of(key, shape, cuts, smallest, largest):
    loudness = 1.0
    for axis_at, parts in cuts:
        steps = jax.random.uniform(jax.random.fold_in(jax.random.fold_in(key, 6), axis_at), (parts,), jnp.float32, smallest / len(cuts), largest / len(cuts))
        loudness = loudness * jnp.repeat(jnp.exp(steps), shape[axis_at] // parts).reshape((-1,) + (1,) * (len(shape) - 1 - axis_at))
    return loudness


def bell_draw(stream_key, dims, deviation, reach, cuts=(), kind=jnp.bfloat16):
    loudness = level_of(stream_key, dims, cuts, -0.22, 0.18) if cuts else 1.0
    result = jax.random.normal(stream_key, dims, jnp.float32) * deviation * loudness
    return jnp.minimum(jnp.maximum(result, -reach), reach).astype(kind)


def setup_inputs(seed: int = 0) -> dict:
    seeds = jax.random.split(jax.random.key(seed), 16)
    return {
        "layer_input": bell_draw(seeds[0], (2, SEQS, LEN, D), 1.0, 6.0, ((0, 2), (1, 16))),
        "out_cotangent": bell_draw(seeds[1], (2, SEQS, LEN, D), 1.0, 6.0, ((0, 2), (1, 16))),
        "block_size": draw_block_size(jax.random.fold_in(seeds[15], 71), 0),
        "norm1_gain": jnp.clip(1.0 + 0.1 * jax.random.normal(seeds[3], (D,), jnp.float32), 0.5, 1.5),
        "norm1_bias": bell_draw(seeds[4], (D,), 0.2, 1.0, (), jnp.float32),
        "qkv_weight": bell_draw(seeds[5], (D, 3 * D), D ** -0.5, 0.21875),
        "qkv_bias": bell_draw(seeds[6], (3 * D,), 0.2, 1.0, (), jnp.float32),
        "proj_weight": bell_draw(seeds[7], (D, D), (D // 16) ** -0.5, 0.875),
        "proj_bias": bell_draw(seeds[8], (D,), 0.2, 1.0, (), jnp.float32),
        "norm2_gain": jnp.clip(1.0 + 0.1 * jax.random.normal(seeds[9], (D,), jnp.float32), 0.5, 1.5),
        "norm2_bias": bell_draw(seeds[10], (D,), 0.2, 1.0, (), jnp.float32),
        "up_weight": bell_draw(seeds[11], (D, FF), D ** -0.5, 0.21875),
        "up_bias": bell_draw(seeds[12], (FF,), 0.2, 1.0, (), jnp.float32),
        "down_weight": bell_draw(seeds[13], (FF, D), FF ** -0.5, 0.109375),
        "down_bias": bell_draw(seeds[14], (D,), 0.2, 1.0, (), jnp.float32),
    }


@jax.custom_vjp
def low(v):
    return lax.optimization_barrier(v.astype(jnp.bfloat16)).astype(jnp.float32)

@jax.custom_vjp
def low_back(v):
    return v

def low_keep(v):
    return (low(v), None)

def low_pass(kept, grad):
    return (grad,)

def back_keep(v):
    return (v, None)

def back_low(kept, grad):
    return (low(grad),)
low.defvjp(low_keep, low_pass)
low_back.defvjp(back_keep, back_low)
masked_value = -1e+30
epsilon = 1e-05
highest = lax.Precision.HIGHEST

def layer_norm(values, gain, bias):
    mean = lax.optimization_barrier(jnp.mean(values, axis=-1, keepdims=True))
    centred = values - mean
    spread = lax.optimization_barrier(jnp.mean(centred * centred, axis=-1, keepdims=True))
    return centred * lax.rsqrt(spread + epsilon) * gain + bias

def rotary_tables(length, width):
    places = jnp.arange(length, dtype=jnp.float32)[:, None]
    column = jnp.arange(width, dtype=jnp.int32) % HEAD
    index = (column % (HEAD // 2)).astype(jnp.float32)
    angle = places * jnp.exp(index * (-2.0 * math.log(10000.0) / HEAD))[None, :]
    return (jnp.cos(angle), jnp.sin(angle))

def turn(values):
    shape = values.shape
    split = values.reshape(shape[:-1] + (shape[-1] // HEAD, 2, HEAD // 2))
    turned = jnp.concatenate((-split[..., 1:, :], split[..., :1, :]), axis=-2)
    return turned.reshape(shape)

def softmax_rows(scores):
    top = lax.optimization_barrier(jnp.max(scores, axis=-1, keepdims=True))
    spread = jnp.exp(scores - top)
    return spread / lax.optimization_barrier(jnp.sum(spread, axis=-1, keepdims=True))

def sequence_forward(clean, noisy, size, weights):
    gain1, bias1, qkv_weight, qkv_bias, proj_weight, proj_bias, gain2, bias2, up_weight, up_bias, down_weight, down_bias = weights
    length, width = clean.shape
    cosine, sine = rotary_tables(length, width)
    blocks = jnp.arange(length, dtype=jnp.int32) // size
    same = blocks[:, None] == blocks[None, :]
    earlier = blocks[:, None] > blocks[None, :]
    factor = 1.0 / math.sqrt(HEAD)

    def project(rows):
        hidden = low(layer_norm(rows, gain1, bias1))
        mixed = low_back(jnp.dot(hidden, qkv_weight, precision=highest)) + qkv_bias
        query = mixed[:, :width]
        keys = mixed[:, width:2 * width]
        query = low(query * cosine + turn(query) * sine)
        keys = low(keys * cosine + turn(keys) * sine)
        values = low(mixed[:, 2 * width:])
        return (query, keys, values)

    def scores_of(query, keys, allowed):
        raw = jnp.einsum('qhd,khd->hqk', query.reshape(length, HEADS, HEAD), keys.reshape(length, HEADS, HEAD), precision=highest)
        return jnp.where(allowed[None], low_back(raw * factor), masked_value)

    def mix_values(probs, values):
        return jnp.einsum('hqk,khd->qhd', probs, values.reshape(length, HEADS, HEAD), precision=highest).reshape(length, width)

    def finish(rows, attended):
        attended = low(low_back(attended))
        middle = rows + low_back(jnp.dot(attended, proj_weight, precision=highest)) + proj_bias
        hidden = low(layer_norm(middle, gain2, bias2))
        upward = low_back(jnp.dot(hidden, up_weight, precision=highest)) + up_bias
        active = low(jax.nn.gelu(upward))
        return middle + jnp.dot(active, down_weight, precision=highest) + down_bias
    clean_q, clean_k, clean_v = project(clean)
    noisy_q, noisy_k, noisy_v = project(noisy)
    clean_p = low(softmax_rows(scores_of(clean_q, clean_k, same | earlier)))
    clean_o = mix_values(clean_p, clean_v)
    joint = jnp.concatenate((scores_of(noisy_q, noisy_k, same), scores_of(noisy_q, clean_k, earlier)), axis=-1)
    noisy_p = low(softmax_rows(joint))
    noisy_o = mix_values(noisy_p[..., :length], noisy_v) + mix_values(noisy_p[..., length:], clean_v)
    return (finish(clean, clean_o), finish(noisy, noisy_o))

def reference(layer_input, out_cotangent, block_size, norm1_gain, norm1_bias, qkv_weight, qkv_bias, proj_weight, proj_bias, norm2_gain, norm2_bias, up_weight, up_bias, down_weight, down_bias):
    weights = tuple((w.astype(jnp.float32) for w in (norm1_gain, norm1_bias, qkv_weight, qkv_bias, proj_weight, proj_bias, norm2_gain, norm2_bias, up_weight, up_bias, down_weight, down_bias)))
    inputs = layer_input.astype(jnp.float32)
    grads = out_cotangent.astype(jnp.float32)

    def step(total, item):
        clean, noisy, grad_clean, grad_noisy, size = item

        def forward(first, second, params):
            return sequence_forward(first, second, size, params)
        outputs, pull = jax.vjp(forward, clean, noisy, weights)
        back_clean, back_noisy, back_weights = pull((grad_clean, grad_noisy))
        total = jax.tree.map(jnp.add, total, back_weights)
        return (total, (outputs[0], outputs[1], back_clean, back_noisy))
    zeros = tuple((jnp.zeros_like(w) for w in weights))
    total, (out_clean, out_noisy, back_clean, back_noisy) = lax.scan(step, zeros, (inputs[0], inputs[1], grads[0], grads[1], block_size))
    layer_output = jnp.stack((out_clean, out_noisy)).astype(jnp.bfloat16)
    input_grad = jnp.stack((back_clean, back_noisy))
    return (layer_output, input_grad, total[0], total[1], total[2], total[3], total[4], total[5], total[6], total[7], total[8], total[9], total[10], total[11])
```

```python
from functools import partial
import math

import jax
import jax.numpy as jnp
from jax import lax
from jax.experimental import pallas as pl
from jax.experimental.pallas import tpu as pltpu
from jax.sharding import PartitionSpec as P
import numpy as np

HEAD = 64
PAIR = 2 * HEAD
ROWS = 256
TILE = 256

masked_value = -1e30
epsilon = 1e-05
low = jnp.bfloat16
wide = jnp.float32
score_scale = math.log2(math.e) / math.sqrt(HEAD)
ln2 = math.log(2.0)
gelu_c = math.sqrt(2.0 / math.pi)
gelu_k = 0.044715
mega = 1024 * 1024


def dot_nn(left, right):
    return lax.dot_general(left, right, (((1,), (0,)), ((), ())), preferred_element_type=wide)


def dot_nt(left, right):
    return lax.dot_general(left, right, (((1,), (1,)), ((), ())), preferred_element_type=wide)


def dot_tn(left, right):
    return lax.dot_general(left, right, (((0,), (0,)), ((), ())), preferred_element_type=wide)


def params(limit_mib):
    return pltpu.CompilerParams(
        dimension_semantics=("arbitrary",), vmem_limit_bytes=limit_mib * mega
    )


def cost(flops, nbytes, trans=0):
    return pl.CostEstimate(
        flops=int(flops), bytes_accessed=int(nbytes), transcendentals=int(trans)
    )


def whole_spec(shape):
    zeros = (0,) * len(shape)
    return pl.BlockSpec(shape, lambda *_: zeros, pipeline_mode=pl.Buffered(1))


def row_spec(width, rows=ROWS):
    return pl.BlockSpec((rows, width), lambda i: (i, 0))


def normalize(values):
    mean = jnp.mean(values, axis=-1, keepdims=True)
    centred = values - mean
    factor = lax.rsqrt(jnp.mean(centred * centred, axis=-1, keepdims=True) + epsilon)
    return (centred * factor, factor)


def norm_back(grad_normed, normed, factor):
    first = jnp.mean(grad_normed, axis=-1, keepdims=True)
    second = jnp.mean(grad_normed * normed, axis=-1, keepdims=True)
    return factor * (grad_normed - first - normed * second)


def rotary_tables(length):
    places = np.arange(length, dtype=np.float64)[:, None]
    column = np.arange(PAIR) % HEAD
    angle = places * (10000.0 ** (-2.0 * (column % (HEAD // 2)) / HEAD))[None, :]
    upper = (column >= HEAD // 2)[None, :]
    cosine, sine = np.cos(angle), np.sin(angle)
    tables = (cosine, np.where(upper, sine, 0.0), np.where(upper, 0.0, -sine))
    return tuple(jnp.asarray(t, dtype=wide) for t in tables)


def rotate(values, cosine, sine_a, sine_b):
    return (
        values * cosine
        + pltpu.roll(values, HEAD // 2, 1) * sine_a
        + pltpu.roll(values, PAIR - HEAD // 2, 1) * sine_b
    )


def rotate_back(values, cosine, sine_a, sine_b):
    return (
        values * cosine
        - pltpu.roll(values, HEAD // 2, 1) * sine_a
        - pltpu.roll(values, PAIR - HEAD // 2, 1) * sine_b
    )


def project_kernel(x_ref, w_ref, bias_ref, gain1_ref, bias1_ref, cos_ref, sa_ref, sb_ref,
                   h_ref, q_ref, k_ref, v_ref):
    width = x_ref.shape[1]
    normed, _ = normalize(x_ref[...].astype(wide))
    hidden = (normed * gain1_ref[...] + bias1_ref[...]).astype(low)
    h_ref[...] = hidden
    cosine, sa, sb = cos_ref[...], sa_ref[...], sb_ref[...]
    for out, part in ((q_ref, 0), (k_ref, 1), (v_ref, 2)):
        cols = slice(part * width, (part + 1) * width)
        mixed = dot_nn(hidden, w_ref[:, cols]) + bias_ref[:, cols]
        if part == 2:
            out[...] = mixed.astype(low)
            continue
        for group in range(width // PAIR):
            at = slice(group * PAIR, (group + 1) * PAIR)
            turned = rotate(mixed[:, at], cosine, sa, sb)
            if part == 0:
                turned = turned * score_scale
            out[:, at] = turned.astype(low)


def project_far_kernel(noisy_ref, x_ref, far_ref, wk_ref, wv_ref, bias_ref, gain1_ref, bias1_ref,
                       cos_ref, sa_ref, sb_ref, h_ref, k_ref, v_ref):
    width = x_ref.shape[1]
    source = jnp.where(noisy_ref[0] == 1, far_ref[...].astype(wide), x_ref[...].astype(wide))
    normed, _ = normalize(source)
    hidden = (normed * gain1_ref[...] + bias1_ref[...]).astype(low)
    h_ref[...] = hidden
    cosine, sa, sb = cos_ref[...], sa_ref[...], sb_ref[...]
    mixed = dot_nn(hidden, wk_ref[...]) + bias_ref[:, width : 2 * width]
    for group in range(width // PAIR):
        at = slice(group * PAIR, (group + 1) * PAIR)
        k_ref[:, at] = rotate(mixed[:, at], cosine, sa, sb).astype(low)
    mixed = dot_nn(hidden, wv_ref[...]) + bias_ref[:, 2 * width :]
    v_ref[...] = mixed.astype(low)


def project(x, weight, bias, gain1, bias1, tables):
    count, width = x.shape
    row = jax.ShapeDtypeStruct((count, width), low)
    return pl.pallas_call(
        project_kernel,
        grid=(count // ROWS,),
        in_specs=[
            row_spec(width),
            whole_spec(weight.shape),
            whole_spec(bias.shape),
            whole_spec(gain1.shape),
            whole_spec(bias1.shape),
            row_spec(PAIR),
            row_spec(PAIR),
            row_spec(PAIR),
        ],
        out_specs=[row_spec(width)] * 4,
        out_shape=[row] * 4,
        compiler_params=params(40),
        cost_estimate=cost(2 * count * width * 3 * width, 16e6),
        name="project",
    )(x, weight, bias, gain1, bias1, *tables)


def project_far(noisy, x, far, weight, bias, gain1, bias1, tables):
    count, width = x.shape
    row = jax.ShapeDtypeStruct((count, width), low)
    return pl.pallas_call(
        project_far_kernel,
        grid=(count // ROWS,),
        in_specs=[
            pl.BlockSpec(memory_space=pltpu.SMEM),
            row_spec(width),
            row_spec(width),
            pl.BlockSpec((width, width), lambda i: (0, 1), pipeline_mode=pl.Buffered(1)),
            pl.BlockSpec((width, width), lambda i: (0, 2), pipeline_mode=pl.Buffered(1)),
            whole_spec(bias.shape),
            whole_spec(gain1.shape),
            whole_spec(bias1.shape),
            row_spec(PAIR),
            row_spec(PAIR),
            row_spec(PAIR),
        ],
        out_specs=[row_spec(width)] * 3,
        out_shape=[row] * 3,
        compiler_params=params(40),
        cost_estimate=cost(2 * count * width * 2 * width, 12e6),
        name="project_far",
    )(noisy, x, far, weight, weight, bias, gain1, bias1, *tables)


def head_masks():
    lane = lax.broadcasted_iota(jnp.int32, (1, PAIR), 1)
    return (lane < HEAD, lane >= HEAD)


def attend_kernel(krow_ref, qcol_ref, q_ref, kn_ref, vn_ref, kf_ref, vf_ref, o_ref, lse_ref):
    length = q_ref.shape[0]
    kb, qb = krow_ref[...], qcol_ref[...]
    near = kb == qb
    far = kb < qb
    masks = head_masks()
    vf_t = vf_ref[...].astype(wide).T.astype(low)
    vn_t = vn_ref[...].astype(wide).T.astype(low)
    for tile in range(length // TILE):
        here = slice(tile * TILE, (tile + 1) * TILE)
        query = q_ref[here, :]
        pieces = []
        for head in range(2):
            rows = slice(head * HEAD, (head + 1) * HEAD)
            mine = jnp.where(masks[head], query, jnp.zeros_like(query))
            scores_near = dot_nt(kn_ref[here, :], mine)
            scores_diag = dot_nt(kf_ref[here, :], mine)
            diag = jnp.where(near, scores_near, jnp.where(far, scores_diag, masked_value))
            top = jnp.max(diag, axis=0, keepdims=True)
            if tile:
                past = dot_nt(kf_ref[: tile * TILE, :], mine)
                top = jnp.maximum(top, jnp.max(past, axis=0, keepdims=True))
            prob = jnp.exp2(diag - top)
            total = jnp.sum(prob, axis=0, keepdims=True)
            prob_near = jnp.where(near, prob, 0.0).astype(low)
            prob_far = jnp.where(near, 0.0, prob).astype(low)
            mixed = dot_nn(vn_t[rows, here], prob_near) + dot_nn(vf_t[rows, here], prob_far)
            if tile:
                prob = jnp.exp2(past - top)
                total = total + jnp.sum(prob, axis=0, keepdims=True)
                mixed = mixed + dot_nn(vf_t[rows, : tile * TILE], prob.astype(low))
            lse_ref[0, head : head + 1, here] = top + jnp.log2(total)
            pieces.append(mixed * (1.0 / total))
        o_ref[here, :] = jnp.concatenate(pieces, axis=0).T.astype(low)


def attend(krow, qcol, q, kn, vn, kf, vf):
    count, width = q.shape
    pairs = width // PAIR
    pair_spec = pl.BlockSpec((count, PAIR), lambda p: (0, p))
    return pl.pallas_call(
        attend_kernel,
        grid=(pairs,),
        in_specs=[whole_spec(krow.shape), whole_spec(qcol.shape)] + [pair_spec] * 5,
        out_specs=[pair_spec, pl.BlockSpec((1, 2, count), lambda p: (p, 0, 0))],
        out_shape=[
            jax.ShapeDtypeStruct((count, width), low),
            jax.ShapeDtypeStruct((pairs, 2, count), wide),
        ],
        compiler_params=params(48),
        cost_estimate=cost(20e9, 10e6, 6e6),
        name="attend",
    )(krow, qcol, q, kn, vn, kf, vf)


def middle_kernel(x_ref, o_ref, g_ref, wp_ref, bp_ref, gain2_ref, bias2_ref, wu_ref, bu_ref,
                  wd_ref, bd_ref, out_ref, h2_ref, a_ref, du_ref, dy_ref, dyl_ref, do_ref,
                  downb_ref, upb_ref, gain2g_ref, bias2g_ref, projb_ref):
    width = x_ref.shape[1]
    ff = wu_ref.shape[1]

    @pl.when(pl.program_id(0) == 0)
    def _():
        for ref in (downb_ref, upb_ref, gain2g_ref, bias2g_ref, projb_ref):
            ref[...] = jnp.zeros_like(ref)

    y = x_ref[...].astype(wide) + dot_nn(o_ref[...], wp_ref[...]) + bp_ref[...]
    normed, factor = normalize(y)
    hidden = (normed * gain2_ref[...] + bias2_ref[...]).astype(low)
    h2_ref[...] = hidden
    grad = g_ref[...]
    grad_wide = grad.astype(wide)
    result = y + bd_ref[...]
    dh2 = jnp.zeros_like(y)
    for part in range(ff // width):
        cols = slice(part * width, (part + 1) * width)
        up = dot_nn(hidden, wu_ref[:, cols]) + bu_ref[:, cols]
        da = dot_nt(grad, wd_ref[cols, :])
        square = up * up
        half = 0.5 + 0.5 * jnp.tanh(up * (gelu_c + (gelu_c * gelu_k) * square))
        active = (up * half).astype(low)
        slope = half + (up * (2.0 * gelu_c + (6.0 * gelu_c * gelu_k) * square)) * (
            half * (1.0 - half)
        )
        du = da * slope
        du_low = du.astype(low)
        a_ref[:, cols] = active
        du_ref[:, cols] = du_low
        upb_ref[:, cols] += jnp.sum(du, axis=0, keepdims=True)
        result = result + dot_nn(active, wd_ref[cols, :])
        dh2 = dh2 + dot_nt(du_low, wu_ref[:, cols])
    out_ref[...] = result.astype(low)
    downb_ref[...] += jnp.sum(grad_wide, axis=0, keepdims=True)
    gain2g_ref[...] += jnp.sum(dh2 * normed, axis=0, keepdims=True)
    bias2g_ref[...] += jnp.sum(dh2, axis=0, keepdims=True)
    dy = grad_wide + norm_back(dh2 * gain2_ref[...], normed, factor)
    dy_ref[...] = dy
    projb_ref[...] += jnp.sum(dy, axis=0, keepdims=True)
    dy_low = dy.astype(low)
    dyl_ref[...] = dy_low
    do_ref[...] = dot_nt(dy_low, wp_ref[...]).astype(low)


def middle(x, o, g, wp, bp, gain2, bias2, wu, bu, wd, bd):
    count, width = x.shape
    ff = wu.shape[1]
    row = jax.ShapeDtypeStruct((count, width), low)
    vec = jax.ShapeDtypeStruct((1, width), wide)
    return pl.pallas_call(
        middle_kernel,
        grid=(count // ROWS,),
        in_specs=[row_spec(width)] * 3
        + [whole_spec(a.shape) for a in (wp, bp, gain2, bias2, wu, bu, wd, bd)],
        out_specs=[
            row_spec(width),
            row_spec(width),
            row_spec(ff),
            row_spec(ff),
            row_spec(width),
            row_spec(width),
            row_spec(width),
        ]
        + [whole_spec((1, n)) for n in (width, ff, width, width, width)],
        out_shape=[
            row,
            row,
            jax.ShapeDtypeStruct((count, ff), low),
            jax.ShapeDtypeStruct((count, ff), low),
            jax.ShapeDtypeStruct((count, width), wide),
            row,
            row,
            vec,
            jax.ShapeDtypeStruct((1, ff), wide),
            vec,
            vec,
            vec,
        ],
        compiler_params=params(52),
        cost_estimate=cost(2 * count * width * (4 * ff + 2 * width), 40e6, count * ff),
        name="middle",
    )(x, o, g, wp, bp, gain2, bias2, wu, bu, wd, bd)


def outer_kernel(left_ref, right_ref, out_ref):
    out_ref[...] = dot_tn(left_ref[...], right_ref[...]).astype(low)


def outer(left, right, tile=256):
    count, tall = left.shape
    width = right.shape[1]
    return pl.pallas_call(
        outer_kernel,
        grid=(tall // tile,),
        in_specs=[pl.BlockSpec((count, tile), lambda i: (0, i)), whole_spec(right.shape)],
        out_specs=pl.BlockSpec((tile, width), lambda i: (i, 0)),
        out_shape=jax.ShapeDtypeStruct((tall, width), low),
        compiler_params=params(48),
        cost_estimate=cost(2 * count * tall * width, 2 * (tall * width + count * (tall + width))),
        name="outer",
    )(left, right)


def attend_back_kernel(krow_ref, qcol_ref, q_ref, kn_ref, vn_ref, kf_ref, vf_ref, do_ref, o_ref,
                       lse_ref, cos_ref, sa_ref, sb_ref,
                       dq_ref, dkn_ref, dvn_ref, dkf_ref, dvf_ref, sums_ref,
                       dqt_acc, dkf_acc, dvf_acc):
    length = q_ref.shape[0]
    kb, qb = krow_ref[...], qcol_ref[...]
    near = kb == qb
    far = kb < qb
    masks = head_masks()
    kf_t = kf_ref[...].astype(wide).T.astype(low)
    kn_t = kn_ref[...].astype(wide).T.astype(low)
    product = do_ref[...].astype(wide) * o_ref[...].astype(wide)
    high = product.astype(low)
    rest = (product - high.astype(wide)).astype(low)
    head_row = lax.broadcasted_iota(jnp.int32, (8, PAIR), 0)
    head_lane = lax.broadcasted_iota(jnp.int32, (8, PAIR), 1) // HEAD
    picker = jnp.where(head_row == head_lane, 1.0, 0.0).astype(low)
    deltas = dot_nt(picker, high) + dot_nt(picker, rest)
    cosine, sa, sb = cos_ref[...], sa_ref[...], sb_ref[...]
    sum_q = jnp.zeros((1, PAIR), wide)
    sum_kn = jnp.zeros((1, PAIR), wide)
    sum_vn = jnp.zeros((1, PAIR), wide)
    for tile in range(length // TILE):
        here = slice(tile * TILE, (tile + 1) * TILE)
        query, grad = q_ref[here, :], do_ref[here, :]
        dkn = jnp.zeros((TILE, PAIR), wide)
        dvn = jnp.zeros((TILE, PAIR), wide)
        for head in range(2):
            rows = slice(head * HEAD, (head + 1) * HEAD)
            mine = jnp.where(masks[head], query, jnp.zeros_like(query))
            grad_mine = jnp.where(masks[head], grad, jnp.zeros_like(grad))
            lse = lse_ref[0, head : head + 1, here]
            delta = deltas[head : head + 1, here]
            scores = jnp.where(
                near,
                dot_nt(kn_ref[here, :], mine),
                jnp.where(far, dot_nt(kf_ref[here, :], mine), masked_value),
            )
            prob = jnp.exp2(scores - lse)
            dprob = jnp.where(
                near, dot_nt(vn_ref[here, :], grad_mine), dot_nt(vf_ref[here, :], grad_mine)
            )
            dscore = prob * (dprob - delta)
            prob_near = jnp.where(near, prob, 0.0).astype(low)
            prob_far = jnp.where(near, 0.0, prob).astype(low)
            ds_near = jnp.where(near, dscore, 0.0).astype(low)
            ds_far = jnp.where(near, 0.0, dscore).astype(low)
            dkn = dkn + dot_nn(ds_near, mine)
            dvn = dvn + dot_nn(prob_near, grad_mine)
            dkf = dot_nn(ds_far, mine)
            dvf = dot_nn(prob_far, grad_mine)
            if head:
                dkf_acc[here, :] += dkf
                dvf_acc[here, :] += dvf
            else:
                dkf_acc[here, :] = dkf
                dvf_acc[here, :] = dvf
            dqt = dot_nn(kn_t[rows, here], ds_near) + dot_nn(kf_t[rows, here], ds_far)
            for other in range(tile):
                there = slice(other * TILE, (other + 1) * TILE)
                prob = jnp.exp2(dot_nt(kf_ref[there, :], mine) - lse)
                dprob = dot_nt(vf_ref[there, :], grad_mine)
                dscore = (prob * (dprob - delta)).astype(low)
                dkf_acc[there, :] += dot_nn(dscore, mine)
                dvf_acc[there, :] += dot_nn(prob.astype(low), grad_mine)
                dqt = dqt + dot_nn(kf_t[rows, there], dscore)
            dqt_acc[rows, :] = dqt
        dq = dqt_acc[...].T * (1.0 / math.sqrt(HEAD))
        dq = rotate_back(dq, cosine[here], sa[here], sb[here])
        dq_ref[here, :] = dq.astype(low)
        sum_q = sum_q + jnp.sum(dq, axis=0, keepdims=True)
        dkn = rotate_back(dkn * ln2, cosine[here], sa[here], sb[here])
        dkn_ref[here, :] = dkn.astype(low)
        sum_kn = sum_kn + jnp.sum(dkn, axis=0, keepdims=True)
        dvn_ref[here, :] = dvn.astype(low)
        sum_vn = sum_vn + jnp.sum(dvn, axis=0, keepdims=True)
    dkf = rotate_back(dkf_acc[...] * ln2, cosine, sa, sb)
    dvf = dvf_acc[...]
    dkf_ref[...] = dkf.astype(low)
    dvf_ref[...] = dvf.astype(low)
    sums_ref[0, 0:1, :] = sum_q
    sums_ref[0, 1:2, :] = sum_kn + jnp.sum(dkf, axis=0, keepdims=True)
    sums_ref[0, 2:3, :] = sum_vn + jnp.sum(dvf, axis=0, keepdims=True)


def attend_back(krow, qcol, q, kn, vn, kf, vf, do, o, lse, tables):
    count, width = q.shape
    pairs = width // PAIR
    pair_spec = pl.BlockSpec((count, PAIR), lambda p: (0, p))
    row = jax.ShapeDtypeStruct((count, width), low)
    return pl.pallas_call(
        attend_back_kernel,
        grid=(pairs,),
        in_specs=[whole_spec(krow.shape), whole_spec(qcol.shape)]
        + [pair_spec] * 7
        + [pl.BlockSpec((1, 2, count), lambda p: (p, 0, 0))]
        + [whole_spec(t.shape) for t in tables],
        out_specs=[pair_spec] * 5 + [pl.BlockSpec((1, 3, PAIR), lambda p: (p, 0, 0))],
        out_shape=[row] * 5 + [jax.ShapeDtypeStruct((pairs, 3, PAIR), wide)],
        scratch_shapes=[
            pltpu.VMEM((PAIR, TILE), wide),
            pltpu.VMEM((count, PAIR), wide),
            pltpu.VMEM((count, PAIR), wide),
        ],
        compiler_params=params(48),
        cost_estimate=cost(50e9, 20e6, 6e6),
        name="attend_back",
    )(krow, qcol, q, kn, vn, kf, vf, do, o, lse, *tables)


def outer_qkv_kernel(h_ref, hf_ref, dq_ref, dk_ref, dv_ref, dkf_ref, dvf_ref, out_ref):
    width = dq_ref.shape[1]
    own, clean = h_ref[...], hf_ref[...]
    out_ref[:, :width] = dot_tn(own, dq_ref[...]).astype(low)
    out_ref[:, width : 2 * width] = (
        dot_tn(own, dk_ref[...]) + dot_tn(clean, dkf_ref[...])
    ).astype(low)
    out_ref[:, 2 * width :] = (
        dot_tn(own, dv_ref[...]) + dot_tn(clean, dvf_ref[...])
    ).astype(low)


def outer_qkv(h, hf, dq, dk, dv, dkf, dvf, tile=256):
    count, width = h.shape
    return pl.pallas_call(
        outer_qkv_kernel,
        grid=(width // tile,),
        in_specs=[pl.BlockSpec((count, tile), lambda i: (0, i))] * 2
        + [whole_spec((count, width))] * 5,
        out_specs=pl.BlockSpec((tile, 3 * width), lambda i: (i, 0)),
        out_shape=jax.ShapeDtypeStruct((width, 3 * width), low),
        compiler_params=params(48),
        cost_estimate=cost(10 * count * width * width, 16e6),
        name="outer_qkv",
    )(h, hf, dq, dk, dv, dkf, dvf)


def project_back_kernel(noisy_ref, x_ref, far_ref, dy_ref, dq_ref, dk_ref, dv_ref, dkf_ref,
                        dvf_ref, w_ref, gain1_ref, dx_ref, dfar_ref, gain1g_ref, bias1g_ref):
    width = x_ref.shape[1]

    @pl.when(pl.program_id(0) == 0)
    def _():
        for ref in (gain1g_ref, bias1g_ref):
            ref[...] = jnp.zeros_like(ref)

    parts = [w_ref[:, i * width : (i + 1) * width] for i in range(3)]
    noisy = noisy_ref[0] == 1
    own = x_ref[...].astype(wide)
    source = jnp.where(noisy, far_ref[...].astype(wide), own)
    normed, factor = normalize(own)
    normed_far, factor_far = normalize(source)
    dh = dot_nt(dq_ref[...], parts[0]) + dot_nt(dk_ref[...], parts[1]) + dot_nt(
        dv_ref[...], parts[2]
    )
    dh_far = dot_nt(dkf_ref[...], parts[1]) + dot_nt(dvf_ref[...], parts[2])
    gain1g_ref[...] += jnp.sum(dh * normed + dh_far * normed_far, axis=0, keepdims=True)
    bias1g_ref[...] += jnp.sum(dh + dh_far, axis=0, keepdims=True)
    gain = gain1_ref[...]
    dx = dy_ref[...] + norm_back(dh * gain, normed, factor)
    dfar = norm_back(dh_far * gain, normed_far, factor_far)
    dx_ref[...] = dx + jnp.where(noisy, 0.0, dfar)
    dfar_ref[...] = dfar.astype(low)


def project_back(noisy, x, far, dy, dq, dk, dv, dkf, dvf, weight, gain1):
    count, width = x.shape
    vec = jax.ShapeDtypeStruct((1, width), wide)
    return pl.pallas_call(
        project_back_kernel,
        grid=(count // ROWS,),
        in_specs=[pl.BlockSpec(memory_space=pltpu.SMEM)]
        + [row_spec(width)] * 8
        + [whole_spec(weight.shape), whole_spec(gain1.shape)],
        out_specs=[row_spec(width), row_spec(width), whole_spec((1, width)), whole_spec((1, width))],
        out_shape=[
            jax.ShapeDtypeStruct((count, width), wide),
            jax.ShapeDtypeStruct((count, width), low),
            vec,
            vec,
        ],
        compiler_params=params(48),
        cost_estimate=cost(10 * count * width * width, 24e6),
        name="project_back",
    )(noisy, x, far, dy, dq, dk, dv, dkf, dvf, weight, gain1)


def reduce_rows(part):
    part = lax.psum_scatter(part, "batch", scatter_dimension=0, tiled=True)
    return lax.psum(part, "stream").astype(wide)


def reduce_vectors(vectors, batch):
    packed = jnp.concatenate([v.reshape(batch, -1) for v in vectors], axis=1)
    width = packed.shape[1]
    padded = jnp.pad(packed, ((0, 0), (0, -width % 128)))
    summed = lax.psum_scatter(padded, "batch", scatter_dimension=0, tiled=True)
    summed = lax.psum(summed, "stream")[0]
    sizes = [v.size // batch for v in vectors]
    starts = [sum(sizes[:i]) for i in range(len(sizes))]
    return [summed[s : s + n] for s, n in zip(starts, sizes)]


def local(
    layer_input,
    out_cotangent,
    block_size,
    norm1_gain,
    norm1_bias,
    qkv_weight,
    qkv_bias,
    proj_weight,
    proj_bias,
    norm2_gain,
    norm2_bias,
    up_weight,
    up_bias,
    down_weight,
    down_bias,
):
    length, width = layer_input.shape[2:]
    batch = lax.axis_size("batch")
    noisy = lax.axis_index("stream").astype(jnp.int32).reshape(1)
    x = layer_input.reshape(length, width)
    g = out_cotangent.reshape(length, width)
    far_x = lax.ppermute(x, "stream", [(0, 1)])
    tables = rotary_tables(length)
    qkv_bias, norm1_gain, norm1_bias, proj_bias, norm2_gain, norm2_bias, up_bias, down_bias = (
        v.reshape(1, -1)
        for v in (
            qkv_bias,
            norm1_gain,
            norm1_bias,
            proj_bias,
            norm2_gain,
            norm2_bias,
            up_bias,
            down_bias,
        )
    )
    places = jnp.arange(TILE, dtype=jnp.int32) // block_size[0]
    krow, qcol = places[:, None], places[None, :]
    h, q, k, v = project(x, qkv_weight, qkv_bias, norm1_gain, norm1_bias, tables)
    hf, kf, vf = project_far(
        noisy, x, far_x, qkv_weight, qkv_bias, norm1_gain, norm1_bias, tables
    )
    o, lse = attend(krow, qcol, q, k, v, kf, vf)
    (
        out,
        h2,
        a,
        du,
        dy,
        dy_low,
        do,
        downb_grad,
        upb_grad,
        gain2_grad,
        bias2_grad,
        projb_grad,
    ) = middle(
        x,
        o,
        g,
        proj_weight,
        proj_bias,
        norm2_gain,
        norm2_bias,
        up_weight,
        up_bias,
        down_weight,
        down_bias,
    )
    downw = outer(a, g)
    upw = outer(h2, du)
    projw = outer(o, dy_low)
    dq, dk, dv, dkf, dvf, sums = attend_back(krow, qcol, q, k, v, kf, vf, do, o, lse, tables)
    qkvb_grad = sums.transpose(1, 0, 2).reshape(1, -1)
    qkvw = outer_qkv(h, hf, dq, dk, dv, dkf, dvf)
    dx, dfar, gain1_grad, bias1_grad = project_back(
        noisy, x, far_x, dy, dq, dk, dv, dkf, dvf, qkv_weight, norm1_gain
    )
    input_grad = (dx + lax.ppermute(dfar, "stream", [(1, 0)]).astype(wide)).reshape(
        layer_input.shape
    )
    downw_grad, upw_grad, projw_grad, qkvw_grad = (
        reduce_rows(part) for part in (downw, upw, projw, qkvw)
    )
    (
        gain1_grad,
        bias1_grad,
        qkvb_grad,
        projb_grad,
        gain2_grad,
        bias2_grad,
        upb_grad,
        downb_grad,
    ) = reduce_vectors(
        (
            gain1_grad,
            bias1_grad,
            qkvb_grad,
            projb_grad,
            gain2_grad,
            bias2_grad,
            upb_grad,
            downb_grad,
        ),
        batch,
    )
    return (
        out.reshape(layer_input.shape),
        input_grad,
        gain1_grad,
        bias1_grad,
        qkvw_grad,
        qkvb_grad,
        projw_grad,
        projb_grad,
        gain2_grad,
        bias2_grad,
        upw_grad,
        upb_grad,
        downw_grad,
        downb_grad,
    )


def solution(mesh):
    rows = P("stream", "batch", None, None)
    return jax.shard_map(
        local,
        mesh=mesh,
        in_specs=(rows, rows, P("batch")) + (P(),) * 12,
        out_specs=(
            rows,
            rows,
            P("batch"),
            P("batch"),
            P("batch", None),
            P("batch"),
            P("batch", None),
            P("batch"),
            P("batch"),
            P("batch"),
            P("batch", None),
            P("batch"),
            P("batch", None),
            P("batch"),
        ),
        check_vma=False,
    )
```

```python
from functools import partial
import math

import jax
import jax.numpy as jnp
from jax import lax
from jax.experimental import pallas as pl
from jax.experimental.pallas import tpu as pltpu
from jax.sharding import PartitionSpec as P
import numpy as np

HEAD = 64
PAIR = 2 * HEAD
ROWS = 256
TILE = 256
CUTS = 3
full_vmem = 60

masked_value = -1e30
epsilon = 1e-05
low = jnp.bfloat16
wide = jnp.float32
score_scale = math.log2(math.e) / math.sqrt(HEAD)
ln2 = math.log(2.0)
gelu_c = math.sqrt(2.0 / math.pi)
gelu_k = 0.044715
mega = 1024 * 1024


def dot_nn(left, right):
    return lax.dot_general(left, right, (((1,), (0,)), ((), ())), preferred_element_type=wide)


def dot_nt(left, right):
    return lax.dot_general(left, right, (((1,), (1,)), ((), ())), preferred_element_type=wide)


def dot_tn(left, right):
    return lax.dot_general(left, right, (((0,), (0,)), ((), ())), preferred_element_type=wide)


def params(limit_mib):
    return pltpu.CompilerParams(
        dimension_semantics=("arbitrary",), vmem_limit_bytes=limit_mib * mega
    )


def cost(flops, nbytes, trans=0):
    return pl.CostEstimate(
        flops=int(flops), bytes_accessed=int(nbytes), transcendentals=int(trans)
    )


def ordered_call(kernel, after, grid, in_specs, operands, prefetch=(), work=4e9, **rest):
    skip = len(prefetch) + len(operands)

    def body(*refs):
        kernel(*refs[:skip], *refs[skip + len(after) :])

    out_specs = rest.pop("out_specs")
    scratch = rest.pop("scratch_shapes", [])
    return pl.pallas_call(
        body,
        grid_spec=pltpu.PrefetchScalarGridSpec(
            num_scalar_prefetch=len(prefetch),
            grid=grid,
            in_specs=list(in_specs) + [pl.BlockSpec(memory_space=pl.ANY)] * len(after),
            out_specs=out_specs,
            scratch_shapes=scratch,
        ),
        compiler_params=pltpu.CompilerParams(
            dimension_semantics=("arbitrary",) * len(grid), vmem_limit_bytes=full_vmem * mega
        ),
        cost_estimate=cost(work, 1000),
        **rest,
    )(*prefetch, *operands, *after)


def whole_spec(shape):
    zeros = (0,) * len(shape)
    return pl.BlockSpec(shape, lambda *_: zeros, pipeline_mode=pl.Buffered(1))


def row_spec(width, rows=ROWS):
    return pl.BlockSpec((rows, width), lambda i: (i, 0))


def normalize(values):
    mean = jnp.mean(values, axis=-1, keepdims=True)
    centred = values - mean
    factor = lax.rsqrt(jnp.mean(centred * centred, axis=-1, keepdims=True) + epsilon)
    return (centred * factor, factor)


def norm_back(grad_normed, normed, factor):
    first = jnp.mean(grad_normed, axis=-1, keepdims=True)
    second = jnp.mean(grad_normed * normed, axis=-1, keepdims=True)
    return factor * (grad_normed - first - normed * second)


def rotary_tables(length):
    places = np.arange(length, dtype=np.float64)[:, None]
    column = np.arange(PAIR) % HEAD
    angle = places * (10000.0 ** (-2.0 * (column % (HEAD // 2)) / HEAD))[None, :]
    upper = (column >= HEAD // 2)[None, :]
    cosine, sine = np.cos(angle), np.sin(angle)
    tables = (cosine, np.where(upper, sine, 0.0), np.where(upper, 0.0, -sine))
    return tuple(jnp.asarray(t, dtype=wide) for t in tables)


def rotate(values, cosine, sine_a, sine_b):
    return (
        values * cosine
        + pltpu.roll(values, HEAD // 2, 1) * sine_a
        + pltpu.roll(values, PAIR - HEAD // 2, 1) * sine_b
    )


def rotate_back(values, cosine, sine_a, sine_b):
    return (
        values * cosine
        - pltpu.roll(values, HEAD // 2, 1) * sine_a
        - pltpu.roll(values, PAIR - HEAD // 2, 1) * sine_b
    )


def project_kernel(x_ref, w_ref, bias_ref, gain1_ref, bias1_ref, cos_ref, sa_ref, sb_ref,
                   h_ref, q_ref, k_ref, v_ref):
    width = x_ref.shape[1]
    normed, _ = normalize(x_ref[...].astype(wide))
    hidden = (normed * gain1_ref[...] + bias1_ref[...]).astype(low)
    h_ref[...] = hidden
    cosine, sa, sb = cos_ref[...], sa_ref[...], sb_ref[...]
    for out, part in ((q_ref, 0), (k_ref, 1), (v_ref, 2)):
        cols = slice(part * width, (part + 1) * width)
        mixed = dot_nn(hidden, w_ref[:, cols]) + bias_ref[:, cols]
        if part == 2:
            out[...] = mixed.astype(low)
            continue
        for group in range(width // PAIR):
            at = slice(group * PAIR, (group + 1) * PAIR)
            turned = rotate(mixed[:, at], cosine, sa, sb)
            if part == 0:
                turned = turned * score_scale
            out[:, at] = turned.astype(low)


def project_far_kernel(noisy_ref, x_ref, far_ref, wk_ref, wv_ref, bias_ref, gain1_ref, bias1_ref,
                       cos_ref, sa_ref, sb_ref, h_ref, k_ref, v_ref):
    width = x_ref.shape[1]
    source = jnp.where(noisy_ref[0] == 1, far_ref[...].astype(wide), x_ref[...].astype(wide))
    normed, _ = normalize(source)
    hidden = (normed * gain1_ref[...] + bias1_ref[...]).astype(low)
    h_ref[...] = hidden
    cosine, sa, sb = cos_ref[...], sa_ref[...], sb_ref[...]
    mixed = dot_nn(hidden, wk_ref[...]) + bias_ref[:, width : 2 * width]
    for group in range(width // PAIR):
        at = slice(group * PAIR, (group + 1) * PAIR)
        k_ref[:, at] = rotate(mixed[:, at], cosine, sa, sb).astype(low)
    mixed = dot_nn(hidden, wv_ref[...]) + bias_ref[:, 2 * width :]
    v_ref[...] = mixed.astype(low)


def project(x, weight, bias, gain1, bias1, tables):
    count, width = x.shape
    row = jax.ShapeDtypeStruct((count, width), low)
    return pl.pallas_call(
        project_kernel,
        grid=(count // ROWS,),
        in_specs=[
            row_spec(width),
            whole_spec(weight.shape),
            whole_spec(bias.shape),
            whole_spec(gain1.shape),
            whole_spec(bias1.shape),
            row_spec(PAIR),
            row_spec(PAIR),
            row_spec(PAIR),
        ],
        out_specs=[row_spec(width)] * 4,
        out_shape=[row] * 4,
        compiler_params=params(full_vmem),
        cost_estimate=cost(2 * count * width * 3 * width, 16e6),
        name="project",
    )(x, weight, bias, gain1, bias1, *tables)


def project_far(noisy, x, far, weight, bias, gain1, bias1, tables):
    count, width = x.shape
    row = jax.ShapeDtypeStruct((count, width), low)
    return pl.pallas_call(
        project_far_kernel,
        grid=(count // ROWS,),
        in_specs=[
            pl.BlockSpec(memory_space=pltpu.SMEM),
            row_spec(width),
            row_spec(width),
            pl.BlockSpec((width, width), lambda i: (0, 1), pipeline_mode=pl.Buffered(1)),
            pl.BlockSpec((width, width), lambda i: (0, 2), pipeline_mode=pl.Buffered(1)),
            whole_spec(bias.shape),
            whole_spec(gain1.shape),
            whole_spec(bias1.shape),
            row_spec(PAIR),
            row_spec(PAIR),
            row_spec(PAIR),
        ],
        out_specs=[row_spec(width)] * 3,
        out_shape=[row] * 3,
        compiler_params=params(full_vmem),
        cost_estimate=cost(2 * count * width * 2 * width, 12e6),
        name="project_far",
    )(noisy, x, far, weight, weight, bias, gain1, bias1, *tables)


def head_masks():
    lane = lax.broadcasted_iota(jnp.int32, (1, PAIR), 1)
    return (lane < HEAD, lane >= HEAD)


def attend_kernel(krow_ref, qcol_ref, q_ref, kn_ref, vn_ref, kf_ref, vf_ref, o_ref, lse_ref):
    length = q_ref.shape[0]
    kb, qb = krow_ref[...], qcol_ref[...]
    near = kb == qb
    far = kb < qb
    masks = head_masks()
    vf_t = vf_ref[...].astype(wide).T.astype(low)
    vn_t = vn_ref[...].astype(wide).T.astype(low)
    for tile in range(length // TILE):
        here = slice(tile * TILE, (tile + 1) * TILE)
        query = q_ref[here, :]
        pieces = []
        for head in range(2):
            rows = slice(head * HEAD, (head + 1) * HEAD)
            mine = jnp.where(masks[head], query, jnp.zeros_like(query))
            scores_near = dot_nt(kn_ref[here, :], mine)
            scores_diag = dot_nt(kf_ref[here, :], mine)
            diag = jnp.where(near, scores_near, jnp.where(far, scores_diag, masked_value))
            top = jnp.max(diag, axis=0, keepdims=True)
            if tile:
                past = dot_nt(kf_ref[: tile * TILE, :], mine)
                top = jnp.maximum(top, jnp.max(past, axis=0, keepdims=True))
            prob = jnp.exp2(diag - top)
            total = jnp.sum(prob, axis=0, keepdims=True)
            prob_near = jnp.where(near, prob, 0.0).astype(low)
            prob_far = jnp.where(near, 0.0, prob).astype(low)
            mixed = dot_nn(vn_t[rows, here], prob_near) + dot_nn(vf_t[rows, here], prob_far)
            if tile:
                prob = jnp.exp2(past - top)
                total = total + jnp.sum(prob, axis=0, keepdims=True)
                mixed = mixed + dot_nn(vf_t[rows, : tile * TILE], prob.astype(low))
            lse_ref[0, head : head + 1, here] = top + jnp.log2(total)
            pieces.append(mixed * (1.0 / total))
        o_ref[here, :] = jnp.concatenate(pieces, axis=0).T.astype(low)


def attend(krow, qcol, q, kn, vn, kf, vf):
    count, width = q.shape
    pairs = width // PAIR
    pair_spec = pl.BlockSpec((count, PAIR), lambda p: (0, p))
    return pl.pallas_call(
        attend_kernel,
        grid=(pairs,),
        in_specs=[whole_spec(krow.shape), whole_spec(qcol.shape)] + [pair_spec] * 5,
        out_specs=[pair_spec, pl.BlockSpec((1, 2, count), lambda p: (p, 0, 0))],
        out_shape=[
            jax.ShapeDtypeStruct((count, width), low),
            jax.ShapeDtypeStruct((pairs, 2, count), wide),
        ],
        compiler_params=params(full_vmem),
        cost_estimate=cost(20e9, 10e6, 6e6),
        name="attend",
    )(krow, qcol, q, kn, vn, kf, vf)


def middle_kernel(x_ref, o_ref, g_ref, wp_ref, bp_ref, gain2_ref, bias2_ref, wu_ref, bu_ref,
                  wd_ref, bd_ref, out_ref, h2_ref, a_ref, du_ref, dy_ref, dyl_ref, do_ref,
                  downb_ref, upb_ref, gain2g_ref, bias2g_ref, projb_ref):
    width = x_ref.shape[1]
    ff = wu_ref.shape[1]

    @pl.when(pl.program_id(0) == 0)
    def _():
        for ref in (downb_ref, upb_ref, gain2g_ref, bias2g_ref, projb_ref):
            ref[...] = jnp.zeros_like(ref)

    y = x_ref[...].astype(wide) + dot_nn(o_ref[...], wp_ref[...]) + bp_ref[...]
    normed, factor = normalize(y)
    hidden = (normed * gain2_ref[...] + bias2_ref[...]).astype(low)
    h2_ref[...] = hidden
    grad = g_ref[...]
    grad_wide = grad.astype(wide)
    result = y + bd_ref[...]
    dh2 = jnp.zeros_like(y)
    for part in range(ff // width):
        cols = slice(part * width, (part + 1) * width)
        up = dot_nn(hidden, wu_ref[:, cols]) + bu_ref[:, cols]
        da = dot_nt(grad, wd_ref[cols, :])
        square = up * up
        half = 0.5 + 0.5 * jnp.tanh(up * (gelu_c + (gelu_c * gelu_k) * square))
        active = (up * half).astype(low)
        slope = half + (up * (2.0 * gelu_c + (6.0 * gelu_c * gelu_k) * square)) * (
            half * (1.0 - half)
        )
        du = da * slope
        du_low = du.astype(low)
        a_ref[:, cols] = active
        du_ref[:, cols] = du_low
        upb_ref[:, cols] += jnp.sum(du, axis=0, keepdims=True)
        result = result + dot_nn(active, wd_ref[cols, :])
        dh2 = dh2 + dot_nt(du_low, wu_ref[:, cols])
    out_ref[...] = result.astype(low)
    downb_ref[...] += jnp.sum(grad_wide, axis=0, keepdims=True)
    gain2g_ref[...] += jnp.sum(dh2 * normed, axis=0, keepdims=True)
    bias2g_ref[...] += jnp.sum(dh2, axis=0, keepdims=True)
    dy = grad_wide + norm_back(dh2 * gain2_ref[...], normed, factor)
    dy_ref[...] = dy
    projb_ref[...] += jnp.sum(dy, axis=0, keepdims=True)
    dy_low = dy.astype(low)
    dyl_ref[...] = dy_low
    do_ref[...] = dot_nt(dy_low, wp_ref[...]).astype(low)


def middle(x, o, g, wp, bp, gain2, bias2, wu, bu, wd, bd):
    count, width = x.shape
    ff = wu.shape[1]
    row = jax.ShapeDtypeStruct((count, width), low)
    vec = jax.ShapeDtypeStruct((1, width), wide)
    return pl.pallas_call(
        middle_kernel,
        grid=(count // ROWS,),
        in_specs=[row_spec(width)] * 3
        + [whole_spec(a.shape) for a in (wp, bp, gain2, bias2, wu, bu, wd, bd)],
        out_specs=[
            row_spec(width),
            row_spec(width),
            row_spec(ff),
            row_spec(ff),
            row_spec(width),
            row_spec(width),
            row_spec(width),
        ]
        + [whole_spec((1, n)) for n in (width, ff, width, width, width)],
        out_shape=[
            row,
            row,
            jax.ShapeDtypeStruct((count, ff), low),
            jax.ShapeDtypeStruct((count, ff), low),
            jax.ShapeDtypeStruct((count, width), wide),
            row,
            row,
            vec,
            jax.ShapeDtypeStruct((1, ff), wide),
            vec,
            vec,
            vec,
        ],
        compiler_params=params(full_vmem),
        cost_estimate=cost(1000, 1000),
        name="middle",
    )(x, o, g, wp, bp, gain2, bias2, wu, bu, wd, bd)


def stages_of(batch):
    bits = list(range(1, batch.bit_length() - 1))
    stages = [bits[:1]]
    rest = bits[1:]
    while rest:
        stages.append(rest[:2])
        rest = rest[2:]
    return [s for s in stages if s]


def mask_of(bits, digit):
    return sum(((digit >> i) & 1) << bit for i, bit in enumerate(bits))


def places_of(batch, me):
    relative = jnp.arange(0, batch, 2, dtype=jnp.int32) ^ (me - me % 2)
    place = jnp.zeros_like(relative)
    for bits in stages_of(batch):
        place = place * 2 ** len(bits)
        for i, bit in enumerate(bits):
            place = place + (((relative >> bit) & 1) << i)
    return place


def store_shards(place_ref, core_ref, result, keep_ref, send_ref, first=0):
    shards = keep_ref.shape[0]
    rows = result.shape[0] // (2 * shards)
    core = core_ref[0] == 0
    for pair in range(shards):
        even = result[2 * pair * rows : (2 * pair + 1) * rows]
        odd = result[(2 * pair + 1) * rows : (2 * pair + 2) * rows]
        at = place_ref[first + pair]
        keep_ref[at] = jnp.where(core, even, odd).astype(low)
        send_ref[at] = jnp.where(core, odd, even).astype(low)


def split_shards(full, place, core):
    batch = 2 * place.shape[0]
    shards = full.reshape((batch // 2, 2, full.shape[0] // batch) + full.shape[1:])
    order = jnp.argsort(place)
    shards = jnp.take(shards, order, axis=0)
    return (
        jnp.where(core == 0, shards[:, 0], shards[:, 1]),
        jnp.where(core == 0, shards[:, 1], shards[:, 0]),
    )


def aligned(tall, batch):
    return tall % batch == 0 and (tall // batch) % 16 == 0


def down_kernel(place_ref, core_ref, left_ref, right_ref, keep_ref, send_ref):
    rows = left_ref.shape[1] // 2
    result = dot_tn(left_ref[...], right_ref[...])
    core = core_ref[0] == 0
    keep_ref[0] = jnp.where(core, result[:rows], result[rows:]).astype(low)
    send_ref[0] = jnp.where(core, result[rows:], result[:rows]).astype(low)


def down_plain_kernel(left_ref, right_ref, out_ref):
    out_ref[...] = dot_tn(left_ref[...], right_ref[...]).astype(low)


def outer_down(a, g, place, core):
    count, tall = a.shape
    width = g.shape[1]
    batch = 2 * place.shape[0]
    spent = cost(1000, 1000)
    rows = tall // batch
    if not aligned(tall, batch) or (2 * rows) % 128:
        tile = 256
        full = pl.pallas_call(
            down_plain_kernel,
            grid=(tall // tile,),
            in_specs=[pl.BlockSpec((count, tile), lambda i: (0, i)), whole_spec(g.shape)],
            out_specs=pl.BlockSpec((tile, width), lambda i: (i, 0)),
            out_shape=jax.ShapeDtypeStruct((tall, width), low),
            compiler_params=params(full_vmem),
            cost_estimate=spent,
            name="outer_down",
        )(a, g)
        return split_shards(full, place, core[0])
    half = jax.ShapeDtypeStruct((batch // 2, rows, width), low)
    half_spec = pl.BlockSpec((1, rows, width), lambda i, p, c: (p[i], 0, 0))
    return pl.pallas_call(
        down_kernel,
        grid_spec=pltpu.PrefetchScalarGridSpec(
            num_scalar_prefetch=2,
            grid=(batch // 2,),
            in_specs=[
                pl.BlockSpec((count, 2 * rows), lambda i, p, c: (0, i)),
                whole_spec(g.shape),
            ],
            out_specs=[half_spec, half_spec],
        ),
        out_shape=[half, half],
        compiler_params=params(full_vmem),
        cost_estimate=spent,
        name="outer_down",
    )(place, core, a, g)


def write_columns(place_ref, core_ref, result, outs):
    if len(outs) == 1:
        outs[0][...] = result.astype(low)
    else:
        store_shards(place_ref, core_ref, result, *outs)


def columns_call(kernel, place, core, operands, in_specs, columns, steps, width, scratch, name, after, work):
    batch = 2 * place.shape[0]
    if aligned(width, batch):
        rows = width // batch
        half = jax.ShapeDtypeStruct((batch // 2, rows, columns), low)
        out_shape = [half, half]
        out_specs = [
            pl.BlockSpec((batch // 2, rows, columns // steps), lambda i, p, c: (0, 0, i))
        ] * 2
    else:
        out_shape = [jax.ShapeDtypeStruct((width, columns), low)]
        out_specs = [pl.BlockSpec((width, columns // steps), lambda i, p, c: (0, i))]
    result = ordered_call(
        kernel,
        after,
        (steps,),
        in_specs,
        operands,
        (place, core),
        out_specs=out_specs,
        scratch_shapes=scratch,
        out_shape=out_shape,
        work=work,
        name=name,
    )
    if len(result) == 1:
        return split_shards(result[0], place, core[0])
    return result


def up_kernel(steps, place_ref, core_ref, h2_ref, o_ref, du_ref, dy_ref, *outs):
    *outs, left_t = outs
    step = pl.program_id(0)

    @pl.when(step == 0)
    def _():
        left_t[...] = h2_ref[...].T

    @pl.when(step == steps)
    def _():
        left_t[...] = o_ref[...].T

    @pl.when(step < steps)
    def _():
        write_columns(place_ref, core_ref, dot_nn(left_t[...], du_ref[...]), outs)

    @pl.when(step >= steps)
    def _():
        write_columns(place_ref, core_ref, dot_nn(left_t[...], dy_ref[...]), outs)


def outer_up(h2, du, o, dy_low, place, core, after):
    count, width = h2.shape
    ff = du.shape[1]
    steps = ff // width
    return columns_call(
        partial(up_kernel, steps),
        place,
        core,
        (h2, o, du, dy_low),
        [
            whole_spec(h2.shape),
            whole_spec(o.shape),
            pl.BlockSpec((count, width), lambda i, p, c: (0, jnp.minimum(i, steps - 1))),
            whole_spec(dy_low.shape),
        ],
        ff + width,
        steps + 1,
        width,
        [pltpu.VMEM((width, count), low)],
        "outer_up",
        after,
        2e10,
    )


def attend_back_kernel(krow_ref, qcol_ref, q_ref, kn_ref, vn_ref, kf_ref, vf_ref, do_ref, o_ref,
                       lse_ref, cos_ref, sa_ref, sb_ref,
                       own_ref, clean_ref, sums_ref, dqt_acc, dkf_acc, dvf_acc):
    length = q_ref.shape[0]
    kb, qb = krow_ref[...], qcol_ref[...]
    near = kb == qb
    far = kb < qb
    masks = head_masks()
    kf_t = kf_ref[...].astype(wide).T.astype(low)
    kn_t = kn_ref[...].astype(wide).T.astype(low)
    product = do_ref[...].astype(wide) * o_ref[...].astype(wide)
    high = product.astype(low)
    rest = (product - high.astype(wide)).astype(low)
    head_row = lax.broadcasted_iota(jnp.int32, (8, PAIR), 0)
    head_lane = lax.broadcasted_iota(jnp.int32, (8, PAIR), 1) // HEAD
    picker = jnp.where(head_row == head_lane, 1.0, 0.0).astype(low)
    deltas = dot_nt(picker, high) + dot_nt(picker, rest)
    cosine, sa, sb = cos_ref[...], sa_ref[...], sb_ref[...]
    sum_q = jnp.zeros((1, PAIR), wide)
    sum_kn = jnp.zeros((1, PAIR), wide)
    sum_vn = jnp.zeros((1, PAIR), wide)
    for tile in range(length // TILE):
        here = slice(tile * TILE, (tile + 1) * TILE)
        query, grad = q_ref[here, :], do_ref[here, :]
        dkn = jnp.zeros((TILE, PAIR), wide)
        dvn = jnp.zeros((TILE, PAIR), wide)
        for head in range(2):
            rows = slice(head * HEAD, (head + 1) * HEAD)
            mine = jnp.where(masks[head], query, jnp.zeros_like(query))
            grad_mine = jnp.where(masks[head], grad, jnp.zeros_like(grad))
            lse = lse_ref[0, head : head + 1, here]
            delta = deltas[head : head + 1, here]
            scores = jnp.where(
                near,
                dot_nt(kn_ref[here, :], mine),
                jnp.where(far, dot_nt(kf_ref[here, :], mine), masked_value),
            )
            prob = jnp.exp2(scores - lse)
            dprob = jnp.where(
                near, dot_nt(vn_ref[here, :], grad_mine), dot_nt(vf_ref[here, :], grad_mine)
            )
            dscore = prob * (dprob - delta)
            prob_near = jnp.where(near, prob, 0.0).astype(low)
            prob_far = jnp.where(near, 0.0, prob).astype(low)
            ds_near = jnp.where(near, dscore, 0.0).astype(low)
            ds_far = jnp.where(near, 0.0, dscore).astype(low)
            dkn = dkn + dot_nn(ds_near, mine)
            dvn = dvn + dot_nn(prob_near, grad_mine)
            dkf = dot_nn(ds_far, mine)
            dvf = dot_nn(prob_far, grad_mine)
            if head:
                dkf_acc[here, :] += dkf
                dvf_acc[here, :] += dvf
            else:
                dkf_acc[here, :] = dkf
                dvf_acc[here, :] = dvf
            dqt = dot_nn(kn_t[rows, here], ds_near) + dot_nn(kf_t[rows, here], ds_far)
            for other in range(tile):
                there = slice(other * TILE, (other + 1) * TILE)
                prob = jnp.exp2(dot_nt(kf_ref[there, :], mine) - lse)
                dprob = dot_nt(vf_ref[there, :], grad_mine)
                dscore = (prob * (dprob - delta)).astype(low)
                dkf_acc[there, :] += dot_nn(dscore, mine)
                dvf_acc[there, :] += dot_nn(prob.astype(low), grad_mine)
                dqt = dqt + dot_nn(kf_t[rows, there], dscore)
            dqt_acc[rows, :] = dqt
        dq = dqt_acc[...].T * (1.0 / math.sqrt(HEAD))
        dq = rotate_back(dq, cosine[here], sa[here], sb[here])
        own_ref[0, here, :] = dq.astype(low)
        sum_q = sum_q + jnp.sum(dq, axis=0, keepdims=True)
        dkn = rotate_back(dkn * ln2, cosine[here], sa[here], sb[here])
        own_ref[1, here, :] = dkn.astype(low)
        sum_kn = sum_kn + jnp.sum(dkn, axis=0, keepdims=True)
        own_ref[2, here, :] = dvn.astype(low)
        sum_vn = sum_vn + jnp.sum(dvn, axis=0, keepdims=True)
    dkf = rotate_back(dkf_acc[...] * ln2, cosine, sa, sb)
    dvf = dvf_acc[...]
    clean_ref[0] = dkf.astype(low)
    clean_ref[1] = dvf.astype(low)
    sums_ref[0, 0:1, :] = sum_q
    sums_ref[0, 1:2, :] = sum_kn + jnp.sum(dkf, axis=0, keepdims=True)
    sums_ref[0, 2:3, :] = sum_vn + jnp.sum(dvf, axis=0, keepdims=True)


def attend_back(krow, qcol, q, kn, vn, kf, vf, do, o, lse, tables, first, pairs, after, work):
    count = q.shape[0]
    pair_spec = pl.BlockSpec((count, PAIR), lambda p: (0, p + first))
    width = pairs * PAIR
    return ordered_call(
        attend_back_kernel,
        after,
        (pairs,),
        [whole_spec(krow.shape), whole_spec(qcol.shape)]
        + [pair_spec] * 7
        + [pl.BlockSpec((1, 2, count), lambda p: (p + first, 0, 0))]
        + [whole_spec(t.shape) for t in tables],
        (krow, qcol, q, kn, vn, kf, vf, do, o, lse, *tables),
        out_specs=[
            pl.BlockSpec((3, count, PAIR), lambda p: (0, 0, p)),
            pl.BlockSpec((2, count, PAIR), lambda p: (0, 0, p)),
            pl.BlockSpec((1, 3, PAIR), lambda p: (p, 0, 0)),
        ],
        out_shape=[
            jax.ShapeDtypeStruct((3, count, width), low),
            jax.ShapeDtypeStruct((2, count, width), low),
            jax.ShapeDtypeStruct((pairs, 3, PAIR), wide),
        ],
        scratch_shapes=[
            pltpu.VMEM((PAIR, TILE), wide),
            pltpu.VMEM((count, PAIR), wide),
            pltpu.VMEM((count, PAIR), wide),
        ],
        work=work,
        name="attend_back",
    )


def qkv_kernel(cuts, place_ref, core_ref, h_ref, hf_ref, *rest):
    own, clean = rest[:cuts], rest[cuts : 2 * cuts]
    outs, (own_t, clean_t) = rest[2 * cuts : -2], rest[-2:]
    step = pl.program_id(0)

    @pl.when(step == 0)
    def _():
        own_t[...] = h_ref[...].T
        clean_t[...] = hf_ref[...].T
        right = jnp.concatenate([r[0] for r in own], axis=1)
        write_columns(place_ref, core_ref, dot_nn(own_t[...], right), outs)

    @pl.when(step > 0)
    def _():
        right = jnp.concatenate([r[0] for r in own], axis=1)
        right_clean = jnp.concatenate([r[0] for r in clean], axis=1)
        result = dot_nn(own_t[...], right) + dot_nn(clean_t[...], right_clean)
        write_columns(place_ref, core_ref, result, outs)


def outer_qkv(h, hf, own, clean, place, core, after):
    count, width = h.shape
    return columns_call(
        partial(qkv_kernel, len(own)),
        place,
        core,
        (h, hf, *own, *clean),
        [whole_spec(h.shape)] * 2
        + [pl.BlockSpec((1, count, r.shape[2]), lambda i, p, c: (i, 0, 0)) for r in own]
        + [
            pl.BlockSpec((1, count, r.shape[2]), lambda i, p, c: (jnp.maximum(i - 1, 0), 0, 0))
            for r in clean
        ],
        3 * width,
        3,
        width,
        [pltpu.VMEM((width, count), low)] * 2,
        "outer_qkv",
        after,
        2e9,
    )


def weight_parts(w_ref, part, cuts):
    width = w_ref.shape[0]
    step = width // cuts
    base = part * width
    return [w_ref[:, base + i * step : base + (i + 1) * step] for i in range(cuts)]


def project_far_back_kernel(cuts, noisy_ref, x_ref, far_ref, *rest):
    clean = rest[:cuts]
    w_ref, gain1_ref, dfar_ref, gain1g_ref, bias1g_ref = rest[cuts:]

    @pl.when(pl.program_id(0) == 0)
    def _():
        for ref in (gain1g_ref, bias1g_ref):
            ref[...] = jnp.zeros_like(ref)

    noisy = noisy_ref[0] == 1
    source = jnp.where(noisy, far_ref[...].astype(wide), x_ref[...].astype(wide))
    normed, factor = normalize(source)
    dh = jnp.zeros_like(source)
    for part in range(2):
        grads = jnp.concatenate([c[part] for c in clean], axis=1)
        dh = dh + dot_nt(grads, weight_parts(w_ref, part + 1, 1)[0])
    gain1g_ref[...] += jnp.sum(dh * normed, axis=0, keepdims=True)
    bias1g_ref[...] += jnp.sum(dh, axis=0, keepdims=True)
    dfar_ref[...] = norm_back(dh * gain1_ref[...], normed, factor).astype(low)


def project_far_back(noisy, x, far, clean, weight, gain1, after):
    count, width = x.shape
    vec = jax.ShapeDtypeStruct((1, width), wide)
    return ordered_call(
        partial(project_far_back_kernel, len(clean)),
        after,
        (count // ROWS,),
        [pl.BlockSpec(memory_space=pltpu.SMEM)]
        + [row_spec(width)] * 2
        + [pl.BlockSpec((2, ROWS, c.shape[2]), lambda i: (0, i, 0)) for c in clean]
        + [whole_spec(weight.shape), whole_spec(gain1.shape)],
        (noisy, x, far, *clean, weight, gain1),
        out_specs=[row_spec(width), whole_spec((1, width)), whole_spec((1, width))],
        out_shape=[jax.ShapeDtypeStruct((count, width), low), vec, vec],
        work=2e10,
        name="project_far_back",
    )


def project_back_kernel(cuts, x_ref, dy_ref, *rest):
    own = rest[:cuts]
    w_ref, gain1_ref, gainf_ref, biasf_ref, dx_ref, gain1g_ref, bias1g_ref = rest[cuts:]

    @pl.when(pl.program_id(0) == 0)
    def _():
        gain1g_ref[...] = gainf_ref[...]
        bias1g_ref[...] = biasf_ref[...]

    normed, factor = normalize(x_ref[...].astype(wide))
    dh = jnp.zeros_like(dy_ref)
    for part in range(3):
        grads = jnp.concatenate([c[part] for c in own], axis=1)
        dh = dh + dot_nt(grads, weight_parts(w_ref, part, 1)[0])
    gain1g_ref[...] += jnp.sum(dh * normed, axis=0, keepdims=True)
    bias1g_ref[...] += jnp.sum(dh, axis=0, keepdims=True)
    dx_ref[...] = dy_ref[...] + norm_back(dh * gain1_ref[...], normed, factor)


def project_back(x, dy, own, weight, gain1, gain_far, bias_far, after):
    count, width = x.shape
    vec = jax.ShapeDtypeStruct((1, width), wide)
    return ordered_call(
        partial(project_back_kernel, len(own)),
        after,
        (count // ROWS,),
        [row_spec(width)] * 2
        + [pl.BlockSpec((3, ROWS, c.shape[2]), lambda i: (0, i, 0)) for c in own]
        + [whole_spec(weight.shape)]
        + [whole_spec(gain1.shape)] * 3,
        (x, dy, *own, weight, gain1, gain_far, bias_far),
        out_specs=[row_spec(width), whole_spec((1, width)), whole_spec((1, width))],
        out_shape=[jax.ShapeDtypeStruct((count, width), wide), vec, vec],
        work=2e9,
        name="project_back",
    )


def flip(values, mask):
    batch = lax.axis_size("batch")
    return lax.ppermute(values, "batch", [(i, i ^ mask) for i in range(batch)])


def flip_stream(values):
    return lax.ppermute(values, "stream", [(0, 1), (1, 0)])


def total(terms):
    result = terms[0].astype(wide)
    for term in terms[1:]:
        result = result + term.astype(wide)
    return result


def combine_kernel(terms, pieces, *refs):
    ins, outs = refs[: terms * pieces], refs[terms * pieces :]
    for piece, out in enumerate(outs):
        out[...] = total([r[...] for r in ins[piece * terms : (piece + 1) * terms]]).astype(low)


def combine(terms, firsts, size, after, name):
    _, rows, columns = terms[0].shape
    block = 16
    if rows % block:
        block = rows
    else:
        while rows % (2 * block) == 0 and block * columns < 100000:
            block *= 2
        if rows // block == 3 and len(firsts) == 1:
            block = rows

    def spec(first):
        return pl.BlockSpec((1, block, columns), lambda i, j: (first + i, j, 0))

    return ordered_call(
        partial(combine_kernel, len(terms), len(firsts)),
        after,
        (size, rows // block),
        [spec(first) for first in firsts for _ in terms],
        [t for _ in firsts for t in terms],
        out_specs=[spec(0)] * len(firsts),
        out_shape=[jax.ShapeDtypeStruct((size, rows, columns), low)] * len(firsts),
        work=5e8,
        name=name,
    )


class Reduction:
    def __init__(self, name, shards):
        keep, send = shards
        self.name = name
        self.terms = [keep, flip(send, 1)]
        self.stages = stages_of(2 * keep.shape[0])
        self.size = keep.shape[0]

    def step(self, after):
        bits = self.stages.pop(0)
        parts = 2 ** len(bits)
        size = self.size // parts
        pieces = combine(
            self.terms, [j * size for j in range(1, parts)], size, after, "combine_" + self.name
        )
        arrived = [flip(p, mask_of(bits, j + 1)) for j, p in enumerate(pieces)]
        self.terms = self.terms + arrived
        self.size = size
        return pieces[:1]

    def last(self, after):
        while self.stages:
            after = self.step(after)
        (self.mine,) = combine(self.terms, [0], 1, after, "combine_" + self.name)
        self.other = flip_stream(self.mine)
        return [self.mine]

    def result(self, first, count):
        at = slice(first, first + count)
        return self.mine[0][:, at].astype(wide) + self.other[0][:, at].astype(wide)


def reduce_group(keep, send):
    batch = lax.axis_size("batch")
    terms = [keep, flip(send, 1)]
    for bits in stages_of(batch):
        parts = 2 ** len(bits)
        size = terms[0].shape[0] // parts
        arrived = [
            flip(total([t[j * size : (j + 1) * size] for t in terms]), mask_of(bits, j))
            for j in range(1, parts)
        ]
        terms = [t[:size] for t in terms] + arrived
    mine = total(terms)
    return (mine + flip_stream(mine))[0]


def reduce_vectors(vectors, place, core):
    batch = 2 * place.shape[0]
    packed = jnp.concatenate([v.reshape(batch, -1) for v in vectors], axis=1)
    keep, send = split_shards(packed, place, core[0])
    summed = reduce_group(keep, send)[0]
    sizes = [v.size // batch for v in vectors]
    starts = [sum(sizes[:i]) for i in range(len(sizes))]
    return [summed[s : s + n] for s, n in zip(starts, sizes)]


def local(
    layer_input,
    out_cotangent,
    block_size,
    norm1_gain,
    norm1_bias,
    qkv_weight,
    qkv_bias,
    proj_weight,
    proj_bias,
    norm2_gain,
    norm2_bias,
    up_weight,
    up_bias,
    down_weight,
    down_bias,
):
    length, width = layer_input.shape[2:]
    batch = lax.axis_size("batch")
    noisy = lax.axis_index("stream").astype(jnp.int32).reshape(1)
    x = layer_input.reshape(length, width)
    g = out_cotangent.reshape(length, width)
    far_x = lax.ppermute(x, "stream", [(0, 1)])
    tables = rotary_tables(length)
    qkv_bias, norm1_gain, norm1_bias, proj_bias, norm2_gain, norm2_bias, up_bias, down_bias = (
        v.reshape(1, -1)
        for v in (
            qkv_bias,
            norm1_gain,
            norm1_bias,
            proj_bias,
            norm2_gain,
            norm2_bias,
            up_bias,
            down_bias,
        )
    )
    places = jnp.arange(TILE, dtype=jnp.int32) // block_size[0]
    krow, qcol = places[:, None], places[None, :]
    me = lax.axis_index("batch").astype(jnp.int32)
    place, core = places_of(batch, me), (me % 2).reshape(1)
    h, q, k, v = project(x, qkv_weight, qkv_bias, norm1_gain, norm1_bias, tables)
    hf, kf, vf = project_far(
        noisy, x, far_x, qkv_weight, qkv_bias, norm1_gain, norm1_bias, tables
    )
    o, lse = attend(krow, qcol, q, k, v, kf, vf)
    (
        out,
        h2,
        a,
        du,
        dy,
        dy_low,
        do,
        downb_grad,
        upb_grad,
        gain2_grad,
        bias2_grad,
        projb_grad,
    ) = middle(
        x,
        o,
        g,
        proj_weight,
        proj_bias,
        norm2_gain,
        norm2_bias,
        up_weight,
        up_bias,
        down_weight,
        down_bias,
    )
    downw = outer_down(a, g, place, core)
    upw = outer_up(h2, du, o, dy_low, place, core, downw[:1])
    pairs = width // PAIR // CUTS

    def back_part(i, after):
        return attend_back(
            krow, qcol, q, k, v, kf, vf, do, o, lse, tables, i * pairs, pairs, after,
            2e9 if i else 2e10,
        )

    down, up = Reduction("down", downw), Reduction("up", upw)
    backs = [back_part(0, down.step(upw[:1]))]
    backs.append(back_part(1, up.step(backs[0][:1])))
    backs.append(back_part(2, down.step(backs[1][:1])))
    own, clean = [b[0] for b in backs], [b[1] for b in backs]
    qkvb_grad = jnp.concatenate([b[2] for b in backs]).transpose(1, 0, 2).reshape(1, -1)
    qkvw = outer_qkv(h, hf, own, clean, place, core, [])
    qkv = Reduction("qkv", qkvw)
    dfar, gain_far, bias_far = project_far_back(
        noisy, x, far_x, clean, qkv_weight, norm1_gain, up.step(qkvw[:1])
    )
    back_x = lax.ppermute(dfar, "stream", [(1, 0)])
    after = qkv.step([dfar])
    after = down.last(after)
    dx, gain1_grad, bias1_grad = project_back(
        x, dy, own, qkv_weight, norm1_gain, gain_far, bias_far, after
    )
    after = qkv.step([dx])
    after = up.last(after)
    after = qkv.last(after)
    back_x = jnp.where(noisy[0] == 0, back_x.astype(wide) + dfar.astype(wide), 0.0)
    input_grad = (dx + back_x).reshape(layer_input.shape)
    ff = up_weight.shape[1]
    downw_grad = down.result(0, width)
    upw_grad, projw_grad = up.result(0, ff), up.result(ff, width)
    qkvw_grad = qkv.result(0, 3 * width)
    (
        gain1_grad,
        bias1_grad,
        qkvb_grad,
        projb_grad,
        gain2_grad,
        bias2_grad,
        upb_grad,
        downb_grad,
    ) = reduce_vectors(
        (
            gain1_grad,
            bias1_grad,
            qkvb_grad,
            projb_grad,
            gain2_grad,
            bias2_grad,
            upb_grad,
            downb_grad,
        ),
        place,
        core,
    )
    return (
        out.reshape(layer_input.shape),
        input_grad,
        gain1_grad,
        bias1_grad,
        qkvw_grad,
        qkvb_grad,
        projw_grad,
        projb_grad,
        gain2_grad,
        bias2_grad,
        upw_grad,
        upb_grad,
        downw_grad,
        downb_grad,
    )


def solution(mesh):
    rows = P("stream", "batch", None, None)
    return jax.shard_map(
        local,
        mesh=mesh,
        in_specs=(rows, rows, P("batch")) + (P(),) * 12,
        out_specs=(
            rows,
            rows,
            P("batch"),
            P("batch"),
            P("batch", None),
            P("batch"),
            P("batch", None),
            P("batch"),
            P("batch"),
            P("batch"),
            P("batch", None),
            P("batch"),
            P("batch", None),
            P("batch"),
        ),
        check_vma=False,
    )
```

```python
from functools import partial
import math

import jax
import jax.numpy as jnp
from jax import lax
from jax.experimental import pallas as pl
from jax.experimental.pallas import tpu as pltpu
from jax.sharding import PartitionSpec as P
import numpy as np

HEAD = 64
PAIR = 2 * HEAD
ROWS = 256
TILE = 256
HALVES = 2
CUTS = ((0, 1), (1, 3), (4, 2))
full_vmem = 60

masked_value = -1e30
epsilon = 1e-05
low = jnp.bfloat16
wide = jnp.float32
score_scale = math.log2(math.e) / math.sqrt(HEAD)
ln2 = math.log(2.0)
gelu_c = math.sqrt(2.0 / math.pi)
gelu_k = 0.044715
mega = 1024 * 1024


def dot_nn(left, right):
    return lax.dot_general(left, right, (((1,), (0,)), ((), ())), preferred_element_type=wide)


def dot_nt(left, right):
    return lax.dot_general(left, right, (((1,), (1,)), ((), ())), preferred_element_type=wide)


def dot_tn(left, right):
    return lax.dot_general(left, right, (((0,), (0,)), ((), ())), preferred_element_type=wide)


def params(limit_mib):
    return pltpu.CompilerParams(
        dimension_semantics=("arbitrary",), vmem_limit_bytes=limit_mib * mega
    )


def cost(flops, nbytes, trans=0):
    return pl.CostEstimate(
        flops=int(flops), bytes_accessed=int(nbytes), transcendentals=int(trans)
    )


def ordered_call(
    kernel, after, grid, in_specs, operands, prefetch=(), work=4e9, into=(), **rest
):
    skip = len(prefetch) + len(operands)
    after = list(into) + list(after)

    def body(*refs):
        kernel(*refs[:skip], *refs[skip + len(after) :])

    out_specs = rest.pop("out_specs")
    scratch = rest.pop("scratch_shapes", [])
    call = pl.pallas_call(
        body,
        grid_spec=pltpu.PrefetchScalarGridSpec(
            num_scalar_prefetch=len(prefetch),
            grid=grid,
            in_specs=list(in_specs) + [pl.BlockSpec(memory_space=pl.ANY)] * len(after),
            out_specs=out_specs,
            scratch_shapes=scratch,
        ),
        compiler_params=pltpu.CompilerParams(
            dimension_semantics=("arbitrary",) * len(grid), vmem_limit_bytes=full_vmem * mega
        ),
        cost_estimate=cost(work, 1000),
        input_output_aliases={skip + i: i for i in range(len(into))},
        **rest,
    )
    return call(*prefetch, *operands, *after)


def row_of(ref, at=slice(None)):
    return ref[at].reshape(1, -1)


def whole_spec(shape):
    zeros = (0,) * len(shape)
    return pl.BlockSpec(shape, lambda *_: zeros, pipeline_mode=pl.Buffered(1))


def row_spec(width, rows=ROWS):
    return pl.BlockSpec((rows, width), lambda i: (i, 0))


def normalize(values):
    mean = jnp.mean(values, axis=-1, keepdims=True)
    centred = values - mean
    factor = lax.rsqrt(jnp.mean(centred * centred, axis=-1, keepdims=True) + epsilon)
    return (centred * factor, factor)


def norm_back(grad_normed, normed, factor):
    first = jnp.mean(grad_normed, axis=-1, keepdims=True)
    second = jnp.mean(grad_normed * normed, axis=-1, keepdims=True)
    return factor * (grad_normed - first - normed * second)


def rotary_tables(length):
    places = np.arange(length, dtype=np.float64)[:, None]
    column = np.arange(PAIR) % HEAD
    angle = places * (10000.0 ** (-2.0 * (column % (HEAD // 2)) / HEAD))[None, :]
    upper = (column >= HEAD // 2)[None, :]
    cosine, sine = np.cos(angle), np.sin(angle)
    tables = (cosine, np.where(upper, sine, 0.0), np.where(upper, 0.0, -sine))
    return tuple(jnp.asarray(t, dtype=wide) for t in tables)


def rotate(values, cosine, sine_a, sine_b):
    return (
        values * cosine
        + pltpu.roll(values, HEAD // 2, 1) * sine_a
        + pltpu.roll(values, PAIR - HEAD // 2, 1) * sine_b
    )


def rotate_back(values, cosine, sine_a, sine_b):
    return (
        values * cosine
        - pltpu.roll(values, HEAD // 2, 1) * sine_a
        - pltpu.roll(values, PAIR - HEAD // 2, 1) * sine_b
    )


def project_kernel(x_ref, w_ref, bias_ref, gain1_ref, bias1_ref, cos_ref, sa_ref, sb_ref,
                   h_ref, q_ref, k_ref, v_ref):
    width = x_ref.shape[1]
    normed, _ = normalize(x_ref[...].astype(wide))
    hidden = (normed * row_of(gain1_ref) + row_of(bias1_ref)).astype(low)
    h_ref[...] = hidden
    cosine, sa, sb = cos_ref[...], sa_ref[...], sb_ref[...]
    for out, part in ((q_ref, 0), (k_ref, 1), (v_ref, 2)):
        cols = slice(part * width, (part + 1) * width)
        mixed = dot_nn(hidden, w_ref[:, cols]) + row_of(bias_ref, cols)
        if part == 2:
            out[...] = mixed.astype(low)
            continue
        for group in range(width // PAIR):
            at = slice(group * PAIR, (group + 1) * PAIR)
            turned = rotate(mixed[:, at], cosine, sa, sb)
            if part == 0:
                turned = turned * score_scale
            out[:, at] = turned.astype(low)


def project_far_kernel(noisy_ref, x_ref, far_ref, wk_ref, wv_ref, bias_ref, gain1_ref, bias1_ref,
                       cos_ref, sa_ref, sb_ref, h_ref, k_ref, v_ref):
    width = x_ref.shape[1]
    source = jnp.where(noisy_ref[0] == 1, far_ref[...].astype(wide), x_ref[...].astype(wide))
    normed, _ = normalize(source)
    hidden = (normed * row_of(gain1_ref) + row_of(bias1_ref)).astype(low)
    h_ref[...] = hidden
    cosine, sa, sb = cos_ref[...], sa_ref[...], sb_ref[...]
    mixed = dot_nn(hidden, wk_ref[...]) + row_of(bias_ref, slice(width, 2 * width))
    for group in range(width // PAIR):
        at = slice(group * PAIR, (group + 1) * PAIR)
        k_ref[:, at] = rotate(mixed[:, at], cosine, sa, sb).astype(low)
    mixed = dot_nn(hidden, wv_ref[...]) + row_of(bias_ref, slice(2 * width, None))
    v_ref[...] = mixed.astype(low)


def project(x, weight, bias, gain1, bias1, tables):
    count, width = x.shape
    row = jax.ShapeDtypeStruct((count, width), low)
    return pl.pallas_call(
        project_kernel,
        grid=(count // ROWS,),
        in_specs=[
            row_spec(width),
            whole_spec(weight.shape),
            whole_spec(bias.shape),
            whole_spec(gain1.shape),
            whole_spec(bias1.shape),
            row_spec(PAIR),
            row_spec(PAIR),
            row_spec(PAIR),
        ],
        out_specs=[row_spec(width)] * 4,
        out_shape=[row] * 4,
        compiler_params=params(full_vmem),
        cost_estimate=cost(2 * count * width * 3 * width, 16e6),
        name="project",
    )(x, weight, bias, gain1, bias1, *tables)


def project_far(noisy, x, far, weight, bias, gain1, bias1, tables, part, into):
    count, width = x.shape
    steps = far.shape[0] // ROWS
    row = jax.ShapeDtypeStruct((count, width), low)

    def part_rows(columns):
        return pl.BlockSpec((ROWS, columns), lambda i: (part * steps + i, 0))

    return ordered_call(
        project_far_kernel,
        [],
        (steps,),
        [
            pl.BlockSpec(memory_space=pltpu.SMEM),
            part_rows(width),
            row_spec(width),
            pl.BlockSpec((width, width), lambda i: (0, 1), pipeline_mode=pl.Buffered(1)),
            pl.BlockSpec((width, width), lambda i: (0, 2), pipeline_mode=pl.Buffered(1)),
            whole_spec(bias.shape),
            whole_spec(gain1.shape),
            whole_spec(bias1.shape),
            part_rows(PAIR),
            part_rows(PAIR),
            part_rows(PAIR),
        ],
        (noisy, x, far, weight, weight, bias, gain1, bias1, *tables),
        into=into,
        out_specs=[part_rows(width)] * 3,
        out_shape=[row] * 3,
        name="project_far",
    )


def block_masks(size_ref):
    key = lax.broadcasted_iota(jnp.int32, (TILE, TILE), 0)
    query = lax.broadcasted_iota(jnp.int32, (TILE, TILE), 1)
    near = (key ^ query) < size_ref[0]
    return near, key < query


def head_masks():
    lane = lax.broadcasted_iota(jnp.int32, (1, PAIR), 1)
    return (lane < HEAD, lane >= HEAD)


def attend_kernel(first, size_ref, q_ref, kn_ref, vn_ref, kf_ref, vf_ref, o_ref, lse_ref):
    near, far = block_masks(size_ref)
    masks = head_masks()
    vf_t = vf_ref[...].astype(wide).T.astype(low)
    vn_t = vn_ref[...].astype(wide).T.astype(low)
    for part in range(q_ref.shape[0] // TILE):
        tile = first + part
        here = slice(tile * TILE, (tile + 1) * TILE)
        own = slice(part * TILE, (part + 1) * TILE)
        query = q_ref[own, :]
        pieces = []
        for head in range(2):
            rows = slice(head * HEAD, (head + 1) * HEAD)
            mine = jnp.where(masks[head], query, jnp.zeros_like(query))
            scores_near = dot_nt(kn_ref[own, :], mine)
            scores_diag = dot_nt(kf_ref[here, :], mine)
            diag = jnp.where(near, scores_near, jnp.where(far, scores_diag, masked_value))
            top = jnp.max(diag, axis=0, keepdims=True)
            if tile:
                past = dot_nt(kf_ref[: tile * TILE, :], mine)
                top = jnp.maximum(top, jnp.max(past, axis=0, keepdims=True))
            prob = jnp.exp2(diag - top)
            total = jnp.sum(prob, axis=0, keepdims=True)
            prob_near = jnp.where(near, prob, 0.0).astype(low)
            prob_far = jnp.where(near, 0.0, prob).astype(low)
            mixed = dot_nn(vn_t[rows, own], prob_near) + dot_nn(vf_t[rows, here], prob_far)
            if tile:
                prob = jnp.exp2(past - top)
                total = total + jnp.sum(prob, axis=0, keepdims=True)
                mixed = mixed + dot_nn(vf_t[rows, : tile * TILE], prob.astype(low))
            lse_ref[0, head : head + 1, own] = top + jnp.log2(total)
            pieces.append(mixed * (1.0 / total))
        o_ref[own, :] = jnp.concatenate(pieces, axis=0).T.astype(low)


def attend(size, q, kn, vn, kf, vf, part, parts, into):
    count, width = q.shape
    pairs = width // PAIR
    rows = count // parts
    own_spec = pl.BlockSpec((rows, PAIR), lambda p: (part, p))
    far_spec = pl.BlockSpec(((part + 1) * rows, PAIR), lambda p: (0, p))
    return ordered_call(
        partial(attend_kernel, part * rows // TILE),
        [],
        (pairs,),
        [pl.BlockSpec(memory_space=pltpu.SMEM)] + [own_spec] * 3 + [far_spec] * 2,
        (size, q, kn, vn, kf, vf),
        into=into,
        out_specs=[own_spec, pl.BlockSpec((1, 2, rows), lambda p: (p, 0, part))],
        out_shape=[
            jax.ShapeDtypeStruct((count, width), low),
            jax.ShapeDtypeStruct((pairs, 2, count), wide),
        ],
        name="attend",
    )


def stages_of(batch):
    bits = list(range(1, batch.bit_length() - 1))
    stages = [bits[:1]]
    rest = bits[1:]
    while rest:
        stages.append(rest[:2])
        rest = rest[2:]
    return [s for s in stages if s]


def mask_of(bits, digit):
    return sum(((digit >> i) & 1) << bit for i, bit in enumerate(bits))


def places_of(batch, me):
    relative = jnp.arange(0, batch, 2, dtype=jnp.int32) ^ (me - me % 2)
    place = jnp.zeros_like(relative)
    for bits in stages_of(batch):
        place = place * 2 ** len(bits)
        for i, bit in enumerate(bits):
            place = place + (((relative >> bit) & 1) << i)
    return place


def store_shards(place_ref, core_ref, result, keep_ref, send_ref, columns=slice(None)):
    shards = keep_ref.shape[0]
    rows = result.shape[0] // (2 * shards)

    def store(first_ref, second_ref):
        for pair in range(shards):
            at = place_ref[pair]
            start = 2 * pair * rows
            first_ref[at, :, columns] = result[start : start + rows].astype(low)
            second_ref[at, :, columns] = result[start + rows : start + 2 * rows].astype(low)

    pl.when(core_ref[0] == 0)(lambda: store(keep_ref, send_ref))
    pl.when(core_ref[0] == 1)(lambda: store(send_ref, keep_ref))


def split_shards(full, place, core):
    batch = 2 * place.shape[0]
    shards = full.reshape((batch // 2, 2, full.shape[0] // batch) + full.shape[1:])
    order = jnp.argsort(place)
    shards = jnp.take(shards, order, axis=0)
    return (
        jnp.where(core == 0, shards[:, 0], shards[:, 1]),
        jnp.where(core == 0, shards[:, 1], shards[:, 0]),
    )


def aligned(tall, batch):
    return tall % batch == 0 and (tall // batch) % 16 == 0


def store_columns(place_ref, core_ref, result, outs, columns=slice(None)):
    if len(outs) == 1:
        outs[0][:, columns] = result.astype(low)
    else:
        store_shards(place_ref, core_ref, result, *outs, columns)


def store_tall(place_ref, core_ref, step, result, outs):
    if len(outs) == 1:
        outs[0][...] = result.astype(low)
        return
    rows = outs[0].shape[2]
    places = place_ref.shape[0] // 2

    def store(first_ref, second_ref):
        for x in range(2):
            at = place_ref[2 * step + x] // places
            start = 2 * x * rows
            first_ref[at, 0] = result[start : start + rows].astype(low)
            second_ref[at, 0] = result[start + rows : start + 2 * rows].astype(low)

    pl.when(core_ref[0] == 0)(lambda: store(*outs))
    pl.when(core_ref[0] == 1)(lambda: store(*outs[::-1]))


def middle_kernel(row_steps, down_steps, tall_outs, place_ref, core_ref, x_ref, o_ref, g_ref,
                  wp_ref, bp_ref, gain2_ref, bias2_ref, wu_ref, bu_ref, wd_ref, bd_ref,
                  out_ref, dy_ref, do_ref, sums_ref,
                  *rest):
    downs, ups = rest[:tall_outs], rest[tall_outs:-5]
    a_all, right_all, hidden_all, o_all, g_all = rest[-5:]
    width = x_ref.shape[1]
    ff = wu_ref.shape[1]
    step = pl.program_id(0)

    def add_sum(start, values):
        at = slice(start, start + values.shape[1])
        sums_ref[:, at] += jnp.sum(values, axis=0, keepdims=True)

    @pl.when(step == 0)
    def _():
        sums_ref[...] = jnp.zeros_like(sums_ref)

    @pl.when(step < row_steps)
    def _():
        rows = pl.ds(pl.multiple_of(step * ROWS, ROWS), ROWS)
        o_all[rows, :] = o_ref[...]
        y = x_ref[...].astype(wide) + dot_nn(o_ref[...], wp_ref[...]) + row_of(bp_ref)
        normed, factor = normalize(y)
        hidden = (normed * row_of(gain2_ref) + row_of(bias2_ref)).astype(low)
        hidden_all[rows, :] = hidden
        grad = g_ref[...]
        g_all[rows, :] = grad
        grad_wide = grad.astype(wide)
        result = y + row_of(bd_ref)
        dh2 = jnp.zeros_like(y)
        for part in range(ff // width):
            cols = slice(part * width, (part + 1) * width)
            up = dot_nn(hidden, wu_ref[:, cols]) + row_of(bu_ref, cols)
            da = dot_nt(grad, wd_ref[cols, :])
            square = up * up
            half = 0.5 + 0.5 * jnp.tanh(up * (gelu_c + (gelu_c * gelu_k) * square))
            active = (up * half).astype(low)
            slope = half + (up * (2.0 * gelu_c + (6.0 * gelu_c * gelu_k) * square)) * (
                half * (1.0 - half)
            )
            du = da * slope
            du_low = du.astype(low)
            a_all[rows, cols] = active
            right_all[rows, cols] = du_low
            add_sum(4 * width + part * width, du)
            result = result + dot_nn(active, wd_ref[cols, :])
            dh2 = dh2 + dot_nt(du_low, wu_ref[:, cols])
        out_ref[...] = result.astype(low)
        add_sum(0, grad_wide)
        add_sum(width, dh2 * normed)
        add_sum(2 * width, dh2)
        dy = grad_wide + norm_back(dh2 * row_of(gain2_ref), normed, factor)
        dy_ref[...] = dy
        add_sum(3 * width, dy)
        dy_low = dy.astype(low)
        right_all[rows, ff:] = dy_low
        do_ref[...] = dot_nt(dy_low, wp_ref[...]).astype(low)

    down_step = step - row_steps
    tile = ff // down_steps

    @pl.when((down_step >= 0) & (down_step < down_steps))
    def _():
        cols = pl.ds(pl.multiple_of(down_step * tile, 128), tile)
        store_tall(place_ref, core_ref, down_step, dot_tn(a_all[:, cols], g_all[...]), downs)

    up_step = down_step - down_steps
    up_steps = ff // width

    @pl.when((up_step >= 0) & (up_step < up_steps))
    def _():
        cols = pl.ds(pl.multiple_of(up_step * width, 128), width)
        store_columns(place_ref, core_ref, dot_tn(hidden_all[...], right_all[:, cols]), ups)

    @pl.when(up_step == up_steps)
    def _():
        store_columns(place_ref, core_ref, dot_tn(o_all[...], right_all[:, ff:]), ups)


def middle(place, core, x, o, g, wp, bp, gain2, bias2, wu, bu, wd, bd):
    count, width = x.shape
    ff = wu.shape[1]
    batch = 2 * place.shape[0]
    row_steps, up_steps = count // ROWS, ff // width + 1
    rows = ff // batch
    tall_aligned = aligned(ff, batch) and (4 * rows) % 128 == 0 and batch >= 8
    down_steps = batch // 4 if tall_aligned else ff // width

    def row(columns):
        return pl.BlockSpec((ROWS, columns), lambda i, p, c: (jnp.minimum(i, row_steps - 1), 0))

    def down_at(i):
        return jnp.clip(i - row_steps, 0, down_steps - 1)

    def up_at(i):
        return jnp.clip(i - row_steps - down_steps, 0, up_steps - 1)

    if tall_aligned:
        deep = batch // 4
        down_shape = [jax.ShapeDtypeStruct((2, deep, rows, width), low)] * 2
        down_specs = [
            pl.BlockSpec(
                (2, 1, rows, width), lambda i, p, c: (0, p[2 * down_at(i)] % deep, 0, 0)
            )
        ] * 2
    else:
        down_shape = [jax.ShapeDtypeStruct((ff, width), low)]
        down_specs = [pl.BlockSpec((ff // down_steps, width), lambda i, p, c: (down_at(i), 0))]
    if aligned(width, batch):
        shape = (batch // 2, width // batch)
        up_shape = [jax.ShapeDtypeStruct(shape + (ff + width,), low)] * 2
        up_specs = [pl.BlockSpec(shape + (width,), lambda i, p, c: (0, 0, up_at(i)))] * 2
    else:
        up_shape = [jax.ShapeDtypeStruct((width, ff + width), low)]
        up_specs = [pl.BlockSpec((width, width), lambda i, p, c: (0, up_at(i)))]
    sums = 4 * width + ff
    result = ordered_call(
        partial(middle_kernel, row_steps, down_steps, len(down_shape)),
        [],
        (row_steps + down_steps + up_steps,),
        [row(width)] * 3 + [whole_spec(a.shape) for a in (wp, bp, gain2, bias2, wu, bu, wd, bd)],
        (x, o, g, wp, bp, gain2, bias2, wu, bu, wd, bd),
        (place, core),
        out_specs=[row(width)] * 3
        + [whole_spec((1, sums))]
        + down_specs
        + up_specs,
        out_shape=[
            jax.ShapeDtypeStruct((count, width), low),
            jax.ShapeDtypeStruct((count, width), wide),
            jax.ShapeDtypeStruct((count, width), low),
        ]
        + [jax.ShapeDtypeStruct((1, sums), wide)]
        + down_shape
        + up_shape,
        scratch_shapes=[
            pltpu.VMEM((count, ff), low),
            pltpu.VMEM((count, ff + width), low),
            pltpu.VMEM((count, width), low),
            pltpu.VMEM((count, width), low),
            pltpu.VMEM((count, width), low),
        ],
        name="middle",
    )
    rest = result[4:]
    if tall_aligned:
        downw = [r.reshape(batch // 2, rows, width) for r in rest[:2]]
    else:
        downw = split_shards(rest[0], place, core[0])
    ups = rest[len(down_shape) :]
    upw = ups if len(ups) == 2 else split_shards(ups[0], place, core[0])
    return result[:4], downw, upw


def attend_back_kernel(size_ref, q_ref, kn_ref, vn_ref, kf_ref, vf_ref, do_ref, o_ref,
                       lse_ref, cos_ref, sa_ref, sb_ref,
                       own_ref, clean_ref, sums_ref, dqt_acc, dkf_acc, dvf_acc):
    length = q_ref.shape[0]
    near, far = block_masks(size_ref)
    masks = head_masks()
    kf_t = kf_ref[...].astype(wide).T.astype(low)
    kn_t = kn_ref[...].astype(wide).T.astype(low)
    product = do_ref[...].astype(wide) * o_ref[...].astype(wide)
    high = product.astype(low)
    rest = (product - high.astype(wide)).astype(low)
    head_row = lax.broadcasted_iota(jnp.int32, (8, PAIR), 0)
    head_lane = lax.broadcasted_iota(jnp.int32, (8, PAIR), 1) // HEAD
    picker = jnp.where(head_row == head_lane, 1.0, 0.0).astype(low)
    deltas = dot_nt(picker, high) + dot_nt(picker, rest)
    cosine, sa, sb = cos_ref[...], sa_ref[...], sb_ref[...]
    sum_q = jnp.zeros((1, PAIR), wide)
    sum_kn = jnp.zeros((1, PAIR), wide)
    sum_vn = jnp.zeros((1, PAIR), wide)
    for tile in range(length // TILE):
        here = slice(tile * TILE, (tile + 1) * TILE)
        query, grad = q_ref[here, :], do_ref[here, :]
        dkn = jnp.zeros((TILE, PAIR), wide)
        dvn = jnp.zeros((TILE, PAIR), wide)
        for head in range(2):
            rows = slice(head * HEAD, (head + 1) * HEAD)
            mine = jnp.where(masks[head], query, jnp.zeros_like(query))
            grad_mine = jnp.where(masks[head], grad, jnp.zeros_like(grad))
            lse = lse_ref[0, head : head + 1, here]
            delta = deltas[head : head + 1, here]
            scores = jnp.where(
                near,
                dot_nt(kn_ref[here, :], mine),
                jnp.where(far, dot_nt(kf_ref[here, :], mine), masked_value),
            )
            prob = jnp.exp2(scores - lse)
            dprob = jnp.where(
                near, dot_nt(vn_ref[here, :], grad_mine), dot_nt(vf_ref[here, :], grad_mine)
            )
            dscore = prob * (dprob - delta)
            prob_near = jnp.where(near, prob, 0.0).astype(low)
            prob_far = jnp.where(near, 0.0, prob).astype(low)
            ds_near = jnp.where(near, dscore, 0.0).astype(low)
            ds_far = jnp.where(near, 0.0, dscore).astype(low)
            dkn = dkn + dot_nn(ds_near, mine)
            dvn = dvn + dot_nn(prob_near, grad_mine)
            dkf = dot_nn(ds_far, mine)
            dvf = dot_nn(prob_far, grad_mine)
            if head:
                dkf_acc[here, :] += dkf
                dvf_acc[here, :] += dvf
            else:
                dkf_acc[here, :] = dkf
                dvf_acc[here, :] = dvf
            dqt = dot_nn(kn_t[rows, here], ds_near) + dot_nn(kf_t[rows, here], ds_far)
            for other in range(tile):
                there = slice(other * TILE, (other + 1) * TILE)
                prob = jnp.exp2(dot_nt(kf_ref[there, :], mine) - lse)
                dprob = dot_nt(vf_ref[there, :], grad_mine)
                dscore = (prob * (dprob - delta)).astype(low)
                dkf_acc[there, :] += dot_nn(dscore, mine)
                dvf_acc[there, :] += dot_nn(prob.astype(low), grad_mine)
                dqt = dqt + dot_nn(kf_t[rows, there], dscore)
            dqt_acc[rows, :] = dqt
        dq = dqt_acc[...].T * (1.0 / math.sqrt(HEAD))
        dq = rotate_back(dq, cosine[here], sa[here], sb[here])
        own_ref[0, here, :] = dq.astype(low)
        sum_q = sum_q + jnp.sum(dq, axis=0, keepdims=True)
        dkn = rotate_back(dkn * ln2, cosine[here], sa[here], sb[here])
        own_ref[1, here, :] = dkn.astype(low)
        sum_kn = sum_kn + jnp.sum(dkn, axis=0, keepdims=True)
        own_ref[2, here, :] = dvn.astype(low)
        sum_vn = sum_vn + jnp.sum(dvn, axis=0, keepdims=True)
    dkf = rotate_back(dkf_acc[...] * ln2, cosine, sa, sb)
    dvf = dvf_acc[...]
    clean_ref[0] = dkf.astype(low)
    clean_ref[1] = dvf.astype(low)
    sums_ref[0, 0:1, :] = sum_q
    sums_ref[0, 1:2, :] = sum_kn + jnp.sum(dkf, axis=0, keepdims=True)
    sums_ref[0, 2:3, :] = sum_vn + jnp.sum(dvf, axis=0, keepdims=True)


def attend_back(size, q, kn, vn, kf, vf, do, o, lse, tables, first, pairs, after, work):
    count = q.shape[0]
    pair_spec = pl.BlockSpec((count, PAIR), lambda p: (0, p + first))
    width = pairs * PAIR
    return ordered_call(
        attend_back_kernel,
        after,
        (pairs,),
        [pl.BlockSpec(memory_space=pltpu.SMEM)]
        + [pair_spec] * 7
        + [pl.BlockSpec((1, 2, count), lambda p: (p + first, 0, 0))]
        + [whole_spec(t.shape) for t in tables],
        (size, q, kn, vn, kf, vf, do, o, lse, *tables),
        out_specs=[
            pl.BlockSpec((3, count, PAIR), lambda p: (0, 0, p)),
            pl.BlockSpec((2, count, PAIR), lambda p: (0, 0, p)),
            pl.BlockSpec((1, 3, PAIR), lambda p: (p, 0, 0)),
        ],
        out_shape=[
            jax.ShapeDtypeStruct((3, count, width), low),
            jax.ShapeDtypeStruct((2, count, width), low),
            jax.ShapeDtypeStruct((pairs, 3, PAIR), wide),
        ],
        scratch_shapes=[
            pltpu.VMEM((PAIR, TILE), wide),
            pltpu.VMEM((count, PAIR), wide),
            pltpu.VMEM((count, PAIR), wide),
        ],
        work=work,
        name="attend_back",
    )


def spread_lanes(columns, batch):
    rows = columns.shape[0] // batch
    lane = lax.broadcasted_iota(jnp.int32, (rows, PAIR), 1)
    shards = []
    for shard in range(batch):
        block = columns[shard * rows : (shard + 1) * rows]
        for first, share in ((4, 4), (8, 3)):
            for j in range(share):
                chunk = share * shard + j
                at, start = first + chunk // batch, chunk % batch * rows
                block = jnp.where(
                    lane == first + j, columns[start : start + rows, at : at + 1], block
                )
        shards.append(block)
    return jnp.concatenate(shards, axis=0)


def qkv_kernel(cuts, batch, place_ref, core_ref, h_ref, hf_ref, w_ref, gain1_ref, bias1_ref,
               early_ref, *rest):
    own, clean, sums, rest = (
        rest[:cuts],
        rest[cuts : 2 * cuts],
        rest[2 * cuts : 3 * cuts],
        rest[3 * cuts :],
    )
    outs, (rows_ref, columns_ref, result_ref) = rest[:-3], rest[-3:]
    step = pl.program_id(0)
    width = h_ref.shape[1]
    result_ref[...] = dot_tn(h_ref[...], jnp.concatenate([r[0] for r in own], axis=1))

    @pl.when(step == 0)
    def _():
        columns_ref[...] = jnp.zeros_like(columns_ref)
        rows_ref[...] = jnp.zeros_like(rows_ref)
        for i in range(8):
            rows_ref[i : i + 1, :] = early_ref[:, i * width : (i + 1) * width]
        rows_ref[13:14, :] = row_of(gain1_ref)
        rows_ref[14:15, :] = row_of(bias1_ref)

    @pl.when(step > 0)
    def _():
        result_ref[...] += dot_tn(hf_ref[...], jnp.concatenate([r[0] for r in clean], axis=1))

    result = result_ref[...]
    cols = pl.ds(pl.multiple_of(step * width, 128), width)
    store_columns(place_ref, core_ref, result, outs, cols)
    weight = w_ref[...].astype(wide)
    totals = jnp.concatenate(
        [r[p, pl.ds(step, 1), :] for r in sums for p in range(r.shape[0])], axis=1
    )
    rows_ref[pl.ds(8 + step, 1), :] = totals
    lane = lax.broadcasted_iota(jnp.int32, (1, PAIR), 1)
    columns_ref[...] += jnp.where(
        lane == 0,
        jnp.sum(weight * result, axis=1, keepdims=True),
        jnp.sum(weight * totals, axis=1, keepdims=True),
    )

    @pl.when(step == 2)
    def _():
        columns = rows_ref[...].T
        bias = columns_ref[:, 1:2]
        gain = (columns_ref[:, 0:1] - columns[:, 14:15] * bias) / columns[:, 13:14]
        columns = jnp.where(lane == 11, gain, jnp.where(lane == 12, bias, columns))
        if len(outs) == 2:
            columns = spread_lanes(columns, batch)
        store_columns(place_ref, core_ref, columns, outs, slice(3 * width, 3 * width + PAIR))


def outer_qkv(h, hf, weight, gain1, bias1, early, own, clean, sums, place, core, after):
    count, width = h.shape
    batch = 2 * place.shape[0]
    columns = 3 * width + PAIR
    if aligned(width, batch):
        out_shape = [jax.ShapeDtypeStruct((batch // 2, width // batch, columns), low)] * 2
    else:
        out_shape = [jax.ShapeDtypeStruct((width, columns), low)]
    result = ordered_call(
        partial(qkv_kernel, len(own), batch),
        after,
        (3,),
        [whole_spec(h.shape)] * 2
        + [pl.BlockSpec((width, width), lambda i, p, c: (0, i))]
        + [whole_spec(v.shape) for v in (gain1, bias1, early)]
        + [pl.BlockSpec((1, count, r.shape[2]), lambda i, p, c: (i, 0, 0)) for r in own]
        + [
            pl.BlockSpec((1, count, r.shape[2]), lambda i, p, c: (jnp.maximum(i - 1, 0), 0, 0))
            for r in clean
        ]
        + [whole_spec(r.shape) for r in sums],
        (h, hf, weight, gain1, bias1, early, *own, *clean, *sums),
        (place, core),
        out_specs=[whole_spec(o.shape) for o in out_shape],
        out_shape=out_shape,
        scratch_shapes=[
            pltpu.VMEM((PAIR, width), wide),
            pltpu.VMEM((width, PAIR), wide),
            pltpu.VMEM((width, width), wide),
        ],
        work=1e8,
        name="outer_qkv",
    )
    if len(result) == 2:
        return result
    (full,) = result
    rows = width // batch
    start = 3 * width
    spread = [full[:, : start + 4]]
    for first, share in ((4, 4), (8, 3)):
        part = full[:, start + first : start + first + share].T.reshape(batch, share, rows)
        spread.append(part.transpose(0, 2, 1).reshape(width, share))
    spread.append(full[:, start + 11 :])
    return split_shards(jnp.concatenate(spread, axis=1), place, core[0])


def project_far_back_kernel(cuts, noisy_ref, x_ref, *rest):
    far, clean = rest[:HALVES], rest[HALVES : HALVES + cuts]
    w_ref, gain1_ref, dfar_ref = rest[HALVES + cuts :]
    width = x_ref.shape[1]
    steps = pl.num_programs(0) // HALVES
    source = x_ref[...].astype(wide)
    for i, ref in enumerate(far):
        chosen = (noisy_ref[0] == 1) & (pl.program_id(0) // steps == i)
        source = jnp.where(chosen, ref[...].astype(wide), source)
    normed, factor = normalize(source)
    dh = jnp.zeros_like(source)
    for part in range(2):
        grads = jnp.concatenate([c[part] for c in clean], axis=1)
        dh = dh + dot_nt(grads, w_ref[:, (part + 1) * width : (part + 2) * width])
    dfar_ref[...] = norm_back(dh * row_of(gain1_ref), normed, factor).astype(low)


def project_far_back(noisy, x, far, clean, weight, gain1, after):
    count, width = x.shape
    return ordered_call(
        partial(project_far_back_kernel, len(clean)),
        after,
        (count // ROWS,),
        [pl.BlockSpec(memory_space=pltpu.SMEM)]
        + [row_spec(width)]
        + [
            pl.BlockSpec(
                (ROWS, width),
                lambda i, first=n * f.shape[0] // ROWS, last=f.shape[0] // ROWS - 1: (
                    jnp.clip(i - first, 0, last),
                    0,
                ),
            )
            for n, f in enumerate(far)
        ]
        + [pl.BlockSpec((2, ROWS, c.shape[2]), lambda i: (0, i, 0)) for c in clean]
        + [whole_spec(weight.shape), whole_spec(gain1.shape)],
        (noisy, x, *far, *clean, weight, gain1),
        out_specs=row_spec(width),
        out_shape=jax.ShapeDtypeStruct((count, width), low),
        work=2.5e10,
        name="project_far_back",
    )


def project_back_kernel(cuts, noisy_ref, x_ref, dy_ref, dfar_ref, *rest):
    own = rest[:cuts]
    w_ref, gain1_ref, dx_ref = rest[cuts:]
    width = x_ref.shape[1]
    normed, factor = normalize(x_ref[...].astype(wide))
    dh = jnp.zeros_like(dy_ref)
    for part in range(3):
        grads = jnp.concatenate([c[part] for c in own], axis=1)
        dh = dh + dot_nt(grads, w_ref[:, part * width : (part + 1) * width])
    dx = dy_ref[...] + norm_back(dh * row_of(gain1_ref), normed, factor)
    dx_ref[...] = dx + jnp.where(noisy_ref[0] == 0, dfar_ref[...].astype(wide), 0.0)


def project_back(noisy, x, dy, dfar, own, weight, gain1, after):
    count, width = x.shape
    return ordered_call(
        partial(project_back_kernel, len(own)),
        after,
        (count // ROWS,),
        [pl.BlockSpec(memory_space=pltpu.SMEM)]
        + [row_spec(width)] * 3
        + [pl.BlockSpec((3, ROWS, c.shape[2]), lambda i: (0, i, 0)) for c in own]
        + [whole_spec(weight.shape), whole_spec(gain1.shape)],
        (noisy, x, dy, dfar, *own, weight, gain1),
        out_specs=row_spec(width),
        out_shape=jax.ShapeDtypeStruct((count, width), wide),
        work=1.2e10,
        name="project_back",
    )


def flip(values, mask):
    batch = lax.axis_size("batch")
    return lax.ppermute(values, "batch", [(i, i ^ mask) for i in range(batch)])


def flip_stream(values):
    return lax.ppermute(values, "stream", [(0, 1), (1, 0)])


def total(terms):
    result = terms[0].astype(wide)
    for term in terms[1:]:
        result = result + term.astype(wide)
    return result


class Reduction:
    def __init__(self, name, shards):
        keep, send = shards
        self.name = name
        self.terms = [keep, flip(send, 1)]
        self.stages = stages_of(2 * keep.shape[0])
        self.size = keep.shape[0]

    def wait_for(self, others):
        self.terms, _ = lax.optimization_barrier((self.terms, list(others)))

    def step(self):
        bits = self.stages.pop(0)
        parts = 2 ** len(bits)
        size = self.size // parts
        pieces = [
            total([t[j * size : (j + 1) * size] for t in self.terms]).astype(low)
            for j in range(1, parts)
        ]
        arrived = [flip(p, mask_of(bits, j + 1)) for j, p in enumerate(pieces)]
        self.terms = self.terms + arrived
        self.arrived = arrived
        self.size = size
        return pieces

    def last(self):
        while self.stages:
            self.step()
        self.mine = total([t[:1] for t in self.terms]).astype(low)
        self.other = flip_stream(self.mine)
        return [self.mine]

    def result(self, first, count):
        at = slice(first, first + count)
        return self.mine[0][:, at].astype(wide) + self.other[0][:, at].astype(wide)


def local(
    layer_input,
    out_cotangent,
    block_size,
    norm1_gain,
    norm1_bias,
    qkv_weight,
    qkv_bias,
    proj_weight,
    proj_bias,
    norm2_gain,
    norm2_bias,
    up_weight,
    up_bias,
    down_weight,
    down_bias,
):
    length, width = layer_input.shape[2:]
    batch = lax.axis_size("batch")
    noisy = lax.axis_index("stream").astype(jnp.int32).reshape(1)
    x = layer_input.reshape(length, width)
    g = out_cotangent.reshape(length, width)
    half = length // HALVES
    far_x = [
        lax.ppermute(x[i * half : (i + 1) * half], "stream", [(0, 1)]) for i in range(HALVES)
    ]
    tables = rotary_tables(length)
    me = lax.axis_index("batch").astype(jnp.int32)
    place, core = places_of(batch, me), (me % 2).reshape(1)
    h, q, k, v = project(x, qkv_weight, qkv_bias, norm1_gain, norm1_bias, tables)
    fars, attended = [], []
    for i in range(HALVES):
        fars = project_far(
            noisy, x, far_x[i], qkv_weight, qkv_bias, norm1_gain, norm1_bias, tables, i, fars
        )
        hf, kf, vf = fars
        attended = attend(block_size, q, k, v, kf, vf, i, HALVES, attended)
    o, lse = attended
    (out, dy, do, early), downw, upw = middle(
        place,
        core,
        x,
        o,
        g,
        proj_weight,
        proj_bias,
        norm2_gain,
        norm2_bias,
        up_weight,
        up_bias,
        down_weight,
        down_bias,
    )
    down, up = Reduction("down", downw), Reduction("up", upw)
    backs, after = [], []
    for i, (first, pairs) in enumerate(CUTS):
        if i == 1:
            after = down.step()
        if i == 2:
            after = up.step() + down.step()
        after = after + [b[0] for b in backs[-1:]]
        backs.append(
            attend_back(
                block_size, q, k, v, kf, vf, do, o, lse, tables, first, pairs, after, 2e10
            )
        )
    own, clean, sums = ([b[i] for b in backs] for i in range(3))
    qkvw = outer_qkv(
        h,
        hf,
        qkv_weight,
        norm1_gain,
        norm1_bias,
        early,
        own,
        clean,
        sums,
        place,
        core,
        [],
    )
    qkv = Reduction("qkv", qkvw)
    arrived = down.arrived
    after = up.step() + arrived
    dfar = project_far_back(noisy, x, far_x, clean, qkv_weight, norm1_gain, after)
    back_x = lax.ppermute(dfar, "stream", [(1, 0)])
    qkv.wait_for([dfar])
    after = qkv.step() + up.arrived[:1]
    dx = project_back(noisy, x, dy, dfar, own, qkv_weight, norm1_gain, after)
    qkv.wait_for([dx])
    after = qkv.step()
    down.wait_for(after)
    down.last()
    up.wait_for(after)
    up.last()
    after = qkv.last()
    dx, _ = lax.optimization_barrier((dx, after))
    input_grad = (dx + back_x.astype(wide)).reshape(layer_input.shape)
    ff = up_weight.shape[1]
    downw_grad = down.result(0, width)
    upw_grad, projw_grad = up.result(0, ff), up.result(ff, width)
    qkvw_grad = qkv.result(0, 3 * width)
    vectors = qkv.result(3 * width, PAIR).T
    downb_grad, gain2_grad, bias2_grad, projb_grad = (vectors[i] for i in range(4))
    upb_grad, qkvb_grad = vectors[4:8].reshape(-1), vectors[8:11].reshape(-1)
    gain1_grad, bias1_grad = vectors[11], vectors[12]
    return (
        out.reshape(layer_input.shape),
        input_grad,
        gain1_grad,
        bias1_grad,
        qkvw_grad,
        qkvb_grad,
        projw_grad,
        projb_grad,
        gain2_grad,
        bias2_grad,
        upw_grad,
        upb_grad,
        downw_grad,
        downb_grad,
    )


def solution(mesh):
    rows = P("stream", "batch", None, None)
    return jax.shard_map(
        local,
        mesh=mesh,
        in_specs=(rows, rows, P("batch")) + (P(),) * 12,
        out_specs=(
            rows,
            rows,
            P("batch"),
            P("batch"),
            P("batch", None),
            P("batch"),
            P("batch", None),
            P("batch"),
            P("batch"),
            P("batch"),
            P("batch", None),
            P("batch"),
            P("batch", None),
            P("batch"),
        ),
        check_vma=False,
    )
```

```python
from functools import partial
import math

import jax
import jax.numpy as jnp
from jax import lax
from jax.experimental import pallas as pl
from jax.experimental.pallas import tpu as pltpu
from jax.sharding import PartitionSpec as P
import numpy as np

HEAD = 64
PAIR = 2 * HEAD
ROWS = 256
SPAN = 128
HALVES = 2
CUTS = ((0, 1), (1, 5))
full_vmem = 60

masked_value = -1e30
epsilon = 1e-05
low = jnp.bfloat16
wide = jnp.float32
score_scale = math.log2(math.e) / math.sqrt(HEAD)
ln2 = math.log(2.0)
gelu_c = math.sqrt(2.0 / math.pi)
gelu_k = 0.044715
mega = 1024 * 1024


def dot_nn(left, right):
    return lax.dot_general(left, right, (((1,), (0,)), ((), ())), preferred_element_type=wide)


def dot_nt(left, right):
    return lax.dot_general(left, right, (((1,), (1,)), ((), ())), preferred_element_type=wide)


def dot_tn(left, right):
    return lax.dot_general(left, right, (((0,), (0,)), ((), ())), preferred_element_type=wide)


def params(limit_mib):
    return pltpu.CompilerParams(
        dimension_semantics=("arbitrary",), vmem_limit_bytes=limit_mib * mega
    )


def cost(flops, nbytes, trans=0):
    return pl.CostEstimate(
        flops=int(flops), bytes_accessed=int(nbytes), transcendentals=int(trans)
    )


def ordered_call(
    kernel, after, grid, in_specs, operands, prefetch=(), work=4e9, into=(), **rest
):
    skip = len(prefetch) + len(operands)
    after = list(into) + list(after)

    def body(*refs):
        kernel(*refs[:skip], *refs[skip + len(after) :])

    out_specs = rest.pop("out_specs")
    scratch = rest.pop("scratch_shapes", [])
    call = pl.pallas_call(
        body,
        grid_spec=pltpu.PrefetchScalarGridSpec(
            num_scalar_prefetch=len(prefetch),
            grid=grid,
            in_specs=list(in_specs) + [pl.BlockSpec(memory_space=pl.ANY)] * len(after),
            out_specs=out_specs,
            scratch_shapes=scratch,
        ),
        compiler_params=pltpu.CompilerParams(
            dimension_semantics=("arbitrary",) * len(grid), vmem_limit_bytes=full_vmem * mega
        ),
        cost_estimate=cost(work, 1000),
        input_output_aliases={skip + i: i for i in range(len(into))},
        **rest,
    )
    return call(*prefetch, *operands, *after)


def row_of(ref, at=slice(None)):
    return ref[at].reshape(1, -1)


def whole_spec(shape):
    zeros = (0,) * len(shape)
    return pl.BlockSpec(shape, lambda *_: zeros, pipeline_mode=pl.Buffered(1))


def row_spec(width, rows=ROWS):
    return pl.BlockSpec((rows, width), lambda i: (i, 0))


def normalize(values):
    mean = jnp.mean(values, axis=-1, keepdims=True)
    centred = values - mean
    factor = lax.rsqrt(jnp.mean(centred * centred, axis=-1, keepdims=True) + epsilon)
    return (centred * factor, factor)


def norm_back(grad_normed, normed, factor):
    first = jnp.mean(grad_normed, axis=-1, keepdims=True)
    second = jnp.mean(grad_normed * normed, axis=-1, keepdims=True)
    return factor * (grad_normed - first - normed * second)


def rotary_tables(length):
    places = np.arange(length, dtype=np.float64)[:, None]
    column = np.arange(PAIR) % HEAD
    angle = places * (10000.0 ** (-2.0 * (column % (HEAD // 2)) / HEAD))[None, :]
    upper = (column >= HEAD // 2)[None, :]
    cosine, sine = np.cos(angle), np.sin(angle)
    tables = (cosine, np.where(upper, sine, 0.0), np.where(upper, 0.0, -sine))
    return tuple(jnp.asarray(t, dtype=wide) for t in tables)


def rotate(values, cosine, sine_a, sine_b):
    return (
        values * cosine
        + pltpu.roll(values, HEAD // 2, 1) * sine_a
        + pltpu.roll(values, PAIR - HEAD // 2, 1) * sine_b
    )


def rotate_back(values, cosine, sine_a, sine_b):
    return (
        values * cosine
        - pltpu.roll(values, HEAD // 2, 1) * sine_a
        - pltpu.roll(values, PAIR - HEAD // 2, 1) * sine_b
    )


def project_kernel(x_ref, w_ref, bias_ref, gain1_ref, bias1_ref, cos_ref, sa_ref, sb_ref,
                   h_ref, q_ref, k_ref, v_ref):
    width = x_ref.shape[1]
    normed, _ = normalize(x_ref[...].astype(wide))
    hidden = (normed * row_of(gain1_ref) + row_of(bias1_ref)).astype(low)
    h_ref[...] = hidden
    cosine, sa, sb = cos_ref[...], sa_ref[...], sb_ref[...]
    for out, part in ((q_ref, 0), (k_ref, 1), (v_ref, 2)):
        cols = slice(part * width, (part + 1) * width)
        mixed = dot_nn(hidden, w_ref[:, cols]) + row_of(bias_ref, cols)
        if part == 2:
            out[...] = mixed.astype(low)
            continue
        for group in range(width // PAIR):
            at = slice(group * PAIR, (group + 1) * PAIR)
            turned = rotate(mixed[:, at], cosine, sa, sb)
            if part == 0:
                turned = turned * score_scale
            out[:, at] = turned.astype(low)


def project_far_kernel(noisy_ref, x_ref, far_ref, wk_ref, wv_ref, bias_ref, gain1_ref, bias1_ref,
                       cos_ref, sa_ref, sb_ref, h_ref, k_ref, v_ref):
    width = x_ref.shape[1]
    source = jnp.where(noisy_ref[0] == 1, far_ref[...].astype(wide), x_ref[...].astype(wide))
    normed, _ = normalize(source)
    hidden = (normed * row_of(gain1_ref) + row_of(bias1_ref)).astype(low)
    h_ref[...] = hidden
    cosine, sa, sb = cos_ref[...], sa_ref[...], sb_ref[...]
    mixed = dot_nn(hidden, wk_ref[...]) + row_of(bias_ref, slice(width, 2 * width))
    for group in range(width // PAIR):
        at = slice(group * PAIR, (group + 1) * PAIR)
        k_ref[:, at] = rotate(mixed[:, at], cosine, sa, sb).astype(low)
    mixed = dot_nn(hidden, wv_ref[...]) + row_of(bias_ref, slice(2 * width, None))
    v_ref[...] = mixed.astype(low)


def project(x, weight, bias, gain1, bias1, tables):
    count, width = x.shape
    row = jax.ShapeDtypeStruct((count, width), low)
    return pl.pallas_call(
        project_kernel,
        grid=(count // ROWS,),
        in_specs=[
            row_spec(width),
            whole_spec(weight.shape),
            whole_spec(bias.shape),
            whole_spec(gain1.shape),
            whole_spec(bias1.shape),
            row_spec(PAIR),
            row_spec(PAIR),
            row_spec(PAIR),
        ],
        out_specs=[row_spec(width)] * 4,
        out_shape=[row] * 4,
        compiler_params=params(full_vmem),
        cost_estimate=cost(2 * count * width * 3 * width, 16e6),
        name="project",
    )(x, weight, bias, gain1, bias1, *tables)


def project_far(noisy, x, far, weight, bias, gain1, bias1, tables, part, into):
    count, width = x.shape
    steps = far.shape[0] // ROWS
    row = jax.ShapeDtypeStruct((count, width), low)

    def part_rows(columns):
        return pl.BlockSpec((ROWS, columns), lambda i: (part * steps + i, 0))

    return ordered_call(
        project_far_kernel,
        [],
        (steps,),
        [
            pl.BlockSpec(memory_space=pltpu.SMEM),
            part_rows(width),
            row_spec(width),
            pl.BlockSpec((width, width), lambda i: (0, 1), pipeline_mode=pl.Buffered(1)),
            pl.BlockSpec((width, width), lambda i: (0, 2), pipeline_mode=pl.Buffered(1)),
            whole_spec(bias.shape),
            whole_spec(gain1.shape),
            whole_spec(bias1.shape),
            part_rows(PAIR),
            part_rows(PAIR),
            part_rows(PAIR),
        ],
        (noisy, x, far, weight, weight, bias, gain1, bias1, *tables),
        into=into,
        out_specs=[part_rows(width)] * 3,
        out_shape=[row] * 3,
        name="project_far",
    )


def block_masks(size_ref):
    key = lax.broadcasted_iota(jnp.int32, (SPAN, 2 * SPAN), 0)
    query = lax.broadcasted_iota(jnp.int32, (SPAN, 2 * SPAN), 1) % SPAN
    near = (key ^ query) < size_ref[0]
    return near, key < query


def both_heads(rows):
    lane = lax.broadcasted_iota(jnp.int32, (1, PAIR), 1)
    none = jnp.zeros_like(rows)
    return jnp.concatenate(
        [jnp.where(lane < HEAD, rows, none), jnp.where(lane >= HEAD, rows, none)], axis=0
    )


def own_blocks(mixed):
    return jnp.concatenate([mixed[:HEAD, :SPAN], mixed[HEAD:, SPAN:]], axis=0).T


def attend_kernel(first, size_ref, q_ref, kn_ref, vn_ref, kf_ref, vf_ref, o_ref, lse_ref):
    near, far = block_masks(size_ref)
    vf_t = vf_ref[...].astype(wide).T.astype(low)
    vn_t = vn_ref[...].astype(wide).T.astype(low)
    parts = range(q_ref.shape[0] // SPAN)
    state = []
    for part in parts:
        past = (first + part) * SPAN
        own = slice(part * SPAN, (part + 1) * SPAN)
        query = both_heads(q_ref[own, :])
        scores = dot_nt(kf_ref[: past + SPAN, :], query)
        diag = jnp.where(
            near, dot_nt(kn_ref[own, :], query), jnp.where(far, scores[past:], masked_value)
        )
        state.append((past, own, scores, diag))
    probs = []
    for past, own, scores, diag in state:
        top = jnp.max(diag, axis=0, keepdims=True)
        if past:
            top = jnp.maximum(top, jnp.max(scores[:past], axis=0, keepdims=True))
        prob = jnp.exp2(diag - top)
        total = jnp.sum(prob, axis=0, keepdims=True)
        prob_near = jnp.where(near, prob, 0.0).astype(low)
        prob_far = jnp.where(near, 0.0, prob).astype(low)
        if past:
            prob = jnp.exp2(scores[:past] - top)
            total = total + jnp.sum(prob, axis=0, keepdims=True)
            prob_far = jnp.concatenate([prob.astype(low), prob_far], axis=0)
        lse = top + jnp.log2(total)
        lse_ref[0, 0:1, own] = lse[:, :SPAN]
        lse_ref[0, 1:2, own] = lse[:, SPAN:]
        probs.append((past, own, prob_near, prob_far, 1.0 / total))
    for past, own, prob_near, prob_far, scale in probs:
        mixed = dot_nn(vn_t[:, own], prob_near) + dot_nn(vf_t[:, : past + SPAN], prob_far)
        o_ref[own, :] = own_blocks(mixed * scale).astype(low)


def attend(size, q, kn, vn, kf, vf, part, parts, into):
    count, width = q.shape
    pairs = width // PAIR
    rows = count // parts
    own_spec = pl.BlockSpec((rows, PAIR), lambda p: (part, p))
    far_spec = pl.BlockSpec(((part + 1) * rows, PAIR), lambda p: (0, p))
    return ordered_call(
        partial(attend_kernel, part * rows // SPAN),
        [],
        (pairs,),
        [pl.BlockSpec(memory_space=pltpu.SMEM)] + [own_spec] * 3 + [far_spec] * 2,
        (size, q, kn, vn, kf, vf),
        into=into,
        out_specs=[own_spec, pl.BlockSpec((1, 2, rows), lambda p: (p, 0, part))],
        out_shape=[
            jax.ShapeDtypeStruct((count, width), low),
            jax.ShapeDtypeStruct((pairs, 2, count), wide),
        ],
        name="attend",
    )


def stages_of(batch):
    bits = list(range(1, batch.bit_length() - 1))
    stages = [bits[:1]]
    rest = bits[1:]
    while rest:
        stages.append(rest[:2])
        rest = rest[2:]
    return [s for s in stages if s]


def mask_of(bits, digit):
    return sum(((digit >> i) & 1) << bit for i, bit in enumerate(bits))


def places_of(batch, me):
    relative = jnp.arange(0, batch, 2, dtype=jnp.int32) ^ (me - me % 2)
    place = jnp.zeros_like(relative)
    for bits in stages_of(batch):
        place = place * 2 ** len(bits)
        for i, bit in enumerate(bits):
            place = place + (((relative >> bit) & 1) << i)
    return place


def store_shards(place_ref, core_ref, result, keep_ref, send_ref, columns=slice(None)):
    shards = keep_ref.shape[0]
    rows = result.shape[0] // (2 * shards)

    def store(first_ref, second_ref):
        for pair in range(shards):
            at = place_ref[pair]
            start = 2 * pair * rows
            first_ref[at, :, columns] = result[start : start + rows].astype(low)
            second_ref[at, :, columns] = result[start + rows : start + 2 * rows].astype(low)

    pl.when(core_ref[0] == 0)(lambda: store(keep_ref, send_ref))
    pl.when(core_ref[0] == 1)(lambda: store(send_ref, keep_ref))


def split_shards(full, place, core):
    batch = 2 * place.shape[0]
    shards = full.reshape((batch // 2, 2, full.shape[0] // batch) + full.shape[1:])
    order = jnp.argsort(place)
    shards = jnp.take(shards, order, axis=0)
    return (
        jnp.where(core == 0, shards[:, 0], shards[:, 1]),
        jnp.where(core == 0, shards[:, 1], shards[:, 0]),
    )


def aligned(tall, batch):
    return tall % batch == 0 and (tall // batch) % 16 == 0


def store_columns(place_ref, core_ref, result, outs, columns=slice(None)):
    if len(outs) == 1:
        outs[0][:, columns] = result.astype(low)
    else:
        store_shards(place_ref, core_ref, result, *outs, columns)


def store_tall(place_ref, core_ref, step, result, outs):
    if len(outs) == 1:
        outs[0][...] = result.astype(low)
        return
    rows = outs[0].shape[2]
    places = place_ref.shape[0] // 2

    def store(first_ref, second_ref):
        for x in range(2):
            at = place_ref[2 * step + x] // places
            start = 2 * x * rows
            first_ref[at, 0] = result[start : start + rows].astype(low)
            second_ref[at, 0] = result[start + rows : start + 2 * rows].astype(low)

    pl.when(core_ref[0] == 0)(lambda: store(*outs))
    pl.when(core_ref[0] == 1)(lambda: store(*outs[::-1]))


def middle_kernel(row_steps, down_steps, tall_outs, place_ref, core_ref, x_ref, o_ref, g_ref,
                  wp_ref, bp_ref, gain2_ref, bias2_ref, wu_ref, bu_ref, wd_ref, bd_ref,
                  out_ref, dy_ref, do_ref, sums_ref,
                  *rest):
    downs, ups = rest[:tall_outs], rest[tall_outs:-5]
    a_all, right_all, hidden_all, o_all, g_all = rest[-5:]
    width = x_ref.shape[1]
    ff = wu_ref.shape[1]
    step = pl.program_id(0)

    def add_sum(start, values):
        at = slice(start, start + values.shape[1])
        sums_ref[:, at] += jnp.sum(values, axis=0, keepdims=True)

    @pl.when(step == 0)
    def _():
        sums_ref[...] = jnp.zeros_like(sums_ref)

    @pl.when(step < row_steps)
    def _():
        rows = pl.ds(pl.multiple_of(step * ROWS, ROWS), ROWS)
        parts = [slice(i * width, (i + 1) * width) for i in range(ff // width)]
        grad = g_ref[...]
        y = x_ref[...].astype(wide) + dot_nn(o_ref[...], wp_ref[...]) + row_of(bp_ref)
        das = [dot_nt(grad, wd_ref[cols, :]) for cols in parts]
        normed, factor = normalize(y)
        hidden = (normed * row_of(gain2_ref) + row_of(bias2_ref)).astype(low)
        o_all[rows, :] = o_ref[...]
        hidden_all[rows, :] = hidden
        g_all[rows, :] = grad
        grad_wide = grad.astype(wide)
        ups = [dot_nn(hidden, wu_ref[:, cols]) + row_of(bu_ref, cols) for cols in parts]
        acts, dus = [], []
        for part, cols in enumerate(parts):
            up = ups[part]
            square = up * up
            half = 0.5 + 0.5 * jnp.tanh(up * (gelu_c + (gelu_c * gelu_k) * square))
            active = (up * half).astype(low)
            slope = half + (up * (2.0 * gelu_c + (6.0 * gelu_c * gelu_k) * square)) * (
                half * (1.0 - half)
            )
            du = das[part] * slope
            du_low = du.astype(low)
            a_all[rows, cols] = active
            right_all[rows, cols] = du_low
            add_sum(4 * width + part * width, du)
            acts.append(active)
            dus.append(du_low)
        result = y + row_of(bd_ref)
        dh2 = jnp.zeros_like(y)
        for part, cols in enumerate(parts):
            dh2 = dh2 + dot_nt(dus[part], wu_ref[:, cols])
            result = result + dot_nn(acts[part], wd_ref[cols, :])
        out_ref[...] = result.astype(low)
        add_sum(0, grad_wide)
        add_sum(width, dh2 * normed)
        add_sum(2 * width, dh2)
        dy = grad_wide + norm_back(dh2 * row_of(gain2_ref), normed, factor)
        dy_ref[...] = dy
        add_sum(3 * width, dy)
        dy_low = dy.astype(low)
        right_all[rows, ff:] = dy_low
        do_ref[...] = dot_nt(dy_low, wp_ref[...]).astype(low)

    down_step = step - row_steps
    tile = ff // down_steps

    @pl.when((down_step >= 0) & (down_step < down_steps))
    def _():
        cols = pl.ds(pl.multiple_of(down_step * tile, 128), tile)
        store_tall(place_ref, core_ref, down_step, dot_tn(a_all[:, cols], g_all[...]), downs)

    up_step = down_step - down_steps
    up_steps = ff // width

    @pl.when((up_step >= 0) & (up_step < up_steps))
    def _():
        cols = pl.ds(pl.multiple_of(up_step * width, 128), width)
        store_columns(place_ref, core_ref, dot_tn(hidden_all[...], right_all[:, cols]), ups)

    @pl.when(up_step == up_steps)
    def _():
        store_columns(place_ref, core_ref, dot_tn(o_all[...], right_all[:, ff:]), ups)


def middle(place, core, x, o, g, wp, bp, gain2, bias2, wu, bu, wd, bd):
    count, width = x.shape
    ff = wu.shape[1]
    batch = 2 * place.shape[0]
    row_steps, up_steps = count // ROWS, ff // width + 1
    rows = ff // batch
    tall_aligned = aligned(ff, batch) and (4 * rows) % 128 == 0 and batch >= 8
    down_steps = batch // 4 if tall_aligned else ff // width

    def row(columns):
        return pl.BlockSpec((ROWS, columns), lambda i, p, c: (jnp.minimum(i, row_steps - 1), 0))

    def down_at(i):
        return jnp.clip(i - row_steps, 0, down_steps - 1)

    def up_at(i):
        return jnp.clip(i - row_steps - down_steps, 0, up_steps - 1)

    if tall_aligned:
        deep = batch // 4
        down_shape = [jax.ShapeDtypeStruct((2, deep, rows, width), low)] * 2
        down_specs = [
            pl.BlockSpec(
                (2, 1, rows, width), lambda i, p, c: (0, p[2 * down_at(i)] % deep, 0, 0)
            )
        ] * 2
    else:
        down_shape = [jax.ShapeDtypeStruct((ff, width), low)]
        down_specs = [pl.BlockSpec((ff // down_steps, width), lambda i, p, c: (down_at(i), 0))]
    if aligned(width, batch):
        shape = (batch // 2, width // batch)
        up_shape = [jax.ShapeDtypeStruct(shape + (ff + width,), low)] * 2
        up_specs = [pl.BlockSpec(shape + (width,), lambda i, p, c: (0, 0, up_at(i)))] * 2
    else:
        up_shape = [jax.ShapeDtypeStruct((width, ff + width), low)]
        up_specs = [pl.BlockSpec((width, width), lambda i, p, c: (0, up_at(i)))]
    sums = 4 * width + ff
    result = ordered_call(
        partial(middle_kernel, row_steps, down_steps, len(down_shape)),
        [],
        (row_steps + down_steps + up_steps,),
        [row(width)] * 3 + [whole_spec(a.shape) for a in (wp, bp, gain2, bias2, wu, bu, wd, bd)],
        (x, o, g, wp, bp, gain2, bias2, wu, bu, wd, bd),
        (place, core),
        out_specs=[row(width)] * 3
        + [whole_spec((1, sums))]
        + down_specs
        + up_specs,
        out_shape=[
            jax.ShapeDtypeStruct((count, width), low),
            jax.ShapeDtypeStruct((count, width), wide),
            jax.ShapeDtypeStruct((count, width), low),
        ]
        + [jax.ShapeDtypeStruct((1, sums), wide)]
        + down_shape
        + up_shape,
        scratch_shapes=[
            pltpu.VMEM((count, ff), low),
            pltpu.VMEM((count, ff + width), low),
            pltpu.VMEM((count, width), low),
            pltpu.VMEM((count, width), low),
            pltpu.VMEM((count, width), low),
        ],
        name="middle",
    )
    rest = result[4:]
    if tall_aligned:
        downw = [r.reshape(batch // 2, rows, width) for r in rest[:2]]
    else:
        downw = split_shards(rest[0], place, core[0])
    ups = rest[len(down_shape) :]
    upw = ups if len(ups) == 2 else split_shards(ups[0], place, core[0])
    return result[:4], downw, upw


def attend_back_kernel(size_ref, q_ref, kn_ref, vn_ref, kf_ref, vf_ref, do_ref, o_ref,
                       lse_ref, cos_ref, sa_ref, sb_ref,
                       own_ref, clean_ref, sums_ref, dkf_acc, dvf_acc):
    length = q_ref.shape[0]
    near, far = block_masks(size_ref)
    kf_t = kf_ref[...].astype(wide).T.astype(low)
    kn_t = kn_ref[...].astype(wide).T.astype(low)
    product = do_ref[...].astype(wide) * o_ref[...].astype(wide)
    high = product.astype(low)
    rest = (product - high.astype(wide)).astype(low)
    head_row = lax.broadcasted_iota(jnp.int32, (8, PAIR), 0)
    head_lane = lax.broadcasted_iota(jnp.int32, (8, PAIR), 1) // HEAD
    picker = jnp.where(head_row == head_lane, 1.0, 0.0).astype(low)
    deltas = dot_nt(picker, high) + dot_nt(picker, rest)
    cosine, sa, sb = cos_ref[...], sa_ref[...], sb_ref[...]
    sum_q = jnp.zeros((1, PAIR), wide)
    sum_kn = jnp.zeros((1, PAIR), wide)
    sum_vn = jnp.zeros((1, PAIR), wide)
    tiles = []
    for tile in range(length // SPAN):
        past = tile * SPAN
        here = slice(past, past + SPAN)
        query, grad = both_heads(q_ref[here, :]), both_heads(do_ref[here, :])
        scores = dot_nt(kf_ref[: past + SPAN, :], query)
        dprob = dot_nt(vf_ref[: past + SPAN, :], grad)
        diag = jnp.where(
            near,
            dot_nt(kn_ref[here, :], query),
            jnp.where(far, scores[past:], masked_value),
        )
        dprob_diag = jnp.where(near, dot_nt(vn_ref[here, :], grad), dprob[past:])
        tiles.append((past, here, query, grad, scores[:past], dprob[:past], diag, dprob_diag))
    results = []
    for past, here, query, grad, scores, dprob, diag, dprob_diag in tiles:
        lse = jnp.concatenate([lse_ref[0, 0:1, here], lse_ref[0, 1:2, here]], axis=1)
        delta = jnp.concatenate([deltas[0:1, here], deltas[1:2, here]], axis=1)
        prob_diag = jnp.exp2(diag - lse)
        ds_diag = prob_diag * (dprob_diag - delta)
        prob_near = jnp.where(near, prob_diag, 0.0).astype(low)
        ds_near = jnp.where(near, ds_diag, 0.0).astype(low)
        prob = jnp.where(near, 0.0, prob_diag).astype(low)
        dscore = jnp.where(near, 0.0, ds_diag).astype(low)
        if past:
            prob_past = jnp.exp2(scores - lse)
            ds_past = prob_past * (dprob - delta)
            prob = jnp.concatenate([prob_past.astype(low), prob], axis=0)
            dscore = jnp.concatenate([ds_past.astype(low), dscore], axis=0)
        results.append((past, here, query, grad, prob_near, ds_near, prob, dscore))
    for past, here, query, grad, prob_near, ds_near, prob, dscore in results:
        dkf, dvf = dot_nn(dscore, query), dot_nn(prob, grad)
        if past:
            dkf_acc[:past, :] += dkf[:past]
            dvf_acc[:past, :] += dvf[:past]
        dkf_acc[here, :] = dkf[past:]
        dvf_acc[here, :] = dvf[past:]
        dkn, dvn = dot_nn(ds_near, query), dot_nn(prob_near, grad)
        dqt = dot_nn(kn_t[:, here], ds_near) + dot_nn(kf_t[:, : past + SPAN], dscore)
        dq = own_blocks(dqt) * (1.0 / math.sqrt(HEAD))
        dq = rotate_back(dq, cosine[here], sa[here], sb[here])
        own_ref[0, here, :] = dq.astype(low)
        sum_q = sum_q + jnp.sum(dq, axis=0, keepdims=True)
        dkn = rotate_back(dkn * ln2, cosine[here], sa[here], sb[here])
        own_ref[1, here, :] = dkn.astype(low)
        sum_kn = sum_kn + jnp.sum(dkn, axis=0, keepdims=True)
        own_ref[2, here, :] = dvn.astype(low)
        sum_vn = sum_vn + jnp.sum(dvn, axis=0, keepdims=True)
    dkf = rotate_back(dkf_acc[...] * ln2, cosine, sa, sb)
    dvf = dvf_acc[...]
    clean_ref[0] = dkf.astype(low)
    clean_ref[1] = dvf.astype(low)
    sums_ref[0, 0:1, :] = sum_q
    sums_ref[0, 1:2, :] = sum_kn + jnp.sum(dkf, axis=0, keepdims=True)
    sums_ref[0, 2:3, :] = sum_vn + jnp.sum(dvf, axis=0, keepdims=True)


def attend_back(size, q, kn, vn, kf, vf, do, o, lse, tables, first, pairs, after, work):
    count = q.shape[0]
    pair_spec = pl.BlockSpec((count, PAIR), lambda p: (0, p + first))
    width = pairs * PAIR
    return ordered_call(
        attend_back_kernel,
        after,
        (pairs,),
        [pl.BlockSpec(memory_space=pltpu.SMEM)]
        + [pair_spec] * 7
        + [pl.BlockSpec((1, 2, count), lambda p: (p + first, 0, 0))]
        + [whole_spec(t.shape) for t in tables],
        (size, q, kn, vn, kf, vf, do, o, lse, *tables),
        out_specs=[
            pl.BlockSpec((3, count, PAIR), lambda p: (0, 0, p)),
            pl.BlockSpec((2, count, PAIR), lambda p: (0, 0, p)),
            pl.BlockSpec((1, 3, PAIR), lambda p: (p, 0, 0)),
        ],
        out_shape=[
            jax.ShapeDtypeStruct((3, count, width), low),
            jax.ShapeDtypeStruct((2, count, width), low),
            jax.ShapeDtypeStruct((pairs, 3, PAIR), wide),
        ],
        scratch_shapes=[
            pltpu.VMEM((count, PAIR), wide),
            pltpu.VMEM((count, PAIR), wide),
        ],
        work=work,
        name="attend_back",
    )


def spread_lanes(columns, batch):
    rows = columns.shape[0] // batch
    lane = lax.broadcasted_iota(jnp.int32, (rows, PAIR), 1)
    shards = []
    for shard in range(batch):
        block = columns[shard * rows : (shard + 1) * rows]
        for first, share in ((4, 4), (8, 3)):
            for j in range(share):
                chunk = share * shard + j
                at, start = first + chunk // batch, chunk % batch * rows
                block = jnp.where(
                    lane == first + j, columns[start : start + rows, at : at + 1], block
                )
        shards.append(block)
    return jnp.concatenate(shards, axis=0)


def qkv_kernel(cuts, batch, place_ref, core_ref, h_ref, hf_ref, w_ref, gain1_ref, bias1_ref,
               early_ref, *rest):
    own, clean, sums, rest = (
        rest[:cuts],
        rest[cuts : 2 * cuts],
        rest[2 * cuts : 3 * cuts],
        rest[3 * cuts :],
    )
    outs, (rows_ref, columns_ref, result_ref) = rest[:-3], rest[-3:]
    step = pl.program_id(0)
    width = h_ref.shape[1]
    result_ref[...] = dot_tn(h_ref[...], jnp.concatenate([r[0] for r in own], axis=1))

    @pl.when(step == 0)
    def _():
        columns_ref[...] = jnp.zeros_like(columns_ref)
        rows_ref[...] = jnp.zeros_like(rows_ref)
        for i in range(8):
            rows_ref[i : i + 1, :] = early_ref[:, i * width : (i + 1) * width]
        rows_ref[13:14, :] = row_of(gain1_ref)
        rows_ref[14:15, :] = row_of(bias1_ref)

    @pl.when(step > 0)
    def _():
        result_ref[...] += dot_tn(hf_ref[...], jnp.concatenate([r[0] for r in clean], axis=1))

    result = result_ref[...]
    cols = pl.ds(pl.multiple_of(step * width, 128), width)
    store_columns(place_ref, core_ref, result, outs, cols)
    weight = w_ref[...].astype(wide)
    totals = jnp.concatenate(
        [r[p, pl.ds(step, 1), :] for r in sums for p in range(r.shape[0])], axis=1
    )
    rows_ref[pl.ds(8 + step, 1), :] = totals
    lane = lax.broadcasted_iota(jnp.int32, (1, PAIR), 1)
    columns_ref[...] += jnp.where(
        lane == 0,
        jnp.sum(weight * result, axis=1, keepdims=True),
        jnp.sum(weight * totals, axis=1, keepdims=True),
    )

    @pl.when(step == 2)
    def _():
        columns = rows_ref[...].T
        bias = columns_ref[:, 1:2]
        gain = (columns_ref[:, 0:1] - columns[:, 14:15] * bias) / columns[:, 13:14]
        columns = jnp.where(lane == 11, gain, jnp.where(lane == 12, bias, columns))
        if len(outs) == 2:
            columns = spread_lanes(columns, batch)
        store_columns(place_ref, core_ref, columns, outs, slice(3 * width, 3 * width + PAIR))


def outer_qkv(h, hf, weight, gain1, bias1, early, own, clean, sums, place, core, after):
    count, width = h.shape
    batch = 2 * place.shape[0]
    columns = 3 * width + PAIR
    if aligned(width, batch):
        out_shape = [jax.ShapeDtypeStruct((batch // 2, width // batch, columns), low)] * 2
    else:
        out_shape = [jax.ShapeDtypeStruct((width, columns), low)]
    result = ordered_call(
        partial(qkv_kernel, len(own), batch),
        after,
        (3,),
        [whole_spec(h.shape)] * 2
        + [pl.BlockSpec((width, width), lambda i, p, c: (0, i))]
        + [whole_spec(v.shape) for v in (gain1, bias1, early)]
        + [pl.BlockSpec((1, count, r.shape[2]), lambda i, p, c: (i, 0, 0)) for r in own]
        + [
            pl.BlockSpec((1, count, r.shape[2]), lambda i, p, c: (jnp.maximum(i - 1, 0), 0, 0))
            for r in clean
        ]
        + [whole_spec(r.shape) for r in sums],
        (h, hf, weight, gain1, bias1, early, *own, *clean, *sums),
        (place, core),
        out_specs=[whole_spec(o.shape) for o in out_shape],
        out_shape=out_shape,
        scratch_shapes=[
            pltpu.VMEM((PAIR, width), wide),
            pltpu.VMEM((width, PAIR), wide),
            pltpu.VMEM((width, width), wide),
        ],
        work=1e8,
        name="outer_qkv",
    )
    if len(result) == 2:
        return result
    (full,) = result
    rows = width // batch
    start = 3 * width
    spread = [full[:, : start + 4]]
    for first, share in ((4, 4), (8, 3)):
        part = full[:, start + first : start + first + share].T.reshape(batch, share, rows)
        spread.append(part.transpose(0, 2, 1).reshape(width, share))
    spread.append(full[:, start + 11 :])
    return split_shards(jnp.concatenate(spread, axis=1), place, core[0])


def project_far_back_kernel(cuts, noisy_ref, x_ref, *rest):
    far, clean = rest[:HALVES], rest[HALVES : HALVES + cuts]
    w_ref, gain1_ref, dfar_ref = rest[HALVES + cuts :]
    width = x_ref.shape[1]
    steps = pl.num_programs(0) // HALVES
    source = x_ref[...].astype(wide)
    for i, ref in enumerate(far):
        chosen = (noisy_ref[0] == 1) & (pl.program_id(0) // steps == i)
        source = jnp.where(chosen, ref[...].astype(wide), source)
    normed, factor = normalize(source)
    dh = jnp.zeros_like(source)
    for part in range(2):
        grads = jnp.concatenate([c[part] for c in clean], axis=1)
        dh = dh + dot_nt(grads, w_ref[:, (part + 1) * width : (part + 2) * width])
    dfar_ref[...] = norm_back(dh * row_of(gain1_ref), normed, factor).astype(low)


def project_far_back(noisy, x, far, clean, weight, gain1, after):
    count, width = x.shape
    return ordered_call(
        partial(project_far_back_kernel, len(clean)),
        after,
        (count // ROWS,),
        [pl.BlockSpec(memory_space=pltpu.SMEM)]
        + [row_spec(width)]
        + [
            pl.BlockSpec(
                (ROWS, width),
                lambda i, first=n * f.shape[0] // ROWS, last=f.shape[0] // ROWS - 1: (
                    jnp.clip(i - first, 0, last),
                    0,
                ),
            )
            for n, f in enumerate(far)
        ]
        + [pl.BlockSpec((2, ROWS, c.shape[2]), lambda i: (0, i, 0)) for c in clean]
        + [whole_spec(weight.shape), whole_spec(gain1.shape)],
        (noisy, x, *far, *clean, weight, gain1),
        out_specs=row_spec(width),
        out_shape=jax.ShapeDtypeStruct((count, width), low),
        work=1e8,
        name="project_far_back",
    )


def project_back_kernel(cuts, noisy_ref, x_ref, dy_ref, dfar_ref, *rest):
    own = rest[:cuts]
    w_ref, gain1_ref, dx_ref = rest[cuts:]
    width = x_ref.shape[1]
    normed, factor = normalize(x_ref[...].astype(wide))
    dh = jnp.zeros_like(dy_ref)
    for part in range(3):
        grads = jnp.concatenate([c[part] for c in own], axis=1)
        dh = dh + dot_nt(grads, w_ref[:, part * width : (part + 1) * width])
    dx = dy_ref[...] + norm_back(dh * row_of(gain1_ref), normed, factor)
    dx_ref[...] = dx + jnp.where(noisy_ref[0] == 0, dfar_ref[...].astype(wide), 0.0)


def project_back(noisy, x, dy, dfar, own, weight, gain1, after):
    count, width = x.shape
    return ordered_call(
        partial(project_back_kernel, len(own)),
        after,
        (count // ROWS,),
        [pl.BlockSpec(memory_space=pltpu.SMEM)]
        + [row_spec(width)] * 3
        + [pl.BlockSpec((3, ROWS, c.shape[2]), lambda i: (0, i, 0)) for c in own]
        + [whole_spec(weight.shape), whole_spec(gain1.shape)],
        (noisy, x, dy, dfar, *own, weight, gain1),
        out_specs=row_spec(width),
        out_shape=jax.ShapeDtypeStruct((count, width), wide),
        work=1.5e10,
        name="project_back",
    )


def flip(values, mask):
    batch = lax.axis_size("batch")
    return lax.ppermute(values, "batch", [(i, i ^ mask) for i in range(batch)])


def flip_stream(values):
    return lax.ppermute(values, "stream", [(0, 1), (1, 0)])


def total(terms):
    result = terms[0].astype(wide)
    for term in terms[1:]:
        result = result + term.astype(wide)
    return result


class Reduction:
    def __init__(self, name, shards):
        keep, send = shards
        self.name = name
        self.terms = [keep, flip(send, 1)]
        self.stages = stages_of(2 * keep.shape[0])
        self.size = keep.shape[0]

    def wait_for(self, others):
        self.terms, _ = lax.optimization_barrier((self.terms, list(others)))

    def step(self):
        bits = self.stages.pop(0)
        parts = 2 ** len(bits)
        size = self.size // parts
        pieces = [
            total([t[j * size : (j + 1) * size] for t in self.terms]).astype(low)
            for j in range(1, parts)
        ]
        arrived = [flip(p, mask_of(bits, j + 1)) for j, p in enumerate(pieces)]
        self.terms = self.terms + arrived
        self.arrived = arrived
        self.size = size
        return pieces

    def last(self):
        while self.stages:
            self.step()
        self.mine = total([t[:1] for t in self.terms]).astype(low)
        self.other = flip_stream(self.mine)
        return [self.mine]

    def result(self, first, count):
        at = slice(first, first + count)
        return self.mine[0][:, at].astype(wide) + self.other[0][:, at].astype(wide)


def local(
    layer_input,
    out_cotangent,
    block_size,
    norm1_gain,
    norm1_bias,
    qkv_weight,
    qkv_bias,
    proj_weight,
    proj_bias,
    norm2_gain,
    norm2_bias,
    up_weight,
    up_bias,
    down_weight,
    down_bias,
):
    length, width = layer_input.shape[2:]
    batch = lax.axis_size("batch")
    noisy = lax.axis_index("stream").astype(jnp.int32).reshape(1)
    x = layer_input.reshape(length, width)
    g = out_cotangent.reshape(length, width)
    half = length // HALVES
    far_x = [
        lax.ppermute(x[i * half : (i + 1) * half], "stream", [(0, 1)]) for i in range(HALVES)
    ]
    tables = rotary_tables(length)
    me = lax.axis_index("batch").astype(jnp.int32)
    place, core = places_of(batch, me), (me % 2).reshape(1)
    h, q, k, v = project(x, qkv_weight, qkv_bias, norm1_gain, norm1_bias, tables)
    fars, attended = [], []
    for i in range(HALVES):
        fars = project_far(
            noisy, x, far_x[i], qkv_weight, qkv_bias, norm1_gain, norm1_bias, tables, i, fars
        )
        hf, kf, vf = fars
        attended = attend(block_size, q, k, v, kf, vf, i, HALVES, attended)
    o, lse = attended
    (out, dy, do, early), downw, upw = middle(
        place,
        core,
        x,
        o,
        g,
        proj_weight,
        proj_bias,
        norm2_gain,
        norm2_bias,
        up_weight,
        up_bias,
        down_weight,
        down_bias,
    )
    down, up = Reduction("down", downw), Reduction("up", upw)
    backs, after = [], []
    for i, (first, pairs) in enumerate(CUTS):
        if i == 1:
            down.wait_for(backs[0])
            after = down.step()
        after = after + [b[0] for b in backs[-1:]]
        backs.append(
            attend_back(
                block_size, q, k, v, kf, vf, do, o, lse, tables, first, pairs, after, 2e10
            )
        )
    own, clean, sums = ([b[i] for b in backs] for i in range(3))
    up.wait_for(backs[-1])
    down.wait_for(backs[-1])
    after = up.step() + down.step()
    dfar = project_far_back(noisy, x, far_x, clean, qkv_weight, norm1_gain, after)
    back_x = lax.ppermute(dfar, "stream", [(1, 0)])
    qkvw = outer_qkv(
        h,
        hf,
        qkv_weight,
        norm1_gain,
        norm1_bias,
        early,
        own,
        clean,
        sums,
        place,
        core,
        [dfar],
    )
    qkvw, _ = lax.optimization_barrier((list(qkvw), up.arrived + down.arrived))
    qkv = Reduction("qkv", qkvw)
    qkv.wait_for(up.step())
    after = qkv.step()
    dx = project_back(noisy, x, dy, dfar, own, qkv_weight, norm1_gain, after)
    qkv.wait_for([dx])
    after = qkv.step()
    down.wait_for(after)
    down.last()
    up.wait_for(after)
    up.last()
    after = qkv.last()
    dx, _ = lax.optimization_barrier((dx, after))
    input_grad = (dx + back_x.astype(wide)).reshape(layer_input.shape)
    ff = up_weight.shape[1]
    downw_grad = down.result(0, width)
    upw_grad, projw_grad = up.result(0, ff), up.result(ff, width)
    qkvw_grad = qkv.result(0, 3 * width)
    vectors = qkv.result(3 * width, PAIR).T
    downb_grad, gain2_grad, bias2_grad, projb_grad = (vectors[i] for i in range(4))
    upb_grad, qkvb_grad = vectors[4:8].reshape(-1), vectors[8:11].reshape(-1)
    gain1_grad, bias1_grad = vectors[11], vectors[12]
    return (
        out.reshape(layer_input.shape),
        input_grad,
        gain1_grad,
        bias1_grad,
        qkvw_grad,
        qkvb_grad,
        projw_grad,
        projb_grad,
        gain2_grad,
        bias2_grad,
        upw_grad,
        upb_grad,
        downw_grad,
        downb_grad,
    )


def solution(mesh):
    rows = P("stream", "batch", None, None)
    return jax.shard_map(
        local,
        mesh=mesh,
        in_specs=(rows, rows, P("batch")) + (P(),) * 12,
        out_specs=(
            rows,
            rows,
            P("batch"),
            P("batch"),
            P("batch", None),
            P("batch"),
            P("batch", None),
            P("batch"),
            P("batch"),
            P("batch"),
            P("batch", None),
            P("batch"),
            P("batch", None),
            P("batch"),
        ),
        check_vma=False,
    )
```

```python
from functools import partial
import math

import jax
import jax.numpy as jnp
from jax import lax
from jax.experimental import pallas as pl
from jax.experimental.pallas import tpu as pltpu
from jax.sharding import PartitionSpec as P
import numpy as np

HEAD = 64
PAIR = 2 * HEAD
ROWS = 256
SPAN = 128
HALVES = 2
CUTS = ((0, 2), (2, 4))
full_vmem = 60

masked_value = -1e30
epsilon = 1e-05
low = jnp.bfloat16
wide = jnp.float32
score_scale = math.log2(math.e) / math.sqrt(HEAD)
ln2 = math.log(2.0)
gelu_c = math.sqrt(2.0 / math.pi)
gelu_k = 0.044715
mega = 1024 * 1024


def dot_nn(left, right):
    return lax.dot_general(left, right, (((1,), (0,)), ((), ())), preferred_element_type=wide)


def dot_nt(left, right):
    return lax.dot_general(left, right, (((1,), (1,)), ((), ())), preferred_element_type=wide)


def dot_tn(left, right):
    return lax.dot_general(left, right, (((0,), (0,)), ((), ())), preferred_element_type=wide)


def params(limit_mib):
    return pltpu.CompilerParams(
        dimension_semantics=("arbitrary",), vmem_limit_bytes=limit_mib * mega
    )


def cost(flops, nbytes, trans=0):
    return pl.CostEstimate(
        flops=int(flops), bytes_accessed=int(nbytes), transcendentals=int(trans)
    )


def ordered_call(
    kernel, after, grid, in_specs, operands, prefetch=(), work=4e9, into=(), **rest
):
    skip = len(prefetch) + len(operands)
    after = list(into) + list(after)

    def body(*refs):
        kernel(*refs[:skip], *refs[skip + len(after) :])

    out_specs = rest.pop("out_specs")
    scratch = rest.pop("scratch_shapes", [])
    call = pl.pallas_call(
        body,
        grid_spec=pltpu.PrefetchScalarGridSpec(
            num_scalar_prefetch=len(prefetch),
            grid=grid,
            in_specs=list(in_specs) + [pl.BlockSpec(memory_space=pl.ANY)] * len(after),
            out_specs=out_specs,
            scratch_shapes=scratch,
        ),
        compiler_params=pltpu.CompilerParams(
            dimension_semantics=("arbitrary",) * len(grid), vmem_limit_bytes=full_vmem * mega
        ),
        cost_estimate=cost(work, 1000),
        input_output_aliases={skip + i: i for i in range(len(into))},
        **rest,
    )
    return call(*prefetch, *operands, *after)


def row_of(ref, at=slice(None)):
    return ref[at].reshape(1, -1)


def whole_spec(shape):
    zeros = (0,) * len(shape)
    return pl.BlockSpec(shape, lambda *_: zeros, pipeline_mode=pl.Buffered(1))


def row_spec(width, rows=ROWS):
    return pl.BlockSpec((rows, width), lambda i: (i, 0))


def normalize(values):
    mean = jnp.mean(values, axis=-1, keepdims=True)
    centred = values - mean
    factor = lax.rsqrt(jnp.mean(centred * centred, axis=-1, keepdims=True) + epsilon)
    return (centred * factor, factor)


def norm_back(grad_normed, normed, factor):
    first = jnp.mean(grad_normed, axis=-1, keepdims=True)
    second = jnp.mean(grad_normed * normed, axis=-1, keepdims=True)
    return factor * (grad_normed - first - normed * second)


def rotary_tables(length):
    places = np.arange(length, dtype=np.float64)[:, None]
    column = np.arange(PAIR) % HEAD
    angle = places * (10000.0 ** (-2.0 * (column % (HEAD // 2)) / HEAD))[None, :]
    upper = (column >= HEAD // 2)[None, :]
    cosine, sine = np.cos(angle), np.sin(angle)
    tables = (cosine, np.where(upper, sine, 0.0), np.where(upper, 0.0, -sine))
    return tuple(jnp.asarray(t, dtype=wide) for t in tables)


def rotate(values, cosine, sine_a, sine_b):
    return (
        values * cosine
        + pltpu.roll(values, HEAD // 2, 1) * sine_a
        + pltpu.roll(values, PAIR - HEAD // 2, 1) * sine_b
    )


def rotate_back(values, cosine, sine_a, sine_b):
    return (
        values * cosine
        - pltpu.roll(values, HEAD // 2, 1) * sine_a
        - pltpu.roll(values, PAIR - HEAD // 2, 1) * sine_b
    )


def project_kernel(x_ref, w_ref, bias_ref, gain1_ref, bias1_ref, cos_ref, sa_ref, sb_ref,
                   h_ref, q_ref, k_ref, v_ref):
    width = x_ref.shape[1]
    normed, _ = normalize(x_ref[...].astype(wide))
    hidden = (normed * row_of(gain1_ref) + row_of(bias1_ref)).astype(low)
    h_ref[...] = hidden
    cosine, sa, sb = cos_ref[...], sa_ref[...], sb_ref[...]
    for out, part in ((q_ref, 0), (k_ref, 1), (v_ref, 2)):
        cols = slice(part * width, (part + 1) * width)
        mixed = dot_nn(hidden, w_ref[:, cols]) + row_of(bias_ref, cols)
        if part == 2:
            out[...] = mixed.astype(low)
            continue
        for group in range(width // PAIR):
            at = slice(group * PAIR, (group + 1) * PAIR)
            turned = rotate(mixed[:, at], cosine, sa, sb)
            if part == 0:
                turned = turned * score_scale
            out[:, at] = turned.astype(low)


def project_far_kernel(noisy_ref, x_ref, far_ref, wk_ref, wv_ref, bias_ref, gain1_ref, bias1_ref,
                       cos_ref, sa_ref, sb_ref, h_ref, k_ref, v_ref):
    width = x_ref.shape[1]
    source = jnp.where(noisy_ref[0] == 1, far_ref[...].astype(wide), x_ref[...].astype(wide))
    normed, _ = normalize(source)
    hidden = (normed * row_of(gain1_ref) + row_of(bias1_ref)).astype(low)
    h_ref[...] = hidden
    cosine, sa, sb = cos_ref[...], sa_ref[...], sb_ref[...]
    mixed = dot_nn(hidden, wk_ref[...]) + row_of(bias_ref, slice(width, 2 * width))
    for group in range(width // PAIR):
        at = slice(group * PAIR, (group + 1) * PAIR)
        k_ref[:, at] = rotate(mixed[:, at], cosine, sa, sb).astype(low)
    mixed = dot_nn(hidden, wv_ref[...]) + row_of(bias_ref, slice(2 * width, None))
    v_ref[...] = mixed.astype(low)


def project(x, weight, bias, gain1, bias1, tables):
    count, width = x.shape
    row = jax.ShapeDtypeStruct((count, width), low)
    return pl.pallas_call(
        project_kernel,
        grid=(count // ROWS,),
        in_specs=[
            row_spec(width),
            whole_spec(weight.shape),
            whole_spec(bias.shape),
            whole_spec(gain1.shape),
            whole_spec(bias1.shape),
            row_spec(PAIR),
            row_spec(PAIR),
            row_spec(PAIR),
        ],
        out_specs=[row_spec(width)] * 4,
        out_shape=[row] * 4,
        compiler_params=params(full_vmem),
        cost_estimate=cost(2 * count * width * 3 * width, 16e6),
        name="project",
    )(x, weight, bias, gain1, bias1, *tables)


def project_far(noisy, x, far, weight, bias, gain1, bias1, tables, part, into):
    count, width = x.shape
    steps = far.shape[0] // ROWS
    row = jax.ShapeDtypeStruct((count, width), low)

    def part_rows(columns):
        return pl.BlockSpec((ROWS, columns), lambda i: (part * steps + i, 0))

    return ordered_call(
        project_far_kernel,
        [],
        (steps,),
        [
            pl.BlockSpec(memory_space=pltpu.SMEM),
            part_rows(width),
            row_spec(width),
            pl.BlockSpec((width, width), lambda i: (0, 1), pipeline_mode=pl.Buffered(1)),
            pl.BlockSpec((width, width), lambda i: (0, 2), pipeline_mode=pl.Buffered(1)),
            whole_spec(bias.shape),
            whole_spec(gain1.shape),
            whole_spec(bias1.shape),
            part_rows(PAIR),
            part_rows(PAIR),
            part_rows(PAIR),
        ],
        (noisy, x, far, weight, weight, bias, gain1, bias1, *tables),
        into=into,
        out_specs=[part_rows(width)] * 3,
        out_shape=[row] * 3,
        name="project_far",
    )


def block_masks(size_ref):
    key = lax.broadcasted_iota(jnp.int32, (SPAN, 2 * SPAN), 0)
    query = lax.broadcasted_iota(jnp.int32, (SPAN, 2 * SPAN), 1) % SPAN
    near = (key ^ query) < size_ref[0]
    return near, key < query


def both_heads(rows):
    lane = lax.broadcasted_iota(jnp.int32, (1, PAIR), 1)
    none = jnp.zeros_like(rows)
    return jnp.concatenate(
        [jnp.where(lane < HEAD, rows, none), jnp.where(lane >= HEAD, rows, none)], axis=0
    )


def own_blocks(mixed):
    return jnp.concatenate([mixed[:HEAD, :SPAN], mixed[HEAD:, SPAN:]], axis=0).T


def attend_kernel(first, size_ref, q_ref, kn_ref, vn_ref, kf_ref, vf_ref, o_ref, lse_ref):
    near, far = block_masks(size_ref)
    vf_t = vf_ref[...].astype(wide).T.astype(low)
    vn_t = vn_ref[...].astype(wide).T.astype(low)
    parts = range(q_ref.shape[0] // SPAN)
    state = []
    for part in parts:
        past = (first + part) * SPAN
        own = slice(part * SPAN, (part + 1) * SPAN)
        query = both_heads(q_ref[own, :])
        scores = dot_nt(kf_ref[: past + SPAN, :], query)
        diag = jnp.where(
            near, dot_nt(kn_ref[own, :], query), jnp.where(far, scores[past:], masked_value)
        )
        state.append((past, own, scores, diag))
    probs = []
    for past, own, scores, diag in state:
        top = jnp.max(diag, axis=0, keepdims=True)
        if past:
            top = jnp.maximum(top, jnp.max(scores[:past], axis=0, keepdims=True))
        prob = jnp.exp2(diag - top)
        total = jnp.sum(prob, axis=0, keepdims=True)
        prob_near = jnp.where(near, prob, 0.0).astype(low)
        prob_far = jnp.where(near, 0.0, prob).astype(low)
        if past:
            prob = jnp.exp2(scores[:past] - top)
            total = total + jnp.sum(prob, axis=0, keepdims=True)
            prob_far = jnp.concatenate([prob.astype(low), prob_far], axis=0)
        lse = top + jnp.log2(total)
        lse_ref[0, 0:1, own] = lse[:, :SPAN]
        lse_ref[0, 1:2, own] = lse[:, SPAN:]
        probs.append((past, own, prob_near, prob_far, 1.0 / total))
    for past, own, prob_near, prob_far, scale in probs:
        mixed = dot_nn(vn_t[:, own], prob_near) + dot_nn(vf_t[:, : past + SPAN], prob_far)
        o_ref[own, :] = own_blocks(mixed * scale).astype(low)


def attend(size, q, kn, vn, kf, vf, part, parts, into):
    count, width = q.shape
    pairs = width // PAIR
    rows = count // parts
    own_spec = pl.BlockSpec((rows, PAIR), lambda p: (part, p))
    far_spec = pl.BlockSpec(((part + 1) * rows, PAIR), lambda p: (0, p))
    return ordered_call(
        partial(attend_kernel, part * rows // SPAN),
        [],
        (pairs,),
        [pl.BlockSpec(memory_space=pltpu.SMEM)] + [own_spec] * 3 + [far_spec] * 2,
        (size, q, kn, vn, kf, vf),
        into=into,
        out_specs=[own_spec, pl.BlockSpec((1, 2, rows), lambda p: (p, 0, part))],
        out_shape=[
            jax.ShapeDtypeStruct((count, width), low),
            jax.ShapeDtypeStruct((pairs, 2, count), wide),
        ],
        name="attend",
    )


def stages_of(batch):
    bits = list(range(1, batch.bit_length() - 1))
    stages = [bits[:1]]
    rest = bits[1:]
    while rest:
        stages.append(rest[:2])
        rest = rest[2:]
    return [s for s in stages if s]


def mask_of(bits, digit):
    return sum(((digit >> i) & 1) << bit for i, bit in enumerate(bits))


def places_of(batch, me):
    relative = jnp.arange(0, batch, 2, dtype=jnp.int32) ^ (me - me % 2)
    place = jnp.zeros_like(relative)
    for bits in stages_of(batch):
        place = place * 2 ** len(bits)
        for i, bit in enumerate(bits):
            place = place + (((relative >> bit) & 1) << i)
    return place


def store_shards(place_ref, core_ref, result, keep_ref, send_ref, columns=slice(None)):
    shards = keep_ref.shape[0]
    rows = result.shape[0] // (2 * shards)

    def store(first_ref, second_ref):
        for pair in range(shards):
            at = place_ref[pair]
            start = 2 * pair * rows
            first_ref[at, :, columns] = result[start : start + rows].astype(low)
            second_ref[at, :, columns] = result[start + rows : start + 2 * rows].astype(low)

    pl.when(core_ref[0] == 0)(lambda: store(keep_ref, send_ref))
    pl.when(core_ref[0] == 1)(lambda: store(send_ref, keep_ref))


def split_shards(full, place, core):
    batch = 2 * place.shape[0]
    shards = full.reshape((batch // 2, 2, full.shape[0] // batch) + full.shape[1:])
    order = jnp.argsort(place)
    shards = jnp.take(shards, order, axis=0)
    return (
        jnp.where(core == 0, shards[:, 0], shards[:, 1]),
        jnp.where(core == 0, shards[:, 1], shards[:, 0]),
    )


def aligned(tall, batch):
    return tall % batch == 0 and (tall // batch) % 16 == 0


def store_columns(place_ref, core_ref, result, outs, columns=slice(None)):
    if len(outs) == 1:
        outs[0][:, columns] = result.astype(low)
    else:
        store_shards(place_ref, core_ref, result, *outs, columns)


def store_tall(place_ref, core_ref, step, result, outs):
    if len(outs) == 1:
        outs[0][...] = result.astype(low)
        return
    rows = outs[0].shape[2]
    places = place_ref.shape[0] // 2

    def store(first_ref, second_ref):
        for x in range(2):
            at = place_ref[2 * step + x] // places
            start = 2 * x * rows
            first_ref[at, 0] = result[start : start + rows].astype(low)
            second_ref[at, 0] = result[start + rows : start + 2 * rows].astype(low)

    pl.when(core_ref[0] == 0)(lambda: store(*outs))
    pl.when(core_ref[0] == 1)(lambda: store(*outs[::-1]))


def middle_kernel(row_steps, down_steps, tall_outs, place_ref, core_ref, side_ref, x_ref, o_ref, g_ref,
                  wp_ref, bp_ref, gain2_ref, bias2_ref, wu_ref, bu_ref, wd_ref, bd_ref,
                  out_ref, dy_ref, do_ref, sums_ref,
                  *rest):
    downs, ups = rest[:tall_outs], rest[tall_outs:-5]
    a_all, right_all, hidden_all, o_all, g_all = rest[-5:]
    width = x_ref.shape[1]
    ff = wu_ref.shape[1]
    step = pl.program_id(0)

    def add_sum(start, values):
        at = slice(start, start + values.shape[1])
        sums_ref[:, at] += jnp.sum(values, axis=0, keepdims=True)

    @pl.when(step == 0)
    def _():
        sums_ref[...] = jnp.zeros_like(sums_ref)

    @pl.when(step < row_steps)
    def _():
        rows = pl.ds(pl.multiple_of(step * ROWS, ROWS), ROWS)
        parts = [slice(i * width, (i + 1) * width) for i in range(ff // width)]
        grad = g_ref[...]
        y = x_ref[...].astype(wide) + dot_nn(o_ref[...], wp_ref[...]) + row_of(bp_ref)
        das = [dot_nt(grad, wd_ref[cols, :]) for cols in parts]
        normed, factor = normalize(y)
        hidden = (normed * row_of(gain2_ref) + row_of(bias2_ref)).astype(low)
        o_all[rows, :] = o_ref[...]
        hidden_all[rows, :] = hidden
        g_all[rows, :] = grad
        grad_wide = grad.astype(wide)
        ups = [dot_nn(hidden, wu_ref[:, cols]) + row_of(bu_ref, cols) for cols in parts]
        acts, dus = [], []
        for part, cols in enumerate(parts):
            up = ups[part]
            square = up * up
            half = 0.5 + 0.5 * jnp.tanh(up * (gelu_c + (gelu_c * gelu_k) * square))
            active = (up * half).astype(low)
            slope = half + (up * (2.0 * gelu_c + (6.0 * gelu_c * gelu_k) * square)) * (
                half * (1.0 - half)
            )
            du = das[part] * slope
            du_low = du.astype(low)
            a_all[rows, cols] = active
            right_all[rows, cols] = du_low
            add_sum(4 * width + part * width, du)
            acts.append(active)
            dus.append(du_low)
        result = y + row_of(bd_ref)
        dh2 = jnp.zeros_like(y)
        for part, cols in enumerate(parts):
            dh2 = dh2 + dot_nt(dus[part], wu_ref[:, cols])
            result = result + dot_nn(acts[part], wd_ref[cols, :])
        out_ref[...] = result.astype(low)
        add_sum(0, grad_wide)
        add_sum(width, dh2 * normed)
        add_sum(2 * width, dh2)
        dy = grad_wide + norm_back(dh2 * row_of(gain2_ref), normed, factor)
        dy_ref[...] = dy
        add_sum(3 * width, dy)
        dy_low = dy.astype(low)
        right_all[rows, ff:] = dy_low
        do_ref[...] = dot_nt(dy_low, wp_ref[...]).astype(low)

    down_step = step - row_steps
    tile = ff // down_steps

    @pl.when((down_step >= 0) & (down_step < down_steps))
    def _():
        cols = pl.ds(pl.multiple_of(down_step * tile, 128), tile)
        store_tall(place_ref, core_ref, down_step, dot_tn(a_all[:, cols], g_all[...]), downs)

    half = down_step - down_steps

    @pl.when(half >= 0)
    def _():
        outs = [u.at[0] for u in ups] if len(ups) == 2 else ups
        for start in range(0, ff // 2, width):
            cols = pl.ds(pl.multiple_of(half * (ff // 2) + start, 128), width)
            result = dot_tn(hidden_all[...], right_all[:, cols])
            store_columns(place_ref, core_ref, result, outs, slice(start, start + width))
        cols = pl.ds(pl.multiple_of(ff + half * (width // 2), 128), width // 2)
        result = dot_tn(o_all[...], right_all[:, cols])
        store_columns(
            place_ref, core_ref, result, outs, slice(ff // 2, ff // 2 + width // 2)
        )


def middle(place, core, side, x, o, g, wp, bp, gain2, bias2, wu, bu, wd, bd):
    count, width = x.shape
    ff = wu.shape[1]
    batch = 2 * place.shape[0]
    row_steps, up_steps = count // ROWS, 2
    rows = ff // batch
    tall_aligned = aligned(ff, batch) and (4 * rows) % 128 == 0 and batch >= 8
    down_steps = batch // 4 if tall_aligned else ff // width

    def row(columns):
        return pl.BlockSpec((ROWS, columns), lambda i, *_: (jnp.minimum(i, row_steps - 1), 0))

    def down_at(i):
        return jnp.clip(i - row_steps, 0, down_steps - 1)

    def up_at(i):
        return jnp.clip(i - row_steps - down_steps, 0, up_steps - 1)

    if tall_aligned:
        deep = batch // 4
        down_shape = [jax.ShapeDtypeStruct((2, deep, rows, width), low)] * 2
        down_specs = [
            pl.BlockSpec(
                (2, 1, rows, width), lambda i, p, c, s: (0, p[2 * down_at(i)] % deep, 0, 0)
            )
        ] * 2
    else:
        down_shape = [jax.ShapeDtypeStruct((ff, width), low)]
        down_specs = [pl.BlockSpec((ff // down_steps, width), lambda i, *_: (down_at(i), 0))]
    columns = (ff + width) // 2
    if aligned(width, batch):
        shape = (batch // 2, width // batch, columns)
        up_shape = [jax.ShapeDtypeStruct((2,) + shape, low)] * 2
        up_specs = [pl.BlockSpec((1,) + shape, lambda i, p, c, s: (up_at(i) ^ s[0], 0, 0, 0))] * 2
    else:
        up_shape = [jax.ShapeDtypeStruct((width, ff + width), low)]
        up_specs = [pl.BlockSpec((width, columns), lambda i, *_: (0, up_at(i)))]
    sums = 4 * width + ff
    result = ordered_call(
        partial(middle_kernel, row_steps, down_steps, len(down_shape)),
        [],
        (row_steps + down_steps + up_steps,),
        [row(width)] * 3 + [whole_spec(a.shape) for a in (wp, bp, gain2, bias2, wu, bu, wd, bd)],
        (x, o, g, wp, bp, gain2, bias2, wu, bu, wd, bd),
        (place, core, side),
        out_specs=[row(width)] * 3
        + [whole_spec((1, sums))]
        + down_specs
        + up_specs,
        out_shape=[
            jax.ShapeDtypeStruct((count, width), low),
            jax.ShapeDtypeStruct((count, width), wide),
            jax.ShapeDtypeStruct((count, width), low),
        ]
        + [jax.ShapeDtypeStruct((1, sums), wide)]
        + down_shape
        + up_shape,
        scratch_shapes=[
            pltpu.VMEM((count, ff), low),
            pltpu.VMEM((count, ff + width), low),
            pltpu.VMEM((count, width), low),
            pltpu.VMEM((count, width), low),
            pltpu.VMEM((count, width), low),
        ],
        name="middle",
    )
    rest = result[4:]
    if tall_aligned:
        downw = [r.reshape(batch // 2, rows, width) for r in rest[:2]]
    else:
        downw = split_shards(rest[0], place, core[0])
    ups = rest[len(down_shape) :]
    if len(ups) == 2:
        return result[:4], downw, ups
    parts = [
        split_shards(ups[0][:, i * columns : (i + 1) * columns], place, core[0]) for i in range(2)
    ]
    upw = []
    for first, second in zip(*parts):
        both = jnp.stack([first, second])
        upw.append(jnp.where(side[0] == 0, both, both[::-1]))
    return result[:4], downw, upw


def attend_back_kernel(size_ref, q_ref, kn_ref, vn_ref, kf_ref, vf_ref, do_ref, o_ref,
                       lse_ref, cos_ref, sa_ref, sb_ref,
                       own_ref, clean_ref, sums_ref, dkf_acc, dvf_acc):
    length = q_ref.shape[0]
    near, far = block_masks(size_ref)
    kf_t = kf_ref[...].astype(wide).T.astype(low)
    kn_t = kn_ref[...].astype(wide).T.astype(low)
    product = do_ref[...].astype(wide) * o_ref[...].astype(wide)
    high = product.astype(low)
    rest = (product - high.astype(wide)).astype(low)
    head_row = lax.broadcasted_iota(jnp.int32, (8, PAIR), 0)
    head_lane = lax.broadcasted_iota(jnp.int32, (8, PAIR), 1) // HEAD
    picker = jnp.where(head_row == head_lane, 1.0, 0.0).astype(low)
    deltas = dot_nt(picker, high) + dot_nt(picker, rest)
    cosine, sa, sb = cos_ref[...], sa_ref[...], sb_ref[...]
    sum_q = jnp.zeros((1, PAIR), wide)
    sum_kn = jnp.zeros((1, PAIR), wide)
    sum_vn = jnp.zeros((1, PAIR), wide)
    tiles = []
    for tile in range(length // SPAN):
        past = tile * SPAN
        here = slice(past, past + SPAN)
        query, grad = both_heads(q_ref[here, :]), both_heads(do_ref[here, :])
        scores = dot_nt(kf_ref[: past + SPAN, :], query)
        dprob = dot_nt(vf_ref[: past + SPAN, :], grad)
        diag = jnp.where(
            near,
            dot_nt(kn_ref[here, :], query),
            jnp.where(far, scores[past:], masked_value),
        )
        dprob_diag = jnp.where(near, dot_nt(vn_ref[here, :], grad), dprob[past:])
        tiles.append((past, here, query, grad, scores[:past], dprob[:past], diag, dprob_diag))
    results = []
    for past, here, query, grad, scores, dprob, diag, dprob_diag in tiles:
        lse = jnp.concatenate([lse_ref[0, 0:1, here], lse_ref[0, 1:2, here]], axis=1)
        delta = jnp.concatenate([deltas[0:1, here], deltas[1:2, here]], axis=1)
        prob_diag = jnp.exp2(diag - lse)
        ds_diag = prob_diag * (dprob_diag - delta)
        prob_near = jnp.where(near, prob_diag, 0.0).astype(low)
        ds_near = jnp.where(near, ds_diag, 0.0).astype(low)
        prob = jnp.where(near, 0.0, prob_diag).astype(low)
        dscore = jnp.where(near, 0.0, ds_diag).astype(low)
        if past:
            prob_past = jnp.exp2(scores - lse)
            ds_past = prob_past * (dprob - delta)
            prob = jnp.concatenate([prob_past.astype(low), prob], axis=0)
            dscore = jnp.concatenate([ds_past.astype(low), dscore], axis=0)
        results.append((past, here, query, grad, prob_near, ds_near, prob, dscore))
    for past, here, query, grad, prob_near, ds_near, prob, dscore in results:
        dkf, dvf = dot_nn(dscore, query), dot_nn(prob, grad)
        if past:
            dkf_acc[:past, :] += dkf[:past]
            dvf_acc[:past, :] += dvf[:past]
        dkf_acc[here, :] = dkf[past:]
        dvf_acc[here, :] = dvf[past:]
        dkn, dvn = dot_nn(ds_near, query), dot_nn(prob_near, grad)
        dqt = dot_nn(kn_t[:, here], ds_near) + dot_nn(kf_t[:, : past + SPAN], dscore)
        dq = own_blocks(dqt) * (1.0 / math.sqrt(HEAD))
        dq = rotate_back(dq, cosine[here], sa[here], sb[here])
        own_ref[0, here, :] = dq.astype(low)
        sum_q = sum_q + jnp.sum(dq, axis=0, keepdims=True)
        dkn = rotate_back(dkn * ln2, cosine[here], sa[here], sb[here])
        own_ref[1, here, :] = dkn.astype(low)
        sum_kn = sum_kn + jnp.sum(dkn, axis=0, keepdims=True)
        own_ref[2, here, :] = dvn.astype(low)
        sum_vn = sum_vn + jnp.sum(dvn, axis=0, keepdims=True)
    dkf = rotate_back(dkf_acc[...] * ln2, cosine, sa, sb)
    dvf = dvf_acc[...]
    clean_ref[0] = dkf.astype(low)
    clean_ref[1] = dvf.astype(low)
    sums_ref[0, 0:1, :] = sum_q
    sums_ref[0, 1:2, :] = sum_kn + jnp.sum(dkf, axis=0, keepdims=True)
    sums_ref[0, 2:3, :] = sum_vn + jnp.sum(dvf, axis=0, keepdims=True)


def attend_back(size, q, kn, vn, kf, vf, do, o, lse, tables, first, pairs, after, work):
    count = q.shape[0]
    pair_spec = pl.BlockSpec((count, PAIR), lambda p: (0, p + first))
    width = pairs * PAIR
    return ordered_call(
        attend_back_kernel,
        after,
        (pairs,),
        [pl.BlockSpec(memory_space=pltpu.SMEM)]
        + [pair_spec] * 7
        + [pl.BlockSpec((1, 2, count), lambda p: (p + first, 0, 0))]
        + [whole_spec(t.shape) for t in tables],
        (size, q, kn, vn, kf, vf, do, o, lse, *tables),
        out_specs=[
            pl.BlockSpec((3, count, PAIR), lambda p: (0, 0, p)),
            pl.BlockSpec((2, count, PAIR), lambda p: (0, 0, p)),
            pl.BlockSpec((1, 3, PAIR), lambda p: (p, 0, 0)),
        ],
        out_shape=[
            jax.ShapeDtypeStruct((3, count, width), low),
            jax.ShapeDtypeStruct((2, count, width), low),
            jax.ShapeDtypeStruct((pairs, 3, PAIR), wide),
        ],
        scratch_shapes=[
            pltpu.VMEM((count, PAIR), wide),
            pltpu.VMEM((count, PAIR), wide),
        ],
        work=work,
        name="attend_back",
    )


def spread_lanes(columns, batch):
    rows = columns.shape[0] // batch
    lane = lax.broadcasted_iota(jnp.int32, (rows, PAIR), 1)
    shards = []
    for shard in range(batch):
        block = columns[shard * rows : (shard + 1) * rows]
        for first, share in ((4, 4), (8, 3)):
            for j in range(share):
                chunk = share * shard + j
                at, start = first + chunk // batch, chunk % batch * rows
                block = jnp.where(
                    lane == first + j, columns[start : start + rows, at : at + 1], block
                )
        shards.append(block)
    return jnp.concatenate(shards, axis=0)


def qkv_kernel(cuts, batch, place_ref, core_ref, h_ref, hf_ref, w_ref, gain1_ref, bias1_ref,
               early_ref, *rest):
    own, clean, sums, rest = (
        rest[:cuts],
        rest[cuts : 2 * cuts],
        rest[2 * cuts : 3 * cuts],
        rest[3 * cuts :],
    )
    outs, (rows_ref, columns_ref, result_ref) = rest[:-3], rest[-3:]
    step = pl.program_id(0)
    width = h_ref.shape[1]
    result_ref[...] = dot_tn(h_ref[...], jnp.concatenate([r[0] for r in own], axis=1))

    @pl.when(step == 0)
    def _():
        columns_ref[...] = jnp.zeros_like(columns_ref)
        rows_ref[...] = jnp.zeros_like(rows_ref)
        for i in range(8):
            rows_ref[i : i + 1, :] = early_ref[:, i * width : (i + 1) * width]
        rows_ref[13:14, :] = row_of(gain1_ref)
        rows_ref[14:15, :] = row_of(bias1_ref)

    @pl.when(step > 0)
    def _():
        result_ref[...] += dot_tn(hf_ref[...], jnp.concatenate([r[0] for r in clean], axis=1))

    result = result_ref[...]
    cols = pl.ds(pl.multiple_of(step * width, 128), width)
    store_columns(place_ref, core_ref, result, outs, cols)
    weight = w_ref[...].astype(wide)
    totals = jnp.concatenate(
        [r[p, pl.ds(step, 1), :] for r in sums for p in range(r.shape[0])], axis=1
    )
    rows_ref[pl.ds(8 + step, 1), :] = totals
    lane = lax.broadcasted_iota(jnp.int32, (1, PAIR), 1)
    columns_ref[...] += jnp.where(
        lane == 0,
        jnp.sum(weight * result, axis=1, keepdims=True),
        jnp.sum(weight * totals, axis=1, keepdims=True),
    )

    @pl.when(step == 2)
    def _():
        columns = rows_ref[...].T
        bias = columns_ref[:, 1:2]
        gain = (columns_ref[:, 0:1] - columns[:, 14:15] * bias) / columns[:, 13:14]
        columns = jnp.where(lane == 11, gain, jnp.where(lane == 12, bias, columns))
        if len(outs) == 2:
            columns = spread_lanes(columns, batch)
        store_columns(place_ref, core_ref, columns, outs, slice(3 * width, 3 * width + PAIR))


def outer_qkv(h, hf, weight, gain1, bias1, early, own, clean, sums, place, core, after):
    count, width = h.shape
    batch = 2 * place.shape[0]
    columns = 3 * width + PAIR
    if aligned(width, batch):
        out_shape = [jax.ShapeDtypeStruct((batch // 2, width // batch, columns), low)] * 2
    else:
        out_shape = [jax.ShapeDtypeStruct((width, columns), low)]
    result = ordered_call(
        partial(qkv_kernel, len(own), batch),
        after,
        (3,),
        [whole_spec(h.shape)] * 2
        + [pl.BlockSpec((width, width), lambda i, p, c: (0, i))]
        + [whole_spec(v.shape) for v in (gain1, bias1, early)]
        + [pl.BlockSpec((1, count, r.shape[2]), lambda i, p, c: (i, 0, 0)) for r in own]
        + [
            pl.BlockSpec((1, count, r.shape[2]), lambda i, p, c: (jnp.maximum(i - 1, 0), 0, 0))
            for r in clean
        ]
        + [whole_spec(r.shape) for r in sums],
        (h, hf, weight, gain1, bias1, early, *own, *clean, *sums),
        (place, core),
        out_specs=[whole_spec(o.shape) for o in out_shape],
        out_shape=out_shape,
        scratch_shapes=[
            pltpu.VMEM((PAIR, width), wide),
            pltpu.VMEM((width, PAIR), wide),
            pltpu.VMEM((width, width), wide),
        ],
        work=1e8,
        name="outer_qkv",
    )
    if len(result) == 2:
        return result
    (full,) = result
    rows = width // batch
    start = 3 * width
    spread = [full[:, : start + 4]]
    for first, share in ((4, 4), (8, 3)):
        part = full[:, start + first : start + first + share].T.reshape(batch, share, rows)
        spread.append(part.transpose(0, 2, 1).reshape(width, share))
    spread.append(full[:, start + 11 :])
    return split_shards(jnp.concatenate(spread, axis=1), place, core[0])


def project_far_back_kernel(cuts, noisy_ref, x_ref, *rest):
    far, clean = rest[:HALVES], rest[HALVES : HALVES + cuts]
    w_ref, gain1_ref, dfar_ref = rest[HALVES + cuts :]
    width = x_ref.shape[1]
    steps = pl.num_programs(0) // HALVES
    source = x_ref[...].astype(wide)
    for i, ref in enumerate(far):
        chosen = (noisy_ref[0] == 1) & (pl.program_id(0) // steps == i)
        source = jnp.where(chosen, ref[...].astype(wide), source)
    normed, factor = normalize(source)
    dh = jnp.zeros_like(source)
    for part in range(2):
        grads = jnp.concatenate([c[part] for c in clean], axis=1)
        dh = dh + dot_nt(grads, w_ref[:, (part + 1) * width : (part + 2) * width])
    dfar_ref[...] = norm_back(dh * row_of(gain1_ref), normed, factor).astype(low)


def project_far_back(noisy, x, far, clean, weight, gain1, after):
    count, width = x.shape
    return ordered_call(
        partial(project_far_back_kernel, len(clean)),
        after,
        (count // ROWS,),
        [pl.BlockSpec(memory_space=pltpu.SMEM)]
        + [row_spec(width)]
        + [
            pl.BlockSpec(
                (ROWS, width),
                lambda i, first=n * f.shape[0] // ROWS, last=f.shape[0] // ROWS - 1: (
                    jnp.clip(i - first, 0, last),
                    0,
                ),
            )
            for n, f in enumerate(far)
        ]
        + [pl.BlockSpec((2, ROWS, c.shape[2]), lambda i: (0, i, 0)) for c in clean]
        + [whole_spec(weight.shape), whole_spec(gain1.shape)],
        (noisy, x, *far, *clean, weight, gain1),
        out_specs=row_spec(width),
        out_shape=jax.ShapeDtypeStruct((count, width), low),
        work=1.5e10,
        name="project_far_back",
    )


def project_back_kernel(cuts, noisy_ref, x_ref, dy_ref, dfar_ref, *rest):
    own = rest[:cuts]
    w_ref, gain1_ref, dx_ref = rest[cuts:]
    width = x_ref.shape[1]
    normed, factor = normalize(x_ref[...].astype(wide))
    dh = jnp.zeros_like(dy_ref)
    for part in range(3):
        grads = jnp.concatenate([c[part] for c in own], axis=1)
        dh = dh + dot_nt(grads, w_ref[:, part * width : (part + 1) * width])
    dx = dy_ref[...] + norm_back(dh * row_of(gain1_ref), normed, factor)
    dx_ref[...] = dx + jnp.where(noisy_ref[0] == 0, dfar_ref[...].astype(wide), 0.0)


def project_back(noisy, x, dy, dfar, own, weight, gain1, after):
    count, width = x.shape
    return ordered_call(
        partial(project_back_kernel, len(own)),
        after,
        (count // ROWS,),
        [pl.BlockSpec(memory_space=pltpu.SMEM)]
        + [row_spec(width)] * 3
        + [pl.BlockSpec((3, ROWS, c.shape[2]), lambda i: (0, i, 0)) for c in own]
        + [whole_spec(weight.shape), whole_spec(gain1.shape)],
        (noisy, x, dy, dfar, *own, weight, gain1),
        out_specs=row_spec(width),
        out_shape=jax.ShapeDtypeStruct((count, width), wide),
        work=1e8,
        name="project_back",
    )


def flip(values, mask):
    batch = lax.axis_size("batch")
    return lax.ppermute(values, "batch", [(i, i ^ mask) for i in range(batch)])


def flip_stream(values):
    return lax.ppermute(values, "stream", [(0, 1), (1, 0)])


def total(terms):
    result = terms[0].astype(wide)
    for term in terms[1:]:
        result = result + term.astype(wide)
    return result


class Reduction:
    def __init__(self, shards, halved=False):
        keep, send = shards
        self.halved = halved
        self.terms = [keep, flip(send, 1)]
        self.deep = 2 if halved else 0
        self.size = keep.shape[int(halved)]
        self.stages = stages_of(2 * self.size)

    def wait_for(self, others):
        self.terms, _ = lax.optimization_barrier((self.terms, list(others)))

    def part(self, first, size):
        views = [t[0] if i < self.deep else t for i, t in enumerate(self.terms)]
        return total([v[first : first + size] for v in views]).astype(low)

    def step(self):
        if self.halved:
            self.halved = False
            piece = total([t[1] for t in self.terms]).astype(low)
            self.arrived = [flip_stream(piece)]
            self.terms = self.terms + self.arrived
            return [piece]
        bits = self.stages.pop(0)
        parts = 2 ** len(bits)
        size = self.size // parts
        pieces = [self.part(j * size, size) for j in range(1, parts)]
        self.arrived = [flip(p, mask_of(bits, j + 1)) for j, p in enumerate(pieces)]
        self.terms = self.terms + self.arrived
        self.size = size
        return pieces

    def last(self):
        while self.stages:
            self.step()
        self.mine = self.part(0, 1)
        self.other = flip_stream(self.mine)
        return [self.mine]

    def result(self, first, count):
        at = slice(first, first + count)
        return self.mine[0][:, at].astype(wide) + self.other[0][:, at].astype(wide)

    def halves(self, side):
        mine, other = self.mine[0], self.other[0]
        first = jnp.where(side == 0, mine, other)
        second = jnp.where(side == 0, other, mine)
        return first.astype(wide), second.astype(wide)


def local(
    layer_input,
    out_cotangent,
    block_size,
    norm1_gain,
    norm1_bias,
    qkv_weight,
    qkv_bias,
    proj_weight,
    proj_bias,
    norm2_gain,
    norm2_bias,
    up_weight,
    up_bias,
    down_weight,
    down_bias,
):
    length, width = layer_input.shape[2:]
    batch = lax.axis_size("batch")
    noisy = lax.axis_index("stream").astype(jnp.int32).reshape(1)
    x = layer_input.reshape(length, width)
    g = out_cotangent.reshape(length, width)
    half = length // HALVES
    far_x = [
        lax.ppermute(x[i * half : (i + 1) * half], "stream", [(0, 1)]) for i in range(HALVES)
    ]
    tables = rotary_tables(length)
    me = lax.axis_index("batch").astype(jnp.int32)
    place, core = places_of(batch, me), (me % 2).reshape(1)
    h, q, k, v = project(x, qkv_weight, qkv_bias, norm1_gain, norm1_bias, tables)
    fars, attended = [], []
    for i in range(HALVES):
        fars = project_far(
            noisy, x, far_x[i], qkv_weight, qkv_bias, norm1_gain, norm1_bias, tables, i, fars
        )
        hf, kf, vf = fars
        attended = attend(block_size, q, k, v, kf, vf, i, HALVES, attended)
    o, lse = attended
    (out, dy, do, early), downw, upw = middle(
        place,
        core,
        noisy,
        x,
        o,
        g,
        proj_weight,
        proj_bias,
        norm2_gain,
        norm2_bias,
        up_weight,
        up_bias,
        down_weight,
        down_bias,
    )
    down, up = Reduction(downw), Reduction(upw, True)
    backs, after = [], []
    for i, (first, pairs) in enumerate(CUTS):
        if i == 1:
            down.wait_for(backs[0])
            up.wait_for(backs[0])
            after = down.step() + up.step()
        after = after + [b[0] for b in backs[-1:]]
        backs.append(
            attend_back(
                block_size, q, k, v, kf, vf, do, o, lse, tables, first, pairs, after, 2e10
            )
        )
    own, clean, sums = ([b[i] for b in backs] for i in range(3))
    qkvw = outer_qkv(
        h, hf, qkv_weight, norm1_gain, norm1_bias, early, own, clean, sums, place, core, []
    )
    qkv = Reduction(qkvw)
    up.wait_for(qkvw)
    down.wait_for(qkvw)
    qkv.wait_for(down.step() + up.step())
    after = qkv.step()
    dfar = project_far_back(noisy, x, far_x, clean, qkv_weight, norm1_gain, after)
    back_x = lax.ppermute(dfar, "stream", [(1, 0)])
    dx = project_back(noisy, x, dy, dfar, own, qkv_weight, norm1_gain, [])
    up.wait_for([dx])
    after = up.step()
    qkv.wait_for(after)
    after = qkv.step()
    down.wait_for(after)
    up.wait_for(qkv.arrived[:1])
    down.last()
    up.last()
    after = qkv.last()
    dx, down.other, up.other, _ = lax.optimization_barrier((dx, down.other, up.other, after))
    input_grad = (dx + back_x.astype(wide)).reshape(layer_input.shape)
    qkv.other, input_grad = lax.optimization_barrier((qkv.other, input_grad))
    ff = up_weight.shape[1]
    downw_grad = down.result(0, width)
    first, second = up.halves(noisy[0])
    upw_grad = jnp.concatenate([first[:, : ff // 2], second[:, : ff // 2]], axis=1)
    projw_grad = jnp.concatenate([first[:, ff // 2 :], second[:, ff // 2 :]], axis=1)
    qkvw_grad = qkv.result(0, 3 * width)
    vectors = qkv.result(3 * width, PAIR).T
    downb_grad, gain2_grad, bias2_grad, projb_grad = (vectors[i] for i in range(4))
    upb_grad, qkvb_grad = vectors[4:8].reshape(-1), vectors[8:11].reshape(-1)
    gain1_grad, bias1_grad = vectors[11], vectors[12]
    return (
        out.reshape(layer_input.shape),
        input_grad,
        gain1_grad,
        bias1_grad,
        qkvw_grad,
        qkvb_grad,
        projw_grad,
        projb_grad,
        gain2_grad,
        bias2_grad,
        upw_grad,
        upb_grad,
        downw_grad,
        downb_grad,
    )


def solution(mesh):
    rows = P("stream", "batch", None, None)
    return jax.shard_map(
        local,
        mesh=mesh,
        in_specs=(rows, rows, P("batch")) + (P(),) * 12,
        out_specs=(
            rows,
            rows,
            P("batch"),
            P("batch"),
            P("batch", None),
            P("batch"),
            P("batch", None),
            P("batch"),
            P("batch"),
            P("batch"),
            P("batch", None),
            P("batch"),
            P("batch", None),
            P("batch"),
        ),
        check_vma=False,
    )
```

```python
from functools import partial
import math

import jax
import jax.numpy as jnp
from jax import lax
from jax.experimental import pallas as pl
from jax.experimental.pallas import tpu as pltpu
from jax.sharding import PartitionSpec as P
import numpy as np

HEAD = 64
PAIR = 2 * HEAD
ROWS = 256
SPAN = 128
HALVES = 2
CUTS = ((0, 1), (1, 5))
full_vmem = 60

masked_value = -1e30
epsilon = 1e-05
low = jnp.bfloat16
wide = jnp.float32
score_scale = math.log2(math.e) / math.sqrt(HEAD)
ln2 = math.log(2.0)
gelu_c = math.sqrt(2.0 / math.pi)
gelu_k = 0.044715
mega = 1024 * 1024


def dot_nn(left, right):
    return lax.dot_general(left, right, (((1,), (0,)), ((), ())), preferred_element_type=wide)


def dot_nt(left, right):
    return lax.dot_general(left, right, (((1,), (1,)), ((), ())), preferred_element_type=wide)


def dot_tn(left, right):
    return lax.dot_general(left, right, (((0,), (0,)), ((), ())), preferred_element_type=wide)


def params(limit_mib):
    return pltpu.CompilerParams(
        dimension_semantics=("arbitrary",), vmem_limit_bytes=limit_mib * mega
    )


def cost(flops, nbytes, trans=0):
    return pl.CostEstimate(
        flops=int(flops), bytes_accessed=int(nbytes), transcendentals=int(trans)
    )


def ordered_call(
    kernel, after, grid, in_specs, operands, prefetch=(), work=4e9, into=(), **rest
):
    skip = len(prefetch) + len(operands)
    after = list(into) + list(after)

    def body(*refs):
        kernel(*refs[:skip], *refs[skip + len(after) :])

    out_specs = rest.pop("out_specs")
    scratch = rest.pop("scratch_shapes", [])
    call = pl.pallas_call(
        body,
        grid_spec=pltpu.PrefetchScalarGridSpec(
            num_scalar_prefetch=len(prefetch),
            grid=grid,
            in_specs=list(in_specs) + [pl.BlockSpec(memory_space=pl.ANY)] * len(after),
            out_specs=out_specs,
            scratch_shapes=scratch,
        ),
        compiler_params=pltpu.CompilerParams(
            dimension_semantics=("arbitrary",) * len(grid), vmem_limit_bytes=full_vmem * mega
        ),
        cost_estimate=cost(work, 1000),
        input_output_aliases={skip + i: i for i in range(len(into))},
        **rest,
    )
    return call(*prefetch, *operands, *after)


def row_of(ref, at=slice(None)):
    return ref[at].reshape(1, -1)


def whole_spec(shape):
    zeros = (0,) * len(shape)
    return pl.BlockSpec(shape, lambda *_: zeros, pipeline_mode=pl.Buffered(1))


def row_spec(width, rows=ROWS):
    return pl.BlockSpec((rows, width), lambda i: (i, 0))


def normalize(values):
    mean = jnp.mean(values, axis=-1, keepdims=True)
    centred = values - mean
    factor = lax.rsqrt(jnp.mean(centred * centred, axis=-1, keepdims=True) + epsilon)
    return (centred * factor, factor)


def norm_back(grad_normed, normed, factor):
    first = jnp.mean(grad_normed, axis=-1, keepdims=True)
    second = jnp.mean(grad_normed * normed, axis=-1, keepdims=True)
    return factor * (grad_normed - first - normed * second)


def rotary_tables(length):
    places = np.arange(length, dtype=np.float64)[:, None]
    column = np.arange(PAIR) % HEAD
    angle = places * (10000.0 ** (-2.0 * (column % (HEAD // 2)) / HEAD))[None, :]
    upper = (column >= HEAD // 2)[None, :]
    cosine, sine = np.cos(angle), np.sin(angle)
    tables = (cosine, np.where(upper, sine, 0.0), np.where(upper, 0.0, -sine))
    return tuple(jnp.asarray(t, dtype=wide) for t in tables)


def rotate(values, cosine, sine_a, sine_b):
    return (
        values * cosine
        + pltpu.roll(values, HEAD // 2, 1) * sine_a
        + pltpu.roll(values, PAIR - HEAD // 2, 1) * sine_b
    )


def rotate_back(values, cosine, sine_a, sine_b):
    return (
        values * cosine
        - pltpu.roll(values, HEAD // 2, 1) * sine_a
        - pltpu.roll(values, PAIR - HEAD // 2, 1) * sine_b
    )


def project_kernel(x_ref, w_ref, bias_ref, gain1_ref, bias1_ref, cos_ref, sa_ref, sb_ref,
                   h_ref, q_ref, k_ref, v_ref):
    width = x_ref.shape[1]
    normed, _ = normalize(x_ref[...].astype(wide))
    hidden = (normed * row_of(gain1_ref) + row_of(bias1_ref)).astype(low)
    h_ref[...] = hidden
    cosine, sa, sb = cos_ref[...], sa_ref[...], sb_ref[...]
    for out, part in ((q_ref, 0), (k_ref, 1), (v_ref, 2)):
        cols = slice(part * width, (part + 1) * width)
        mixed = dot_nn(hidden, w_ref[:, cols]) + row_of(bias_ref, cols)
        if part == 2:
            out[...] = mixed.astype(low)
            continue
        for group in range(width // PAIR):
            at = slice(group * PAIR, (group + 1) * PAIR)
            turned = rotate(mixed[:, at], cosine, sa, sb)
            if part == 0:
                turned = turned * score_scale
            out[:, at] = turned.astype(low)


def project_far_kernel(noisy_ref, x_ref, far_ref, wk_ref, wv_ref, bias_ref, gain1_ref, bias1_ref,
                       cos_ref, sa_ref, sb_ref, h_ref, k_ref, v_ref):
    width = x_ref.shape[1]
    source = jnp.where(noisy_ref[0] == 1, far_ref[...].astype(wide), x_ref[...].astype(wide))
    normed, _ = normalize(source)
    hidden = (normed * row_of(gain1_ref) + row_of(bias1_ref)).astype(low)
    h_ref[...] = hidden
    cosine, sa, sb = cos_ref[...], sa_ref[...], sb_ref[...]
    mixed = dot_nn(hidden, wk_ref[...]) + row_of(bias_ref, slice(width, 2 * width))
    for group in range(width // PAIR):
        at = slice(group * PAIR, (group + 1) * PAIR)
        k_ref[:, at] = rotate(mixed[:, at], cosine, sa, sb).astype(low)
    mixed = dot_nn(hidden, wv_ref[...]) + row_of(bias_ref, slice(2 * width, None))
    v_ref[...] = mixed.astype(low)


def project(x, weight, bias, gain1, bias1, tables):
    count, width = x.shape
    row = jax.ShapeDtypeStruct((count, width), low)
    return pl.pallas_call(
        project_kernel,
        grid=(count // ROWS,),
        in_specs=[
            row_spec(width),
            whole_spec(weight.shape),
            whole_spec(bias.shape),
            whole_spec(gain1.shape),
            whole_spec(bias1.shape),
            row_spec(PAIR),
            row_spec(PAIR),
            row_spec(PAIR),
        ],
        out_specs=[row_spec(width)] * 4,
        out_shape=[row] * 4,
        compiler_params=params(full_vmem),
        cost_estimate=cost(2 * count * width * 3 * width, 16e6),
        name="project",
    )(x, weight, bias, gain1, bias1, *tables)


def project_far(noisy, x, far, weight, bias, gain1, bias1, tables, part, into):
    count, width = x.shape
    steps = far.shape[0] // ROWS
    row = jax.ShapeDtypeStruct((count, width), low)

    def part_rows(columns):
        return pl.BlockSpec((ROWS, columns), lambda i: (part * steps + i, 0))

    return ordered_call(
        project_far_kernel,
        [],
        (steps,),
        [
            pl.BlockSpec(memory_space=pltpu.SMEM),
            part_rows(width),
            row_spec(width),
            pl.BlockSpec((width, width), lambda i: (0, 1), pipeline_mode=pl.Buffered(1)),
            pl.BlockSpec((width, width), lambda i: (0, 2), pipeline_mode=pl.Buffered(1)),
            whole_spec(bias.shape),
            whole_spec(gain1.shape),
            whole_spec(bias1.shape),
            part_rows(PAIR),
            part_rows(PAIR),
            part_rows(PAIR),
        ],
        (noisy, x, far, weight, weight, bias, gain1, bias1, *tables),
        into=into,
        out_specs=[part_rows(width)] * 3,
        out_shape=[row] * 3,
        name="project_far",
    )


def block_masks(size_ref):
    key = lax.broadcasted_iota(jnp.int32, (SPAN, 2 * SPAN), 0)
    query = lax.broadcasted_iota(jnp.int32, (SPAN, 2 * SPAN), 1) % SPAN
    near = (key ^ query) < size_ref[0]
    return near, key < query


def both_heads(rows):
    lane = lax.broadcasted_iota(jnp.int32, (1, PAIR), 1)
    none = jnp.zeros_like(rows)
    return jnp.concatenate(
        [jnp.where(lane < HEAD, rows, none), jnp.where(lane >= HEAD, rows, none)], axis=0
    )


def own_blocks(mixed):
    return jnp.concatenate([mixed[:HEAD, :SPAN], mixed[HEAD:, SPAN:]], axis=0).T


def attend_kernel(first, size_ref, q_ref, kn_ref, vn_ref, kf_ref, vf_ref, o_ref, lse_ref):
    near, far = block_masks(size_ref)
    vf_t = vf_ref[...].astype(wide).T.astype(low)
    vn_t = vn_ref[...].astype(wide).T.astype(low)
    parts = range(q_ref.shape[0] // SPAN)
    state = []
    for part in parts:
        past = (first + part) * SPAN
        own = slice(part * SPAN, (part + 1) * SPAN)
        query = both_heads(q_ref[own, :])
        scores = dot_nt(kf_ref[: past + SPAN, :], query)
        diag = jnp.where(
            near, dot_nt(kn_ref[own, :], query), jnp.where(far, scores[past:], masked_value)
        )
        state.append((past, own, scores, diag))
    probs = []
    for past, own, scores, diag in state:
        top = jnp.max(diag, axis=0, keepdims=True)
        if past:
            top = jnp.maximum(top, jnp.max(scores[:past], axis=0, keepdims=True))
        prob = jnp.exp2(diag - top)
        total = jnp.sum(prob, axis=0, keepdims=True)
        prob_near = jnp.where(near, prob, 0.0).astype(low)
        prob_far = jnp.where(near, 0.0, prob).astype(low)
        if past:
            prob = jnp.exp2(scores[:past] - top)
            total = total + jnp.sum(prob, axis=0, keepdims=True)
            prob_far = jnp.concatenate([prob.astype(low), prob_far], axis=0)
        lse = top + jnp.log2(total)
        lse_ref[0, 0:1, own] = lse[:, :SPAN]
        lse_ref[0, 1:2, own] = lse[:, SPAN:]
        probs.append((past, own, prob_near, prob_far, 1.0 / total))
    for past, own, prob_near, prob_far, scale in probs:
        mixed = dot_nn(vn_t[:, own], prob_near) + dot_nn(vf_t[:, : past + SPAN], prob_far)
        o_ref[own, :] = own_blocks(mixed * scale).astype(low)


def attend(size, q, kn, vn, kf, vf, part, parts, into):
    count, width = q.shape
    pairs = width // PAIR
    rows = count // parts
    own_spec = pl.BlockSpec((rows, PAIR), lambda p: (part, p))
    far_spec = pl.BlockSpec(((part + 1) * rows, PAIR), lambda p: (0, p))
    return ordered_call(
        partial(attend_kernel, part * rows // SPAN),
        [],
        (pairs,),
        [pl.BlockSpec(memory_space=pltpu.SMEM)] + [own_spec] * 3 + [far_spec] * 2,
        (size, q, kn, vn, kf, vf),
        into=into,
        out_specs=[own_spec, pl.BlockSpec((1, 2, rows), lambda p: (p, 0, part))],
        out_shape=[
            jax.ShapeDtypeStruct((count, width), low),
            jax.ShapeDtypeStruct((pairs, 2, count), wide),
        ],
        name="attend",
    )


def stages_of(batch):
    bits = list(range(1, batch.bit_length() - 1))
    rest = bits[1:]
    return [s for s in [bits[:1]] + [rest[i : i + 2] for i in range(0, len(rest), 2)] if s]


def mask_of(bits, digit):
    return sum(((digit >> i) & 1) << bit for i, bit in enumerate(bits))


def places_of(batch, me):
    relative = jnp.arange(0, batch, 2, dtype=jnp.int32) ^ (me - me % 2)
    place = jnp.zeros_like(relative)
    for bits in stages_of(batch):
        place = place * 2 ** len(bits)
        for i, bit in enumerate(bits):
            place = place + (((relative >> bit) & 1) << i)
    return place


def store_shards(place_ref, core_ref, result, keep_ref, send_ref, columns=slice(None)):
    shards = keep_ref.shape[0]
    rows = result.shape[0] // (2 * shards)

    def store(first_ref, second_ref):
        for pair in range(shards):
            at = place_ref[pair]
            start = 2 * pair * rows
            first_ref[at, :, columns] = result[start : start + rows].astype(low)
            second_ref[at, :, columns] = result[start + rows : start + 2 * rows].astype(low)

    pl.when(core_ref[0] == 0)(lambda: store(keep_ref, send_ref))
    pl.when(core_ref[0] == 1)(lambda: store(send_ref, keep_ref))


def split_shards(full, place, core):
    batch = 2 * place.shape[0]
    shards = full.reshape((batch // 2, 2, full.shape[0] // batch) + full.shape[1:])
    order = jnp.argsort(place)
    shards = jnp.take(shards, order, axis=0)
    return (
        jnp.where(core == 0, shards[:, 0], shards[:, 1]),
        jnp.where(core == 0, shards[:, 1], shards[:, 0]),
    )


def aligned(tall, batch):
    return tall % batch == 0 and (tall // batch) % 16 == 0


def store_columns(place_ref, core_ref, result, outs, columns=slice(None)):
    if len(outs) == 1:
        outs[0][:, columns] = result.astype(low)
    else:
        store_shards(place_ref, core_ref, result, *outs, columns)


def store_tall(place_ref, core_ref, step, result, outs):
    if len(outs) == 1:
        outs[0][...] = result.astype(low)
        return
    rows = outs[0].shape[2]

    def store(first_ref, second_ref):
        for x in range(2):
            at = place_ref[2 * step + x] % 2
            start = 2 * x * rows
            first_ref[0, at] = result[start : start + rows].astype(low)
            second_ref[0, at] = result[start + rows : start + 2 * rows].astype(low)

    pl.when(core_ref[0] == 0)(lambda: store(*outs))
    pl.when(core_ref[0] == 1)(lambda: store(*outs[::-1]))


def middle_kernel(row_steps, down_steps, tall_outs, place_ref, core_ref, tall_ref, x_ref, o_ref, g_ref,
                  wp_ref, bp_ref, gain2_ref, bias2_ref, wu_ref, bu_ref, wd_ref, bd_ref,
                  out_ref, dy_ref, do_ref, sums_ref,
                  *rest):
    downs, ups = rest[:tall_outs], rest[tall_outs:-5]
    a_all, right_all, hidden_all, o_all, g_all = rest[-5:]
    width = x_ref.shape[1]
    ff = wu_ref.shape[1]
    step = pl.program_id(0)

    def add_sum(start, values):
        at = slice(start, start + values.shape[1])
        sums_ref[:, at] += jnp.sum(values, axis=0, keepdims=True)

    @pl.when(step == 0)
    def _():
        sums_ref[...] = jnp.zeros_like(sums_ref)

    @pl.when(step < row_steps)
    def _():
        rows = pl.ds(pl.multiple_of(step * ROWS, ROWS), ROWS)
        parts = [slice(i * width, (i + 1) * width) for i in range(ff // width)]
        grad = g_ref[...]
        y = x_ref[...].astype(wide) + dot_nn(o_ref[...], wp_ref[...]) + row_of(bp_ref)
        das = [dot_nt(grad, wd_ref[cols, :]) for cols in parts]
        normed, factor = normalize(y)
        hidden = (normed * row_of(gain2_ref) + row_of(bias2_ref)).astype(low)
        o_all[rows, :] = o_ref[...]
        hidden_all[rows, :] = hidden
        g_all[rows, :] = grad
        grad_wide = grad.astype(wide)
        ups = [dot_nn(hidden, wu_ref[:, cols]) + row_of(bu_ref, cols) for cols in parts]
        acts, dus = [], []
        for part, cols in enumerate(parts):
            up = ups[part]
            square = up * up
            half = 0.5 + 0.5 * jnp.tanh(up * (gelu_c + (gelu_c * gelu_k) * square))
            active = (up * half).astype(low)
            slope = half + (up * (2.0 * gelu_c + (6.0 * gelu_c * gelu_k) * square)) * (
                half * (1.0 - half)
            )
            du = das[part] * slope
            du_low = du.astype(low)
            a_all[rows, cols] = active
            right_all[rows, cols] = du_low
            add_sum(4 * width + part * width, du)
            acts.append(active)
            dus.append(du_low)
        result = y + row_of(bd_ref)
        dh2 = jnp.zeros_like(y)
        for part, cols in enumerate(parts):
            dh2 = dh2 + dot_nt(dus[part], wu_ref[:, cols])
            result = result + dot_nn(acts[part], wd_ref[cols, :])
        out_ref[...] = result.astype(low)
        add_sum(0, grad_wide)
        add_sum(width, dh2 * normed)
        add_sum(2 * width, dh2)
        dy = grad_wide + norm_back(dh2 * row_of(gain2_ref), normed, factor)
        dy_ref[...] = dy
        add_sum(3 * width, dy)
        dy_low = dy.astype(low)
        right_all[rows, ff:] = dy_low
        do_ref[...] = dot_nt(dy_low, wp_ref[...]).astype(low)

    down_step = step - row_steps
    tile = ff // down_steps

    @pl.when((down_step >= 0) & (down_step < down_steps))
    def _():
        cols = pl.ds(pl.multiple_of(down_step * tile, 128), tile)
        store_tall(tall_ref, core_ref, down_step, dot_tn(a_all[:, cols], g_all[...]), downs)

    up_step = down_step - down_steps
    up_steps = ff // width

    @pl.when((up_step >= 0) & (up_step < up_steps))
    def _():
        cols = pl.ds(pl.multiple_of(up_step * width, 128), width)
        store_columns(place_ref, core_ref, dot_tn(hidden_all[...], right_all[:, cols]), ups)

    @pl.when(up_step == up_steps)
    def _():
        store_columns(place_ref, core_ref, dot_tn(o_all[...], right_all[:, ff:]), ups)


def middle(place, core, tall, x, o, g, wp, bp, gain2, bias2, wu, bu, wd, bd):
    count, width = x.shape
    ff = wu.shape[1]
    batch = 2 * place.shape[0]
    row_steps, up_steps = count // ROWS, ff // width + 1
    rows = ff // batch
    tall_aligned = aligned(ff, batch) and (4 * rows) % 128 == 0 and batch >= 8
    down_steps = batch // 4 if tall_aligned else ff // width

    def row(columns):
        return pl.BlockSpec((ROWS, columns), lambda i, *_: (jnp.minimum(i, row_steps - 1), 0))

    def down_at(i):
        return jnp.clip(i - row_steps, 0, down_steps - 1)

    def up_at(i):
        return jnp.clip(i - row_steps - down_steps, 0, up_steps - 1)

    if tall_aligned:
        deep = batch // 4
        down_shape = [jax.ShapeDtypeStruct((deep, 2, rows, width), low)] * 2
        down_specs = [
            pl.BlockSpec((1, 2, rows, width), lambda i, p, c, t: (t[2 * down_at(i)] // 2, 0, 0, 0))
        ] * 2
    else:
        down_shape = [jax.ShapeDtypeStruct((ff, width), low)]
        down_specs = [pl.BlockSpec((ff // down_steps, width), lambda i, *_: (down_at(i), 0))]
    if aligned(width, batch):
        shape = (batch // 2, width // batch)
        up_shape = [jax.ShapeDtypeStruct(shape + (ff + width,), low)] * 2
        up_specs = [pl.BlockSpec(shape + (width,), lambda i, *_: (0, 0, up_at(i)))] * 2
    else:
        up_shape = [jax.ShapeDtypeStruct((width, ff + width), low)]
        up_specs = [pl.BlockSpec((width, width), lambda i, *_: (0, up_at(i)))]
    sums = 4 * width + ff
    result = ordered_call(
        partial(middle_kernel, row_steps, down_steps, len(down_shape)),
        [],
        (row_steps + down_steps + up_steps,),
        [row(width)] * 3 + [whole_spec(a.shape) for a in (wp, bp, gain2, bias2, wu, bu, wd, bd)],
        (x, o, g, wp, bp, gain2, bias2, wu, bu, wd, bd),
        (place, core, tall),
        out_specs=[row(width)] * 3
        + [whole_spec((1, sums))]
        + down_specs
        + up_specs,
        out_shape=[
            jax.ShapeDtypeStruct((count, width), low),
            jax.ShapeDtypeStruct((count, width), wide),
            jax.ShapeDtypeStruct((count, width), low),
        ]
        + [jax.ShapeDtypeStruct((1, sums), wide)]
        + down_shape
        + up_shape,
        scratch_shapes=[
            pltpu.VMEM((count, ff), low),
            pltpu.VMEM((count, ff + width), low),
            pltpu.VMEM((count, width), low),
            pltpu.VMEM((count, width), low),
            pltpu.VMEM((count, width), low),
        ],
        name="middle",
    )
    rest = result[4:]
    if tall_aligned:
        downw = [r.reshape(batch // 2, rows, width) for r in rest[:2]]
    else:
        downw = split_shards(rest[0], tall, core[0])
    ups = rest[len(down_shape) :]
    upw = ups if len(ups) == 2 else split_shards(ups[0], place, core[0])
    return result[:4], downw, upw


def attend_back_kernel(size_ref, q_ref, kn_ref, vn_ref, kf_ref, vf_ref, do_ref, o_ref,
                       lse_ref, cos_ref, sa_ref, sb_ref,
                       own_ref, clean_ref, sums_ref, dkf_acc, dvf_acc):
    length = q_ref.shape[0]
    near, far = block_masks(size_ref)
    kf_t = kf_ref[...].astype(wide).T.astype(low)
    kn_t = kn_ref[...].astype(wide).T.astype(low)
    product = do_ref[...].astype(wide) * o_ref[...].astype(wide)
    high = product.astype(low)
    rest = (product - high.astype(wide)).astype(low)
    head_row = lax.broadcasted_iota(jnp.int32, (8, PAIR), 0)
    head_lane = lax.broadcasted_iota(jnp.int32, (8, PAIR), 1) // HEAD
    picker = jnp.where(head_row == head_lane, 1.0, 0.0).astype(low)
    deltas = dot_nt(picker, high) + dot_nt(picker, rest)
    cosine, sa, sb = cos_ref[...], sa_ref[...], sb_ref[...]
    sum_q = jnp.zeros((1, PAIR), wide)
    sum_kn = jnp.zeros((1, PAIR), wide)
    sum_vn = jnp.zeros((1, PAIR), wide)
    tiles = []
    for tile in range(length // SPAN):
        past = tile * SPAN
        here = slice(past, past + SPAN)
        query, grad = both_heads(q_ref[here, :]), both_heads(do_ref[here, :])
        scores = dot_nt(kf_ref[: past + SPAN, :], query)
        dprob = dot_nt(vf_ref[: past + SPAN, :], grad)
        diag = jnp.where(
            near,
            dot_nt(kn_ref[here, :], query),
            jnp.where(far, scores[past:], masked_value),
        )
        dprob_diag = jnp.where(near, dot_nt(vn_ref[here, :], grad), dprob[past:])
        tiles.append((past, here, query, grad, scores[:past], dprob[:past], diag, dprob_diag))
    results = []
    for past, here, query, grad, scores, dprob, diag, dprob_diag in tiles:
        lse = jnp.concatenate([lse_ref[0, 0:1, here], lse_ref[0, 1:2, here]], axis=1)
        delta = jnp.concatenate([deltas[0:1, here], deltas[1:2, here]], axis=1)
        prob_diag = jnp.exp2(diag - lse)
        ds_diag = prob_diag * (dprob_diag - delta)
        prob_near = jnp.where(near, prob_diag, 0.0).astype(low)
        ds_near = jnp.where(near, ds_diag, 0.0).astype(low)
        prob = jnp.where(near, 0.0, prob_diag).astype(low)
        dscore = jnp.where(near, 0.0, ds_diag).astype(low)
        if past:
            prob_past = jnp.exp2(scores - lse)
            ds_past = prob_past * (dprob - delta)
            prob = jnp.concatenate([prob_past.astype(low), prob], axis=0)
            dscore = jnp.concatenate([ds_past.astype(low), dscore], axis=0)
        results.append((past, here, query, grad, prob_near, ds_near, prob, dscore))
    for past, here, query, grad, prob_near, ds_near, prob, dscore in results:
        dkf, dvf = dot_nn(dscore, query), dot_nn(prob, grad)
        if past:
            dkf_acc[:past, :] += dkf[:past]
            dvf_acc[:past, :] += dvf[:past]
        dkf_acc[here, :] = dkf[past:]
        dvf_acc[here, :] = dvf[past:]
        dkn, dvn = dot_nn(ds_near, query), dot_nn(prob_near, grad)
        dqt = dot_nn(kn_t[:, here], ds_near) + dot_nn(kf_t[:, : past + SPAN], dscore)
        dq = own_blocks(dqt) * (1.0 / math.sqrt(HEAD))
        dq = rotate_back(dq, cosine[here], sa[here], sb[here])
        own_ref[0, here, :] = dq.astype(low)
        sum_q = sum_q + jnp.sum(dq, axis=0, keepdims=True)
        dkn = rotate_back(dkn * ln2, cosine[here], sa[here], sb[here])
        own_ref[1, here, :] = dkn.astype(low)
        sum_kn = sum_kn + jnp.sum(dkn, axis=0, keepdims=True)
        own_ref[2, here, :] = dvn.astype(low)
        sum_vn = sum_vn + jnp.sum(dvn, axis=0, keepdims=True)
    dkf = rotate_back(dkf_acc[...] * ln2, cosine, sa, sb)
    dvf = dvf_acc[...]
    clean_ref[0] = dkf.astype(low)
    clean_ref[1] = dvf.astype(low)
    sums_ref[0, 0:1, :] = sum_q
    sums_ref[0, 1:2, :] = sum_kn + jnp.sum(dkf, axis=0, keepdims=True)
    sums_ref[0, 2:3, :] = sum_vn + jnp.sum(dvf, axis=0, keepdims=True)


def attend_back(size, q, kn, vn, kf, vf, do, o, lse, tables, first, pairs, after, work):
    count = q.shape[0]
    pair_spec = pl.BlockSpec((count, PAIR), lambda p: (0, p + first))
    width = pairs * PAIR
    return ordered_call(
        attend_back_kernel,
        after,
        (pairs,),
        [pl.BlockSpec(memory_space=pltpu.SMEM)]
        + [pair_spec] * 7
        + [pl.BlockSpec((1, 2, count), lambda p: (p + first, 0, 0))]
        + [whole_spec(t.shape) for t in tables],
        (size, q, kn, vn, kf, vf, do, o, lse, *tables),
        out_specs=[
            pl.BlockSpec((3, count, PAIR), lambda p: (0, 0, p)),
            pl.BlockSpec((2, count, PAIR), lambda p: (0, 0, p)),
            pl.BlockSpec((1, 3, PAIR), lambda p: (p, 0, 0)),
        ],
        out_shape=[
            jax.ShapeDtypeStruct((3, count, width), low),
            jax.ShapeDtypeStruct((2, count, width), low),
            jax.ShapeDtypeStruct((pairs, 3, PAIR), wide),
        ],
        scratch_shapes=[
            pltpu.VMEM((count, PAIR), wide),
            pltpu.VMEM((count, PAIR), wide),
        ],
        work=work,
        name="attend_back",
    )


def spread_lanes(columns, batch):
    rows = columns.shape[0] // batch
    lane = lax.broadcasted_iota(jnp.int32, (rows, PAIR), 1)
    shards = []
    for shard in range(batch):
        block = columns[shard * rows : (shard + 1) * rows]
        for first, share in ((4, 4), (8, 3)):
            for j in range(share):
                chunk = share * shard + j
                at, start = first + chunk // batch, chunk % batch * rows
                block = jnp.where(
                    lane == first + j, columns[start : start + rows, at : at + 1], block
                )
        shards.append(block)
    return jnp.concatenate(shards, axis=0)


def qkv_kernel(cuts, batch, place_ref, core_ref, h_ref, hf_ref, w_ref, gain1_ref, bias1_ref,
               early_ref, *rest):
    own, clean, sums, rest = (
        rest[:cuts],
        rest[cuts : 2 * cuts],
        rest[2 * cuts : 3 * cuts],
        rest[3 * cuts :],
    )
    outs, (rows_ref, columns_ref, result_ref) = rest[:-3], rest[-3:]
    step = pl.program_id(0)
    width = h_ref.shape[1]
    result_ref[...] = dot_tn(h_ref[...], jnp.concatenate([r[0] for r in own], axis=1))

    @pl.when(step == 0)
    def _():
        columns_ref[...] = jnp.zeros_like(columns_ref)
        rows_ref[...] = jnp.zeros_like(rows_ref)
        for i in range(8):
            rows_ref[i : i + 1, :] = early_ref[:, i * width : (i + 1) * width]
        rows_ref[13:14, :] = row_of(gain1_ref)
        rows_ref[14:15, :] = row_of(bias1_ref)

    @pl.when(step > 0)
    def _():
        result_ref[...] += dot_tn(hf_ref[...], jnp.concatenate([r[0] for r in clean], axis=1))

    result = result_ref[...]
    cols = pl.ds(pl.multiple_of(step * width, 128), width)
    store_columns(place_ref, core_ref, result, outs, cols)
    weight = w_ref[...].astype(wide)
    totals = jnp.concatenate(
        [r[p, pl.ds(step, 1), :] for r in sums for p in range(r.shape[0])], axis=1
    )
    rows_ref[pl.ds(8 + step, 1), :] = totals
    lane = lax.broadcasted_iota(jnp.int32, (1, PAIR), 1)
    columns_ref[...] += jnp.where(
        lane == 0,
        jnp.sum(weight * result, axis=1, keepdims=True),
        jnp.sum(weight * totals, axis=1, keepdims=True),
    )

    @pl.when(step == 2)
    def _():
        columns = rows_ref[...].T
        bias = columns_ref[:, 1:2]
        gain = (columns_ref[:, 0:1] - columns[:, 14:15] * bias) / columns[:, 13:14]
        columns = jnp.where(lane == 11, gain, jnp.where(lane == 12, bias, columns))
        if len(outs) == 2:
            columns = spread_lanes(columns, batch)
        store_columns(place_ref, core_ref, columns, outs, slice(3 * width, 3 * width + PAIR))


def outer_qkv(h, hf, weight, gain1, bias1, early, own, clean, sums, place, core, after):
    count, width = h.shape
    batch = 2 * place.shape[0]
    columns = 3 * width + PAIR
    if aligned(width, batch):
        out_shape = [jax.ShapeDtypeStruct((batch // 2, width // batch, columns), low)] * 2
    else:
        out_shape = [jax.ShapeDtypeStruct((width, columns), low)]
    result = ordered_call(
        partial(qkv_kernel, len(own), batch),
        after,
        (3,),
        [whole_spec(h.shape)] * 2
        + [pl.BlockSpec((width, width), lambda i, p, c: (0, i))]
        + [whole_spec(v.shape) for v in (gain1, bias1, early)]
        + [pl.BlockSpec((1, count, r.shape[2]), lambda i, p, c: (i, 0, 0)) for r in own]
        + [
            pl.BlockSpec((1, count, r.shape[2]), lambda i, p, c: (jnp.maximum(i - 1, 0), 0, 0))
            for r in clean
        ]
        + [whole_spec(r.shape) for r in sums],
        (h, hf, weight, gain1, bias1, early, *own, *clean, *sums),
        (place, core),
        out_specs=[whole_spec(o.shape) for o in out_shape],
        out_shape=out_shape,
        scratch_shapes=[
            pltpu.VMEM((PAIR, width), wide),
            pltpu.VMEM((width, PAIR), wide),
            pltpu.VMEM((width, width), wide),
        ],
        work=1e8,
        name="outer_qkv",
    )
    if len(result) == 2:
        return result
    (full,) = result
    rows = width // batch
    start = 3 * width
    spread = [full[:, : start + 4]]
    for first, share in ((4, 4), (8, 3)):
        part = full[:, start + first : start + first + share].T.reshape(batch, share, rows)
        spread.append(part.transpose(0, 2, 1).reshape(width, share))
    spread.append(full[:, start + 11 :])
    return split_shards(jnp.concatenate(spread, axis=1), place, core[0])


def project_far_back_kernel(cuts, noisy_ref, x_ref, *rest):
    far, clean = rest[:HALVES], rest[HALVES : HALVES + cuts]
    w_ref, gain1_ref, dfar_ref = rest[HALVES + cuts :]
    width = x_ref.shape[1]
    steps = pl.num_programs(0) // HALVES
    source = x_ref[...].astype(wide)
    for i, ref in enumerate(far):
        chosen = (noisy_ref[0] == 1) & (pl.program_id(0) // steps == i)
        source = jnp.where(chosen, ref[...].astype(wide), source)
    normed, factor = normalize(source)
    dh = jnp.zeros_like(source)
    for part in range(2):
        grads = jnp.concatenate([c[part] for c in clean], axis=1)
        dh = dh + dot_nt(grads, w_ref[:, (part + 1) * width : (part + 2) * width])
    dfar_ref[...] = norm_back(dh * row_of(gain1_ref), normed, factor).astype(low)


def project_far_back(noisy, x, far, clean, weight, gain1, after):
    count, width = x.shape
    return ordered_call(
        partial(project_far_back_kernel, len(clean)),
        after,
        (count // ROWS,),
        [pl.BlockSpec(memory_space=pltpu.SMEM)]
        + [row_spec(width)]
        + [
            pl.BlockSpec(
                (ROWS, width),
                lambda i, first=n * f.shape[0] // ROWS, last=f.shape[0] // ROWS - 1: (
                    jnp.clip(i - first, 0, last),
                    0,
                ),
            )
            for n, f in enumerate(far)
        ]
        + [pl.BlockSpec((2, ROWS, c.shape[2]), lambda i: (0, i, 0)) for c in clean]
        + [whole_spec(weight.shape), whole_spec(gain1.shape)],
        (noisy, x, *far, *clean, weight, gain1),
        out_specs=row_spec(width),
        out_shape=jax.ShapeDtypeStruct((count, width), low),
        work=1.5e10,
        name="project_far_back",
    )


def project_back_kernel(cuts, noisy_ref, x_ref, dy_ref, dfar_ref, *rest):
    own = rest[:cuts]
    w_ref, gain1_ref, dx_ref = rest[cuts:]
    width = x_ref.shape[1]
    normed, factor = normalize(x_ref[...].astype(wide))
    dh = jnp.zeros_like(dy_ref)
    for part in range(3):
        grads = jnp.concatenate([c[part] for c in own], axis=1)
        dh = dh + dot_nt(grads, w_ref[:, part * width : (part + 1) * width])
    dx = dy_ref[...] + norm_back(dh * row_of(gain1_ref), normed, factor)
    dx_ref[...] = dx + jnp.where(noisy_ref[0] == 0, dfar_ref[...].astype(wide), 0.0)


def project_back(noisy, x, dy, dfar, own, weight, gain1, after):
    count, width = x.shape
    return ordered_call(
        partial(project_back_kernel, len(own)),
        after,
        (count // ROWS,),
        [pl.BlockSpec(memory_space=pltpu.SMEM)]
        + [row_spec(width)] * 3
        + [pl.BlockSpec((3, ROWS, c.shape[2]), lambda i: (0, i, 0)) for c in own]
        + [whole_spec(weight.shape), whole_spec(gain1.shape)],
        (noisy, x, dy, dfar, *own, weight, gain1),
        out_specs=row_spec(width),
        out_shape=jax.ShapeDtypeStruct((count, width), wide),
        work=1e8,
        name="project_back",
    )


def flip(values, mask):
    batch = lax.axis_size("batch")
    return lax.ppermute(values, "batch", [(i, i ^ mask) for i in range(batch)])


def flip_stream(values):
    return lax.ppermute(values, "stream", [(0, 1), (1, 0)])


def total(terms):
    result = terms[0].astype(wide)
    for term in terms[1:]:
        result = result + term.astype(wide)
    return result


class Reduction:
    def __init__(self, shards):
        keep, send = shards
        self.terms = [keep, flip(send, 1)]
        self.stages = stages_of(2 * keep.shape[0])
        self.size = keep.shape[0]

    def wait_for(self, others):
        self.terms, _ = lax.optimization_barrier((self.terms, list(others)))

    def step(self):
        bits = self.stages.pop(0)
        parts = 2 ** len(bits)
        size = self.size // parts
        pieces = [
            total([t[j * size : (j + 1) * size] for t in self.terms]).astype(low)
            for j in range(1, parts)
        ]
        arrived = [flip(p, mask_of(bits, j + 1)) for j, p in enumerate(pieces)]
        self.terms = self.terms + arrived
        self.arrived = arrived
        self.size = size
        return pieces

    def last(self):
        while self.stages:
            self.step()
        self.mine = total([t[:1] for t in self.terms]).astype(low)
        self.other = flip_stream(self.mine)
        return [self.mine]

    def result(self, first, count):
        at = slice(first, first + count)
        return self.mine[0][:, at].astype(wide) + self.other[0][:, at].astype(wide)


def local(
    layer_input,
    out_cotangent,
    block_size,
    norm1_gain,
    norm1_bias,
    qkv_weight,
    qkv_bias,
    proj_weight,
    proj_bias,
    norm2_gain,
    norm2_bias,
    up_weight,
    up_bias,
    down_weight,
    down_bias,
):
    length, width = layer_input.shape[2:]
    batch = lax.axis_size("batch")
    noisy = lax.axis_index("stream").astype(jnp.int32).reshape(1)
    x = layer_input.reshape(length, width)
    g = out_cotangent.reshape(length, width)
    half = length // HALVES
    far_x = [
        lax.ppermute(x[i * half : (i + 1) * half], "stream", [(0, 1)]) for i in range(HALVES)
    ]
    tables = rotary_tables(length)
    me = lax.axis_index("batch").astype(jnp.int32)
    place, core = places_of(batch, me), (me % 2).reshape(1)
    natural = jnp.arange(batch // 2, dtype=jnp.int32)
    h, q, k, v = project(x, qkv_weight, qkv_bias, norm1_gain, norm1_bias, tables)
    fars, attended = [], []
    for i in range(HALVES):
        fars = project_far(
            noisy, x, far_x[i], qkv_weight, qkv_bias, norm1_gain, norm1_bias, tables, i, fars
        )
        hf, kf, vf = fars
        attended = attend(block_size, q, k, v, kf, vf, i, HALVES, attended)
    o, lse = attended
    (out, dy, do, early), downw, upw = middle(
        place,
        core,
        natural,
        x,
        o,
        g,
        proj_weight,
        proj_bias,
        norm2_gain,
        norm2_bias,
        up_weight,
        up_bias,
        down_weight,
        down_bias,
    )
    up = Reduction(upw)
    down_terms = [downw[0], flip(downw[1], 1)]
    backs, after = [], []
    for i, (first, pairs) in enumerate(CUTS):
        if i == 1:
            down_terms, _ = lax.optimization_barrier((down_terms, backs[0]))
            down_sum = total(down_terms).astype(low)
            up.wait_for(backs[0])
            after = [down_sum] + up.step()
        after = after + [b[0] for b in backs[-1:]]
        backs.append(
            attend_back(
                block_size, q, k, v, kf, vf, do, o, lse, tables, first, pairs, after, 2e10
            )
        )
    own, clean, sums = ([b[i] for b in backs] for i in range(3))
    qkvw = outer_qkv(
        h, hf, qkv_weight, norm1_gain, norm1_bias, early, own, clean, sums, place, core, []
    )
    qkvw, _ = lax.optimization_barrier((list(qkvw), up.arrived))
    qkv = Reduction(qkvw)
    qkv.wait_for(up.step())
    after = qkv.step()
    dfar = project_far_back(noisy, x, far_x, clean, qkv_weight, norm1_gain, after)
    back_x = lax.ppermute(dfar, "stream", [(1, 0)])
    dx = project_back(noisy, x, dy, dfar, own, qkv_weight, norm1_gain, [])
    qkv.wait_for([dx])
    pieces = qkv.step()
    up.wait_for(pieces)
    up.last()
    after = qkv.last()
    down_mine = lax.psum_scatter(
        down_sum,
        "batch",
        scatter_dimension=0,
        tiled=True,
        axis_index_groups=[[c + 2 * i for i in range(batch // 2)] for c in range(2)],
    )
    down_mine, _ = lax.optimization_barrier((down_mine, qkv.arrived[:1]))
    down_other = flip_stream(down_mine)
    dx, down_other, up.other, _ = lax.optimization_barrier((dx, down_other, up.other, after))
    input_grad = (dx + back_x.astype(wide)).reshape(layer_input.shape)
    qkv.other, input_grad = lax.optimization_barrier((qkv.other, input_grad))
    ff = up_weight.shape[1]
    downw_grad = (down_mine.astype(wide) + down_other.astype(wide))[0]
    upw_grad, projw_grad = up.result(0, ff), up.result(ff, width)
    qkvw_grad = qkv.result(0, 3 * width)
    vectors = qkv.result(3 * width, PAIR).T
    downb_grad, gain2_grad, bias2_grad, projb_grad = (vectors[i] for i in range(4))
    upb_grad, qkvb_grad = vectors[4:8].reshape(-1), vectors[8:11].reshape(-1)
    gain1_grad, bias1_grad = vectors[11], vectors[12]
    return (
        out.reshape(layer_input.shape),
        input_grad,
        gain1_grad,
        bias1_grad,
        qkvw_grad,
        qkvb_grad,
        projw_grad,
        projb_grad,
        gain2_grad,
        bias2_grad,
        upw_grad,
        upb_grad,
        downw_grad,
        downb_grad,
    )


def solution(mesh):
    rows = P("stream", "batch", None, None)
    return jax.shard_map(
        local,
        mesh=mesh,
        in_specs=(rows, rows, P("batch")) + (P(),) * 12,
        out_specs=(
            rows,
            rows,
            P("batch"),
            P("batch"),
            P("batch", None),
            P("batch"),
            P("batch", None),
            P("batch"),
            P("batch"),
            P("batch"),
            P("batch", None),
            P("batch"),
            P("batch", None),
            P("batch"),
        ),
        check_vma=False,
    )
```

```python
from functools import partial
import math

import jax
import jax.numpy as jnp
from jax import lax
from jax.experimental import pallas as pl
from jax.experimental.pallas import tpu as pltpu
from jax.sharding import PartitionSpec as P
import numpy as np

HEAD = 64
PAIR = 2 * HEAD
ROWS = 256
SPAN = 128
HALVES = 2
CUTS = ((0, 1), (1, 5))
full_vmem = 60

masked_value = -1e30
epsilon = 1e-05
low = jnp.bfloat16
wide = jnp.float32
score_scale = math.log2(math.e) / math.sqrt(HEAD)
ln2 = math.log(2.0)
gelu_c = math.sqrt(2.0 / math.pi)
gelu_k = 0.044715
mega = 1024 * 1024


def dot_nn(left, right):
    return lax.dot_general(left, right, (((1,), (0,)), ((), ())), preferred_element_type=wide)


def dot_nt(left, right):
    return lax.dot_general(left, right, (((1,), (1,)), ((), ())), preferred_element_type=wide)


def dot_tn(left, right):
    return lax.dot_general(left, right, (((0,), (0,)), ((), ())), preferred_element_type=wide)


def params(limit_mib):
    return pltpu.CompilerParams(
        dimension_semantics=("arbitrary",), vmem_limit_bytes=limit_mib * mega
    )


def cost(flops, nbytes, trans=0):
    return pl.CostEstimate(
        flops=int(flops), bytes_accessed=int(nbytes), transcendentals=int(trans)
    )


def ordered_call(
    kernel, after, grid, in_specs, operands, prefetch=(), work=4e9, into=(), **rest
):
    skip = len(prefetch) + len(operands)
    after = list(into) + list(after)

    def body(*refs):
        kernel(*refs[:skip], *refs[skip + len(after) :])

    out_specs = rest.pop("out_specs")
    scratch = rest.pop("scratch_shapes", [])
    call = pl.pallas_call(
        body,
        grid_spec=pltpu.PrefetchScalarGridSpec(
            num_scalar_prefetch=len(prefetch),
            grid=grid,
            in_specs=list(in_specs) + [pl.BlockSpec(memory_space=pl.ANY)] * len(after),
            out_specs=out_specs,
            scratch_shapes=scratch,
        ),
        compiler_params=pltpu.CompilerParams(
            dimension_semantics=("arbitrary",) * len(grid), vmem_limit_bytes=full_vmem * mega
        ),
        cost_estimate=cost(work, 1000),
        input_output_aliases={skip + i: i for i in range(len(into))},
        **rest,
    )
    return call(*prefetch, *operands, *after)


def row_of(ref, at=slice(None)):
    return ref[at].reshape(1, -1)


def whole_spec(shape):
    zeros = (0,) * len(shape)
    return pl.BlockSpec(shape, lambda *_: zeros, pipeline_mode=pl.Buffered(1))


def row_spec(width, rows=ROWS):
    return pl.BlockSpec((rows, width), lambda i: (i, 0))


def normalize(values):
    mean = jnp.mean(values, axis=-1, keepdims=True)
    centred = values - mean
    factor = lax.rsqrt(jnp.mean(centred * centred, axis=-1, keepdims=True) + epsilon)
    return (centred * factor, factor)


def norm_back(grad_normed, normed, factor):
    first = jnp.mean(grad_normed, axis=-1, keepdims=True)
    second = jnp.mean(grad_normed * normed, axis=-1, keepdims=True)
    return factor * (grad_normed - first - normed * second)


def rotary_tables(length):
    places = np.arange(length, dtype=np.float64)[:, None]
    column = np.arange(PAIR) % HEAD
    angle = places * (10000.0 ** (-2.0 * (column % (HEAD // 2)) / HEAD))[None, :]
    upper = (column >= HEAD // 2)[None, :]
    cosine, sine = np.cos(angle), np.sin(angle)
    tables = (cosine, np.where(upper, sine, 0.0), np.where(upper, 0.0, -sine))
    return tuple(jnp.asarray(t, dtype=wide) for t in tables)


def rotate(values, cosine, sine_a, sine_b):
    return (
        values * cosine
        + pltpu.roll(values, HEAD // 2, 1) * sine_a
        + pltpu.roll(values, PAIR - HEAD // 2, 1) * sine_b
    )


def rotate_back(values, cosine, sine_a, sine_b):
    return (
        values * cosine
        - pltpu.roll(values, HEAD // 2, 1) * sine_a
        - pltpu.roll(values, PAIR - HEAD // 2, 1) * sine_b
    )


def project_kernel(x_ref, w_ref, bias_ref, gain1_ref, bias1_ref, cos_ref, sa_ref, sb_ref,
                   h_ref, q_ref, k_ref, v_ref):
    width = x_ref.shape[1]
    normed, _ = normalize(x_ref[...].astype(wide))
    hidden = (normed * row_of(gain1_ref) + row_of(bias1_ref)).astype(low)
    h_ref[...] = hidden
    cosine, sa, sb = cos_ref[...], sa_ref[...], sb_ref[...]
    for out, part in ((q_ref, 0), (k_ref, 1), (v_ref, 2)):
        cols = slice(part * width, (part + 1) * width)
        mixed = dot_nn(hidden, w_ref[:, cols]) + row_of(bias_ref, cols)
        if part == 2:
            out[...] = mixed.astype(low)
            continue
        for group in range(width // PAIR):
            at = slice(group * PAIR, (group + 1) * PAIR)
            turned = rotate(mixed[:, at], cosine, sa, sb)
            if part == 0:
                turned = turned * score_scale
            out[:, at] = turned.astype(low)


def project_far_kernel(noisy_ref, x_ref, far_ref, wk_ref, wv_ref, bias_ref, gain1_ref, bias1_ref,
                       cos_ref, sa_ref, sb_ref, h_ref, k_ref, v_ref):
    width = x_ref.shape[1]
    source = jnp.where(noisy_ref[0] == 1, far_ref[...].astype(wide), x_ref[...].astype(wide))
    normed, _ = normalize(source)
    hidden = (normed * row_of(gain1_ref) + row_of(bias1_ref)).astype(low)
    h_ref[...] = hidden
    cosine, sa, sb = cos_ref[...], sa_ref[...], sb_ref[...]
    mixed = dot_nn(hidden, wk_ref[...]) + row_of(bias_ref, slice(width, 2 * width))
    for group in range(width // PAIR):
        at = slice(group * PAIR, (group + 1) * PAIR)
        k_ref[:, at] = rotate(mixed[:, at], cosine, sa, sb).astype(low)
    mixed = dot_nn(hidden, wv_ref[...]) + row_of(bias_ref, slice(2 * width, None))
    v_ref[...] = mixed.astype(low)


def project(x, weight, bias, gain1, bias1, tables):
    count, width = x.shape
    row = jax.ShapeDtypeStruct((count, width), low)
    return pl.pallas_call(
        project_kernel,
        grid=(count // ROWS,),
        in_specs=[
            row_spec(width),
            whole_spec(weight.shape),
            whole_spec(bias.shape),
            whole_spec(gain1.shape),
            whole_spec(bias1.shape),
            row_spec(PAIR),
            row_spec(PAIR),
            row_spec(PAIR),
        ],
        out_specs=[row_spec(width)] * 4,
        out_shape=[row] * 4,
        compiler_params=params(full_vmem),
        cost_estimate=cost(2 * count * width * 3 * width, 16e6),
        name="project",
    )(x, weight, bias, gain1, bias1, *tables)


def project_far(noisy, x, far, weight, bias, gain1, bias1, tables, part, into):
    count, width = x.shape
    steps = far.shape[0] // ROWS
    row = jax.ShapeDtypeStruct((count, width), low)

    def part_rows(columns):
        return pl.BlockSpec((ROWS, columns), lambda i: (part * steps + i, 0))

    return ordered_call(
        project_far_kernel,
        [],
        (steps,),
        [
            pl.BlockSpec(memory_space=pltpu.SMEM),
            part_rows(width),
            row_spec(width),
            pl.BlockSpec((width, width), lambda i: (0, 1), pipeline_mode=pl.Buffered(1)),
            pl.BlockSpec((width, width), lambda i: (0, 2), pipeline_mode=pl.Buffered(1)),
            whole_spec(bias.shape),
            whole_spec(gain1.shape),
            whole_spec(bias1.shape),
            part_rows(PAIR),
            part_rows(PAIR),
            part_rows(PAIR),
        ],
        (noisy, x, far, weight, weight, bias, gain1, bias1, *tables),
        into=into,
        out_specs=[part_rows(width)] * 3,
        out_shape=[row] * 3,
        name="project_far",
    )


def block_masks(size_ref):
    key = lax.broadcasted_iota(jnp.int32, (SPAN, 2 * SPAN), 0)
    query = lax.broadcasted_iota(jnp.int32, (SPAN, 2 * SPAN), 1) % SPAN
    near = (key ^ query) < size_ref[0]
    return near, key < query


def both_heads(rows):
    lane = lax.broadcasted_iota(jnp.int32, (1, PAIR), 1)
    none = jnp.zeros_like(rows)
    return jnp.concatenate(
        [jnp.where(lane < HEAD, rows, none), jnp.where(lane >= HEAD, rows, none)], axis=0
    )


def own_blocks(mixed):
    return jnp.concatenate([mixed[:HEAD, :SPAN], mixed[HEAD:, SPAN:]], axis=0).T


def attend_kernel(first, size_ref, q_ref, kn_ref, vn_ref, kf_ref, vf_ref, o_ref, lse_ref):
    near, far = block_masks(size_ref)
    vf_t = vf_ref[...].astype(wide).T.astype(low)
    vn_t = vn_ref[...].astype(wide).T.astype(low)
    parts = range(q_ref.shape[0] // SPAN)
    state = []
    for part in parts:
        past = (first + part) * SPAN
        own = slice(part * SPAN, (part + 1) * SPAN)
        query = both_heads(q_ref[own, :])
        scores = dot_nt(kf_ref[: past + SPAN, :], query)
        diag = jnp.where(
            near, dot_nt(kn_ref[own, :], query), jnp.where(far, scores[past:], masked_value)
        )
        state.append((past, own, scores, diag))
    probs = []
    for past, own, scores, diag in state:
        top = jnp.max(diag, axis=0, keepdims=True)
        if past:
            top = jnp.maximum(top, jnp.max(scores[:past], axis=0, keepdims=True))
        prob = jnp.exp2(diag - top)
        total = jnp.sum(prob, axis=0, keepdims=True)
        prob_near = jnp.where(near, prob, 0.0).astype(low)
        prob_far = jnp.where(near, 0.0, prob).astype(low)
        if past:
            prob = jnp.exp2(scores[:past] - top)
            total = total + jnp.sum(prob, axis=0, keepdims=True)
            prob_far = jnp.concatenate([prob.astype(low), prob_far], axis=0)
        lse = top + jnp.log2(total)
        lse_ref[0, 0:1, own] = lse[:, :SPAN]
        lse_ref[0, 1:2, own] = lse[:, SPAN:]
        probs.append((past, own, prob_near, prob_far, 1.0 / total))
    for past, own, prob_near, prob_far, scale in probs:
        mixed = dot_nn(vn_t[:, own], prob_near) + dot_nn(vf_t[:, : past + SPAN], prob_far)
        o_ref[own, :] = own_blocks(mixed * scale).astype(low)


def attend(size, q, kn, vn, kf, vf, part, parts, into):
    count, width = q.shape
    pairs = width // PAIR
    rows = count // parts
    own_spec = pl.BlockSpec((rows, PAIR), lambda p: (part, p))
    far_spec = pl.BlockSpec(((part + 1) * rows, PAIR), lambda p: (0, p))
    return ordered_call(
        partial(attend_kernel, part * rows // SPAN),
        [],
        (pairs,),
        [pl.BlockSpec(memory_space=pltpu.SMEM)] + [own_spec] * 3 + [far_spec] * 2,
        (size, q, kn, vn, kf, vf),
        into=into,
        out_specs=[own_spec, pl.BlockSpec((1, 2, rows), lambda p: (p, 0, part))],
        out_shape=[
            jax.ShapeDtypeStruct((count, width), low),
            jax.ShapeDtypeStruct((pairs, 2, count), wide),
        ],
        name="attend",
    )


def stages_of(batch):
    bits = list(range(1, batch.bit_length() - 1))
    stages = [bits[:1]]
    rest = bits[1:]
    while rest:
        stages.append(rest[:2])
        rest = rest[2:]
    return [s for s in stages if s]


def mask_of(bits, digit):
    return sum(((digit >> i) & 1) << bit for i, bit in enumerate(bits))


def places_of(batch, me):
    relative = jnp.arange(0, batch, 2, dtype=jnp.int32) ^ (me - me % 2)
    place = jnp.zeros_like(relative)
    for bits in stages_of(batch):
        place = place * 2 ** len(bits)
        for i, bit in enumerate(bits):
            place = place + (((relative >> bit) & 1) << i)
    return place


def store_shards(place_ref, core_ref, result, keep_ref, send_ref, columns=slice(None)):
    shards = keep_ref.shape[0]
    rows = result.shape[0] // (2 * shards)

    def store(first_ref, second_ref):
        for pair in range(shards):
            at = place_ref[pair]
            start = 2 * pair * rows
            first_ref[at, :, columns] = result[start : start + rows].astype(low)
            second_ref[at, :, columns] = result[start + rows : start + 2 * rows].astype(low)

    pl.when(core_ref[0] == 0)(lambda: store(keep_ref, send_ref))
    pl.when(core_ref[0] == 1)(lambda: store(send_ref, keep_ref))


def split_shards(full, place, core):
    batch = 2 * place.shape[0]
    shards = full.reshape((batch // 2, 2, full.shape[0] // batch) + full.shape[1:])
    order = jnp.argsort(place)
    shards = jnp.take(shards, order, axis=0)
    return (
        jnp.where(core == 0, shards[:, 0], shards[:, 1]),
        jnp.where(core == 0, shards[:, 1], shards[:, 0]),
    )


def aligned(tall, batch):
    return tall % batch == 0 and (tall // batch) % 16 == 0


def store_columns(place_ref, core_ref, result, outs, columns=slice(None)):
    if len(outs) == 1:
        outs[0][:, columns] = result.astype(low)
    else:
        store_shards(place_ref, core_ref, result, *outs, columns)


def store_tall(place_ref, core_ref, step, result, outs):
    if len(outs) == 1:
        outs[0][...] = result.astype(low)
        return
    rows = outs[0].shape[2]
    places = place_ref.shape[0] // 2

    def store(first_ref, second_ref):
        for x in range(2):
            at = place_ref[2 * step + x] // places
            start = 2 * x * rows
            first_ref[at, 0] = result[start : start + rows].astype(low)
            second_ref[at, 0] = result[start + rows : start + 2 * rows].astype(low)

    pl.when(core_ref[0] == 0)(lambda: store(*outs))
    pl.when(core_ref[0] == 1)(lambda: store(*outs[::-1]))


def middle_kernel(row_steps, down_steps, tall_outs, place_ref, core_ref, side_ref, x_ref, o_ref, g_ref,
                  wp_ref, bp_ref, gain2_ref, bias2_ref, wu_ref, bu_ref, wd_ref, bd_ref,
                  out_ref, dy_ref, do_ref, sums_ref,
                  *rest):
    downs, ups = rest[:tall_outs], rest[tall_outs:-5]
    a_all, right_all, hidden_all, o_all, g_all = rest[-5:]
    width = x_ref.shape[1]
    ff = wu_ref.shape[1]
    step = pl.program_id(0)

    def add_sum(start, values):
        at = slice(start, start + values.shape[1])
        sums_ref[:, at] += jnp.sum(values, axis=0, keepdims=True)

    @pl.when(step == 0)
    def _():
        sums_ref[...] = jnp.zeros_like(sums_ref)

    @pl.when(step < row_steps)
    def _():
        rows = pl.ds(pl.multiple_of(step * ROWS, ROWS), ROWS)
        parts = [slice(i * width, (i + 1) * width) for i in range(ff // width)]
        grad = g_ref[...]
        y = x_ref[...].astype(wide) + dot_nn(o_ref[...], wp_ref[...]) + row_of(bp_ref)
        das = [dot_nt(grad, wd_ref[cols, :]) for cols in parts]
        normed, factor = normalize(y)
        hidden = (normed * row_of(gain2_ref) + row_of(bias2_ref)).astype(low)
        o_all[rows, :] = o_ref[...]
        hidden_all[rows, :] = hidden
        g_all[rows, :] = grad
        grad_wide = grad.astype(wide)
        ups = [dot_nn(hidden, wu_ref[:, cols]) + row_of(bu_ref, cols) for cols in parts]
        acts, dus = [], []
        for part, cols in enumerate(parts):
            up = ups[part]
            square = up * up
            half = 0.5 + 0.5 * jnp.tanh(up * (gelu_c + (gelu_c * gelu_k) * square))
            active = (up * half).astype(low)
            slope = half + (up * (2.0 * gelu_c + (6.0 * gelu_c * gelu_k) * square)) * (
                half * (1.0 - half)
            )
            du = das[part] * slope
            du_low = du.astype(low)
            a_all[rows, cols] = active
            right_all[rows, cols] = du_low
            add_sum(4 * width + part * width, du)
            acts.append(active)
            dus.append(du_low)
        result = y + row_of(bd_ref)
        dh2 = jnp.zeros_like(y)
        for part, cols in enumerate(parts):
            dh2 = dh2 + dot_nt(dus[part], wu_ref[:, cols])
            result = result + dot_nn(acts[part], wd_ref[cols, :])
        out_ref[...] = result.astype(low)
        add_sum(0, grad_wide)
        add_sum(width, dh2 * normed)
        add_sum(2 * width, dh2)
        dy = grad_wide + norm_back(dh2 * row_of(gain2_ref), normed, factor)
        dy_ref[...] = dy
        add_sum(3 * width, dy)
        dy_low = dy.astype(low)
        right_all[rows, ff:] = dy_low
        do_ref[...] = dot_nt(dy_low, wp_ref[...]).astype(low)

    down_step = step - row_steps
    tile = ff // down_steps

    @pl.when((down_step >= 0) & (down_step < down_steps))
    def _():
        cols = pl.ds(pl.multiple_of(down_step * tile, 128), tile)
        store_tall(place_ref, core_ref, down_step, dot_tn(a_all[:, cols], g_all[...]), downs)

    half = down_step - down_steps

    @pl.when(half >= 0)
    def _():
        outs = [u.at[0] for u in ups] if len(ups) == 2 else ups
        for start in range(0, ff // 2, width):
            cols = pl.ds(pl.multiple_of(half * (ff // 2) + start, 128), width)
            result = dot_tn(hidden_all[...], right_all[:, cols])
            store_columns(place_ref, core_ref, result, outs, slice(start, start + width))
        cols = pl.ds(pl.multiple_of(ff + half * (width // 2), 128), width // 2)
        result = dot_tn(o_all[...], right_all[:, cols])
        store_columns(
            place_ref, core_ref, result, outs, slice(ff // 2, ff // 2 + width // 2)
        )


def middle(place, core, side, x, o, g, wp, bp, gain2, bias2, wu, bu, wd, bd):
    count, width = x.shape
    ff = wu.shape[1]
    batch = 2 * place.shape[0]
    row_steps, up_steps = count // ROWS, 2
    rows = ff // batch
    tall_aligned = aligned(ff, batch) and (4 * rows) % 128 == 0 and batch >= 8
    down_steps = batch // 4 if tall_aligned else ff // width

    def row(columns):
        return pl.BlockSpec((ROWS, columns), lambda i, *_: (jnp.minimum(i, row_steps - 1), 0))

    def down_at(i):
        return jnp.clip(i - row_steps, 0, down_steps - 1)

    def up_at(i):
        return jnp.clip(i - row_steps - down_steps, 0, up_steps - 1)

    if tall_aligned:
        deep = batch // 4
        down_shape = [jax.ShapeDtypeStruct((2, deep, rows, width), low)] * 2
        down_specs = [
            pl.BlockSpec(
                (2, 1, rows, width), lambda i, p, c, s: (0, p[2 * down_at(i)] % deep, 0, 0)
            )
        ] * 2
    else:
        down_shape = [jax.ShapeDtypeStruct((ff, width), low)]
        down_specs = [pl.BlockSpec((ff // down_steps, width), lambda i, *_: (down_at(i), 0))]
    columns = (ff + width) // 2
    if aligned(width, batch):
        shape = (batch // 2, width // batch, columns)
        up_shape = [jax.ShapeDtypeStruct((2,) + shape, low)] * 2
        up_specs = [pl.BlockSpec((1,) + shape, lambda i, p, c, s: (up_at(i) ^ s[0], 0, 0, 0))] * 2
    else:
        up_shape = [jax.ShapeDtypeStruct((width, ff + width), low)]
        up_specs = [pl.BlockSpec((width, columns), lambda i, *_: (0, up_at(i)))]
    sums = 4 * width + ff
    result = ordered_call(
        partial(middle_kernel, row_steps, down_steps, len(down_shape)),
        [],
        (row_steps + down_steps + up_steps,),
        [row(width)] * 3 + [whole_spec(a.shape) for a in (wp, bp, gain2, bias2, wu, bu, wd, bd)],
        (x, o, g, wp, bp, gain2, bias2, wu, bu, wd, bd),
        (place, core, side),
        out_specs=[row(width)] * 3
        + [whole_spec((1, sums))]
        + down_specs
        + up_specs,
        out_shape=[
            jax.ShapeDtypeStruct((count, width), low),
            jax.ShapeDtypeStruct((count, width), wide),
            jax.ShapeDtypeStruct((count, width), low),
        ]
        + [jax.ShapeDtypeStruct((1, sums), wide)]
        + down_shape
        + up_shape,
        scratch_shapes=[
            pltpu.VMEM((count, ff), low),
            pltpu.VMEM((count, ff + width), low),
            pltpu.VMEM((count, width), low),
            pltpu.VMEM((count, width), low),
            pltpu.VMEM((count, width), low),
        ],
        name="middle",
    )
    rest = result[4:]
    if tall_aligned:
        downw = [r.reshape(batch // 2, rows, width) for r in rest[:2]]
    else:
        downw = split_shards(rest[0], place, core[0])
    ups = rest[len(down_shape) :]
    if len(ups) == 2:
        return result[:4], downw, ups
    parts = [
        split_shards(ups[0][:, i * columns : (i + 1) * columns], place, core[0]) for i in range(2)
    ]
    upw = []
    for first, second in zip(*parts):
        both = jnp.stack([first, second])
        upw.append(jnp.where(side[0] == 0, both, both[::-1]))
    return result[:4], downw, upw


def attend_back_kernel(size_ref, q_ref, kn_ref, vn_ref, kf_ref, vf_ref, do_ref, o_ref,
                       lse_ref, cos_ref, sa_ref, sb_ref,
                       own_ref, clean_ref, sums_ref, dkf_acc, dvf_acc):
    length = q_ref.shape[0]
    near, far = block_masks(size_ref)
    kf_t = kf_ref[...].astype(wide).T.astype(low)
    kn_t = kn_ref[...].astype(wide).T.astype(low)
    product = do_ref[...].astype(wide) * o_ref[...].astype(wide)
    high = product.astype(low)
    rest = (product - high.astype(wide)).astype(low)
    head_row = lax.broadcasted_iota(jnp.int32, (8, PAIR), 0)
    head_lane = lax.broadcasted_iota(jnp.int32, (8, PAIR), 1) // HEAD
    picker = jnp.where(head_row == head_lane, 1.0, 0.0).astype(low)
    deltas = dot_nt(picker, high) + dot_nt(picker, rest)
    cosine, sa, sb = cos_ref[...], sa_ref[...], sb_ref[...]
    sum_q = jnp.zeros((1, PAIR), wide)
    sum_kn = jnp.zeros((1, PAIR), wide)
    sum_vn = jnp.zeros((1, PAIR), wide)
    tiles = []
    for tile in range(length // SPAN):
        past = tile * SPAN
        here = slice(past, past + SPAN)
        query, grad = both_heads(q_ref[here, :]), both_heads(do_ref[here, :])
        scores = dot_nt(kf_ref[: past + SPAN, :], query)
        dprob = dot_nt(vf_ref[: past + SPAN, :], grad)
        diag = jnp.where(
            near,
            dot_nt(kn_ref[here, :], query),
            jnp.where(far, scores[past:], masked_value),
        )
        dprob_diag = jnp.where(near, dot_nt(vn_ref[here, :], grad), dprob[past:])
        tiles.append((past, here, query, grad, scores[:past], dprob[:past], diag, dprob_diag))
    results = []
    for past, here, query, grad, scores, dprob, diag, dprob_diag in tiles:
        lse = jnp.concatenate([lse_ref[0, 0:1, here], lse_ref[0, 1:2, here]], axis=1)
        delta = jnp.concatenate([deltas[0:1, here], deltas[1:2, here]], axis=1)
        prob_diag = jnp.exp2(diag - lse)
        ds_diag = prob_diag * (dprob_diag - delta)
        prob_near = jnp.where(near, prob_diag, 0.0).astype(low)
        ds_near = jnp.where(near, ds_diag, 0.0).astype(low)
        prob = jnp.where(near, 0.0, prob_diag).astype(low)
        dscore = jnp.where(near, 0.0, ds_diag).astype(low)
        if past:
            prob_past = jnp.exp2(scores - lse)
            ds_past = prob_past * (dprob - delta)
            prob = jnp.concatenate([prob_past.astype(low), prob], axis=0)
            dscore = jnp.concatenate([ds_past.astype(low), dscore], axis=0)
        results.append((past, here, query, grad, prob_near, ds_near, prob, dscore))
    for past, here, query, grad, prob_near, ds_near, prob, dscore in results:
        dkf, dvf = dot_nn(dscore, query), dot_nn(prob, grad)
        if past:
            dkf_acc[:past, :] += dkf[:past]
            dvf_acc[:past, :] += dvf[:past]
        dkf_acc[here, :] = dkf[past:]
        dvf_acc[here, :] = dvf[past:]
        dkn, dvn = dot_nn(ds_near, query), dot_nn(prob_near, grad)
        dqt = dot_nn(kn_t[:, here], ds_near) + dot_nn(kf_t[:, : past + SPAN], dscore)
        dq = own_blocks(dqt) * (1.0 / math.sqrt(HEAD))
        dq = rotate_back(dq, cosine[here], sa[here], sb[here])
        own_ref[0, here, :] = dq.astype(low)
        sum_q = sum_q + jnp.sum(dq, axis=0, keepdims=True)
        dkn = rotate_back(dkn * ln2, cosine[here], sa[here], sb[here])
        own_ref[1, here, :] = dkn.astype(low)
        sum_kn = sum_kn + jnp.sum(dkn, axis=0, keepdims=True)
        own_ref[2, here, :] = dvn.astype(low)
        sum_vn = sum_vn + jnp.sum(dvn, axis=0, keepdims=True)
    dkf = rotate_back(dkf_acc[...] * ln2, cosine, sa, sb)
    dvf = dvf_acc[...]
    clean_ref[0] = dkf.astype(low)
    clean_ref[1] = dvf.astype(low)
    sums_ref[0, 0:1, :] = sum_q
    sums_ref[0, 1:2, :] = sum_kn + jnp.sum(dkf, axis=0, keepdims=True)
    sums_ref[0, 2:3, :] = sum_vn + jnp.sum(dvf, axis=0, keepdims=True)


def attend_back(size, q, kn, vn, kf, vf, do, o, lse, tables, first, pairs, after, work):
    count = q.shape[0]
    pair_spec = pl.BlockSpec((count, PAIR), lambda p: (0, p + first))
    width = pairs * PAIR
    return ordered_call(
        attend_back_kernel,
        after,
        (pairs,),
        [pl.BlockSpec(memory_space=pltpu.SMEM)]
        + [pair_spec] * 7
        + [pl.BlockSpec((1, 2, count), lambda p: (p + first, 0, 0))]
        + [whole_spec(t.shape) for t in tables],
        (size, q, kn, vn, kf, vf, do, o, lse, *tables),
        out_specs=[
            pl.BlockSpec((3, count, PAIR), lambda p: (0, 0, p)),
            pl.BlockSpec((2, count, PAIR), lambda p: (0, 0, p)),
            pl.BlockSpec((1, 3, PAIR), lambda p: (p, 0, 0)),
        ],
        out_shape=[
            jax.ShapeDtypeStruct((3, count, width), low),
            jax.ShapeDtypeStruct((2, count, width), low),
            jax.ShapeDtypeStruct((pairs, 3, PAIR), wide),
        ],
        scratch_shapes=[
            pltpu.VMEM((count, PAIR), wide),
            pltpu.VMEM((count, PAIR), wide),
        ],
        work=work,
        name="attend_back",
    )


def spread_lanes(columns, batch):
    rows = columns.shape[0] // batch
    lane = lax.broadcasted_iota(jnp.int32, (rows, PAIR), 1)
    shards = []
    for shard in range(batch):
        block = columns[shard * rows : (shard + 1) * rows]
        for first, share in ((4, 4), (8, 3)):
            for j in range(share):
                chunk = share * shard + j
                at, start = first + chunk // batch, chunk % batch * rows
                block = jnp.where(
                    lane == first + j, columns[start : start + rows, at : at + 1], block
                )
        shards.append(block)
    return jnp.concatenate(shards, axis=0)


def qkv_kernel(cuts, batch, place_ref, core_ref, h_ref, hf_ref, w_ref, gain1_ref, bias1_ref,
               early_ref, *rest):
    own, clean, sums, rest = (
        rest[:cuts],
        rest[cuts : 2 * cuts],
        rest[2 * cuts : 3 * cuts],
        rest[3 * cuts :],
    )
    outs, (rows_ref, columns_ref, result_ref) = rest[:-3], rest[-3:]
    step = pl.program_id(0)
    width = h_ref.shape[1]
    result_ref[...] = dot_tn(h_ref[...], jnp.concatenate([r[0] for r in own], axis=1))

    @pl.when(step == 0)
    def _():
        columns_ref[...] = jnp.zeros_like(columns_ref)
        rows_ref[...] = jnp.zeros_like(rows_ref)
        for i in range(8):
            rows_ref[i : i + 1, :] = early_ref[:, i * width : (i + 1) * width]
        rows_ref[13:14, :] = row_of(gain1_ref)
        rows_ref[14:15, :] = row_of(bias1_ref)

    @pl.when(step > 0)
    def _():
        result_ref[...] += dot_tn(hf_ref[...], jnp.concatenate([r[0] for r in clean], axis=1))

    result = result_ref[...]
    if len(outs) == 1:
        cols = pl.ds(pl.multiple_of(step * width, 128), width)
        store_columns(place_ref, core_ref, result, outs, cols)
    else:
        pl.when(step == 0)(lambda: store_shards(place_ref, core_ref, result, *outs[:2]))
        for part in range(2):
            cols = slice(part * width, (part + 1) * width)
            pl.when(step == part + 1)(
                partial(store_shards, place_ref, core_ref, result, *outs[2:], cols)
            )
    weight = w_ref[...].astype(wide)
    totals = jnp.concatenate(
        [r[p, pl.ds(step, 1), :] for r in sums for p in range(r.shape[0])], axis=1
    )
    rows_ref[pl.ds(8 + step, 1), :] = totals
    lane = lax.broadcasted_iota(jnp.int32, (1, PAIR), 1)
    columns_ref[...] += jnp.where(
        lane == 0,
        jnp.sum(weight * result, axis=1, keepdims=True),
        jnp.sum(weight * totals, axis=1, keepdims=True),
    )

    @pl.when(step == 2)
    def _():
        columns = rows_ref[...].T
        bias = columns_ref[:, 1:2]
        gain = (columns_ref[:, 0:1] - columns[:, 14:15] * bias) / columns[:, 13:14]
        columns = jnp.where(lane == 11, gain, jnp.where(lane == 12, bias, columns))
        if len(outs) == 1:
            outs[0][:, 3 * width : 3 * width + PAIR] = columns.astype(low)
        else:
            columns = spread_lanes(columns, batch)
            cols = slice(2 * width, 2 * width + PAIR)
            store_shards(place_ref, core_ref, columns, *outs[2:], cols)


def outer_qkv(h, hf, weight, gain1, bias1, early, own, clean, sums, place, core, after):
    count, width = h.shape
    batch = 2 * place.shape[0]
    columns = 3 * width + PAIR
    if aligned(width, batch):
        out_shape = [
            jax.ShapeDtypeStruct((batch // 2, width // batch, n), low)
            for n in (width, width, columns - width, columns - width)
        ]
    else:
        out_shape = [jax.ShapeDtypeStruct((width, columns), low)]
    result = ordered_call(
        partial(qkv_kernel, len(own), batch),
        after,
        (3,),
        [whole_spec(h.shape)] * 2
        + [pl.BlockSpec((width, width), lambda i, p, c: (0, i))]
        + [whole_spec(v.shape) for v in (gain1, bias1, early)]
        + [pl.BlockSpec((1, count, r.shape[2]), lambda i, p, c: (i, 0, 0)) for r in own]
        + [
            pl.BlockSpec((1, count, r.shape[2]), lambda i, p, c: (jnp.maximum(i - 1, 0), 0, 0))
            for r in clean
        ]
        + [whole_spec(r.shape) for r in sums],
        (h, hf, weight, gain1, bias1, early, *own, *clean, *sums),
        (place, core),
        out_specs=[whole_spec(o.shape) for o in out_shape],
        out_shape=out_shape,
        scratch_shapes=[
            pltpu.VMEM((PAIR, width), wide),
            pltpu.VMEM((width, PAIR), wide),
            pltpu.VMEM((width, width), wide),
        ],
        work=1e8,
        name="outer_qkv",
    )
    if len(result) == 4:
        return result[:2], result[2:]
    (full,) = result
    rows = width // batch
    start = 3 * width
    spread = [full[:, : start + 4]]
    for first, share in ((4, 4), (8, 3)):
        part = full[:, start + first : start + first + share].T.reshape(batch, share, rows)
        spread.append(part.transpose(0, 2, 1).reshape(width, share))
    spread.append(full[:, start + 11 :])
    full = jnp.concatenate(spread, axis=1)
    return [split_shards(p, place, core[0]) for p in (full[:, :width], full[:, width:])]


def project_far_back_kernel(cuts, noisy_ref, x_ref, *rest):
    far, clean = rest[:HALVES], rest[HALVES : HALVES + cuts]
    w_ref, gain1_ref, dfar_ref = rest[HALVES + cuts :]
    width = x_ref.shape[1]
    steps = pl.num_programs(0) // HALVES
    source = x_ref[...].astype(wide)
    for i, ref in enumerate(far):
        chosen = (noisy_ref[0] == 1) & (pl.program_id(0) // steps == i)
        source = jnp.where(chosen, ref[...].astype(wide), source)
    normed, factor = normalize(source)
    dh = jnp.zeros_like(source)
    for part in range(2):
        grads = jnp.concatenate([c[part] for c in clean], axis=1)
        dh = dh + dot_nt(grads, w_ref[:, (part + 1) * width : (part + 2) * width])
    dfar_ref[...] = norm_back(dh * row_of(gain1_ref), normed, factor).astype(low)


def project_far_back(noisy, x, far, clean, weight, gain1, after):
    count, width = x.shape
    return ordered_call(
        partial(project_far_back_kernel, len(clean)),
        after,
        (count // ROWS,),
        [pl.BlockSpec(memory_space=pltpu.SMEM)]
        + [row_spec(width)]
        + [
            pl.BlockSpec(
                (ROWS, width),
                lambda i, first=n * f.shape[0] // ROWS, last=f.shape[0] // ROWS - 1: (
                    jnp.clip(i - first, 0, last),
                    0,
                ),
            )
            for n, f in enumerate(far)
        ]
        + [pl.BlockSpec((2, ROWS, c.shape[2]), lambda i: (0, i, 0)) for c in clean]
        + [whole_spec(weight.shape), whole_spec(gain1.shape)],
        (noisy, x, *far, *clean, weight, gain1),
        out_specs=row_spec(width),
        out_shape=jax.ShapeDtypeStruct((count, width), low),
        work=1e8,
        name="project_far_back",
    )


def project_back_kernel(cuts, noisy_ref, x_ref, dy_ref, dfar_ref, *rest):
    own = rest[:cuts]
    w_ref, gain1_ref, dx_ref = rest[cuts:]
    width = x_ref.shape[1]
    normed, factor = normalize(x_ref[...].astype(wide))
    dh = jnp.zeros_like(dy_ref)
    for part in range(3):
        grads = jnp.concatenate([c[part] for c in own], axis=1)
        dh = dh + dot_nt(grads, w_ref[:, part * width : (part + 1) * width])
    dx = dy_ref[...] + norm_back(dh * row_of(gain1_ref), normed, factor)
    dx_ref[...] = dx + jnp.where(noisy_ref[0] == 0, dfar_ref[...].astype(wide), 0.0)


def project_back(noisy, x, dy, dfar, own, weight, gain1, after):
    count, width = x.shape
    return ordered_call(
        partial(project_back_kernel, len(own)),
        after,
        (count // ROWS,),
        [pl.BlockSpec(memory_space=pltpu.SMEM)]
        + [row_spec(width)] * 3
        + [pl.BlockSpec((3, ROWS, c.shape[2]), lambda i: (0, i, 0)) for c in own]
        + [whole_spec(weight.shape), whole_spec(gain1.shape)],
        (noisy, x, dy, dfar, *own, weight, gain1),
        out_specs=row_spec(width),
        out_shape=jax.ShapeDtypeStruct((count, width), wide),
        work=1.5e10,
        name="project_back",
    )


def flip(values, mask):
    batch = lax.axis_size("batch")
    return lax.ppermute(values, "batch", [(i, i ^ mask) for i in range(batch)])


def flip_stream(values):
    return lax.ppermute(values, "stream", [(0, 1), (1, 0)])


def total(terms):
    result = terms[0].astype(wide)
    for term in terms[1:]:
        result = result + term.astype(wide)
    return result


class Reduction:
    def __init__(self, shards, halved=False):
        keep, send = shards
        self.halved = halved
        self.terms = [keep, flip(send, 1)]
        self.deep = 2 if halved else 0
        self.size = keep.shape[int(halved)]
        self.stages = stages_of(2 * self.size)

    def wait_for(self, others):
        self.terms, _ = lax.optimization_barrier((self.terms, list(others)))

    def part(self, first, size):
        views = [t[0] if i < self.deep else t for i, t in enumerate(self.terms)]
        return total([v[first : first + size] for v in views]).astype(low)

    def step(self):
        if self.halved:
            self.halved = False
            piece = total([t[1] for t in self.terms]).astype(low)
            self.arrived = [flip_stream(piece)]
            self.terms = self.terms + self.arrived
            return [piece]
        bits = self.stages.pop(0)
        parts = 2 ** len(bits)
        size = self.size // parts
        pieces = [self.part(j * size, size) for j in range(1, parts)]
        self.arrived = [flip(p, mask_of(bits, j + 1)) for j, p in enumerate(pieces)]
        self.terms = self.terms + self.arrived
        self.size = size
        return pieces

    def last(self):
        while self.stages:
            self.step()
        self.mine = self.part(0, 1)
        self.other = flip_stream(self.mine)
        return [self.mine]

    def result(self, first, count):
        at = slice(first, first + count)
        return self.mine[0][:, at].astype(wide) + self.other[0][:, at].astype(wide)

    def halves(self, side):
        mine, other = self.mine[0], self.other[0]
        first = jnp.where(side == 0, mine, other)
        second = jnp.where(side == 0, other, mine)
        return first.astype(wide), second.astype(wide)


def local(
    layer_input,
    out_cotangent,
    block_size,
    norm1_gain,
    norm1_bias,
    qkv_weight,
    qkv_bias,
    proj_weight,
    proj_bias,
    norm2_gain,
    norm2_bias,
    up_weight,
    up_bias,
    down_weight,
    down_bias,
):
    length, width = layer_input.shape[2:]
    batch = lax.axis_size("batch")
    noisy = lax.axis_index("stream").astype(jnp.int32).reshape(1)
    x = layer_input.reshape(length, width)
    g = out_cotangent.reshape(length, width)
    half = length // HALVES
    far_x = [
        lax.ppermute(x[i * half : (i + 1) * half], "stream", [(0, 1)]) for i in range(HALVES)
    ]
    tables = rotary_tables(length)
    me = lax.axis_index("batch").astype(jnp.int32)
    place, core = places_of(batch, me), (me % 2).reshape(1)
    h, q, k, v = project(x, qkv_weight, qkv_bias, norm1_gain, norm1_bias, tables)
    fars, attended = [], []
    for i in range(HALVES):
        fars = project_far(
            noisy, x, far_x[i], qkv_weight, qkv_bias, norm1_gain, norm1_bias, tables, i, fars
        )
        hf, kf, vf = fars
        attended = attend(block_size, q, k, v, kf, vf, i, HALVES, attended)
    o, lse = attended
    (out, dy, do, early), downw, upw = middle(
        place,
        core,
        noisy,
        x,
        o,
        g,
        proj_weight,
        proj_bias,
        norm2_gain,
        norm2_bias,
        up_weight,
        up_bias,
        down_weight,
        down_bias,
    )
    down, up = Reduction(downw), Reduction(upw, True)
    backs, after = [], []
    for i, (first, pairs) in enumerate(CUTS):
        if i == 1:
            down.wait_for(backs[0])
            after = down.step()
            up.wait_for(after)
            after = after + up.step()
        after = after + [b[0] for b in backs[-1:]]
        backs.append(
            attend_back(
                block_size, q, k, v, kf, vf, do, o, lse, tables, first, pairs, after, 2e10
            )
        )
    own, clean, sums = ([b[i] for b in backs] for i in range(3))
    down.wait_for(backs[-1])
    after = down.step()
    dfar = project_far_back(noisy, x, far_x, clean, qkv_weight, norm1_gain, after)
    back_x = lax.ppermute(dfar, "stream", [(1, 0)])
    up.wait_for([dfar] + down.arrived[:1])
    after = up.step()
    made = outer_qkv(
        h, hf, qkv_weight, norm1_gain, norm1_bias, early, own, clean, sums, place, core, after
    )
    made, _ = lax.optimization_barrier(
        ([list(m) for m in made], down.arrived + up.arrived)
    )
    query, rest = (Reduction(m) for m in made)
    after = query.step()
    rest.wait_for(after)
    up.wait_for(after + rest.step())
    after = up.step()
    query.wait_for(after)
    after = query.step()
    rest.wait_for(after)
    after = rest.step()
    for group in (down, up, query):
        group.wait_for(after)
        after = after + group.last()
    dx = project_back(
        noisy, x, dy, dfar, own, qkv_weight, norm1_gain, after + [back_x]
    )
    rest.wait_for([dx])
    after = rest.last()
    dx, down.other, up.other, query.other, _ = lax.optimization_barrier(
        (dx, down.other, up.other, query.other, after)
    )
    input_grad = (dx + back_x.astype(wide)).reshape(layer_input.shape)
    rest.other, input_grad = lax.optimization_barrier((rest.other, input_grad))
    ff = up_weight.shape[1]
    downw_grad = down.result(0, width)
    first, second = up.halves(noisy[0])
    upw_grad = jnp.concatenate([first[:, : ff // 2], second[:, : ff // 2]], axis=1)
    projw_grad = jnp.concatenate([first[:, ff // 2 :], second[:, ff // 2 :]], axis=1)
    qkvw_grad = jnp.concatenate([query.result(0, width), rest.result(0, 2 * width)], axis=1)
    vectors = rest.result(2 * width, PAIR).T
    downb_grad, gain2_grad, bias2_grad, projb_grad = (vectors[i] for i in range(4))
    upb_grad, qkvb_grad = vectors[4:8].reshape(-1), vectors[8:11].reshape(-1)
    gain1_grad, bias1_grad = vectors[11], vectors[12]
    return (
        out.reshape(layer_input.shape),
        input_grad,
        gain1_grad,
        bias1_grad,
        qkvw_grad,
        qkvb_grad,
        projw_grad,
        projb_grad,
        gain2_grad,
        bias2_grad,
        upw_grad,
        upb_grad,
        downw_grad,
        downb_grad,
    )


def solution(mesh):
    rows = P("stream", "batch", None, None)
    return jax.shard_map(
        local,
        mesh=mesh,
        in_specs=(rows, rows, P("batch")) + (P(),) * 12,
        out_specs=(
            rows,
            rows,
            P("batch"),
            P("batch"),
            P("batch", None),
            P("batch"),
            P("batch", None),
            P("batch"),
            P("batch"),
            P("batch"),
            P("batch", None),
            P("batch"),
            P("batch", None),
            P("batch"),
        ),
        check_vma=False,
    )
```

```python
from functools import partial
import math

import jax
import jax.numpy as jnp
from jax import lax
from jax.experimental import pallas as pl
from jax.experimental.pallas import tpu as pltpu
from jax.sharding import PartitionSpec as P
import numpy as np

HEAD = 64
PAIR = 2 * HEAD
ROWS = 256
SPAN = 128
HALVES = 2
EARLY = 3
CUTS = ((0, 1), (1, 5))
full_vmem = 60

masked_value = -1e30
epsilon = 1e-05
low = jnp.bfloat16
wide = jnp.float32
score_scale = math.log2(math.e) / math.sqrt(HEAD)
ln2 = math.log(2.0)
gelu_c = math.sqrt(2.0 / math.pi)
gelu_k = 0.044715
mega = 1024 * 1024


def dot_nn(left, right):
    return lax.dot_general(left, right, (((1,), (0,)), ((), ())), preferred_element_type=wide)


def dot_nt(left, right):
    return lax.dot_general(left, right, (((1,), (1,)), ((), ())), preferred_element_type=wide)


def dot_tn(left, right):
    return lax.dot_general(left, right, (((0,), (0,)), ((), ())), preferred_element_type=wide)


def params(limit_mib):
    return pltpu.CompilerParams(
        dimension_semantics=("arbitrary",), vmem_limit_bytes=limit_mib * mega
    )


def cost(flops, nbytes, trans=0):
    return pl.CostEstimate(
        flops=int(flops), bytes_accessed=int(nbytes), transcendentals=int(trans)
    )


def ordered_call(
    kernel, after, grid, in_specs, operands, prefetch=(), work=4e9, into=(), **rest
):
    skip = len(prefetch) + len(operands)
    after = list(into) + list(after)

    def body(*refs):
        kernel(*refs[:skip], *refs[skip + len(after) :])

    out_specs = rest.pop("out_specs")
    scratch = rest.pop("scratch_shapes", [])
    call = pl.pallas_call(
        body,
        grid_spec=pltpu.PrefetchScalarGridSpec(
            num_scalar_prefetch=len(prefetch),
            grid=grid,
            in_specs=list(in_specs) + [pl.BlockSpec(memory_space=pl.ANY)] * len(after),
            out_specs=out_specs,
            scratch_shapes=scratch,
        ),
        compiler_params=pltpu.CompilerParams(
            dimension_semantics=("arbitrary",) * len(grid), vmem_limit_bytes=full_vmem * mega
        ),
        cost_estimate=cost(work, 1000),
        input_output_aliases={skip + i: i for i in range(len(into))},
        **rest,
    )
    return call(*prefetch, *operands, *after)


def row_of(ref, at=slice(None)):
    return ref[at].reshape(1, -1)


def whole_spec(shape):
    zeros = (0,) * len(shape)
    return pl.BlockSpec(shape, lambda *_: zeros, pipeline_mode=pl.Buffered(1))


def row_spec(width, rows=ROWS):
    return pl.BlockSpec((rows, width), lambda i: (i, 0))


def normalize(values):
    mean = jnp.mean(values, axis=-1, keepdims=True)
    centred = values - mean
    factor = lax.rsqrt(jnp.mean(centred * centred, axis=-1, keepdims=True) + epsilon)
    return (centred * factor, factor)


def norm_back(grad_normed, normed, factor):
    first = jnp.mean(grad_normed, axis=-1, keepdims=True)
    second = jnp.mean(grad_normed * normed, axis=-1, keepdims=True)
    return factor * (grad_normed - first - normed * second)


def rotary_tables(length):
    places = np.arange(length, dtype=np.float64)[:, None]
    column = np.arange(PAIR) % HEAD
    angle = places * (10000.0 ** (-2.0 * (column % (HEAD // 2)) / HEAD))[None, :]
    upper = (column >= HEAD // 2)[None, :]
    cosine, sine = np.cos(angle), np.sin(angle)
    tables = (cosine, np.where(upper, sine, 0.0), np.where(upper, 0.0, -sine))
    return tuple(jnp.asarray(t, dtype=wide) for t in tables)


def rotate(values, cosine, sine_a, sine_b):
    return (
        values * cosine
        + pltpu.roll(values, HEAD // 2, 1) * sine_a
        + pltpu.roll(values, PAIR - HEAD // 2, 1) * sine_b
    )


def rotate_back(values, cosine, sine_a, sine_b):
    return (
        values * cosine
        - pltpu.roll(values, HEAD // 2, 1) * sine_a
        - pltpu.roll(values, PAIR - HEAD // 2, 1) * sine_b
    )


def project_kernel(x_ref, w_ref, bias_ref, gain1_ref, bias1_ref, cos_ref, sa_ref, sb_ref,
                   h_ref, q_ref, k_ref, v_ref):
    width = x_ref.shape[1]
    normed, _ = normalize(x_ref[...].astype(wide))
    hidden = (normed * row_of(gain1_ref) + row_of(bias1_ref)).astype(low)
    h_ref[...] = hidden
    cosine, sa, sb = cos_ref[...], sa_ref[...], sb_ref[...]
    for out, part in ((q_ref, 0), (k_ref, 1), (v_ref, 2)):
        cols = slice(part * width, (part + 1) * width)
        mixed = dot_nn(hidden, w_ref[:, cols]) + row_of(bias_ref, cols)
        if part == 2:
            out[...] = mixed.astype(low)
            continue
        for group in range(width // PAIR):
            at = slice(group * PAIR, (group + 1) * PAIR)
            turned = rotate(mixed[:, at], cosine, sa, sb)
            if part == 0:
                turned = turned * score_scale
            out[:, at] = turned.astype(low)


def project_far_kernel(noisy_ref, x_ref, far_ref, wk_ref, wv_ref, bias_ref, gain1_ref, bias1_ref,
                       cos_ref, sa_ref, sb_ref, h_ref, k_ref, v_ref):
    width = x_ref.shape[1]
    source = jnp.where(noisy_ref[0] == 1, far_ref[...].astype(wide), x_ref[...].astype(wide))
    normed, _ = normalize(source)
    hidden = (normed * row_of(gain1_ref) + row_of(bias1_ref)).astype(low)
    h_ref[...] = hidden
    cosine, sa, sb = cos_ref[...], sa_ref[...], sb_ref[...]
    mixed = dot_nn(hidden, wk_ref[...]) + row_of(bias_ref, slice(width, 2 * width))
    for group in range(width // PAIR):
        at = slice(group * PAIR, (group + 1) * PAIR)
        k_ref[:, at] = rotate(mixed[:, at], cosine, sa, sb).astype(low)
    mixed = dot_nn(hidden, wv_ref[...]) + row_of(bias_ref, slice(2 * width, None))
    v_ref[...] = mixed.astype(low)


def project(x, weight, bias, gain1, bias1, tables):
    count, width = x.shape
    row = jax.ShapeDtypeStruct((count, width), low)
    return pl.pallas_call(
        project_kernel,
        grid=(count // ROWS,),
        in_specs=[
            row_spec(width),
            whole_spec(weight.shape),
            whole_spec(bias.shape),
            whole_spec(gain1.shape),
            whole_spec(bias1.shape),
            row_spec(PAIR),
            row_spec(PAIR),
            row_spec(PAIR),
        ],
        out_specs=[row_spec(width)] * 4,
        out_shape=[row] * 4,
        compiler_params=params(full_vmem),
        cost_estimate=cost(2 * count * width * 3 * width, 16e6),
        name="project",
    )(x, weight, bias, gain1, bias1, *tables)


def project_far(noisy, x, far, weight, bias, gain1, bias1, tables, part, into, after):
    count, width = x.shape
    steps = far.shape[0] // ROWS
    row = jax.ShapeDtypeStruct((count, width), low)

    def part_rows(columns):
        return pl.BlockSpec((ROWS, columns), lambda i: (part * steps + i, 0))

    return ordered_call(
        project_far_kernel,
        after,
        (steps,),
        [
            pl.BlockSpec(memory_space=pltpu.SMEM),
            part_rows(width),
            row_spec(width),
            pl.BlockSpec((width, width), lambda i: (0, 1), pipeline_mode=pl.Buffered(1)),
            pl.BlockSpec((width, width), lambda i: (0, 2), pipeline_mode=pl.Buffered(1)),
            whole_spec(bias.shape),
            whole_spec(gain1.shape),
            whole_spec(bias1.shape),
            part_rows(PAIR),
            part_rows(PAIR),
            part_rows(PAIR),
        ],
        (noisy, x, far, weight, weight, bias, gain1, bias1, *tables),
        into=into,
        out_specs=[part_rows(width)] * 3,
        out_shape=[row] * 3,
        name="project_far",
    )


def early_kernel(g_ref, w_ref, out_ref):
    out_ref[...] = dot_nt(g_ref[...], w_ref[...]).astype(low)


def early_part(g, weight, chunks):
    count, width = g.shape
    return ordered_call(
        early_kernel,
        [],
        (chunks,),
        [whole_spec(g.shape), pl.BlockSpec((width, width), lambda i: (i, 0))],
        (g, weight),
        out_specs=pl.BlockSpec((count, width), lambda i: (0, i)),
        out_shape=jax.ShapeDtypeStruct((count, chunks * width), low),
        name="early_part",
    )


def block_masks(size_ref):
    key = lax.broadcasted_iota(jnp.int32, (SPAN, 2 * SPAN), 0)
    query = lax.broadcasted_iota(jnp.int32, (SPAN, 2 * SPAN), 1) % SPAN
    near = (key ^ query) < size_ref[0]
    return near, key < query


def both_heads(rows):
    lane = lax.broadcasted_iota(jnp.int32, (1, PAIR), 1)
    none = jnp.zeros_like(rows)
    return jnp.concatenate(
        [jnp.where(lane < HEAD, rows, none), jnp.where(lane >= HEAD, rows, none)], axis=0
    )


def own_blocks(mixed):
    return jnp.concatenate([mixed[:HEAD, :SPAN], mixed[HEAD:, SPAN:]], axis=0).T


def attend_kernel(first, size_ref, q_ref, kn_ref, vn_ref, kf_ref, vf_ref, o_ref, lse_ref):
    near, far = block_masks(size_ref)
    vf_t = vf_ref[...].astype(wide).T.astype(low)
    vn_t = vn_ref[...].astype(wide).T.astype(low)
    parts = range(q_ref.shape[0] // SPAN)
    state = []
    for part in parts:
        past = (first + part) * SPAN
        own = slice(part * SPAN, (part + 1) * SPAN)
        query = both_heads(q_ref[own, :])
        scores = dot_nt(kf_ref[: past + SPAN, :], query)
        diag = jnp.where(
            near, dot_nt(kn_ref[own, :], query), jnp.where(far, scores[past:], masked_value)
        )
        state.append((past, own, scores, diag))
    probs = []
    for past, own, scores, diag in state:
        top = jnp.max(diag, axis=0, keepdims=True)
        if past:
            top = jnp.maximum(top, jnp.max(scores[:past], axis=0, keepdims=True))
        prob = jnp.exp2(diag - top)
        total = jnp.sum(prob, axis=0, keepdims=True)
        prob_near = jnp.where(near, prob, 0.0).astype(low)
        prob_far = jnp.where(near, 0.0, prob).astype(low)
        if past:
            prob = jnp.exp2(scores[:past] - top)
            total = total + jnp.sum(prob, axis=0, keepdims=True)
            prob_far = jnp.concatenate([prob.astype(low), prob_far], axis=0)
        lse = top + jnp.log2(total)
        lse_ref[0, 0:1, own] = lse[:, :SPAN]
        lse_ref[0, 1:2, own] = lse[:, SPAN:]
        probs.append((past, own, prob_near, prob_far, 1.0 / total))
    for past, own, prob_near, prob_far, scale in probs:
        mixed = dot_nn(vn_t[:, own], prob_near) + dot_nn(vf_t[:, : past + SPAN], prob_far)
        o_ref[own, :] = own_blocks(mixed * scale).astype(low)


def attend(size, q, kn, vn, kf, vf, part, parts, into):
    count, width = q.shape
    pairs = width // PAIR
    rows = count // parts
    own_spec = pl.BlockSpec((rows, PAIR), lambda p: (part, p))
    far_spec = pl.BlockSpec(((part + 1) * rows, PAIR), lambda p: (0, p))
    return ordered_call(
        partial(attend_kernel, part * rows // SPAN),
        [],
        (pairs,),
        [pl.BlockSpec(memory_space=pltpu.SMEM)] + [own_spec] * 3 + [far_spec] * 2,
        (size, q, kn, vn, kf, vf),
        into=into,
        out_specs=[own_spec, pl.BlockSpec((1, 2, rows), lambda p: (p, 0, part))],
        out_shape=[
            jax.ShapeDtypeStruct((count, width), low),
            jax.ShapeDtypeStruct((pairs, 2, count), wide),
        ],
        name="attend",
    )


def stages_of(batch):
    bits = list(range(1, batch.bit_length() - 1))
    stages = [bits[:1]]
    rest = bits[1:]
    while rest:
        stages.append(rest[:2])
        rest = rest[2:]
    return [s for s in stages if s]


def mask_of(bits, digit):
    return sum(((digit >> i) & 1) << bit for i, bit in enumerate(bits))


def places_of(batch, me):
    relative = jnp.arange(0, batch, 2, dtype=jnp.int32) ^ (me - me % 2)
    place = jnp.zeros_like(relative)
    for bits in stages_of(batch):
        place = place * 2 ** len(bits)
        for i, bit in enumerate(bits):
            place = place + (((relative >> bit) & 1) << i)
    return place


def store_shards(place_ref, core_ref, result, keep_ref, send_ref, columns=slice(None)):
    shards = keep_ref.shape[0]
    rows = result.shape[0] // (2 * shards)

    def store(first_ref, second_ref):
        for pair in range(shards):
            at = place_ref[pair]
            start = 2 * pair * rows
            first_ref[at, :, columns] = result[start : start + rows].astype(low)
            second_ref[at, :, columns] = result[start + rows : start + 2 * rows].astype(low)

    pl.when(core_ref[0] == 0)(lambda: store(keep_ref, send_ref))
    pl.when(core_ref[0] == 1)(lambda: store(send_ref, keep_ref))


def split_shards(full, place, core):
    batch = 2 * place.shape[0]
    shards = full.reshape((batch // 2, 2, full.shape[0] // batch) + full.shape[1:])
    order = jnp.argsort(place)
    shards = jnp.take(shards, order, axis=0)
    return (
        jnp.where(core == 0, shards[:, 0], shards[:, 1]),
        jnp.where(core == 0, shards[:, 1], shards[:, 0]),
    )


def aligned(tall, batch):
    return tall % batch == 0 and (tall // batch) % 16 == 0


def store_columns(place_ref, core_ref, result, outs, columns=slice(None)):
    if len(outs) == 1:
        outs[0][:, columns] = result.astype(low)
    else:
        store_shards(place_ref, core_ref, result, *outs, columns)


def store_tall(place_ref, core_ref, step, result, outs):
    if len(outs) == 1:
        outs[0][...] = result.astype(low)
        return
    rows = outs[0].shape[2]
    places = place_ref.shape[0] // 2

    def store(first_ref, second_ref):
        for x in range(2):
            at = place_ref[2 * step + x] // places
            start = 2 * x * rows
            first_ref[at, 0] = result[start : start + rows].astype(low)
            second_ref[at, 0] = result[start + rows : start + 2 * rows].astype(low)

    pl.when(core_ref[0] == 0)(lambda: store(*outs))
    pl.when(core_ref[0] == 1)(lambda: store(*outs[::-1]))


def middle_kernel(row_steps, down_steps, tall_outs, place_ref, core_ref, x_ref, o_ref, g_ref, da_ref,
                  wp_ref, bp_ref, gain2_ref, bias2_ref, wu_ref, bu_ref, wd_ref, bd_ref,
                  out_ref, dy_ref, do_ref, sums_ref,
                  *rest):
    downs, ups = rest[:tall_outs], rest[tall_outs:-5]
    a_all, right_all, hidden_all, o_all, g_all = rest[-5:]
    width = x_ref.shape[1]
    ff = wu_ref.shape[1]
    step = pl.program_id(0)

    def add_sum(start, values):
        at = slice(start, start + values.shape[1])
        sums_ref[:, at] += jnp.sum(values, axis=0, keepdims=True)

    @pl.when(step == 0)
    def _():
        sums_ref[...] = jnp.zeros_like(sums_ref)

    @pl.when(step < row_steps)
    def _():
        rows = pl.ds(pl.multiple_of(step * ROWS, ROWS), ROWS)
        parts = [slice(i * width, (i + 1) * width) for i in range(ff // width)]
        grad = g_ref[...]
        y = x_ref[...].astype(wide) + dot_nn(o_ref[...], wp_ref[...]) + row_of(bp_ref)
        das = [da_ref[:, cols].astype(wide) for cols in parts[:EARLY]]
        das += [dot_nt(grad, wd_ref[cols, :]) for cols in parts[EARLY:]]
        normed, factor = normalize(y)
        hidden = (normed * row_of(gain2_ref) + row_of(bias2_ref)).astype(low)
        o_all[rows, :] = o_ref[...]
        hidden_all[rows, :] = hidden
        g_all[rows, :] = grad
        grad_wide = grad.astype(wide)
        ups = [dot_nn(hidden, wu_ref[:, cols]) + row_of(bu_ref, cols) for cols in parts]
        acts, dus = [], []
        for part, cols in enumerate(parts):
            up = ups[part]
            square = up * up
            half = 0.5 + 0.5 * jnp.tanh(up * (gelu_c + (gelu_c * gelu_k) * square))
            active = (up * half).astype(low)
            slope = half + (up * (2.0 * gelu_c + (6.0 * gelu_c * gelu_k) * square)) * (
                half * (1.0 - half)
            )
            du = das[part] * slope
            du_low = du.astype(low)
            a_all[rows, cols] = active
            right_all[rows, cols] = du_low
            add_sum(4 * width + part * width, du)
            acts.append(active)
            dus.append(du_low)
        result = y + row_of(bd_ref)
        dh2 = jnp.zeros_like(y)
        for part, cols in enumerate(parts):
            dh2 = dh2 + dot_nt(dus[part], wu_ref[:, cols])
            result = result + dot_nn(acts[part], wd_ref[cols, :])
        out_ref[...] = result.astype(low)
        add_sum(0, grad_wide)
        add_sum(width, dh2 * normed)
        add_sum(2 * width, dh2)
        dy = grad_wide + norm_back(dh2 * row_of(gain2_ref), normed, factor)
        dy_ref[...] = dy
        add_sum(3 * width, dy)
        dy_low = dy.astype(low)
        right_all[rows, ff:] = dy_low
        do_ref[...] = dot_nt(dy_low, wp_ref[...]).astype(low)

    down_step = step - row_steps
    tile = ff // down_steps

    @pl.when((down_step >= 0) & (down_step < down_steps))
    def _():
        cols = pl.ds(pl.multiple_of(down_step * tile, 128), tile)
        store_tall(place_ref, core_ref, down_step, dot_tn(a_all[:, cols], g_all[...]), downs)

    up_step = down_step - down_steps
    up_steps = ff // width

    @pl.when((up_step >= 0) & (up_step < up_steps))
    def _():
        cols = pl.ds(pl.multiple_of(up_step * width, 128), width)
        store_columns(place_ref, core_ref, dot_tn(hidden_all[...], right_all[:, cols]), ups)

    @pl.when(up_step == up_steps)
    def _():
        store_columns(place_ref, core_ref, dot_tn(o_all[...], right_all[:, ff:]), ups)


def middle(place, core, x, o, g, da, wp, bp, gain2, bias2, wu, bu, wd, bd):
    count, width = x.shape
    ff = wu.shape[1]
    batch = 2 * place.shape[0]
    row_steps, up_steps = count // ROWS, ff // width + 1
    rows = ff // batch
    tall_aligned = aligned(ff, batch) and (4 * rows) % 128 == 0 and batch >= 8
    down_steps = batch // 4 if tall_aligned else ff // width

    def row(columns):
        return pl.BlockSpec((ROWS, columns), lambda i, p, c: (jnp.minimum(i, row_steps - 1), 0))

    def down_at(i):
        return jnp.clip(i - row_steps, 0, down_steps - 1)

    def up_at(i):
        return jnp.clip(i - row_steps - down_steps, 0, up_steps - 1)

    if tall_aligned:
        deep = batch // 4
        down_shape = [jax.ShapeDtypeStruct((2, deep, rows, width), low)] * 2
        down_specs = [
            pl.BlockSpec(
                (2, 1, rows, width), lambda i, p, c: (0, p[2 * down_at(i)] % deep, 0, 0)
            )
        ] * 2
    else:
        down_shape = [jax.ShapeDtypeStruct((ff, width), low)]
        down_specs = [pl.BlockSpec((ff // down_steps, width), lambda i, p, c: (down_at(i), 0))]
    if aligned(width, batch):
        shape = (batch // 2, width // batch)
        up_shape = [jax.ShapeDtypeStruct(shape + (ff + width,), low)] * 2
        up_specs = [pl.BlockSpec(shape + (width,), lambda i, p, c: (0, 0, up_at(i)))] * 2
    else:
        up_shape = [jax.ShapeDtypeStruct((width, ff + width), low)]
        up_specs = [pl.BlockSpec((width, width), lambda i, p, c: (0, up_at(i)))]
    sums = 4 * width + ff
    result = ordered_call(
        partial(middle_kernel, row_steps, down_steps, len(down_shape)),
        [],
        (row_steps + down_steps + up_steps,),
        [row(width)] * 3
        + [row(da.shape[1])]
        + [whole_spec(a.shape) for a in (wp, bp, gain2, bias2, wu, bu, wd, bd)],
        (x, o, g, da, wp, bp, gain2, bias2, wu, bu, wd, bd),
        (place, core),
        out_specs=[row(width)] * 3
        + [whole_spec((1, sums))]
        + down_specs
        + up_specs,
        out_shape=[
            jax.ShapeDtypeStruct((count, width), low),
            jax.ShapeDtypeStruct((count, width), wide),
            jax.ShapeDtypeStruct((count, width), low),
        ]
        + [jax.ShapeDtypeStruct((1, sums), wide)]
        + down_shape
        + up_shape,
        scratch_shapes=[
            pltpu.VMEM((count, ff), low),
            pltpu.VMEM((count, ff + width), low),
            pltpu.VMEM((count, width), low),
            pltpu.VMEM((count, width), low),
            pltpu.VMEM((count, width), low),
        ],
        name="middle",
    )
    rest = result[4:]
    if tall_aligned:
        downw = [r.reshape(batch // 2, rows, width) for r in rest[:2]]
    else:
        downw = split_shards(rest[0], place, core[0])
    ups = rest[len(down_shape) :]
    upw = ups if len(ups) == 2 else split_shards(ups[0], place, core[0])
    return result[:4], downw, upw


def attend_back_kernel(size_ref, q_ref, kn_ref, vn_ref, kf_ref, vf_ref, do_ref, o_ref,
                       lse_ref, cos_ref, sa_ref, sb_ref,
                       own_ref, clean_ref, sums_ref, dkf_acc, dvf_acc):
    length = q_ref.shape[0]
    near, far = block_masks(size_ref)
    kf_t = kf_ref[...].astype(wide).T.astype(low)
    kn_t = kn_ref[...].astype(wide).T.astype(low)
    product = do_ref[...].astype(wide) * o_ref[...].astype(wide)
    high = product.astype(low)
    rest = (product - high.astype(wide)).astype(low)
    head_row = lax.broadcasted_iota(jnp.int32, (8, PAIR), 0)
    head_lane = lax.broadcasted_iota(jnp.int32, (8, PAIR), 1) // HEAD
    picker = jnp.where(head_row == head_lane, 1.0, 0.0).astype(low)
    deltas = dot_nt(picker, high) + dot_nt(picker, rest)
    cosine, sa, sb = cos_ref[...], sa_ref[...], sb_ref[...]
    sum_q = jnp.zeros((1, PAIR), wide)
    sum_kn = jnp.zeros((1, PAIR), wide)
    sum_vn = jnp.zeros((1, PAIR), wide)
    tiles = []
    for tile in range(length // SPAN):
        past = tile * SPAN
        here = slice(past, past + SPAN)
        query, grad = both_heads(q_ref[here, :]), both_heads(do_ref[here, :])
        scores = dot_nt(kf_ref[: past + SPAN, :], query)
        dprob = dot_nt(vf_ref[: past + SPAN, :], grad)
        diag = jnp.where(
            near,
            dot_nt(kn_ref[here, :], query),
            jnp.where(far, scores[past:], masked_value),
        )
        dprob_diag = jnp.where(near, dot_nt(vn_ref[here, :], grad), dprob[past:])
        tiles.append((past, here, query, grad, scores[:past], dprob[:past], diag, dprob_diag))
    results = []
    for past, here, query, grad, scores, dprob, diag, dprob_diag in tiles:
        lse = jnp.concatenate([lse_ref[0, 0:1, here], lse_ref[0, 1:2, here]], axis=1)
        delta = jnp.concatenate([deltas[0:1, here], deltas[1:2, here]], axis=1)
        prob_diag = jnp.exp2(diag - lse)
        ds_diag = prob_diag * (dprob_diag - delta)
        prob_near = jnp.where(near, prob_diag, 0.0).astype(low)
        ds_near = jnp.where(near, ds_diag, 0.0).astype(low)
        prob = jnp.where(near, 0.0, prob_diag).astype(low)
        dscore = jnp.where(near, 0.0, ds_diag).astype(low)
        if past:
            prob_past = jnp.exp2(scores - lse)
            ds_past = prob_past * (dprob - delta)
            prob = jnp.concatenate([prob_past.astype(low), prob], axis=0)
            dscore = jnp.concatenate([ds_past.astype(low), dscore], axis=0)
        results.append((past, here, query, grad, prob_near, ds_near, prob, dscore))
    for past, here, query, grad, prob_near, ds_near, prob, dscore in results:
        dkf, dvf = dot_nn(dscore, query), dot_nn(prob, grad)
        if past:
            dkf_acc[:past, :] += dkf[:past]
            dvf_acc[:past, :] += dvf[:past]
        dkf_acc[here, :] = dkf[past:]
        dvf_acc[here, :] = dvf[past:]
        dkn, dvn = dot_nn(ds_near, query), dot_nn(prob_near, grad)
        dqt = dot_nn(kn_t[:, here], ds_near) + dot_nn(kf_t[:, : past + SPAN], dscore)
        dq = own_blocks(dqt) * (1.0 / math.sqrt(HEAD))
        dq = rotate_back(dq, cosine[here], sa[here], sb[here])
        own_ref[0, here, :] = dq.astype(low)
        sum_q = sum_q + jnp.sum(dq, axis=0, keepdims=True)
        dkn = rotate_back(dkn * ln2, cosine[here], sa[here], sb[here])
        own_ref[1, here, :] = dkn.astype(low)
        sum_kn = sum_kn + jnp.sum(dkn, axis=0, keepdims=True)
        own_ref[2, here, :] = dvn.astype(low)
        sum_vn = sum_vn + jnp.sum(dvn, axis=0, keepdims=True)
    dkf = rotate_back(dkf_acc[...] * ln2, cosine, sa, sb)
    dvf = dvf_acc[...]
    clean_ref[0] = dkf.astype(low)
    clean_ref[1] = dvf.astype(low)
    sums_ref[0, 0:1, :] = sum_q
    sums_ref[0, 1:2, :] = sum_kn + jnp.sum(dkf, axis=0, keepdims=True)
    sums_ref[0, 2:3, :] = sum_vn + jnp.sum(dvf, axis=0, keepdims=True)


def attend_back(size, q, kn, vn, kf, vf, do, o, lse, tables, first, pairs, after, work):
    count = q.shape[0]
    pair_spec = pl.BlockSpec((count, PAIR), lambda p: (0, p + first))
    width = pairs * PAIR
    return ordered_call(
        attend_back_kernel,
        after,
        (pairs,),
        [pl.BlockSpec(memory_space=pltpu.SMEM)]
        + [pair_spec] * 7
        + [pl.BlockSpec((1, 2, count), lambda p: (p + first, 0, 0))]
        + [whole_spec(t.shape) for t in tables],
        (size, q, kn, vn, kf, vf, do, o, lse, *tables),
        out_specs=[
            pl.BlockSpec((3, count, PAIR), lambda p: (0, 0, p)),
            pl.BlockSpec((2, count, PAIR), lambda p: (0, 0, p)),
            pl.BlockSpec((1, 3, PAIR), lambda p: (p, 0, 0)),
        ],
        out_shape=[
            jax.ShapeDtypeStruct((3, count, width), low),
            jax.ShapeDtypeStruct((2, count, width), low),
            jax.ShapeDtypeStruct((pairs, 3, PAIR), wide),
        ],
        scratch_shapes=[
            pltpu.VMEM((count, PAIR), wide),
            pltpu.VMEM((count, PAIR), wide),
        ],
        work=work,
        name="attend_back",
    )


def spread_lanes(columns, batch):
    rows = columns.shape[0] // batch
    lane = lax.broadcasted_iota(jnp.int32, (rows, PAIR), 1)
    shards = []
    for shard in range(batch):
        block = columns[shard * rows : (shard + 1) * rows]
        for first, share in ((4, 4), (8, 3)):
            for j in range(share):
                chunk = share * shard + j
                at, start = first + chunk // batch, chunk % batch * rows
                block = jnp.where(
                    lane == first + j, columns[start : start + rows, at : at + 1], block
                )
        shards.append(block)
    return jnp.concatenate(shards, axis=0)


def qkv_kernel(cuts, batch, place_ref, core_ref, h_ref, hf_ref, w_ref, gain1_ref, bias1_ref,
               early_ref, *rest):
    own, clean, sums, rest = (
        rest[:cuts],
        rest[cuts : 2 * cuts],
        rest[2 * cuts : 3 * cuts],
        rest[3 * cuts :],
    )
    outs, (rows_ref, columns_ref, result_ref) = rest[:-3], rest[-3:]
    step = pl.program_id(0)
    width = h_ref.shape[1]
    result_ref[...] = dot_tn(h_ref[...], jnp.concatenate([r[0] for r in own], axis=1))

    @pl.when(step == 0)
    def _():
        columns_ref[...] = jnp.zeros_like(columns_ref)
        rows_ref[...] = jnp.zeros_like(rows_ref)
        for i in range(8):
            rows_ref[i : i + 1, :] = early_ref[:, i * width : (i + 1) * width]
        rows_ref[13:14, :] = row_of(gain1_ref)
        rows_ref[14:15, :] = row_of(bias1_ref)

    @pl.when(step > 0)
    def _():
        result_ref[...] += dot_tn(hf_ref[...], jnp.concatenate([r[0] for r in clean], axis=1))

    result = result_ref[...]
    cols = pl.ds(pl.multiple_of(step * width, 128), width)
    store_columns(place_ref, core_ref, result, outs, cols)
    weight = w_ref[...].astype(wide)
    totals = jnp.concatenate(
        [r[p, pl.ds(step, 1), :] for r in sums for p in range(r.shape[0])], axis=1
    )
    rows_ref[pl.ds(8 + step, 1), :] = totals
    lane = lax.broadcasted_iota(jnp.int32, (1, PAIR), 1)
    columns_ref[...] += jnp.where(
        lane == 0,
        jnp.sum(weight * result, axis=1, keepdims=True),
        jnp.sum(weight * totals, axis=1, keepdims=True),
    )

    @pl.when(step == 2)
    def _():
        columns = rows_ref[...].T
        bias = columns_ref[:, 1:2]
        gain = (columns_ref[:, 0:1] - columns[:, 14:15] * bias) / columns[:, 13:14]
        columns = jnp.where(lane == 11, gain, jnp.where(lane == 12, bias, columns))
        if len(outs) == 2:
            columns = spread_lanes(columns, batch)
        store_columns(place_ref, core_ref, columns, outs, slice(3 * width, 3 * width + PAIR))


def outer_qkv(h, hf, weight, gain1, bias1, early, own, clean, sums, place, core, after):
    count, width = h.shape
    batch = 2 * place.shape[0]
    columns = 3 * width + PAIR
    if aligned(width, batch):
        out_shape = [jax.ShapeDtypeStruct((batch // 2, width // batch, columns), low)] * 2
    else:
        out_shape = [jax.ShapeDtypeStruct((width, columns), low)]
    result = ordered_call(
        partial(qkv_kernel, len(own), batch),
        after,
        (3,),
        [whole_spec(h.shape)] * 2
        + [pl.BlockSpec((width, width), lambda i, p, c: (0, i))]
        + [whole_spec(v.shape) for v in (gain1, bias1, early)]
        + [pl.BlockSpec((1, count, r.shape[2]), lambda i, p, c: (i, 0, 0)) for r in own]
        + [
            pl.BlockSpec((1, count, r.shape[2]), lambda i, p, c: (jnp.maximum(i - 1, 0), 0, 0))
            for r in clean
        ]
        + [whole_spec(r.shape) for r in sums],
        (h, hf, weight, gain1, bias1, early, *own, *clean, *sums),
        (place, core),
        out_specs=[whole_spec(o.shape) for o in out_shape],
        out_shape=out_shape,
        scratch_shapes=[
            pltpu.VMEM((PAIR, width), wide),
            pltpu.VMEM((width, PAIR), wide),
            pltpu.VMEM((width, width), wide),
        ],
        work=1e8,
        name="outer_qkv",
    )
    if len(result) == 2:
        return result
    (full,) = result
    rows = width // batch
    start = 3 * width
    spread = [full[:, : start + 4]]
    for first, share in ((4, 4), (8, 3)):
        part = full[:, start + first : start + first + share].T.reshape(batch, share, rows)
        spread.append(part.transpose(0, 2, 1).reshape(width, share))
    spread.append(full[:, start + 11 :])
    return split_shards(jnp.concatenate(spread, axis=1), place, core[0])


def project_far_back_kernel(cuts, noisy_ref, x_ref, *rest):
    far, clean = rest[:HALVES], rest[HALVES : HALVES + cuts]
    wk_ref, wv_ref, gain1_ref, dfar_ref = rest[HALVES + cuts :]
    steps = pl.num_programs(0) // HALVES
    source = x_ref[...].astype(wide)
    for i, ref in enumerate(far):
        chosen = (noisy_ref[0] == 1) & (pl.program_id(0) // steps == i)
        source = jnp.where(chosen, ref[...].astype(wide), source)
    normed, factor = normalize(source)
    dh = jnp.zeros_like(source)
    for part, w_ref in enumerate((wk_ref, wv_ref)):
        grads = jnp.concatenate([c[part] for c in clean], axis=1)
        dh = dh + dot_nt(grads, w_ref[...])
    dfar_ref[...] = norm_back(dh * row_of(gain1_ref), normed, factor).astype(low)


def project_far_back(noisy, x, far, clean, weight, gain1, after):
    count, width = x.shape
    return ordered_call(
        partial(project_far_back_kernel, len(clean)),
        after,
        (count // ROWS,),
        [pl.BlockSpec(memory_space=pltpu.SMEM)]
        + [row_spec(width)]
        + [
            pl.BlockSpec(
                (ROWS, width),
                lambda i, first=n * f.shape[0] // ROWS, last=f.shape[0] // ROWS - 1: (
                    jnp.clip(i - first, 0, last),
                    0,
                ),
            )
            for n, f in enumerate(far)
        ]
        + [pl.BlockSpec((2, ROWS, c.shape[2]), lambda i: (0, i, 0)) for c in clean]
        + [
            pl.BlockSpec((width, width), lambda i, part=part: (0, part), pipeline_mode=pl.Buffered(1))
            for part in (1, 2)
        ]
        + [whole_spec(gain1.shape)],
        (noisy, x, *far, *clean, weight, weight, gain1),
        out_specs=row_spec(width),
        out_shape=jax.ShapeDtypeStruct((count, width), low),
        work=1e8,
        name="project_far_back",
    )


def project_back_kernel(cuts, noisy_ref, x_ref, dy_ref, dfar_ref, *rest):
    own = rest[:cuts]
    w_ref, gain1_ref, dx_ref = rest[cuts:]
    width = x_ref.shape[1]
    normed, factor = normalize(x_ref[...].astype(wide))
    dh = jnp.zeros_like(dy_ref)
    for part in range(3):
        grads = jnp.concatenate([c[part] for c in own], axis=1)
        dh = dh + dot_nt(grads, w_ref[:, part * width : (part + 1) * width])
    dx = dy_ref[...] + norm_back(dh * row_of(gain1_ref), normed, factor)
    dx_ref[...] = dx + jnp.where(noisy_ref[0] == 0, dfar_ref[...].astype(wide), 0.0)


def project_back(noisy, x, dy, dfar, own, weight, gain1, after):
    count, width = x.shape
    return ordered_call(
        partial(project_back_kernel, len(own)),
        after,
        (count // ROWS,),
        [pl.BlockSpec(memory_space=pltpu.SMEM)]
        + [row_spec(width)] * 3
        + [pl.BlockSpec((3, ROWS, c.shape[2]), lambda i: (0, i, 0)) for c in own]
        + [whole_spec(weight.shape), whole_spec(gain1.shape)],
        (noisy, x, dy, dfar, *own, weight, gain1),
        out_specs=row_spec(width),
        out_shape=jax.ShapeDtypeStruct((count, width), wide),
        work=1.5e10,
        name="project_back",
    )


def flip(values, mask):
    batch = lax.axis_size("batch")
    return lax.ppermute(values, "batch", [(i, i ^ mask) for i in range(batch)])


def flip_stream(values):
    return lax.ppermute(values, "stream", [(0, 1), (1, 0)])


def total(terms):
    result = terms[0].astype(wide)
    for term in terms[1:]:
        result = result + term.astype(wide)
    return result


class Reduction:
    def __init__(self, name, shards):
        keep, send = shards
        self.name = name
        self.terms = [keep, flip(send, 1)]
        self.stages = stages_of(2 * keep.shape[0])
        self.size = keep.shape[0]

    def wait_for(self, others):
        self.terms, _ = lax.optimization_barrier((self.terms, list(others)))

    def step(self):
        bits = self.stages.pop(0)
        parts = 2 ** len(bits)
        size = self.size // parts
        pieces = [
            total([t[j * size : (j + 1) * size] for t in self.terms]).astype(low)
            for j in range(1, parts)
        ]
        arrived = [flip(p, mask_of(bits, j + 1)) for j, p in enumerate(pieces)]
        self.terms = self.terms + arrived
        self.arrived = arrived
        self.size = size
        return pieces

    def last(self):
        while self.stages:
            self.step()
        self.mine = total([t[:1] for t in self.terms]).astype(low)
        self.other = flip_stream(self.mine)
        return [self.mine]

    def result(self, first, count):
        at = slice(first, first + count)
        return self.mine[0][:, at].astype(wide) + self.other[0][:, at].astype(wide)


def local(
    layer_input,
    out_cotangent,
    block_size,
    norm1_gain,
    norm1_bias,
    qkv_weight,
    qkv_bias,
    proj_weight,
    proj_bias,
    norm2_gain,
    norm2_bias,
    up_weight,
    up_bias,
    down_weight,
    down_bias,
):
    length, width = layer_input.shape[2:]
    batch = lax.axis_size("batch")
    noisy = lax.axis_index("stream").astype(jnp.int32).reshape(1)
    x = layer_input.reshape(length, width)
    g = out_cotangent.reshape(length, width)
    half = length // HALVES
    far_x = [
        lax.ppermute(x[i * half : (i + 1) * half], "stream", [(0, 1)]) for i in range(HALVES)
    ]
    tables = rotary_tables(length)
    me = lax.axis_index("batch").astype(jnp.int32)
    place, core = places_of(batch, me), (me % 2).reshape(1)
    h, q, k, v = project(x, qkv_weight, qkv_bias, norm1_gain, norm1_bias, tables)
    da = early_part(g, down_weight, EARLY)
    fars, attended = [], []
    for i in range(HALVES):
        fars = project_far(
            noisy, x, far_x[i], qkv_weight, qkv_bias, norm1_gain, norm1_bias, tables, i, fars,
            [] if i else [da, h],
        )
        hf, kf, vf = fars
        attended = attend(block_size, q, k, v, kf, vf, i, HALVES, attended)
    o, lse = attended
    (out, dy, do, early), downw, upw = middle(
        place,
        core,
        x,
        o,
        g,
        da,
        proj_weight,
        proj_bias,
        norm2_gain,
        norm2_bias,
        up_weight,
        up_bias,
        down_weight,
        down_bias,
    )
    down, up = Reduction("down", downw), Reduction("up", upw)
    backs, after = [], []
    for i, (first, pairs) in enumerate(CUTS):
        if i == 1:
            down.wait_for(backs[0])
            after = down.step()
        after = after + [b[0] for b in backs[-1:]]
        backs.append(
            attend_back(
                block_size, q, k, v, kf, vf, do, o, lse, tables, first, pairs, after, 2e10
            )
        )
    own, clean, sums = ([b[i] for b in backs] for i in range(3))
    up.wait_for(backs[-1])
    down.wait_for(backs[-1])
    after = up.step() + down.step()
    dfar = project_far_back(noisy, x, far_x, clean, qkv_weight, norm1_gain, after)
    back_x = lax.ppermute(dfar, "stream", [(1, 0)])
    qkvw = outer_qkv(
        h,
        hf,
        qkv_weight,
        norm1_gain,
        norm1_bias,
        early,
        own,
        clean,
        sums,
        place,
        core,
        [dfar],
    )
    qkvw, _ = lax.optimization_barrier((list(qkvw), up.arrived + down.arrived))
    qkv = Reduction("qkv", qkvw)
    qkv.wait_for(up.step())
    after = qkv.step()
    dx = project_back(noisy, x, dy, dfar, own, qkv_weight, norm1_gain, after)
    qkv.wait_for([dx])
    after = qkv.step()
    down.wait_for(after)
    down.last()
    up.wait_for(after)
    up.last()
    after = qkv.last()
    dx, _ = lax.optimization_barrier((dx, after))
    input_grad = (dx + back_x.astype(wide)).reshape(layer_input.shape)
    ff = up_weight.shape[1]
    downw_grad = down.result(0, width)
    upw_grad, projw_grad = up.result(0, ff), up.result(ff, width)
    qkvw_grad = qkv.result(0, 3 * width)
    vectors = qkv.result(3 * width, PAIR).T
    downb_grad, gain2_grad, bias2_grad, projb_grad = (vectors[i] for i in range(4))
    upb_grad, qkvb_grad = vectors[4:8].reshape(-1), vectors[8:11].reshape(-1)
    gain1_grad, bias1_grad = vectors[11], vectors[12]
    return (
        out.reshape(layer_input.shape),
        input_grad,
        gain1_grad,
        bias1_grad,
        qkvw_grad,
        qkvb_grad,
        projw_grad,
        projb_grad,
        gain2_grad,
        bias2_grad,
        upw_grad,
        upb_grad,
        downw_grad,
        downb_grad,
    )


def solution(mesh):
    rows = P("stream", "batch", None, None)
    return jax.shard_map(
        local,
        mesh=mesh,
        in_specs=(rows, rows, P("batch")) + (P(),) * 12,
        out_specs=(
            rows,
            rows,
            P("batch"),
            P("batch"),
            P("batch", None),
            P("batch"),
            P("batch", None),
            P("batch"),
            P("batch"),
            P("batch"),
            P("batch", None),
            P("batch"),
            P("batch", None),
            P("batch"),
        ),
        check_vma=False,
    )
```

```python
from functools import partial
import math

import jax
import jax.numpy as jnp
from jax import lax
from jax.experimental import pallas as pl
from jax.experimental.pallas import tpu as pltpu
from jax.sharding import PartitionSpec as P
import numpy as np

HEAD = 64
PAIR = 2 * HEAD
ROWS = 256
SPAN = 128
HALVES = 2
EARLY = 3
CUTS = ((0, 1), (1, 5))
full_vmem = 60

masked_value = -1e30
epsilon = 1e-05
low = jnp.bfloat16
wide = jnp.float32
score_scale = math.log2(math.e) / math.sqrt(HEAD)
ln2 = math.log(2.0)
gelu_c = math.sqrt(2.0 / math.pi)
gelu_k = 0.044715
mega = 1024 * 1024


def dot_nn(left, right):
    return lax.dot_general(left, right, (((1,), (0,)), ((), ())), preferred_element_type=wide)


def dot_nt(left, right):
    return lax.dot_general(left, right, (((1,), (1,)), ((), ())), preferred_element_type=wide)


def dot_tn(left, right):
    return lax.dot_general(left, right, (((0,), (0,)), ((), ())), preferred_element_type=wide)


def params(limit_mib):
    return pltpu.CompilerParams(
        dimension_semantics=("arbitrary",), vmem_limit_bytes=limit_mib * mega
    )


def cost(flops, nbytes, trans=0):
    return pl.CostEstimate(
        flops=int(flops), bytes_accessed=int(nbytes), transcendentals=int(trans)
    )


def ordered_call(
    kernel, after, grid, in_specs, operands, prefetch=(), work=4e9, into=(), **rest
):
    skip = len(prefetch) + len(operands)
    after = list(into) + list(after)

    def body(*refs):
        kernel(*refs[:skip], *refs[skip + len(after) :])

    out_specs = rest.pop("out_specs")
    scratch = rest.pop("scratch_shapes", [])
    call = pl.pallas_call(
        body,
        grid_spec=pltpu.PrefetchScalarGridSpec(
            num_scalar_prefetch=len(prefetch),
            grid=grid,
            in_specs=list(in_specs) + [pl.BlockSpec(memory_space=pl.ANY)] * len(after),
            out_specs=out_specs,
            scratch_shapes=scratch,
        ),
        compiler_params=pltpu.CompilerParams(
            dimension_semantics=("arbitrary",) * len(grid), vmem_limit_bytes=full_vmem * mega
        ),
        cost_estimate=cost(work, 1000),
        input_output_aliases={skip + i: i for i in range(len(into))},
        **rest,
    )
    return call(*prefetch, *operands, *after)


def row_of(ref, at=slice(None)):
    return ref[at].reshape(1, -1)


def whole_spec(shape):
    zeros = (0,) * len(shape)
    return pl.BlockSpec(shape, lambda *_: zeros, pipeline_mode=pl.Buffered(1))


def row_spec(width, rows=ROWS):
    return pl.BlockSpec((rows, width), lambda i: (i, 0))


def normalize(values):
    mean = jnp.mean(values, axis=-1, keepdims=True)
    centred = values - mean
    factor = lax.rsqrt(jnp.mean(centred * centred, axis=-1, keepdims=True) + epsilon)
    return (centred * factor, factor)


def norm_back(grad_normed, normed, factor):
    first = jnp.mean(grad_normed, axis=-1, keepdims=True)
    second = jnp.mean(grad_normed * normed, axis=-1, keepdims=True)
    return factor * (grad_normed - first - normed * second)


def rotary_tables(length):
    places = np.arange(length, dtype=np.float64)[:, None]
    column = np.arange(PAIR) % HEAD
    angle = places * (10000.0 ** (-2.0 * (column % (HEAD // 2)) / HEAD))[None, :]
    upper = (column >= HEAD // 2)[None, :]
    cosine, sine = np.cos(angle), np.sin(angle)
    tables = (cosine, np.where(upper, sine, 0.0), np.where(upper, 0.0, -sine))
    return tuple(jnp.asarray(t, dtype=wide) for t in tables)


def rotate(values, cosine, sine_a, sine_b):
    return (
        values * cosine
        + pltpu.roll(values, HEAD // 2, 1) * sine_a
        + pltpu.roll(values, PAIR - HEAD // 2, 1) * sine_b
    )


def rotate_back(values, cosine, sine_a, sine_b):
    return (
        values * cosine
        - pltpu.roll(values, HEAD // 2, 1) * sine_a
        - pltpu.roll(values, PAIR - HEAD // 2, 1) * sine_b
    )


def project_kernel(x_ref, w_ref, bias_ref, gain1_ref, bias1_ref, cos_ref, sa_ref, sb_ref,
                   h_ref, q_ref, k_ref, v_ref):
    width = x_ref.shape[1]
    normed, _ = normalize(x_ref[...].astype(wide))
    hidden = (normed * row_of(gain1_ref) + row_of(bias1_ref)).astype(low)
    h_ref[...] = hidden
    cosine, sa, sb = cos_ref[...], sa_ref[...], sb_ref[...]
    for out, part in ((q_ref, 0), (k_ref, 1), (v_ref, 2)):
        cols = slice(part * width, (part + 1) * width)
        mixed = dot_nn(hidden, w_ref[:, cols]) + row_of(bias_ref, cols)
        if part == 2:
            out[...] = mixed.astype(low)
            continue
        for group in range(width // PAIR):
            at = slice(group * PAIR, (group + 1) * PAIR)
            turned = rotate(mixed[:, at], cosine, sa, sb)
            if part == 0:
                turned = turned * score_scale
            out[:, at] = turned.astype(low)


def project_far_kernel(noisy_ref, x_ref, far_ref, wk_ref, wv_ref, bias_ref, gain1_ref, bias1_ref,
                       cos_ref, sa_ref, sb_ref, h_ref, k_ref, v_ref):
    width = x_ref.shape[1]
    source = jnp.where(noisy_ref[0] == 1, far_ref[...].astype(wide), x_ref[...].astype(wide))
    normed, _ = normalize(source)
    hidden = (normed * row_of(gain1_ref) + row_of(bias1_ref)).astype(low)
    h_ref[...] = hidden
    cosine, sa, sb = cos_ref[...], sa_ref[...], sb_ref[...]
    mixed = dot_nn(hidden, wk_ref[...]) + row_of(bias_ref, slice(width, 2 * width))
    for group in range(width // PAIR):
        at = slice(group * PAIR, (group + 1) * PAIR)
        k_ref[:, at] = rotate(mixed[:, at], cosine, sa, sb).astype(low)
    mixed = dot_nn(hidden, wv_ref[...]) + row_of(bias_ref, slice(2 * width, None))
    v_ref[...] = mixed.astype(low)


def project(x, weight, bias, gain1, bias1, tables):
    count, width = x.shape
    row = jax.ShapeDtypeStruct((count, width), low)
    return pl.pallas_call(
        project_kernel,
        grid=(count // ROWS,),
        in_specs=[
            row_spec(width),
            whole_spec(weight.shape),
            whole_spec(bias.shape),
            whole_spec(gain1.shape),
            whole_spec(bias1.shape),
            row_spec(PAIR),
            row_spec(PAIR),
            row_spec(PAIR),
        ],
        out_specs=[row_spec(width)] * 4,
        out_shape=[row] * 4,
        compiler_params=params(full_vmem),
        cost_estimate=cost(2 * count * width * 3 * width, 16e6),
        name="project",
    )(x, weight, bias, gain1, bias1, *tables)


def project_far(noisy, x, far, weight, bias, gain1, bias1, tables, part, into, after):
    count, width = x.shape
    steps = far.shape[0] // ROWS
    row = jax.ShapeDtypeStruct((count, width), low)

    def part_rows(columns):
        return pl.BlockSpec((ROWS, columns), lambda i: (part * steps + i, 0))

    return ordered_call(
        project_far_kernel,
        after,
        (steps,),
        [
            pl.BlockSpec(memory_space=pltpu.SMEM),
            part_rows(width),
            row_spec(width),
            pl.BlockSpec((width, width), lambda i: (0, 1), pipeline_mode=pl.Buffered(1)),
            pl.BlockSpec((width, width), lambda i: (0, 2), pipeline_mode=pl.Buffered(1)),
            whole_spec(bias.shape),
            whole_spec(gain1.shape),
            whole_spec(bias1.shape),
            part_rows(PAIR),
            part_rows(PAIR),
            part_rows(PAIR),
        ],
        (noisy, x, far, weight, weight, bias, gain1, bias1, *tables),
        into=into,
        out_specs=[part_rows(width)] * 3,
        out_shape=[row] * 3,
        name="project_far",
    )


def early_kernel(g_ref, w_ref, out_ref):
    out_ref[...] = dot_nt(g_ref[...], w_ref[...]).astype(low)


def early_part(g, weight, chunks):
    count, width = g.shape
    return ordered_call(
        early_kernel,
        [],
        (chunks,),
        [whole_spec(g.shape), pl.BlockSpec((width, width), lambda i: (i, 0))],
        (g, weight),
        out_specs=pl.BlockSpec((count, width), lambda i: (0, i)),
        out_shape=jax.ShapeDtypeStruct((count, chunks * width), low),
        name="early_part",
    )


def block_masks(size_ref):
    key = lax.broadcasted_iota(jnp.int32, (SPAN, 2 * SPAN), 0)
    query = lax.broadcasted_iota(jnp.int32, (SPAN, 2 * SPAN), 1) % SPAN
    near = (key ^ query) < size_ref[0]
    return near, key < query


def both_heads(rows):
    lane = lax.broadcasted_iota(jnp.int32, (1, PAIR), 1)
    none = jnp.zeros_like(rows)
    return jnp.concatenate(
        [jnp.where(lane < HEAD, rows, none), jnp.where(lane >= HEAD, rows, none)], axis=0
    )


def own_blocks(mixed):
    return jnp.concatenate([mixed[:HEAD, :SPAN], mixed[HEAD:, SPAN:]], axis=0).T


def attend_kernel(first, size_ref, q_ref, kn_ref, vn_ref, kf_ref, vf_ref, o_ref, lse_ref):
    near, far = block_masks(size_ref)
    vf_t = vf_ref[...].astype(wide).T.astype(low)
    vn_t = vn_ref[...].astype(wide).T.astype(low)
    parts = range(q_ref.shape[0] // SPAN)
    state = []
    for part in parts:
        past = (first + part) * SPAN
        own = slice(part * SPAN, (part + 1) * SPAN)
        query = both_heads(q_ref[own, :])
        scores = dot_nt(kf_ref[: past + SPAN, :], query)
        diag = jnp.where(
            near, dot_nt(kn_ref[own, :], query), jnp.where(far, scores[past:], masked_value)
        )
        state.append((past, own, scores, diag))
    probs = []
    for past, own, scores, diag in state:
        top = jnp.max(diag, axis=0, keepdims=True)
        if past:
            top = jnp.maximum(top, jnp.max(scores[:past], axis=0, keepdims=True))
        prob = jnp.exp2(diag - top)
        total = jnp.sum(prob, axis=0, keepdims=True)
        prob_near = jnp.where(near, prob, 0.0).astype(low)
        prob_far = jnp.where(near, 0.0, prob).astype(low)
        if past:
            prob = jnp.exp2(scores[:past] - top)
            total = total + jnp.sum(prob, axis=0, keepdims=True)
            prob_far = jnp.concatenate([prob.astype(low), prob_far], axis=0)
        lse = top + jnp.log2(total)
        lse_ref[0, 0:1, own] = lse[:, :SPAN]
        lse_ref[0, 1:2, own] = lse[:, SPAN:]
        probs.append((past, own, prob_near, prob_far, 1.0 / total))
    for past, own, prob_near, prob_far, scale in probs:
        mixed = dot_nn(vn_t[:, own], prob_near) + dot_nn(vf_t[:, : past + SPAN], prob_far)
        o_ref[own, :] = own_blocks(mixed * scale).astype(low)


def attend(size, q, kn, vn, kf, vf, part, parts, into):
    count, width = q.shape
    pairs = width // PAIR
    rows = count // parts
    own_spec = pl.BlockSpec((rows, PAIR), lambda p: (part, p))
    far_spec = pl.BlockSpec(((part + 1) * rows, PAIR), lambda p: (0, p))
    return ordered_call(
        partial(attend_kernel, part * rows // SPAN),
        [],
        (pairs,),
        [pl.BlockSpec(memory_space=pltpu.SMEM)] + [own_spec] * 3 + [far_spec] * 2,
        (size, q, kn, vn, kf, vf),
        into=into,
        out_specs=[own_spec, pl.BlockSpec((1, 2, rows), lambda p: (p, 0, part))],
        out_shape=[
            jax.ShapeDtypeStruct((count, width), low),
            jax.ShapeDtypeStruct((pairs, 2, count), wide),
        ],
        name="attend",
    )


def stages_of(batch):
    bits = list(range(1, batch.bit_length() - 1))
    stages = [bits[:1]]
    rest = bits[1:]
    while rest:
        stages.append(rest[:2])
        rest = rest[2:]
    return [s for s in stages if s]


def mask_of(bits, digit):
    return sum(((digit >> i) & 1) << bit for i, bit in enumerate(bits))


def places_of(batch, me):
    relative = jnp.arange(0, batch, 2, dtype=jnp.int32) ^ (me - me % 2)
    place = jnp.zeros_like(relative)
    for bits in stages_of(batch):
        place = place * 2 ** len(bits)
        for i, bit in enumerate(bits):
            place = place + (((relative >> bit) & 1) << i)
    return place


def store_shards(place_ref, core_ref, result, keep_ref, send_ref, columns=slice(None)):
    shards = keep_ref.shape[0]
    rows = result.shape[0] // (2 * shards)

    def store(first_ref, second_ref):
        for pair in range(shards):
            at = place_ref[pair]
            start = 2 * pair * rows
            first_ref[at, :, columns] = result[start : start + rows].astype(low)
            second_ref[at, :, columns] = result[start + rows : start + 2 * rows].astype(low)

    pl.when(core_ref[0] == 0)(lambda: store(keep_ref, send_ref))
    pl.when(core_ref[0] == 1)(lambda: store(send_ref, keep_ref))


def split_shards(full, place, core):
    batch = 2 * place.shape[0]
    shards = full.reshape((batch // 2, 2, full.shape[0] // batch) + full.shape[1:])
    order = jnp.argsort(place)
    shards = jnp.take(shards, order, axis=0)
    return (
        jnp.where(core == 0, shards[:, 0], shards[:, 1]),
        jnp.where(core == 0, shards[:, 1], shards[:, 0]),
    )


def aligned(tall, batch):
    return tall % batch == 0 and (tall // batch) % 16 == 0


def store_columns(place_ref, core_ref, result, outs, columns=slice(None)):
    if len(outs) == 1:
        outs[0][:, columns] = result.astype(low)
    else:
        store_shards(place_ref, core_ref, result, *outs, columns)


def store_tall(place_ref, core_ref, step, result, outs):
    if len(outs) == 1:
        outs[0][...] = result.astype(low)
        return
    rows = outs[0].shape[2]
    places = place_ref.shape[0] // 2

    def store(first_ref, second_ref):
        for x in range(2):
            at = place_ref[2 * step + x] // places
            start = 2 * x * rows
            first_ref[at, 0] = result[start : start + rows].astype(low)
            second_ref[at, 0] = result[start + rows : start + 2 * rows].astype(low)

    pl.when(core_ref[0] == 0)(lambda: store(*outs))
    pl.when(core_ref[0] == 1)(lambda: store(*outs[::-1]))


def middle_kernel(row_steps, down_steps, tall_outs, place_ref, core_ref, x_ref, o_ref, g_ref, da_ref,
                  wp_ref, bp_ref, gain2_ref, bias2_ref, wu_ref, bu_ref, wd_ref, bd_ref,
                  out_ref, dy_ref, do_ref, sums_ref,
                  *rest):
    downs, ups = rest[:tall_outs], rest[tall_outs:-5]
    a_all, right_all, hidden_all, o_all, g_all = rest[-5:]
    width = x_ref.shape[1]
    ff = wu_ref.shape[1]
    step = pl.program_id(0)

    def add_sum(start, values):
        at = slice(start, start + values.shape[1])
        sums_ref[:, at] += jnp.sum(values, axis=0, keepdims=True)

    @pl.when(step == 0)
    def _():
        sums_ref[...] = jnp.zeros_like(sums_ref)

    @pl.when(step < row_steps)
    def _():
        rows = pl.ds(pl.multiple_of(step * ROWS, ROWS), ROWS)
        parts = [slice(i * width, (i + 1) * width) for i in range(ff // width)]
        grad = g_ref[...]
        y = x_ref[...].astype(wide) + dot_nn(o_ref[...], wp_ref[...]) + row_of(bp_ref)
        das = [da_ref[:, cols].astype(wide) for cols in parts[:EARLY]]
        das += [dot_nt(grad, wd_ref[cols, :]) for cols in parts[EARLY:]]
        normed, factor = normalize(y)
        hidden = (normed * row_of(gain2_ref) + row_of(bias2_ref)).astype(low)
        o_all[rows, :] = o_ref[...]
        hidden_all[rows, :] = hidden
        g_all[rows, :] = grad
        grad_wide = grad.astype(wide)
        ups = [dot_nn(hidden, wu_ref[:, cols]) + row_of(bu_ref, cols) for cols in parts]
        acts, dus = [], []
        for part, cols in enumerate(parts):
            up = ups[part]
            square = up * up
            half = 0.5 + 0.5 * jnp.tanh(up * (gelu_c + (gelu_c * gelu_k) * square))
            active = (up * half).astype(low)
            slope = half + (up * (2.0 * gelu_c + (6.0 * gelu_c * gelu_k) * square)) * (
                half * (1.0 - half)
            )
            du = das[part] * slope
            du_low = du.astype(low)
            a_all[rows, cols] = active
            right_all[rows, cols] = du_low
            add_sum(4 * width + part * width, du)
            acts.append(active)
            dus.append(du_low)
        result = y + row_of(bd_ref)
        dh2 = jnp.zeros_like(y)
        for part, cols in enumerate(parts):
            dh2 = dh2 + dot_nt(dus[part], wu_ref[:, cols])
            result = result + dot_nn(acts[part], wd_ref[cols, :])
        out_ref[...] = result.astype(low)
        add_sum(0, grad_wide)
        add_sum(width, dh2 * normed)
        add_sum(2 * width, dh2)
        dy = grad_wide + norm_back(dh2 * row_of(gain2_ref), normed, factor)
        dy_ref[...] = dy
        add_sum(3 * width, dy)
        dy_low = dy.astype(low)
        right_all[rows, ff:] = dy_low
        do_ref[...] = dot_nt(dy_low, wp_ref[...]).astype(low)

    down_step = step - row_steps
    tile = ff // down_steps

    @pl.when((down_step >= 0) & (down_step < down_steps))
    def _():
        cols = pl.ds(pl.multiple_of(down_step * tile, 128), tile)
        store_tall(place_ref, core_ref, down_step, dot_tn(a_all[:, cols], g_all[...]), downs)

    up_step = down_step - down_steps
    up_steps = ff // width

    @pl.when((up_step >= 0) & (up_step < up_steps))
    def _():
        cols = pl.ds(pl.multiple_of(up_step * width, 128), width)
        store_columns(place_ref, core_ref, dot_tn(hidden_all[...], right_all[:, cols]), ups)

    @pl.when(up_step == up_steps)
    def _():
        store_columns(place_ref, core_ref, dot_tn(o_all[...], right_all[:, ff:]), ups)


def middle(place, core, x, o, g, da, wp, bp, gain2, bias2, wu, bu, wd, bd):
    count, width = x.shape
    ff = wu.shape[1]
    batch = 2 * place.shape[0]
    row_steps, up_steps = count // ROWS, ff // width + 1
    rows = ff // batch
    tall_aligned = aligned(ff, batch) and (4 * rows) % 128 == 0 and batch >= 8
    down_steps = batch // 4 if tall_aligned else ff // width

    def row(columns):
        return pl.BlockSpec((ROWS, columns), lambda i, p, c: (jnp.minimum(i, row_steps - 1), 0))

    def down_at(i):
        return jnp.clip(i - row_steps, 0, down_steps - 1)

    def up_at(i):
        return jnp.clip(i - row_steps - down_steps, 0, up_steps - 1)

    if tall_aligned:
        deep = batch // 4
        down_shape = [jax.ShapeDtypeStruct((2, deep, rows, width), low)] * 2
        down_specs = [
            pl.BlockSpec(
                (2, 1, rows, width), lambda i, p, c: (0, p[2 * down_at(i)] % deep, 0, 0)
            )
        ] * 2
    else:
        down_shape = [jax.ShapeDtypeStruct((ff, width), low)]
        down_specs = [pl.BlockSpec((ff // down_steps, width), lambda i, p, c: (down_at(i), 0))]
    if aligned(width, batch):
        shape = (batch // 2, width // batch)
        up_shape = [jax.ShapeDtypeStruct(shape + (ff + width,), low)] * 2
        up_specs = [pl.BlockSpec(shape + (width,), lambda i, p, c: (0, 0, up_at(i)))] * 2
    else:
        up_shape = [jax.ShapeDtypeStruct((width, ff + width), low)]
        up_specs = [pl.BlockSpec((width, width), lambda i, p, c: (0, up_at(i)))]
    sums = 4 * width + ff
    result = ordered_call(
        partial(middle_kernel, row_steps, down_steps, len(down_shape)),
        [],
        (row_steps + down_steps + up_steps,),
        [row(width)] * 3
        + [row(da.shape[1])]
        + [whole_spec(a.shape) for a in (wp, bp, gain2, bias2, wu, bu, wd, bd)],
        (x, o, g, da, wp, bp, gain2, bias2, wu, bu, wd, bd),
        (place, core),
        out_specs=[row(width)] * 3
        + [whole_spec((1, sums))]
        + down_specs
        + up_specs,
        out_shape=[
            jax.ShapeDtypeStruct((count, width), low),
            jax.ShapeDtypeStruct((count, width), wide),
            jax.ShapeDtypeStruct((count, width), low),
        ]
        + [jax.ShapeDtypeStruct((1, sums), wide)]
        + down_shape
        + up_shape,
        scratch_shapes=[
            pltpu.VMEM((count, ff), low),
            pltpu.VMEM((count, ff + width), low),
            pltpu.VMEM((count, width), low),
            pltpu.VMEM((count, width), low),
            pltpu.VMEM((count, width), low),
        ],
        name="middle",
    )
    rest = result[4:]
    if tall_aligned:
        downw = [r.reshape(batch // 2, rows, width) for r in rest[:2]]
    else:
        downw = split_shards(rest[0], place, core[0])
    ups = rest[len(down_shape) :]
    upw = ups if len(ups) == 2 else split_shards(ups[0], place, core[0])
    return result[:4], downw, upw


def attend_back_kernel(size_ref, q_ref, kn_ref, vn_ref, kf_ref, vf_ref, do_ref, o_ref,
                       lse_ref, cos_ref, sa_ref, sb_ref,
                       own_ref, clean_ref, sums_ref, dkf_acc, dvf_acc):
    length = q_ref.shape[0]
    near, far = block_masks(size_ref)
    kf_t = kf_ref[...].astype(wide).T.astype(low)
    kn_t = kn_ref[...].astype(wide).T.astype(low)
    product = do_ref[...].astype(wide) * o_ref[...].astype(wide)
    high = product.astype(low)
    rest = (product - high.astype(wide)).astype(low)
    head_row = lax.broadcasted_iota(jnp.int32, (8, PAIR), 0)
    head_lane = lax.broadcasted_iota(jnp.int32, (8, PAIR), 1) // HEAD
    picker = jnp.where(head_row == head_lane, 1.0, 0.0).astype(low)
    deltas = dot_nt(picker, high) + dot_nt(picker, rest)
    cosine, sa, sb = cos_ref[...], sa_ref[...], sb_ref[...]
    sum_q = jnp.zeros((1, PAIR), wide)
    sum_kn = jnp.zeros((1, PAIR), wide)
    sum_vn = jnp.zeros((1, PAIR), wide)
    tiles = []
    for tile in range(length // SPAN):
        past = tile * SPAN
        here = slice(past, past + SPAN)
        query, grad = both_heads(q_ref[here, :]), both_heads(do_ref[here, :])
        scores = dot_nt(kf_ref[: past + SPAN, :], query)
        dprob = dot_nt(vf_ref[: past + SPAN, :], grad)
        diag = jnp.where(
            near,
            dot_nt(kn_ref[here, :], query),
            jnp.where(far, scores[past:], masked_value),
        )
        dprob_diag = jnp.where(near, dot_nt(vn_ref[here, :], grad), dprob[past:])
        tiles.append((past, here, query, grad, scores[:past], dprob[:past], diag, dprob_diag))
    results = []
    for past, here, query, grad, scores, dprob, diag, dprob_diag in tiles:
        lse = jnp.concatenate([lse_ref[0, 0:1, here], lse_ref[0, 1:2, here]], axis=1)
        delta = jnp.concatenate([deltas[0:1, here], deltas[1:2, here]], axis=1)
        prob_diag = jnp.exp2(diag - lse)
        ds_diag = prob_diag * (dprob_diag - delta)
        prob_near = jnp.where(near, prob_diag, 0.0).astype(low)
        ds_near = jnp.where(near, ds_diag, 0.0).astype(low)
        prob = jnp.where(near, 0.0, prob_diag).astype(low)
        dscore = jnp.where(near, 0.0, ds_diag).astype(low)
        if past:
            prob_past = jnp.exp2(scores - lse)
            ds_past = prob_past * (dprob - delta)
            prob = jnp.concatenate([prob_past.astype(low), prob], axis=0)
            dscore = jnp.concatenate([ds_past.astype(low), dscore], axis=0)
        results.append((past, here, query, grad, prob_near, ds_near, prob, dscore))
    for past, here, query, grad, prob_near, ds_near, prob, dscore in results:
        dkf, dvf = dot_nn(dscore, query), dot_nn(prob, grad)
        if past:
            dkf_acc[:past, :] += dkf[:past]
            dvf_acc[:past, :] += dvf[:past]
        dkf_acc[here, :] = dkf[past:]
        dvf_acc[here, :] = dvf[past:]
        dkn, dvn = dot_nn(ds_near, query), dot_nn(prob_near, grad)
        dqt = dot_nn(kn_t[:, here], ds_near) + dot_nn(kf_t[:, : past + SPAN], dscore)
        dq = own_blocks(dqt) * (1.0 / math.sqrt(HEAD))
        dq = rotate_back(dq, cosine[here], sa[here], sb[here])
        own_ref[0, here, :] = dq.astype(low)
        sum_q = sum_q + jnp.sum(dq, axis=0, keepdims=True)
        dkn = rotate_back(dkn * ln2, cosine[here], sa[here], sb[here])
        own_ref[1, here, :] = dkn.astype(low)
        sum_kn = sum_kn + jnp.sum(dkn, axis=0, keepdims=True)
        own_ref[2, here, :] = dvn.astype(low)
        sum_vn = sum_vn + jnp.sum(dvn, axis=0, keepdims=True)
    dkf = rotate_back(dkf_acc[...] * ln2, cosine, sa, sb)
    dvf = dvf_acc[...]
    clean_ref[0] = dkf.astype(low)
    clean_ref[1] = dvf.astype(low)
    sums_ref[0, 0:1, :] = sum_q
    sums_ref[0, 1:2, :] = sum_kn + jnp.sum(dkf, axis=0, keepdims=True)
    sums_ref[0, 2:3, :] = sum_vn + jnp.sum(dvf, axis=0, keepdims=True)


def attend_back(size, q, kn, vn, kf, vf, do, o, lse, tables, first, pairs, after, work):
    count = q.shape[0]
    pair_spec = pl.BlockSpec((count, PAIR), lambda p: (0, p + first))
    width = pairs * PAIR
    return ordered_call(
        attend_back_kernel,
        after,
        (pairs,),
        [pl.BlockSpec(memory_space=pltpu.SMEM)]
        + [pair_spec] * 7
        + [pl.BlockSpec((1, 2, count), lambda p: (p + first, 0, 0))]
        + [whole_spec(t.shape) for t in tables],
        (size, q, kn, vn, kf, vf, do, o, lse, *tables),
        out_specs=[
            pl.BlockSpec((3, count, PAIR), lambda p: (0, 0, p)),
            pl.BlockSpec((2, count, PAIR), lambda p: (0, 0, p)),
            pl.BlockSpec((1, 3, PAIR), lambda p: (p, 0, 0)),
        ],
        out_shape=[
            jax.ShapeDtypeStruct((3, count, width), low),
            jax.ShapeDtypeStruct((2, count, width), low),
            jax.ShapeDtypeStruct((pairs, 3, PAIR), wide),
        ],
        scratch_shapes=[
            pltpu.VMEM((count, PAIR), wide),
            pltpu.VMEM((count, PAIR), wide),
        ],
        work=work,
        name="attend_back",
    )


def spread_lanes(columns, batch):
    rows = columns.shape[0] // batch
    lane = lax.broadcasted_iota(jnp.int32, (rows, PAIR), 1)
    shards = []
    for shard in range(batch):
        block = columns[shard * rows : (shard + 1) * rows]
        for first, share in ((4, 4), (8, 3)):
            for j in range(share):
                chunk = share * shard + j
                at, start = first + chunk // batch, chunk % batch * rows
                block = jnp.where(
                    lane == first + j, columns[start : start + rows, at : at + 1], block
                )
        shards.append(block)
    return jnp.concatenate(shards, axis=0)


def qkv_kernel(cuts, batch, place_ref, core_ref, h_ref, hf_ref, w_ref, gain1_ref, bias1_ref,
               early_ref, *rest):
    own, clean, sums, rest = (
        rest[:cuts],
        rest[cuts : 2 * cuts],
        rest[2 * cuts : 3 * cuts],
        rest[3 * cuts :],
    )
    outs, (rows_ref, columns_ref, result_ref) = rest[:-3], rest[-3:]
    step = pl.program_id(0)
    width = h_ref.shape[1]
    result_ref[...] = dot_tn(h_ref[...], jnp.concatenate([r[0] for r in own], axis=1))

    @pl.when(step == 0)
    def _():
        columns_ref[...] = jnp.zeros_like(columns_ref)
        rows_ref[...] = jnp.zeros_like(rows_ref)
        for i in range(8):
            rows_ref[i : i + 1, :] = early_ref[:, i * width : (i + 1) * width]
        rows_ref[13:14, :] = row_of(gain1_ref)
        rows_ref[14:15, :] = row_of(bias1_ref)

    @pl.when(step > 0)
    def _():
        result_ref[...] += dot_tn(hf_ref[...], jnp.concatenate([r[0] for r in clean], axis=1))

    result = result_ref[...]
    cols = pl.ds(pl.multiple_of(step * width, 128), width)
    store_columns(place_ref, core_ref, result, outs, cols)
    weight = w_ref[...].astype(wide)
    totals = jnp.concatenate(
        [r[p, pl.ds(step, 1), :] for r in sums for p in range(r.shape[0])], axis=1
    )
    rows_ref[pl.ds(8 + step, 1), :] = totals
    lane = lax.broadcasted_iota(jnp.int32, (1, PAIR), 1)
    columns_ref[...] += jnp.where(
        lane == 0,
        jnp.sum(weight * result, axis=1, keepdims=True),
        jnp.sum(weight * totals, axis=1, keepdims=True),
    )

    @pl.when(step == 2)
    def _():
        columns = rows_ref[...].T
        bias = columns_ref[:, 1:2]
        gain = (columns_ref[:, 0:1] - columns[:, 14:15] * bias) / columns[:, 13:14]
        columns = jnp.where(lane == 11, gain, jnp.where(lane == 12, bias, columns))
        if len(outs) == 2:
            columns = spread_lanes(columns, batch)
        store_columns(place_ref, core_ref, columns, outs, slice(3 * width, 3 * width + PAIR))


def outer_qkv(h, hf, weight, gain1, bias1, early, own, clean, sums, place, core, after):
    count, width = h.shape
    batch = 2 * place.shape[0]
    columns = 3 * width + PAIR
    if aligned(width, batch):
        out_shape = [jax.ShapeDtypeStruct((batch // 2, width // batch, columns), low)] * 2
    else:
        out_shape = [jax.ShapeDtypeStruct((width, columns), low)]
    result = ordered_call(
        partial(qkv_kernel, len(own), batch),
        after,
        (3,),
        [whole_spec(h.shape)] * 2
        + [pl.BlockSpec((width, width), lambda i, p, c: (0, i))]
        + [whole_spec(v.shape) for v in (gain1, bias1, early)]
        + [pl.BlockSpec((1, count, r.shape[2]), lambda i, p, c: (i, 0, 0)) for r in own]
        + [
            pl.BlockSpec((1, count, r.shape[2]), lambda i, p, c: (jnp.maximum(i - 1, 0), 0, 0))
            for r in clean
        ]
        + [whole_spec(r.shape) for r in sums],
        (h, hf, weight, gain1, bias1, early, *own, *clean, *sums),
        (place, core),
        out_specs=[whole_spec(o.shape) for o in out_shape],
        out_shape=out_shape,
        scratch_shapes=[
            pltpu.VMEM((PAIR, width), wide),
            pltpu.VMEM((width, PAIR), wide),
            pltpu.VMEM((width, width), wide),
        ],
        work=1e8,
        name="outer_qkv",
    )
    if len(result) == 2:
        return result
    (full,) = result
    rows = width // batch
    start = 3 * width
    spread = [full[:, : start + 4]]
    for first, share in ((4, 4), (8, 3)):
        part = full[:, start + first : start + first + share].T.reshape(batch, share, rows)
        spread.append(part.transpose(0, 2, 1).reshape(width, share))
    spread.append(full[:, start + 11 :])
    return split_shards(jnp.concatenate(spread, axis=1), place, core[0])


def project_far_back_kernel(cuts, noisy_ref, x_ref, *rest):
    far, clean = rest[:HALVES], rest[HALVES : HALVES + cuts]
    wk_ref, wv_ref, gain1_ref, dfar_ref = rest[HALVES + cuts :]
    steps = pl.num_programs(0) // HALVES
    source = x_ref[...].astype(wide)
    for i, ref in enumerate(far):
        chosen = (noisy_ref[0] == 1) & (pl.program_id(0) // steps == i)
        source = jnp.where(chosen, ref[...].astype(wide), source)
    normed, factor = normalize(source)
    dh = jnp.zeros_like(source)
    for part, w_ref in enumerate((wk_ref, wv_ref)):
        grads = jnp.concatenate([c[part] for c in clean], axis=1)
        dh = dh + dot_nt(grads, w_ref[...])
    dfar_ref[...] = norm_back(dh * row_of(gain1_ref), normed, factor).astype(low)


def project_far_back(noisy, x, far, clean, weight, gain1, after):
    count, width = x.shape
    return ordered_call(
        partial(project_far_back_kernel, len(clean)),
        after,
        (count // ROWS,),
        [pl.BlockSpec(memory_space=pltpu.SMEM)]
        + [row_spec(width)]
        + [
            pl.BlockSpec(
                (ROWS, width),
                lambda i, first=n * f.shape[0] // ROWS, last=f.shape[0] // ROWS - 1: (
                    jnp.clip(i - first, 0, last),
                    0,
                ),
            )
            for n, f in enumerate(far)
        ]
        + [pl.BlockSpec((2, ROWS, c.shape[2]), lambda i: (0, i, 0)) for c in clean]
        + [
            pl.BlockSpec((width, width), lambda i, part=part: (0, part), pipeline_mode=pl.Buffered(1))
            for part in (1, 2)
        ]
        + [whole_spec(gain1.shape)],
        (noisy, x, *far, *clean, weight, weight, gain1),
        out_specs=row_spec(width),
        out_shape=jax.ShapeDtypeStruct((count, width), low),
        work=1e8,
        name="project_far_back",
    )


def project_back_kernel(cuts, noisy_ref, x_ref, dy_ref, dfar_ref, *rest):
    own = rest[:cuts]
    w_ref, gain1_ref, dx_ref = rest[cuts:]
    width = x_ref.shape[1]
    normed, factor = normalize(x_ref[...].astype(wide))
    dh = jnp.zeros_like(dy_ref)
    for part in range(3):
        grads = jnp.concatenate([c[part] for c in own], axis=1)
        dh = dh + dot_nt(grads, w_ref[:, part * width : (part + 1) * width])
    dx = dy_ref[...] + norm_back(dh * row_of(gain1_ref), normed, factor)
    dx_ref[...] = dx + jnp.where(noisy_ref[0] == 0, dfar_ref[...].astype(wide), 0.0)


def project_back(noisy, x, dy, dfar, own, weight, gain1, after):
    count, width = x.shape
    return ordered_call(
        partial(project_back_kernel, len(own)),
        after,
        (count // ROWS,),
        [pl.BlockSpec(memory_space=pltpu.SMEM)]
        + [row_spec(width)] * 3
        + [pl.BlockSpec((3, ROWS, c.shape[2]), lambda i: (0, i, 0)) for c in own]
        + [whole_spec(weight.shape), whole_spec(gain1.shape)],
        (noisy, x, dy, dfar, *own, weight, gain1),
        out_specs=row_spec(width),
        out_shape=jax.ShapeDtypeStruct((count, width), wide),
        work=1.5e10,
        name="project_back",
    )


def flip(values, mask):
    batch = lax.axis_size("batch")
    return lax.ppermute(values, "batch", [(i, i ^ mask) for i in range(batch)])


def flip_stream(values):
    return lax.ppermute(values, "stream", [(0, 1), (1, 0)])


def total(terms):
    result = terms[0].astype(wide)
    for term in terms[1:]:
        result = result + term.astype(wide)
    return result


class Reduction:
    def __init__(self, name, shards):
        keep, send = shards
        self.name = name
        self.terms = [keep, flip(send, 1)]
        self.stages = stages_of(2 * keep.shape[0])
        self.size = keep.shape[0]

    def wait_for(self, others):
        self.terms, _ = lax.optimization_barrier((self.terms, list(others)))

    def step(self):
        bits = self.stages.pop(0)
        parts = 2 ** len(bits)
        size = self.size // parts
        pieces = [
            total([t[j * size : (j + 1) * size] for t in self.terms]).astype(low)
            for j in range(1, parts)
        ]
        arrived = [flip(p, mask_of(bits, j + 1)) for j, p in enumerate(pieces)]
        self.terms = self.terms + arrived
        self.arrived = arrived
        self.size = size
        return pieces

    def last(self):
        while self.stages:
            self.step()
        self.mine = total([t[:1] for t in self.terms]).astype(low)
        self.other = flip_stream(self.mine)
        return [self.mine]

    def result(self, first, count):
        at = slice(first, first + count)
        return self.mine[0][:, at].astype(wide) + self.other[0][:, at].astype(wide)


def local(
    layer_input,
    out_cotangent,
    block_size,
    norm1_gain,
    norm1_bias,
    qkv_weight,
    qkv_bias,
    proj_weight,
    proj_bias,
    norm2_gain,
    norm2_bias,
    up_weight,
    up_bias,
    down_weight,
    down_bias,
):
    length, width = layer_input.shape[2:]
    batch = lax.axis_size("batch")
    noisy = lax.axis_index("stream").astype(jnp.int32).reshape(1)
    x = layer_input.reshape(length, width)
    g = out_cotangent.reshape(length, width)
    half = length // HALVES
    far_x, source = [], x
    for i in range(HALVES):
        piece = source[i * half : (i + 1) * half]
        far_x.append(lax.ppermute(piece, "stream", [(0, 1)]))
        source, _ = lax.optimization_barrier((source, piece))
    tables = rotary_tables(length)
    me = lax.axis_index("batch").astype(jnp.int32)
    place, core = places_of(batch, me), (me % 2).reshape(1)
    h, q, k, v = project(x, qkv_weight, qkv_bias, norm1_gain, norm1_bias, tables)
    da = early_part(g, down_weight, EARLY)
    fars, attended = [], []
    for i in range(HALVES):
        fars = project_far(
            noisy, x, far_x[i], qkv_weight, qkv_bias, norm1_gain, norm1_bias, tables, i, fars,
            [] if i else [da, h],
        )
        hf, kf, vf = fars
        attended = attend(block_size, q, k, v, kf, vf, i, HALVES, attended)
    o, lse = attended
    (out, dy, do, early), downw, upw = middle(
        place,
        core,
        x,
        o,
        g,
        da,
        proj_weight,
        proj_bias,
        norm2_gain,
        norm2_bias,
        up_weight,
        up_bias,
        down_weight,
        down_bias,
    )
    down, up = Reduction("down", downw), Reduction("up", upw)
    backs, after = [], []
    for i, (first, pairs) in enumerate(CUTS):
        if i == 1:
            down.wait_for(backs[0])
            after = down.step()
        after = after + [b[0] for b in backs[-1:]]
        backs.append(
            attend_back(
                block_size, q, k, v, kf, vf, do, o, lse, tables, first, pairs, after, 2e10
            )
        )
    own, clean, sums = ([b[i] for b in backs] for i in range(3))
    up.wait_for(backs[-1])
    down.wait_for(backs[-1])
    after = up.step() + down.step()
    dfar = project_far_back(noisy, x, far_x, clean, qkv_weight, norm1_gain, after)
    qkvw = outer_qkv(
        h,
        hf,
        qkv_weight,
        norm1_gain,
        norm1_bias,
        early,
        own,
        clean,
        sums,
        place,
        core,
        [dfar],
    )
    qkvw, _ = lax.optimization_barrier((list(qkvw), up.arrived + down.arrived))
    qkv = Reduction("qkv", qkvw)
    after = up.step()
    leaving, _ = lax.optimization_barrier((dfar, after))
    back_x = lax.ppermute(leaving, "stream", [(1, 0)])
    qkv.wait_for(after)
    after = qkv.step()
    dx = project_back(noisy, x, dy, dfar, own, qkv_weight, norm1_gain, after)
    qkv.wait_for([dx])
    after = qkv.step()
    down.wait_for(after)
    down.last()
    up.wait_for(after)
    up.last()
    arriving, _ = lax.optimization_barrier((back_x, up.mine))
    input_grad = (dx + arriving.astype(wide)).reshape(layer_input.shape)
    qkv.wait_for([input_grad])
    qkv.last()
    ff = up_weight.shape[1]
    downw_grad = down.result(0, width)
    upw_grad, projw_grad = up.result(0, ff), up.result(ff, width)
    qkvw_grad = qkv.result(0, 3 * width)
    vectors = qkv.result(3 * width, PAIR).T
    downb_grad, gain2_grad, bias2_grad, projb_grad = (vectors[i] for i in range(4))
    upb_grad, qkvb_grad = vectors[4:8].reshape(-1), vectors[8:11].reshape(-1)
    gain1_grad, bias1_grad = vectors[11], vectors[12]
    return (
        out.reshape(layer_input.shape),
        input_grad,
        gain1_grad,
        bias1_grad,
        qkvw_grad,
        qkvb_grad,
        projw_grad,
        projb_grad,
        gain2_grad,
        bias2_grad,
        upw_grad,
        upb_grad,
        downw_grad,
        downb_grad,
    )


def solution(mesh):
    rows = P("stream", "batch", None, None)
    return jax.shard_map(
        local,
        mesh=mesh,
        in_specs=(rows, rows, P("batch")) + (P(),) * 12,
        out_specs=(
            rows,
            rows,
            P("batch"),
            P("batch"),
            P("batch", None),
            P("batch"),
            P("batch", None),
            P("batch"),
            P("batch"),
            P("batch"),
            P("batch", None),
            P("batch"),
            P("batch", None),
            P("batch"),
        ),
        check_vma=False,
    )
```

```python
from functools import partial
import math

import jax
import jax.numpy as jnp
from jax import lax
from jax.experimental import pallas as pl
from jax.experimental.pallas import tpu as pltpu
from jax.sharding import PartitionSpec as P
import numpy as np

HEAD = 64
PAIR = 2 * HEAD
ROWS = 256
SPAN = 128
HALVES = 2
EARLY = 3
CUTS = ((0, 1), (1, 5))
full_vmem = 60

masked_value = -1e30
epsilon = 1e-05
low = jnp.bfloat16
wide = jnp.float32
score_scale = math.log2(math.e) / math.sqrt(HEAD)
ln2 = math.log(2.0)
gelu_c = math.sqrt(2.0 / math.pi)
gelu_k = 0.044715
mega = 1024 * 1024


def dot_nn(left, right):
    return lax.dot_general(left, right, (((1,), (0,)), ((), ())), preferred_element_type=wide)


def dot_nt(left, right):
    return lax.dot_general(left, right, (((1,), (1,)), ((), ())), preferred_element_type=wide)


def dot_tn(left, right):
    return lax.dot_general(left, right, (((0,), (0,)), ((), ())), preferred_element_type=wide)


def params(limit_mib):
    return pltpu.CompilerParams(
        dimension_semantics=("arbitrary",), vmem_limit_bytes=limit_mib * mega
    )


def cost(flops, nbytes, trans=0):
    return pl.CostEstimate(
        flops=int(flops), bytes_accessed=int(nbytes), transcendentals=int(trans)
    )


def ordered_call(
    kernel, after, grid, in_specs, operands, prefetch=(), work=4e9, into=(), **rest
):
    skip = len(prefetch) + len(operands)
    after = list(into) + list(after)

    def body(*refs):
        kernel(*refs[:skip], *refs[skip + len(after) :])

    out_specs = rest.pop("out_specs")
    scratch = rest.pop("scratch_shapes", [])
    call = pl.pallas_call(
        body,
        grid_spec=pltpu.PrefetchScalarGridSpec(
            num_scalar_prefetch=len(prefetch),
            grid=grid,
            in_specs=list(in_specs) + [pl.BlockSpec(memory_space=pl.ANY)] * len(after),
            out_specs=out_specs,
            scratch_shapes=scratch,
        ),
        compiler_params=pltpu.CompilerParams(
            dimension_semantics=("arbitrary",) * len(grid), vmem_limit_bytes=full_vmem * mega
        ),
        cost_estimate=cost(work, 1000),
        input_output_aliases={skip + i: i for i in range(len(into))},
        **rest,
    )
    return call(*prefetch, *operands, *after)


def row_of(ref, at=slice(None)):
    return ref[at].reshape(1, -1)


def whole_spec(shape):
    zeros = (0,) * len(shape)
    return pl.BlockSpec(shape, lambda *_: zeros, pipeline_mode=pl.Buffered(1))


def row_spec(width, rows=ROWS):
    return pl.BlockSpec((rows, width), lambda i: (i, 0))


def normalize(values):
    mean = jnp.mean(values, axis=-1, keepdims=True)
    centred = values - mean
    factor = lax.rsqrt(jnp.mean(centred * centred, axis=-1, keepdims=True) + epsilon)
    return (centred * factor, factor)


def norm_back(grad_normed, normed, factor):
    first = jnp.mean(grad_normed, axis=-1, keepdims=True)
    second = jnp.mean(grad_normed * normed, axis=-1, keepdims=True)
    return factor * (grad_normed - first - normed * second)


def rotary_tables(length):
    places = np.arange(length, dtype=np.float64)[:, None]
    column = np.arange(PAIR) % HEAD
    angle = places * (10000.0 ** (-2.0 * (column % (HEAD // 2)) / HEAD))[None, :]
    upper = (column >= HEAD // 2)[None, :]
    cosine, sine = np.cos(angle), np.sin(angle)
    tables = (cosine, np.where(upper, sine, 0.0), np.where(upper, 0.0, -sine))
    return tuple(jnp.asarray(t, dtype=wide) for t in tables)


def rotate(values, cosine, sine_a, sine_b):
    return (
        values * cosine
        + pltpu.roll(values, HEAD // 2, 1) * sine_a
        + pltpu.roll(values, PAIR - HEAD // 2, 1) * sine_b
    )


def rotate_back(values, cosine, sine_a, sine_b):
    return (
        values * cosine
        - pltpu.roll(values, HEAD // 2, 1) * sine_a
        - pltpu.roll(values, PAIR - HEAD // 2, 1) * sine_b
    )


def project_kernel(x_ref, w_ref, bias_ref, gain1_ref, bias1_ref, cos_ref, sa_ref, sb_ref,
                   h_ref, q_ref, k_ref, v_ref):
    width = x_ref.shape[1]
    normed, _ = normalize(x_ref[...].astype(wide))
    hidden = (normed * row_of(gain1_ref) + row_of(bias1_ref)).astype(low)
    h_ref[...] = hidden
    cosine, sa, sb = cos_ref[...], sa_ref[...], sb_ref[...]
    for out, part in ((q_ref, 0), (k_ref, 1), (v_ref, 2)):
        cols = slice(part * width, (part + 1) * width)
        mixed = dot_nn(hidden, w_ref[:, cols]) + row_of(bias_ref, cols)
        if part == 2:
            out[...] = mixed.astype(low)
            continue
        for group in range(width // PAIR):
            at = slice(group * PAIR, (group + 1) * PAIR)
            turned = rotate(mixed[:, at], cosine, sa, sb)
            if part == 0:
                turned = turned * score_scale
            out[:, at] = turned.astype(low)


def project_far_kernel(noisy_ref, x_ref, far_ref, wk_ref, wv_ref, bias_ref, gain1_ref, bias1_ref,
                       cos_ref, sa_ref, sb_ref, h_ref, k_ref, v_ref):
    width = x_ref.shape[1]
    source = jnp.where(noisy_ref[0] == 1, far_ref[...].astype(wide), x_ref[...].astype(wide))
    normed, _ = normalize(source)
    hidden = (normed * row_of(gain1_ref) + row_of(bias1_ref)).astype(low)
    h_ref[...] = hidden
    cosine, sa, sb = cos_ref[...], sa_ref[...], sb_ref[...]
    mixed = dot_nn(hidden, wk_ref[...]) + row_of(bias_ref, slice(width, 2 * width))
    for group in range(width // PAIR):
        at = slice(group * PAIR, (group + 1) * PAIR)
        k_ref[:, at] = rotate(mixed[:, at], cosine, sa, sb).astype(low)
    mixed = dot_nn(hidden, wv_ref[...]) + row_of(bias_ref, slice(2 * width, None))
    v_ref[...] = mixed.astype(low)


def project(x, weight, bias, gain1, bias1, tables):
    count, width = x.shape
    row = jax.ShapeDtypeStruct((count, width), low)
    return pl.pallas_call(
        project_kernel,
        grid=(count // ROWS,),
        in_specs=[
            row_spec(width),
            whole_spec(weight.shape),
            whole_spec(bias.shape),
            whole_spec(gain1.shape),
            whole_spec(bias1.shape),
            row_spec(PAIR),
            row_spec(PAIR),
            row_spec(PAIR),
        ],
        out_specs=[row_spec(width)] * 4,
        out_shape=[row] * 4,
        compiler_params=params(full_vmem),
        cost_estimate=cost(2 * count * width * 3 * width, 16e6),
        name="project",
    )(x, weight, bias, gain1, bias1, *tables)


def project_far(noisy, x, far, weight, bias, gain1, bias1, tables, part, into, after):
    count, width = x.shape
    steps = far.shape[0] // ROWS
    row = jax.ShapeDtypeStruct((count, width), low)

    def part_rows(columns):
        return pl.BlockSpec((ROWS, columns), lambda i: (part * steps + i, 0))

    return ordered_call(
        project_far_kernel,
        after,
        (steps,),
        [
            pl.BlockSpec(memory_space=pltpu.SMEM),
            part_rows(width),
            row_spec(width),
            pl.BlockSpec((width, width), lambda i: (0, 1), pipeline_mode=pl.Buffered(1)),
            pl.BlockSpec((width, width), lambda i: (0, 2), pipeline_mode=pl.Buffered(1)),
            whole_spec(bias.shape),
            whole_spec(gain1.shape),
            whole_spec(bias1.shape),
            part_rows(PAIR),
            part_rows(PAIR),
            part_rows(PAIR),
        ],
        (noisy, x, far, weight, weight, bias, gain1, bias1, *tables),
        into=into,
        out_specs=[part_rows(width)] * 3,
        out_shape=[row] * 3,
        name="project_far",
    )


def early_kernel(g_ref, w_ref, out_ref):
    out_ref[...] = dot_nt(g_ref[...], w_ref[...]).astype(low)


def early_part(g, weight, chunks):
    count, width = g.shape
    return ordered_call(
        early_kernel,
        [],
        (chunks,),
        [whole_spec(g.shape), pl.BlockSpec((width, width), lambda i: (i, 0))],
        (g, weight),
        out_specs=pl.BlockSpec((count, width), lambda i: (0, i)),
        out_shape=jax.ShapeDtypeStruct((count, chunks * width), low),
        name="early_part",
    )


def block_masks(size_ref):
    key = lax.broadcasted_iota(jnp.int32, (SPAN, 2 * SPAN), 0)
    query = lax.broadcasted_iota(jnp.int32, (SPAN, 2 * SPAN), 1) % SPAN
    near = (key ^ query) < size_ref[0]
    return near, key < query


def both_heads(rows):
    lane = lax.broadcasted_iota(jnp.int32, (1, PAIR), 1)
    none = jnp.zeros_like(rows)
    return jnp.concatenate(
        [jnp.where(lane < HEAD, rows, none), jnp.where(lane >= HEAD, rows, none)], axis=0
    )


def own_blocks(mixed):
    return jnp.concatenate([mixed[:HEAD, :SPAN], mixed[HEAD:, SPAN:]], axis=0).T


def attend_kernel(first, size_ref, q_ref, kn_ref, vn_ref, kf_ref, vf_ref, o_ref, lse_ref):
    near, far = block_masks(size_ref)
    vf_t = vf_ref[...].astype(wide).T.astype(low)
    vn_t = vn_ref[...].astype(wide).T.astype(low)
    parts = range(q_ref.shape[0] // SPAN)
    state = []
    for part in parts:
        past = (first + part) * SPAN
        own = slice(part * SPAN, (part + 1) * SPAN)
        query = both_heads(q_ref[own, :])
        scores = dot_nt(kf_ref[: past + SPAN, :], query)
        diag = jnp.where(
            near, dot_nt(kn_ref[own, :], query), jnp.where(far, scores[past:], masked_value)
        )
        state.append((past, own, scores, diag))
    probs = []
    for past, own, scores, diag in state:
        top = jnp.max(diag, axis=0, keepdims=True)
        if past:
            top = jnp.maximum(top, jnp.max(scores[:past], axis=0, keepdims=True))
        prob = jnp.exp2(diag - top)
        total = jnp.sum(prob, axis=0, keepdims=True)
        prob_near = jnp.where(near, prob, 0.0).astype(low)
        prob_far = jnp.where(near, 0.0, prob).astype(low)
        if past:
            prob = jnp.exp2(scores[:past] - top)
            total = total + jnp.sum(prob, axis=0, keepdims=True)
            prob_far = jnp.concatenate([prob.astype(low), prob_far], axis=0)
        lse = top + jnp.log2(total)
        lse_ref[0, 0:1, own] = lse[:, :SPAN]
        lse_ref[0, 1:2, own] = lse[:, SPAN:]
        probs.append((past, own, prob_near, prob_far, 1.0 / total))
    for past, own, prob_near, prob_far, scale in probs:
        mixed = dot_nn(vn_t[:, own], prob_near) + dot_nn(vf_t[:, : past + SPAN], prob_far)
        o_ref[own, :] = own_blocks(mixed * scale).astype(low)


def attend(size, q, kn, vn, kf, vf, part, parts, into):
    count, width = q.shape
    pairs = width // PAIR
    rows = count // parts
    own_spec = pl.BlockSpec((rows, PAIR), lambda p: (part, p))
    far_spec = pl.BlockSpec(((part + 1) * rows, PAIR), lambda p: (0, p))
    return ordered_call(
        partial(attend_kernel, part * rows // SPAN),
        [],
        (pairs,),
        [pl.BlockSpec(memory_space=pltpu.SMEM)] + [own_spec] * 3 + [far_spec] * 2,
        (size, q, kn, vn, kf, vf),
        into=into,
        out_specs=[own_spec, pl.BlockSpec((1, 2, rows), lambda p: (p, 0, part))],
        out_shape=[
            jax.ShapeDtypeStruct((count, width), low),
            jax.ShapeDtypeStruct((pairs, 2, count), wide),
        ],
        name="attend",
    )


def stages_of(batch):
    bits = list(range(1, batch.bit_length() - 1))
    stages = [bits[:1]]
    rest = bits[1:]
    while rest:
        stages.append(rest[:2])
        rest = rest[2:]
    return [s for s in stages if s]


def mask_of(bits, digit):
    return sum(((digit >> i) & 1) << bit for i, bit in enumerate(bits))


def places_of(batch, me):
    relative = jnp.arange(0, batch, 2, dtype=jnp.int32) ^ (me - me % 2)
    place = jnp.zeros_like(relative)
    for bits in stages_of(batch):
        place = place * 2 ** len(bits)
        for i, bit in enumerate(bits):
            place = place + (((relative >> bit) & 1) << i)
    return place


def store_shards(place_ref, core_ref, result, keep_ref, send_ref, columns=slice(None)):
    shards = keep_ref.shape[0]
    rows = result.shape[0] // (2 * shards)

    def store(first_ref, second_ref):
        for pair in range(shards):
            at = place_ref[pair]
            start = 2 * pair * rows
            first_ref[at, :, columns] = result[start : start + rows].astype(low)
            second_ref[at, :, columns] = result[start + rows : start + 2 * rows].astype(low)

    pl.when(core_ref[0] == 0)(lambda: store(keep_ref, send_ref))
    pl.when(core_ref[0] == 1)(lambda: store(send_ref, keep_ref))


def split_shards(full, place, core):
    batch = 2 * place.shape[0]
    shards = full.reshape((batch // 2, 2, full.shape[0] // batch) + full.shape[1:])
    order = jnp.argsort(place)
    shards = jnp.take(shards, order, axis=0)
    return (
        jnp.where(core == 0, shards[:, 0], shards[:, 1]),
        jnp.where(core == 0, shards[:, 1], shards[:, 0]),
    )


def aligned(tall, batch):
    return tall % batch == 0 and (tall // batch) % 16 == 0


def store_columns(place_ref, core_ref, result, outs, columns=slice(None)):
    if len(outs) == 1:
        outs[0][:, columns] = result.astype(low)
    else:
        store_shards(place_ref, core_ref, result, *outs, columns)


def store_tall(place_ref, core_ref, step, result, outs):
    if len(outs) == 1:
        outs[0][...] = result.astype(low)
        return
    rows = outs[0].shape[2]
    places = place_ref.shape[0] // 2

    def store(first_ref, second_ref):
        for x in range(2):
            at = place_ref[2 * step + x] // places
            start = 2 * x * rows
            first_ref[at, 0] = result[start : start + rows].astype(low)
            second_ref[at, 0] = result[start + rows : start + 2 * rows].astype(low)

    pl.when(core_ref[0] == 0)(lambda: store(*outs))
    pl.when(core_ref[0] == 1)(lambda: store(*outs[::-1]))


def middle_kernel(row_steps, down_steps, tall_outs, place_ref, core_ref, x_ref, o_ref, g_ref, da_ref,
                  wp_ref, bp_ref, gain2_ref, bias2_ref, wu_ref, bu_ref, wd_ref, bd_ref,
                  out_ref, dy_ref, do_ref, sums_ref,
                  *rest):
    downs, ups = rest[:tall_outs], rest[tall_outs:-5]
    a_all, right_all, hidden_all, o_all, g_all = rest[-5:]
    width = x_ref.shape[1]
    ff = wu_ref.shape[1]
    step = pl.program_id(0)

    def add_sum(start, values):
        at = slice(start, start + values.shape[1])
        sums_ref[:, at] += jnp.sum(values, axis=0, keepdims=True)

    @pl.when(step == 0)
    def _():
        sums_ref[...] = jnp.zeros_like(sums_ref)

    @pl.when(step < row_steps)
    def _():
        rows = pl.ds(pl.multiple_of(step * ROWS, ROWS), ROWS)
        parts = [slice(i * width, (i + 1) * width) for i in range(ff // width)]
        grad = g_ref[...]
        y = x_ref[...].astype(wide) + dot_nn(o_ref[...], wp_ref[...]) + row_of(bp_ref)
        das = [da_ref[:, cols].astype(wide) for cols in parts[:EARLY]]
        das += [dot_nt(grad, wd_ref[cols, :]) for cols in parts[EARLY:]]
        normed, factor = normalize(y)
        hidden = (normed * row_of(gain2_ref) + row_of(bias2_ref)).astype(low)
        o_all[rows, :] = o_ref[...]
        hidden_all[rows, :] = hidden
        g_all[rows, :] = grad
        grad_wide = grad.astype(wide)
        ups = [dot_nn(hidden, wu_ref[:, cols]) + row_of(bu_ref, cols) for cols in parts]
        acts, dus = [], []
        for part, cols in enumerate(parts):
            up = ups[part]
            square = up * up
            half = 0.5 + 0.5 * jnp.tanh(up * (gelu_c + (gelu_c * gelu_k) * square))
            active = (up * half).astype(low)
            slope = half + (up * (2.0 * gelu_c + (6.0 * gelu_c * gelu_k) * square)) * (
                half * (1.0 - half)
            )
            du = das[part] * slope
            du_low = du.astype(low)
            a_all[rows, cols] = active
            right_all[rows, cols] = du_low
            add_sum(4 * width + part * width, du)
            acts.append(active)
            dus.append(du_low)
        result = y + row_of(bd_ref)
        dh2 = jnp.zeros_like(y)
        for part, cols in enumerate(parts):
            dh2 = dh2 + dot_nt(dus[part], wu_ref[:, cols])
            result = result + dot_nn(acts[part], wd_ref[cols, :])
        out_ref[...] = result.astype(low)
        add_sum(0, grad_wide)
        add_sum(width, dh2 * normed)
        add_sum(2 * width, dh2)
        dy = grad_wide + norm_back(dh2 * row_of(gain2_ref), normed, factor)
        dy_ref[...] = dy
        add_sum(3 * width, dy)
        dy_low = dy.astype(low)
        right_all[rows, ff:] = dy_low
        do_ref[...] = dot_nt(dy_low, wp_ref[...]).astype(low)

    down_step = step - row_steps
    tile = ff // down_steps

    @pl.when((down_step >= 0) & (down_step < down_steps))
    def _():
        cols = pl.ds(pl.multiple_of(down_step * tile, 128), tile)
        store_tall(place_ref, core_ref, down_step, dot_tn(a_all[:, cols], g_all[...]), downs)

    up_step = down_step - down_steps
    up_steps = ff // width

    @pl.when((up_step >= 0) & (up_step < up_steps))
    def _():
        cols = pl.ds(pl.multiple_of(up_step * width, 128), width)
        store_columns(place_ref, core_ref, dot_tn(hidden_all[...], right_all[:, cols]), ups)

    @pl.when(up_step == up_steps)
    def _():
        store_columns(place_ref, core_ref, dot_tn(o_all[...], right_all[:, ff:]), ups)


def middle(place, core, x, o, g, da, wp, bp, gain2, bias2, wu, bu, wd, bd):
    count, width = x.shape
    ff = wu.shape[1]
    batch = 2 * place.shape[0]
    row_steps, up_steps = count // ROWS, ff // width + 1
    rows = ff // batch
    tall_aligned = aligned(ff, batch) and (4 * rows) % 128 == 0 and batch >= 8
    down_steps = batch // 4 if tall_aligned else ff // width

    def row(columns):
        return pl.BlockSpec((ROWS, columns), lambda i, p, c: (jnp.minimum(i, row_steps - 1), 0))

    def down_at(i):
        return jnp.clip(i - row_steps, 0, down_steps - 1)

    def up_at(i):
        return jnp.clip(i - row_steps - down_steps, 0, up_steps - 1)

    if tall_aligned:
        deep = batch // 4
        down_shape = [jax.ShapeDtypeStruct((2, deep, rows, width), low)] * 2
        down_specs = [
            pl.BlockSpec(
                (2, 1, rows, width), lambda i, p, c: (0, p[2 * down_at(i)] % deep, 0, 0)
            )
        ] * 2
    else:
        down_shape = [jax.ShapeDtypeStruct((ff, width), low)]
        down_specs = [pl.BlockSpec((ff // down_steps, width), lambda i, p, c: (down_at(i), 0))]
    if aligned(width, batch):
        shape = (batch // 2, width // batch)
        up_shape = [jax.ShapeDtypeStruct(shape + (ff + width,), low)] * 2
        up_specs = [pl.BlockSpec(shape + (width,), lambda i, p, c: (0, 0, up_at(i)))] * 2
    else:
        up_shape = [jax.ShapeDtypeStruct((width, ff + width), low)]
        up_specs = [pl.BlockSpec((width, width), lambda i, p, c: (0, up_at(i)))]
    sums = 4 * width + ff
    result = ordered_call(
        partial(middle_kernel, row_steps, down_steps, len(down_shape)),
        [],
        (row_steps + down_steps + up_steps,),
        [row(width)] * 3
        + [row(da.shape[1])]
        + [whole_spec(a.shape) for a in (wp, bp, gain2, bias2, wu, bu, wd, bd)],
        (x, o, g, da, wp, bp, gain2, bias2, wu, bu, wd, bd),
        (place, core),
        out_specs=[row(width)] * 3
        + [whole_spec((1, sums))]
        + down_specs
        + up_specs,
        out_shape=[
            jax.ShapeDtypeStruct((count, width), low),
            jax.ShapeDtypeStruct((count, width), wide),
            jax.ShapeDtypeStruct((count, width), low),
        ]
        + [jax.ShapeDtypeStruct((1, sums), wide)]
        + down_shape
        + up_shape,
        scratch_shapes=[
            pltpu.VMEM((count, ff), low),
            pltpu.VMEM((count, ff + width), low),
            pltpu.VMEM((count, width), low),
            pltpu.VMEM((count, width), low),
            pltpu.VMEM((count, width), low),
        ],
        name="middle",
    )
    rest = result[4:]
    if tall_aligned:
        downw = [r.reshape(batch // 2, rows, width) for r in rest[:2]]
    else:
        downw = split_shards(rest[0], place, core[0])
    ups = rest[len(down_shape) :]
    upw = ups if len(ups) == 2 else split_shards(ups[0], place, core[0])
    return result[:4], downw, upw


def attend_back_kernel(size_ref, q_ref, kn_ref, vn_ref, kf_ref, vf_ref, do_ref, o_ref,
                       lse_ref, cos_ref, sa_ref, sb_ref,
                       own_ref, clean_ref, sums_ref, dkf_acc, dvf_acc):
    length = q_ref.shape[0]
    near, far = block_masks(size_ref)
    kf_t = kf_ref[...].astype(wide).T.astype(low)
    kn_t = kn_ref[...].astype(wide).T.astype(low)
    product = do_ref[...].astype(wide) * o_ref[...].astype(wide)
    high = product.astype(low)
    rest = (product - high.astype(wide)).astype(low)
    head_row = lax.broadcasted_iota(jnp.int32, (8, PAIR), 0)
    head_lane = lax.broadcasted_iota(jnp.int32, (8, PAIR), 1) // HEAD
    picker = jnp.where(head_row == head_lane, 1.0, 0.0).astype(low)
    deltas = dot_nt(picker, high) + dot_nt(picker, rest)
    cosine, sa, sb = cos_ref[...], sa_ref[...], sb_ref[...]
    sum_q = jnp.zeros((1, PAIR), wide)
    sum_kn = jnp.zeros((1, PAIR), wide)
    sum_vn = jnp.zeros((1, PAIR), wide)
    tiles = []
    for tile in range(length // SPAN):
        past = tile * SPAN
        here = slice(past, past + SPAN)
        query, grad = both_heads(q_ref[here, :]), both_heads(do_ref[here, :])
        scores = dot_nt(kf_ref[: past + SPAN, :], query)
        dprob = dot_nt(vf_ref[: past + SPAN, :], grad)
        diag = jnp.where(
            near,
            dot_nt(kn_ref[here, :], query),
            jnp.where(far, scores[past:], masked_value),
        )
        dprob_diag = jnp.where(near, dot_nt(vn_ref[here, :], grad), dprob[past:])
        tiles.append((past, here, query, grad, scores[:past], dprob[:past], diag, dprob_diag))
    results = []
    for past, here, query, grad, scores, dprob, diag, dprob_diag in tiles:
        lse = jnp.concatenate([lse_ref[0, 0:1, here], lse_ref[0, 1:2, here]], axis=1)
        delta = jnp.concatenate([deltas[0:1, here], deltas[1:2, here]], axis=1)
        prob_diag = jnp.exp2(diag - lse)
        ds_diag = prob_diag * (dprob_diag - delta)
        prob_near = jnp.where(near, prob_diag, 0.0).astype(low)
        ds_near = jnp.where(near, ds_diag, 0.0).astype(low)
        prob = jnp.where(near, 0.0, prob_diag).astype(low)
        dscore = jnp.where(near, 0.0, ds_diag).astype(low)
        if past:
            prob_past = jnp.exp2(scores - lse)
            ds_past = prob_past * (dprob - delta)
            prob = jnp.concatenate([prob_past.astype(low), prob], axis=0)
            dscore = jnp.concatenate([ds_past.astype(low), dscore], axis=0)
        results.append((past, here, query, grad, prob_near, ds_near, prob, dscore))
    for past, here, query, grad, prob_near, ds_near, prob, dscore in results:
        dkf, dvf = dot_nn(dscore, query), dot_nn(prob, grad)
        if past:
            dkf_acc[:past, :] += dkf[:past]
            dvf_acc[:past, :] += dvf[:past]
        dkf_acc[here, :] = dkf[past:]
        dvf_acc[here, :] = dvf[past:]
        dkn, dvn = dot_nn(ds_near, query), dot_nn(prob_near, grad)
        dqt = dot_nn(kn_t[:, here], ds_near) + dot_nn(kf_t[:, : past + SPAN], dscore)
        dq = own_blocks(dqt) * (1.0 / math.sqrt(HEAD))
        dq = rotate_back(dq, cosine[here], sa[here], sb[here])
        own_ref[0, here, :] = dq.astype(low)
        sum_q = sum_q + jnp.sum(dq, axis=0, keepdims=True)
        dkn = rotate_back(dkn * ln2, cosine[here], sa[here], sb[here])
        own_ref[1, here, :] = dkn.astype(low)
        sum_kn = sum_kn + jnp.sum(dkn, axis=0, keepdims=True)
        own_ref[2, here, :] = dvn.astype(low)
        sum_vn = sum_vn + jnp.sum(dvn, axis=0, keepdims=True)
    dkf = rotate_back(dkf_acc[...] * ln2, cosine, sa, sb)
    dvf = dvf_acc[...]
    clean_ref[0] = dkf.astype(low)
    clean_ref[1] = dvf.astype(low)
    sums_ref[0, 0:1, :] = sum_q
    sums_ref[0, 1:2, :] = sum_kn + jnp.sum(dkf, axis=0, keepdims=True)
    sums_ref[0, 2:3, :] = sum_vn + jnp.sum(dvf, axis=0, keepdims=True)


def attend_back(size, q, kn, vn, kf, vf, do, o, lse, tables, first, pairs, after, work):
    count = q.shape[0]
    pair_spec = pl.BlockSpec((count, PAIR), lambda p: (0, p + first))
    width = pairs * PAIR
    return ordered_call(
        attend_back_kernel,
        after,
        (pairs,),
        [pl.BlockSpec(memory_space=pltpu.SMEM)]
        + [pair_spec] * 7
        + [pl.BlockSpec((1, 2, count), lambda p: (p + first, 0, 0))]
        + [whole_spec(t.shape) for t in tables],
        (size, q, kn, vn, kf, vf, do, o, lse, *tables),
        out_specs=[
            pl.BlockSpec((3, count, PAIR), lambda p: (0, 0, p)),
            pl.BlockSpec((2, count, PAIR), lambda p: (0, 0, p)),
            pl.BlockSpec((1, 3, PAIR), lambda p: (p, 0, 0)),
        ],
        out_shape=[
            jax.ShapeDtypeStruct((3, count, width), low),
            jax.ShapeDtypeStruct((2, count, width), low),
            jax.ShapeDtypeStruct((pairs, 3, PAIR), wide),
        ],
        scratch_shapes=[
            pltpu.VMEM((count, PAIR), wide),
            pltpu.VMEM((count, PAIR), wide),
        ],
        work=work,
        name="attend_back",
    )


def spread_lanes(columns, batch):
    rows = columns.shape[0] // batch
    lane = lax.broadcasted_iota(jnp.int32, (rows, PAIR), 1)
    shards = []
    for shard in range(batch):
        block = columns[shard * rows : (shard + 1) * rows]
        for first, share in ((4, 4), (8, 3)):
            for j in range(share):
                chunk = share * shard + j
                at, start = first + chunk // batch, chunk % batch * rows
                block = jnp.where(
                    lane == first + j, columns[start : start + rows, at : at + 1], block
                )
        shards.append(block)
    return jnp.concatenate(shards, axis=0)


def qkv_kernel(cuts, batch, place_ref, core_ref, h_ref, hf_ref, w_ref, gain1_ref, bias1_ref,
               early_ref, *rest):
    own, clean, sums, rest = (
        rest[:cuts],
        rest[cuts : 2 * cuts],
        rest[2 * cuts : 3 * cuts],
        rest[3 * cuts :],
    )
    outs, (rows_ref, columns_ref, result_ref) = rest[:-3], rest[-3:]
    step = pl.program_id(0)
    width = h_ref.shape[1]
    result_ref[...] = dot_tn(h_ref[...], jnp.concatenate([r[0] for r in own], axis=1))

    @pl.when(step == 0)
    def _():
        columns_ref[...] = jnp.zeros_like(columns_ref)
        rows_ref[...] = jnp.zeros_like(rows_ref)
        for i in range(8):
            rows_ref[i : i + 1, :] = early_ref[:, i * width : (i + 1) * width]
        rows_ref[13:14, :] = row_of(gain1_ref)
        rows_ref[14:15, :] = row_of(bias1_ref)

    @pl.when(step > 0)
    def _():
        result_ref[...] += dot_tn(hf_ref[...], jnp.concatenate([r[0] for r in clean], axis=1))

    result = result_ref[...]
    cols = pl.ds(pl.multiple_of(step * width, 128), width)
    store_columns(place_ref, core_ref, result, outs, cols)
    weight = w_ref[...].astype(wide)
    totals = jnp.concatenate(
        [r[p, pl.ds(step, 1), :] for r in sums for p in range(r.shape[0])], axis=1
    )
    rows_ref[pl.ds(8 + step, 1), :] = totals
    lane = lax.broadcasted_iota(jnp.int32, (1, PAIR), 1)
    columns_ref[...] += jnp.where(
        lane == 0,
        jnp.sum(weight * result, axis=1, keepdims=True),
        jnp.sum(weight * totals, axis=1, keepdims=True),
    )

    @pl.when(step == 2)
    def _():
        columns = rows_ref[...].T
        bias = columns_ref[:, 1:2]
        gain = (columns_ref[:, 0:1] - columns[:, 14:15] * bias) / columns[:, 13:14]
        columns = jnp.where(lane == 11, gain, jnp.where(lane == 12, bias, columns))
        if len(outs) == 2:
            columns = spread_lanes(columns, batch)
        store_columns(place_ref, core_ref, columns, outs, slice(3 * width, 3 * width + PAIR))


def outer_qkv(h, hf, weight, gain1, bias1, early, own, clean, sums, place, core, after):
    count, width = h.shape
    batch = 2 * place.shape[0]
    columns = 3 * width + PAIR
    if aligned(width, batch):
        out_shape = [jax.ShapeDtypeStruct((batch // 2, width // batch, columns), low)] * 2
    else:
        out_shape = [jax.ShapeDtypeStruct((width, columns), low)]
    result = ordered_call(
        partial(qkv_kernel, len(own), batch),
        after,
        (3,),
        [whole_spec(h.shape)] * 2
        + [pl.BlockSpec((width, width), lambda i, p, c: (0, i))]
        + [whole_spec(v.shape) for v in (gain1, bias1, early)]
        + [pl.BlockSpec((1, count, r.shape[2]), lambda i, p, c: (i, 0, 0)) for r in own]
        + [
            pl.BlockSpec((1, count, r.shape[2]), lambda i, p, c: (jnp.maximum(i - 1, 0), 0, 0))
            for r in clean
        ]
        + [whole_spec(r.shape) for r in sums],
        (h, hf, weight, gain1, bias1, early, *own, *clean, *sums),
        (place, core),
        out_specs=[whole_spec(o.shape) for o in out_shape],
        out_shape=out_shape,
        scratch_shapes=[
            pltpu.VMEM((PAIR, width), wide),
            pltpu.VMEM((width, PAIR), wide),
            pltpu.VMEM((width, width), wide),
        ],
        work=1e8,
        name="outer_qkv",
    )
    if len(result) == 2:
        return result
    (full,) = result
    rows = width // batch
    start = 3 * width
    spread = [full[:, : start + 4]]
    for first, share in ((4, 4), (8, 3)):
        part = full[:, start + first : start + first + share].T.reshape(batch, share, rows)
        spread.append(part.transpose(0, 2, 1).reshape(width, share))
    spread.append(full[:, start + 11 :])
    return split_shards(jnp.concatenate(spread, axis=1), place, core[0])


def project_far_back_kernel(cuts, noisy_ref, x_ref, *rest):
    far, clean = rest[:HALVES], rest[HALVES : HALVES + cuts]
    wk_ref, wv_ref, gain1_ref, dfar_ref = rest[HALVES + cuts :]
    steps = pl.num_programs(0) // HALVES
    source = x_ref[...].astype(wide)
    for i, ref in enumerate(far):
        chosen = (noisy_ref[0] == 1) & (pl.program_id(0) // steps == i)
        source = jnp.where(chosen, ref[...].astype(wide), source)
    normed, factor = normalize(source)
    dh = jnp.zeros_like(source)
    for part, w_ref in enumerate((wk_ref, wv_ref)):
        grads = jnp.concatenate([c[part] for c in clean], axis=1)
        dh = dh + dot_nt(grads, w_ref[...])
    dfar_ref[...] = norm_back(dh * row_of(gain1_ref), normed, factor).astype(low)


def project_far_back(noisy, x, far, clean, weight, gain1, after):
    count, width = x.shape
    return ordered_call(
        partial(project_far_back_kernel, len(clean)),
        after,
        (count // ROWS,),
        [pl.BlockSpec(memory_space=pltpu.SMEM)]
        + [row_spec(width)]
        + [
            pl.BlockSpec(
                (ROWS, width),
                lambda i, first=n * f.shape[0] // ROWS, last=f.shape[0] // ROWS - 1: (
                    jnp.clip(i - first, 0, last),
                    0,
                ),
            )
            for n, f in enumerate(far)
        ]
        + [pl.BlockSpec((2, ROWS, c.shape[2]), lambda i: (0, i, 0)) for c in clean]
        + [
            pl.BlockSpec((width, width), lambda i, part=part: (0, part), pipeline_mode=pl.Buffered(1))
            for part in (1, 2)
        ]
        + [whole_spec(gain1.shape)],
        (noisy, x, *far, *clean, weight, weight, gain1),
        out_specs=row_spec(width),
        out_shape=jax.ShapeDtypeStruct((count, width), low),
        work=1e8,
        name="project_far_back",
    )


def project_back_kernel(cuts, noisy_ref, x_ref, dy_ref, dfar_ref, *rest):
    own = rest[:cuts]
    w_ref, gain1_ref, dx_ref = rest[cuts:]
    width = x_ref.shape[1]
    normed, factor = normalize(x_ref[...].astype(wide))
    dh = jnp.zeros_like(dy_ref)
    for part in range(3):
        grads = jnp.concatenate([c[part] for c in own], axis=1)
        dh = dh + dot_nt(grads, w_ref[:, part * width : (part + 1) * width])
    dx = dy_ref[...] + norm_back(dh * row_of(gain1_ref), normed, factor)
    dx_ref[...] = dx + jnp.where(noisy_ref[0] == 0, dfar_ref[...].astype(wide), 0.0)


def project_back(noisy, x, dy, dfar, own, weight, gain1, after):
    count, width = x.shape
    return ordered_call(
        partial(project_back_kernel, len(own)),
        after,
        (count // ROWS,),
        [pl.BlockSpec(memory_space=pltpu.SMEM)]
        + [row_spec(width)] * 3
        + [pl.BlockSpec((3, ROWS, c.shape[2]), lambda i: (0, i, 0)) for c in own]
        + [whole_spec(weight.shape), whole_spec(gain1.shape)],
        (noisy, x, dy, dfar, *own, weight, gain1),
        out_specs=row_spec(width),
        out_shape=jax.ShapeDtypeStruct((count, width), wide),
        work=1.5e10,
        name="project_back",
    )


def flip(values, mask):
    batch = lax.axis_size("batch")
    return lax.ppermute(values, "batch", [(i, i ^ mask) for i in range(batch)])


def flip_stream(values):
    return lax.ppermute(values, "stream", [(0, 1), (1, 0)])


def total(terms):
    result = terms[0].astype(wide)
    for term in terms[1:]:
        result = result + term.astype(wide)
    return result


class Reduction:
    def __init__(self, name, shards):
        keep, send = shards
        self.name = name
        self.terms = [keep, flip(send, 1)]
        self.stages = stages_of(2 * keep.shape[0])
        self.size = keep.shape[0]

    def wait_for(self, others):
        self.terms, _ = lax.optimization_barrier((self.terms, list(others)))

    def step(self):
        bits = self.stages.pop(0)
        parts = 2 ** len(bits)
        size = self.size // parts
        pieces = [
            total([t[j * size : (j + 1) * size] for t in self.terms]).astype(low)
            for j in range(1, parts)
        ]
        arrived = [flip(p, mask_of(bits, j + 1)) for j, p in enumerate(pieces)]
        self.terms = self.terms + arrived
        self.arrived = arrived
        self.size = size
        return pieces

    def last(self):
        while self.stages:
            self.step()
        self.mine = total([t[:1] for t in self.terms]).astype(low)
        self.other = flip_stream(self.mine)
        return [self.mine]

    def result(self, first, count):
        at = slice(first, first + count)
        return self.mine[0][:, at].astype(wide) + self.other[0][:, at].astype(wide)


def local(
    layer_input,
    out_cotangent,
    block_size,
    norm1_gain,
    norm1_bias,
    qkv_weight,
    qkv_bias,
    proj_weight,
    proj_bias,
    norm2_gain,
    norm2_bias,
    up_weight,
    up_bias,
    down_weight,
    down_bias,
):
    length, width = layer_input.shape[2:]
    batch = lax.axis_size("batch")
    noisy = lax.axis_index("stream").astype(jnp.int32).reshape(1)
    x = layer_input.reshape(length, width)
    g = out_cotangent.reshape(length, width)
    half = length // HALVES
    far_x, source = [], x
    for i in range(HALVES):
        piece = source[i * half : (i + 1) * half]
        far_x.append(lax.ppermute(piece, "stream", [(0, 1)]))
        source, _ = lax.optimization_barrier((source, piece))
    tables = rotary_tables(length)
    me = lax.axis_index("batch").astype(jnp.int32)
    place, core = places_of(batch, me), (me % 2).reshape(1)
    h, q, k, v = project(x, qkv_weight, qkv_bias, norm1_gain, norm1_bias, tables)
    da = early_part(g, down_weight, EARLY)
    fars, attended = [], []
    for i in range(HALVES):
        fars = project_far(
            noisy, x, far_x[i], qkv_weight, qkv_bias, norm1_gain, norm1_bias, tables, i, fars,
            [] if i else [da, h],
        )
        hf, kf, vf = fars
        attended = attend(block_size, q, k, v, kf, vf, i, HALVES, attended)
    o, lse = attended
    (out, dy, do, early), downw, upw = middle(
        place,
        core,
        x,
        o,
        g,
        da,
        proj_weight,
        proj_bias,
        norm2_gain,
        norm2_bias,
        up_weight,
        up_bias,
        down_weight,
        down_bias,
    )
    down, up = Reduction("down", downw), Reduction("up", upw)
    backs, after = [], []
    for i, (first, pairs) in enumerate(CUTS):
        if i == 1:
            down.wait_for(backs[0])
            after = down.step()
        after = after + [b[0] for b in backs[-1:]]
        backs.append(
            attend_back(
                block_size, q, k, v, kf, vf, do, o, lse, tables, first, pairs, after, 2e10
            )
        )
    own, clean, sums = ([b[i] for b in backs] for i in range(3))
    up.wait_for(backs[-1])
    down.wait_for(backs[-1])
    after = up.step() + down.step()
    dfar = project_far_back(noisy, x, far_x, clean, qkv_weight, norm1_gain, after)
    qkvw = outer_qkv(
        h,
        hf,
        qkv_weight,
        norm1_gain,
        norm1_bias,
        early,
        own,
        clean,
        sums,
        place,
        core,
        [dfar],
    )
    qkvw, _ = lax.optimization_barrier((list(qkvw), up.arrived + down.arrived))
    qkv = Reduction("qkv", qkvw)
    after = up.step()
    leaving, _ = lax.optimization_barrier((dfar, after))
    back_x = lax.ppermute(leaving, "stream", [(1, 0)])
    qkv.wait_for(after)
    after = qkv.step()
    dx = project_back(noisy, x, dy, dfar, own, qkv_weight, norm1_gain, after)
    down.wait_for([dx])
    qkv.wait_for(down.last())
    after = qkv.step()
    up.wait_for(after)
    up.last()
    arriving, down.other, _ = lax.optimization_barrier((back_x, down.other, up.mine))
    input_grad = (dx + arriving.astype(wide)).reshape(layer_input.shape)
    downw_grad = down.result(0, width)
    qkv.wait_for([input_grad, downw_grad])
    qkv.last()
    ff = up_weight.shape[1]
    upw_grad, projw_grad = up.result(0, ff), up.result(ff, width)
    qkvw_grad = qkv.result(0, 3 * width)
    vectors = qkv.result(3 * width, PAIR).T
    downb_grad, gain2_grad, bias2_grad, projb_grad = (vectors[i] for i in range(4))
    upb_grad, qkvb_grad = vectors[4:8].reshape(-1), vectors[8:11].reshape(-1)
    gain1_grad, bias1_grad = vectors[11], vectors[12]
    return (
        out.reshape(layer_input.shape),
        input_grad,
        gain1_grad,
        bias1_grad,
        qkvw_grad,
        qkvb_grad,
        projw_grad,
        projb_grad,
        gain2_grad,
        bias2_grad,
        upw_grad,
        upb_grad,
        downw_grad,
        downb_grad,
    )


def solution(mesh):
    rows = P("stream", "batch", None, None)
    return jax.shard_map(
        local,
        mesh=mesh,
        in_specs=(rows, rows, P("batch")) + (P(),) * 12,
        out_specs=(
            rows,
            rows,
            P("batch"),
            P("batch"),
            P("batch", None),
            P("batch"),
            P("batch", None),
            P("batch"),
            P("batch"),
            P("batch"),
            P("batch", None),
            P("batch"),
            P("batch", None),
            P("batch"),
        ),
        check_vma=False,
    )
```

```python
from functools import partial
import math

import jax
import jax.numpy as jnp
from jax import lax
from jax.experimental import pallas as pl
from jax.experimental.pallas import tpu as pltpu
from jax.sharding import PartitionSpec as P
import numpy as np

HEAD = 64
PAIR = 2 * HEAD
ROWS = 256
SPAN = 128
HALVES = 2
WIDE = 2
EARLY = 3
CUTS = ((0, 1), (1, 5))
full_vmem = 60

masked_value = -1e30
epsilon = 1e-05
low = jnp.bfloat16
wide = jnp.float32
score_scale = math.log2(math.e) / math.sqrt(HEAD)
ln2 = math.log(2.0)
gelu_c = math.sqrt(2.0 / math.pi)
gelu_k = 0.044715
mega = 1024 * 1024


def dot_nn(left, right):
    return lax.dot_general(left, right, (((1,), (0,)), ((), ())), preferred_element_type=wide)


def dot_nt(left, right):
    return lax.dot_general(left, right, (((1,), (1,)), ((), ())), preferred_element_type=wide)


def dot_tn(left, right):
    return lax.dot_general(left, right, (((0,), (0,)), ((), ())), preferred_element_type=wide)


def params(limit_mib):
    return pltpu.CompilerParams(
        dimension_semantics=("arbitrary",), vmem_limit_bytes=limit_mib * mega
    )


def cost(flops, nbytes, trans=0):
    return pl.CostEstimate(
        flops=int(flops), bytes_accessed=int(nbytes), transcendentals=int(trans)
    )


def ordered_call(
    kernel, after, grid, in_specs, operands, prefetch=(), work=4e9, into=(), **rest
):
    skip = len(prefetch) + len(operands)
    after = list(into) + list(after)

    def body(*refs):
        kernel(*refs[:skip], *refs[skip + len(after) :])

    out_specs = rest.pop("out_specs")
    scratch = rest.pop("scratch_shapes", [])
    call = pl.pallas_call(
        body,
        grid_spec=pltpu.PrefetchScalarGridSpec(
            num_scalar_prefetch=len(prefetch),
            grid=grid,
            in_specs=list(in_specs) + [pl.BlockSpec(memory_space=pl.ANY)] * len(after),
            out_specs=out_specs,
            scratch_shapes=scratch,
        ),
        compiler_params=pltpu.CompilerParams(
            dimension_semantics=("arbitrary",) * len(grid), vmem_limit_bytes=full_vmem * mega
        ),
        cost_estimate=cost(work, 1000),
        input_output_aliases={skip + i: i for i in range(len(into))},
        **rest,
    )
    return call(*prefetch, *operands, *after)


def row_of(ref, at=slice(None)):
    return ref[at].reshape(1, -1)


def whole_spec(shape):
    zeros = (0,) * len(shape)
    return pl.BlockSpec(shape, lambda *_: zeros, pipeline_mode=pl.Buffered(1))


def row_spec(width, rows=ROWS):
    return pl.BlockSpec((rows, width), lambda i: (i, 0))


def normalize(values):
    mean = jnp.mean(values, axis=-1, keepdims=True)
    centred = values - mean
    factor = lax.rsqrt(jnp.mean(centred * centred, axis=-1, keepdims=True) + epsilon)
    return (centred * factor, factor)


def norm_back(grad_normed, normed, factor):
    first = jnp.mean(grad_normed, axis=-1, keepdims=True)
    second = jnp.mean(grad_normed * normed, axis=-1, keepdims=True)
    return factor * (grad_normed - first - normed * second)


def rotary_tables(length):
    places = np.arange(length, dtype=np.float64)[:, None]
    column = np.arange(PAIR) % HEAD
    angle = places * (10000.0 ** (-2.0 * (column % (HEAD // 2)) / HEAD))[None, :]
    upper = (column >= HEAD // 2)[None, :]
    cosine, sine = np.cos(angle), np.sin(angle)
    tables = (cosine, np.where(upper, sine, 0.0), np.where(upper, 0.0, -sine))
    return tuple(jnp.asarray(t, dtype=wide) for t in tables)


def rotate(values, cosine, sine_a, sine_b):
    return (
        values * cosine
        + pltpu.roll(values, HEAD // 2, 1) * sine_a
        + pltpu.roll(values, PAIR - HEAD // 2, 1) * sine_b
    )


def rotate_back(values, cosine, sine_a, sine_b):
    return (
        values * cosine
        - pltpu.roll(values, HEAD // 2, 1) * sine_a
        - pltpu.roll(values, PAIR - HEAD // 2, 1) * sine_b
    )


def project_kernel(x_ref, w_ref, bias_ref, gain1_ref, bias1_ref, cos_ref, sa_ref, sb_ref,
                   h_ref, q_ref, k_ref, v_ref):
    width = x_ref.shape[1]
    normed, _ = normalize(x_ref[...].astype(wide))
    hidden = (normed * row_of(gain1_ref) + row_of(bias1_ref)).astype(low)
    h_ref[...] = hidden
    cosine, sa, sb = cos_ref[...], sa_ref[...], sb_ref[...]
    for out, part in ((q_ref, 0), (k_ref, 1), (v_ref, 2)):
        cols = slice(part * width, (part + 1) * width)
        mixed = dot_nn(hidden, w_ref[:, cols]) + row_of(bias_ref, cols)
        if part == 2:
            out[...] = mixed.astype(low)
            continue
        for group in range(width // PAIR):
            at = slice(group * PAIR, (group + 1) * PAIR)
            turned = rotate(mixed[:, at], cosine, sa, sb)
            if part == 0:
                turned = turned * score_scale
            out[:, at] = turned.astype(low)


def project_far_kernel(noisy_ref, x_ref, far_ref, wk_ref, wv_ref, bias_ref, gain1_ref, bias1_ref,
                       cos_ref, sa_ref, sb_ref, h_ref, k_ref, v_ref):
    width = x_ref.shape[1]
    source = jnp.where(noisy_ref[0] == 1, far_ref[...].astype(wide), x_ref[...].astype(wide))
    normed, _ = normalize(source)
    hidden = (normed * row_of(gain1_ref) + row_of(bias1_ref)).astype(low)
    h_ref[...] = hidden
    cosine, sa, sb = cos_ref[...], sa_ref[...], sb_ref[...]
    mixed = dot_nn(hidden, wk_ref[...]) + row_of(bias_ref, slice(width, 2 * width))
    for group in range(width // PAIR):
        at = slice(group * PAIR, (group + 1) * PAIR)
        k_ref[:, at] = rotate(mixed[:, at], cosine, sa, sb).astype(low)
    mixed = dot_nn(hidden, wv_ref[...]) + row_of(bias_ref, slice(2 * width, None))
    v_ref[...] = mixed.astype(low)


def project(x, weight, bias, gain1, bias1, tables):
    count, width = x.shape
    row = jax.ShapeDtypeStruct((count, width), low)
    return pl.pallas_call(
        project_kernel,
        grid=(count // ROWS,),
        in_specs=[
            row_spec(width),
            whole_spec(weight.shape),
            whole_spec(bias.shape),
            whole_spec(gain1.shape),
            whole_spec(bias1.shape),
            row_spec(PAIR),
            row_spec(PAIR),
            row_spec(PAIR),
        ],
        out_specs=[row_spec(width)] * 4,
        out_shape=[row] * 4,
        compiler_params=params(full_vmem),
        cost_estimate=cost(2 * count * width * 3 * width, 16e6),
        name="project",
    )(x, weight, bias, gain1, bias1, *tables)


def project_far(noisy, x, far, weight, bias, gain1, bias1, tables, part, into, after):
    count, width = x.shape
    steps = far.shape[0] // ROWS
    row = jax.ShapeDtypeStruct((count, width), low)

    def part_rows(columns):
        return pl.BlockSpec((ROWS, columns), lambda i: (part * steps + i, 0))

    return ordered_call(
        project_far_kernel,
        after,
        (steps,),
        [
            pl.BlockSpec(memory_space=pltpu.SMEM),
            part_rows(width),
            row_spec(width),
            pl.BlockSpec((width, width), lambda i: (0, 1), pipeline_mode=pl.Buffered(1)),
            pl.BlockSpec((width, width), lambda i: (0, 2), pipeline_mode=pl.Buffered(1)),
            whole_spec(bias.shape),
            whole_spec(gain1.shape),
            whole_spec(bias1.shape),
            part_rows(PAIR),
            part_rows(PAIR),
            part_rows(PAIR),
        ],
        (noisy, x, far, weight, weight, bias, gain1, bias1, *tables),
        into=into,
        out_specs=[part_rows(width)] * 3,
        out_shape=[row] * 3,
        name="project_far",
    )


def early_kernel(g_ref, w_ref, out_ref):
    out_ref[...] = dot_nt(g_ref[...], w_ref[...]).astype(low)


def early_part(g, weight, chunks):
    count, width = g.shape
    return ordered_call(
        early_kernel,
        [],
        (chunks,),
        [whole_spec(g.shape), pl.BlockSpec((width, width), lambda i: (i, 0))],
        (g, weight),
        out_specs=pl.BlockSpec((count, width), lambda i: (0, i)),
        out_shape=jax.ShapeDtypeStruct((count, chunks * width), low),
        name="early_part",
    )


def block_masks(size_ref):
    key = lax.broadcasted_iota(jnp.int32, (SPAN, 2 * SPAN), 0)
    query = lax.broadcasted_iota(jnp.int32, (SPAN, 2 * SPAN), 1) % SPAN
    near = (key ^ query) < size_ref[0]
    return near, key < query


def both_heads(rows):
    lane = lax.broadcasted_iota(jnp.int32, (1, PAIR), 1)
    none = jnp.zeros_like(rows)
    return jnp.concatenate(
        [jnp.where(lane < HEAD, rows, none), jnp.where(lane >= HEAD, rows, none)], axis=0
    )


def own_blocks(mixed):
    return jnp.concatenate([mixed[:HEAD, :SPAN], mixed[HEAD:, SPAN:]], axis=0).T


def attend_kernel(first, size_ref, q_ref, kn_ref, vn_ref, kf_ref, vf_ref, o_ref, lse_ref):
    near, far = block_masks(size_ref)
    state = []
    for pair in range(WIDE):
        cols = slice(pair * PAIR, (pair + 1) * PAIR)
        vf_t = vf_ref[:, cols].astype(wide).T.astype(low)
        vn_t = vn_ref[:, cols].astype(wide).T.astype(low)
        for part in range(q_ref.shape[0] // SPAN):
            past = (first + part) * SPAN
            own = slice(part * SPAN, (part + 1) * SPAN)
            query = both_heads(q_ref[own, cols])
            scores = dot_nt(kf_ref[: past + SPAN, cols], query)
            diag = jnp.where(
                near,
                dot_nt(kn_ref[own, cols], query),
                jnp.where(far, scores[past:], masked_value),
            )
            state.append((pair, cols, vf_t, vn_t, past, own, scores, diag))
    probs = []
    for pair, cols, vf_t, vn_t, past, own, scores, diag in state:
        top = jnp.max(diag, axis=0, keepdims=True)
        if past:
            top = jnp.maximum(top, jnp.max(scores[:past], axis=0, keepdims=True))
        prob = jnp.exp2(diag - top)
        total = jnp.sum(prob, axis=0, keepdims=True)
        prob_near = jnp.where(near, prob, 0.0).astype(low)
        prob_far = jnp.where(near, 0.0, prob).astype(low)
        if past:
            prob = jnp.exp2(scores[:past] - top)
            total = total + jnp.sum(prob, axis=0, keepdims=True)
            prob_far = jnp.concatenate([prob.astype(low), prob_far], axis=0)
        lse = top + jnp.log2(total)
        lse_ref[pair, 0:1, own] = lse[:, :SPAN]
        lse_ref[pair, 1:2, own] = lse[:, SPAN:]
        probs.append((cols, vf_t, vn_t, past, own, prob_near, prob_far, 1.0 / total))
    for cols, vf_t, vn_t, past, own, prob_near, prob_far, scale in probs:
        mixed = dot_nn(vn_t[:, own], prob_near) + dot_nn(vf_t[:, : past + SPAN], prob_far)
        o_ref[own, cols] = own_blocks(mixed * scale).astype(low)


def attend(size, q, kn, vn, kf, vf, part, parts, into):
    count, width = q.shape
    pairs = width // PAIR
    rows = count // parts
    own_spec = pl.BlockSpec((rows, WIDE * PAIR), lambda p: (part, p))
    far_spec = pl.BlockSpec(((part + 1) * rows, WIDE * PAIR), lambda p: (0, p))
    return ordered_call(
        partial(attend_kernel, part * rows // SPAN),
        [],
        (pairs // WIDE,),
        [pl.BlockSpec(memory_space=pltpu.SMEM)] + [own_spec] * 3 + [far_spec] * 2,
        (size, q, kn, vn, kf, vf),
        into=into,
        out_specs=[own_spec, pl.BlockSpec((WIDE, 2, rows), lambda p: (p, 0, part))],
        out_shape=[
            jax.ShapeDtypeStruct((count, width), low),
            jax.ShapeDtypeStruct((pairs, 2, count), wide),
        ],
        name="attend",
    )


def stages_of(batch):
    bits = list(range(1, batch.bit_length() - 1))
    stages = [bits[:1]]
    rest = bits[1:]
    while rest:
        stages.append(rest[:2])
        rest = rest[2:]
    return [s for s in stages if s]


def mask_of(bits, digit):
    return sum(((digit >> i) & 1) << bit for i, bit in enumerate(bits))


def places_of(batch, me):
    relative = jnp.arange(0, batch, 2, dtype=jnp.int32) ^ (me - me % 2)
    place = jnp.zeros_like(relative)
    for bits in stages_of(batch):
        place = place * 2 ** len(bits)
        for i, bit in enumerate(bits):
            place = place + (((relative >> bit) & 1) << i)
    return place


def store_shards(place_ref, core_ref, result, keep_ref, send_ref, columns=slice(None)):
    shards = keep_ref.shape[0]
    rows = result.shape[0] // (2 * shards)

    def store(first_ref, second_ref):
        for pair in range(shards):
            at = place_ref[pair]
            start = 2 * pair * rows
            first_ref[at, :, columns] = result[start : start + rows].astype(low)
            second_ref[at, :, columns] = result[start + rows : start + 2 * rows].astype(low)

    pl.when(core_ref[0] == 0)(lambda: store(keep_ref, send_ref))
    pl.when(core_ref[0] == 1)(lambda: store(send_ref, keep_ref))


def split_shards(full, place, core):
    batch = 2 * place.shape[0]
    shards = full.reshape((batch // 2, 2, full.shape[0] // batch) + full.shape[1:])
    order = jnp.argsort(place)
    shards = jnp.take(shards, order, axis=0)
    return (
        jnp.where(core == 0, shards[:, 0], shards[:, 1]),
        jnp.where(core == 0, shards[:, 1], shards[:, 0]),
    )


def aligned(tall, batch):
    return tall % batch == 0 and (tall // batch) % 16 == 0


def store_columns(place_ref, core_ref, result, outs, columns=slice(None)):
    if len(outs) == 1:
        outs[0][:, columns] = result.astype(low)
    else:
        store_shards(place_ref, core_ref, result, *outs, columns)


def store_tall(place_ref, core_ref, step, result, outs):
    if len(outs) == 1:
        outs[0][...] = result.astype(low)
        return
    rows = outs[0].shape[2]
    places = place_ref.shape[0] // 2

    def store(first_ref, second_ref):
        for x in range(2):
            at = place_ref[2 * step + x] // places
            start = 2 * x * rows
            first_ref[at, 0] = result[start : start + rows].astype(low)
            second_ref[at, 0] = result[start + rows : start + 2 * rows].astype(low)

    pl.when(core_ref[0] == 0)(lambda: store(*outs))
    pl.when(core_ref[0] == 1)(lambda: store(*outs[::-1]))


def middle_kernel(row_steps, down_steps, tall_outs, place_ref, core_ref, x_ref, o_ref, g_ref, da_ref,
                  wp_ref, bp_ref, gain2_ref, bias2_ref, wu_ref, bu_ref, wd_ref, bd_ref,
                  out_ref, dy_ref, do_ref, sums_ref,
                  *rest):
    downs, ups = rest[:tall_outs], rest[tall_outs:-5]
    a_all, right_all, hidden_all, o_all, g_all = rest[-5:]
    width = x_ref.shape[1]
    ff = wu_ref.shape[1]
    step = pl.program_id(0)

    def add_sum(start, values):
        at = slice(start, start + values.shape[1])
        sums_ref[:, at] += jnp.sum(values, axis=0, keepdims=True)

    @pl.when(step == 0)
    def _():
        sums_ref[...] = jnp.zeros_like(sums_ref)

    @pl.when(step < row_steps)
    def _():
        rows = pl.ds(pl.multiple_of(step * ROWS, ROWS), ROWS)
        parts = [slice(i * width, (i + 1) * width) for i in range(ff // width)]
        grad = g_ref[...]
        y = x_ref[...].astype(wide) + dot_nn(o_ref[...], wp_ref[...]) + row_of(bp_ref)
        das = [da_ref[:, cols].astype(wide) for cols in parts[:EARLY]]
        das += [dot_nt(grad, wd_ref[cols, :]) for cols in parts[EARLY:]]
        normed, factor = normalize(y)
        hidden = (normed * row_of(gain2_ref) + row_of(bias2_ref)).astype(low)
        o_all[rows, :] = o_ref[...]
        hidden_all[rows, :] = hidden
        g_all[rows, :] = grad
        grad_wide = grad.astype(wide)
        ups = [dot_nn(hidden, wu_ref[:, cols]) + row_of(bu_ref, cols) for cols in parts]
        acts, dus = [], []
        for part, cols in enumerate(parts):
            up = ups[part]
            square = up * up
            half = 0.5 + 0.5 * jnp.tanh(up * (gelu_c + (gelu_c * gelu_k) * square))
            active = (up * half).astype(low)
            slope = half + (up * (2.0 * gelu_c + (6.0 * gelu_c * gelu_k) * square)) * (
                half * (1.0 - half)
            )
            du = das[part] * slope
            du_low = du.astype(low)
            a_all[rows, cols] = active
            right_all[rows, cols] = du_low
            add_sum(4 * width + part * width, du)
            acts.append(active)
            dus.append(du_low)
        result = y + row_of(bd_ref)
        dh2 = jnp.zeros_like(y)
        for part, cols in enumerate(parts):
            dh2 = dh2 + dot_nt(dus[part], wu_ref[:, cols])
            result = result + dot_nn(acts[part], wd_ref[cols, :])
        out_ref[...] = result.astype(low)
        add_sum(0, grad_wide)
        add_sum(width, dh2 * normed)
        add_sum(2 * width, dh2)
        dy = grad_wide + norm_back(dh2 * row_of(gain2_ref), normed, factor)
        dy_ref[...] = dy
        add_sum(3 * width, dy)
        dy_low = dy.astype(low)
        right_all[rows, ff:] = dy_low
        do_ref[...] = dot_nt(dy_low, wp_ref[...]).astype(low)

    down_step = step - row_steps
    tile = ff // down_steps

    @pl.when((down_step >= 0) & (down_step < down_steps))
    def _():
        cols = pl.ds(pl.multiple_of(down_step * tile, 128), tile)
        store_tall(place_ref, core_ref, down_step, dot_tn(a_all[:, cols], g_all[...]), downs)

    up_step = down_step - down_steps
    up_steps = ff // width

    @pl.when((up_step >= 0) & (up_step < up_steps))
    def _():
        cols = pl.ds(pl.multiple_of(up_step * width, 128), width)
        store_columns(place_ref, core_ref, dot_tn(hidden_all[...], right_all[:, cols]), ups)

    @pl.when(up_step == up_steps)
    def _():
        store_columns(place_ref, core_ref, dot_tn(o_all[...], right_all[:, ff:]), ups)


def middle(place, core, x, o, g, da, wp, bp, gain2, bias2, wu, bu, wd, bd):
    count, width = x.shape
    ff = wu.shape[1]
    batch = 2 * place.shape[0]
    row_steps, up_steps = count // ROWS, ff // width + 1
    rows = ff // batch
    tall_aligned = aligned(ff, batch) and (4 * rows) % 128 == 0 and batch >= 8
    down_steps = batch // 4 if tall_aligned else ff // width

    def row(columns):
        return pl.BlockSpec((ROWS, columns), lambda i, p, c: (jnp.minimum(i, row_steps - 1), 0))

    def down_at(i):
        return jnp.clip(i - row_steps, 0, down_steps - 1)

    def up_at(i):
        return jnp.clip(i - row_steps - down_steps, 0, up_steps - 1)

    if tall_aligned:
        deep = batch // 4
        down_shape = [jax.ShapeDtypeStruct((2, deep, rows, width), low)] * 2
        down_specs = [
            pl.BlockSpec(
                (2, 1, rows, width), lambda i, p, c: (0, p[2 * down_at(i)] % deep, 0, 0)
            )
        ] * 2
    else:
        down_shape = [jax.ShapeDtypeStruct((ff, width), low)]
        down_specs = [pl.BlockSpec((ff // down_steps, width), lambda i, p, c: (down_at(i), 0))]
    if aligned(width, batch):
        shape = (batch // 2, width // batch)
        up_shape = [jax.ShapeDtypeStruct(shape + (ff + width,), low)] * 2
        up_specs = [pl.BlockSpec(shape + (width,), lambda i, p, c: (0, 0, up_at(i)))] * 2
    else:
        up_shape = [jax.ShapeDtypeStruct((width, ff + width), low)]
        up_specs = [pl.BlockSpec((width, width), lambda i, p, c: (0, up_at(i)))]
    sums = 4 * width + ff
    result = ordered_call(
        partial(middle_kernel, row_steps, down_steps, len(down_shape)),
        [],
        (row_steps + down_steps + up_steps,),
        [row(width)] * 3
        + [row(da.shape[1])]
        + [whole_spec(a.shape) for a in (wp, bp, gain2, bias2, wu, bu, wd, bd)],
        (x, o, g, da, wp, bp, gain2, bias2, wu, bu, wd, bd),
        (place, core),
        out_specs=[row(width)] * 3
        + [whole_spec((1, sums))]
        + down_specs
        + up_specs,
        out_shape=[
            jax.ShapeDtypeStruct((count, width), low),
            jax.ShapeDtypeStruct((count, width), wide),
            jax.ShapeDtypeStruct((count, width), low),
        ]
        + [jax.ShapeDtypeStruct((1, sums), wide)]
        + down_shape
        + up_shape,
        scratch_shapes=[
            pltpu.VMEM((count, ff), low),
            pltpu.VMEM((count, ff + width), low),
            pltpu.VMEM((count, width), low),
            pltpu.VMEM((count, width), low),
            pltpu.VMEM((count, width), low),
        ],
        name="middle",
    )
    rest = result[4:]
    if tall_aligned:
        downw = [r.reshape(batch // 2, rows, width) for r in rest[:2]]
    else:
        downw = split_shards(rest[0], place, core[0])
    ups = rest[len(down_shape) :]
    upw = ups if len(ups) == 2 else split_shards(ups[0], place, core[0])
    return result[:4], downw, upw


def attend_back_kernel(size_ref, q_ref, kn_ref, vn_ref, kf_ref, vf_ref, do_ref, o_ref,
                       lse_ref, cos_ref, sa_ref, sb_ref,
                       own_ref, clean_ref, sums_ref, dkf_acc, dvf_acc):
    length = q_ref.shape[0]
    near, far = block_masks(size_ref)
    kf_t = kf_ref[...].astype(wide).T.astype(low)
    kn_t = kn_ref[...].astype(wide).T.astype(low)
    product = do_ref[...].astype(wide) * o_ref[...].astype(wide)
    high = product.astype(low)
    rest = (product - high.astype(wide)).astype(low)
    head_row = lax.broadcasted_iota(jnp.int32, (8, PAIR), 0)
    head_lane = lax.broadcasted_iota(jnp.int32, (8, PAIR), 1) // HEAD
    picker = jnp.where(head_row == head_lane, 1.0, 0.0).astype(low)
    deltas = dot_nt(picker, high) + dot_nt(picker, rest)
    cosine, sa, sb = cos_ref[...], sa_ref[...], sb_ref[...]
    sum_q = jnp.zeros((1, PAIR), wide)
    sum_kn = jnp.zeros((1, PAIR), wide)
    sum_vn = jnp.zeros((1, PAIR), wide)
    tiles = []
    for tile in range(length // SPAN):
        past = tile * SPAN
        here = slice(past, past + SPAN)
        query, grad = both_heads(q_ref[here, :]), both_heads(do_ref[here, :])
        scores = dot_nt(kf_ref[: past + SPAN, :], query)
        dprob = dot_nt(vf_ref[: past + SPAN, :], grad)
        diag = jnp.where(
            near,
            dot_nt(kn_ref[here, :], query),
            jnp.where(far, scores[past:], masked_value),
        )
        dprob_diag = jnp.where(near, dot_nt(vn_ref[here, :], grad), dprob[past:])
        tiles.append((past, here, query, grad, scores[:past], dprob[:past], diag, dprob_diag))
    results = []
    for past, here, query, grad, scores, dprob, diag, dprob_diag in tiles:
        lse = jnp.concatenate([lse_ref[0, 0:1, here], lse_ref[0, 1:2, here]], axis=1)
        delta = jnp.concatenate([deltas[0:1, here], deltas[1:2, here]], axis=1)
        prob_diag = jnp.exp2(diag - lse)
        ds_diag = prob_diag * (dprob_diag - delta)
        prob_near = jnp.where(near, prob_diag, 0.0).astype(low)
        ds_near = jnp.where(near, ds_diag, 0.0).astype(low)
        prob = jnp.where(near, 0.0, prob_diag).astype(low)
        dscore = jnp.where(near, 0.0, ds_diag).astype(low)
        if past:
            prob_past = jnp.exp2(scores - lse)
            ds_past = prob_past * (dprob - delta)
            prob = jnp.concatenate([prob_past.astype(low), prob], axis=0)
            dscore = jnp.concatenate([ds_past.astype(low), dscore], axis=0)
        results.append((past, here, query, grad, prob_near, ds_near, prob, dscore))
    for past, here, query, grad, prob_near, ds_near, prob, dscore in results:
        dkf, dvf = dot_nn(dscore, query), dot_nn(prob, grad)
        if past:
            dkf_acc[:past, :] += dkf[:past]
            dvf_acc[:past, :] += dvf[:past]
        dkf_acc[here, :] = dkf[past:]
        dvf_acc[here, :] = dvf[past:]
        dkn, dvn = dot_nn(ds_near, query), dot_nn(prob_near, grad)
        dqt = dot_nn(kn_t[:, here], ds_near) + dot_nn(kf_t[:, : past + SPAN], dscore)
        dq = own_blocks(dqt) * (1.0 / math.sqrt(HEAD))
        dq = rotate_back(dq, cosine[here], sa[here], sb[here])
        own_ref[0, here, :] = dq.astype(low)
        sum_q = sum_q + jnp.sum(dq, axis=0, keepdims=True)
        dkn = rotate_back(dkn * ln2, cosine[here], sa[here], sb[here])
        own_ref[1, here, :] = dkn.astype(low)
        sum_kn = sum_kn + jnp.sum(dkn, axis=0, keepdims=True)
        own_ref[2, here, :] = dvn.astype(low)
        sum_vn = sum_vn + jnp.sum(dvn, axis=0, keepdims=True)
    dkf = rotate_back(dkf_acc[...] * ln2, cosine, sa, sb)
    dvf = dvf_acc[...]
    clean_ref[0] = dkf.astype(low)
    clean_ref[1] = dvf.astype(low)
    sums_ref[0, 0:1, :] = sum_q
    sums_ref[0, 1:2, :] = sum_kn + jnp.sum(dkf, axis=0, keepdims=True)
    sums_ref[0, 2:3, :] = sum_vn + jnp.sum(dvf, axis=0, keepdims=True)


def attend_back(size, q, kn, vn, kf, vf, do, o, lse, tables, first, pairs, after, work):
    count = q.shape[0]
    pair_spec = pl.BlockSpec((count, PAIR), lambda p: (0, p + first))
    width = pairs * PAIR
    return ordered_call(
        attend_back_kernel,
        after,
        (pairs,),
        [pl.BlockSpec(memory_space=pltpu.SMEM)]
        + [pair_spec] * 7
        + [pl.BlockSpec((1, 2, count), lambda p: (p + first, 0, 0))]
        + [whole_spec(t.shape) for t in tables],
        (size, q, kn, vn, kf, vf, do, o, lse, *tables),
        out_specs=[
            pl.BlockSpec((3, count, PAIR), lambda p: (0, 0, p)),
            pl.BlockSpec((2, count, PAIR), lambda p: (0, 0, p)),
            pl.BlockSpec((1, 3, PAIR), lambda p: (p, 0, 0)),
        ],
        out_shape=[
            jax.ShapeDtypeStruct((3, count, width), low),
            jax.ShapeDtypeStruct((2, count, width), low),
            jax.ShapeDtypeStruct((pairs, 3, PAIR), wide),
        ],
        scratch_shapes=[
            pltpu.VMEM((count, PAIR), wide),
            pltpu.VMEM((count, PAIR), wide),
        ],
        work=work,
        name="attend_back",
    )


def spread_lanes(columns, batch):
    rows = columns.shape[0] // batch
    lane = lax.broadcasted_iota(jnp.int32, (rows, PAIR), 1)
    shards = []
    for shard in range(batch):
        block = columns[shard * rows : (shard + 1) * rows]
        for first, share in ((4, 4), (8, 3)):
            for j in range(share):
                chunk = share * shard + j
                at, start = first + chunk // batch, chunk % batch * rows
                block = jnp.where(
                    lane == first + j, columns[start : start + rows, at : at + 1], block
                )
        shards.append(block)
    return jnp.concatenate(shards, axis=0)


def qkv_kernel(cuts, batch, place_ref, core_ref, h_ref, hf_ref, w_ref, gain1_ref, bias1_ref,
               early_ref, *rest):
    own, clean, sums, rest = (
        rest[:cuts],
        rest[cuts : 2 * cuts],
        rest[2 * cuts : 3 * cuts],
        rest[3 * cuts :],
    )
    outs, (rows_ref, columns_ref, result_ref) = rest[:-3], rest[-3:]
    step = pl.program_id(0)
    width = h_ref.shape[1]
    result_ref[...] = dot_tn(h_ref[...], jnp.concatenate([r[0] for r in own], axis=1))

    @pl.when(step == 0)
    def _():
        columns_ref[...] = jnp.zeros_like(columns_ref)
        rows_ref[...] = jnp.zeros_like(rows_ref)
        for i in range(8):
            rows_ref[i : i + 1, :] = early_ref[:, i * width : (i + 1) * width]
        rows_ref[13:14, :] = row_of(gain1_ref)
        rows_ref[14:15, :] = row_of(bias1_ref)

    @pl.when(step > 0)
    def _():
        result_ref[...] += dot_tn(hf_ref[...], jnp.concatenate([r[0] for r in clean], axis=1))

    result = result_ref[...]
    cols = pl.ds(pl.multiple_of(step * width, 128), width)
    store_columns(place_ref, core_ref, result, outs, cols)
    weight = w_ref[...].astype(wide)
    totals = jnp.concatenate(
        [r[p, pl.ds(step, 1), :] for r in sums for p in range(r.shape[0])], axis=1
    )
    rows_ref[pl.ds(8 + step, 1), :] = totals
    lane = lax.broadcasted_iota(jnp.int32, (1, PAIR), 1)
    columns_ref[...] += jnp.where(
        lane == 0,
        jnp.sum(weight * result, axis=1, keepdims=True),
        jnp.sum(weight * totals, axis=1, keepdims=True),
    )

    @pl.when(step == 2)
    def _():
        columns = rows_ref[...].T
        bias = columns_ref[:, 1:2]
        gain = (columns_ref[:, 0:1] - columns[:, 14:15] * bias) / columns[:, 13:14]
        columns = jnp.where(lane == 11, gain, jnp.where(lane == 12, bias, columns))
        if len(outs) == 2:
            columns = spread_lanes(columns, batch)
        store_columns(place_ref, core_ref, columns, outs, slice(3 * width, 3 * width + PAIR))


def outer_qkv(h, hf, weight, gain1, bias1, early, own, clean, sums, place, core, after):
    count, width = h.shape
    batch = 2 * place.shape[0]
    columns = 3 * width + PAIR
    if aligned(width, batch):
        out_shape = [jax.ShapeDtypeStruct((batch // 2, width // batch, columns), low)] * 2
    else:
        out_shape = [jax.ShapeDtypeStruct((width, columns), low)]
    result = ordered_call(
        partial(qkv_kernel, len(own), batch),
        after,
        (3,),
        [whole_spec(h.shape)] * 2
        + [pl.BlockSpec((width, width), lambda i, p, c: (0, i))]
        + [whole_spec(v.shape) for v in (gain1, bias1, early)]
        + [pl.BlockSpec((1, count, r.shape[2]), lambda i, p, c: (i, 0, 0)) for r in own]
        + [
            pl.BlockSpec((1, count, r.shape[2]), lambda i, p, c: (jnp.maximum(i - 1, 0), 0, 0))
            for r in clean
        ]
        + [whole_spec(r.shape) for r in sums],
        (h, hf, weight, gain1, bias1, early, *own, *clean, *sums),
        (place, core),
        out_specs=[whole_spec(o.shape) for o in out_shape],
        out_shape=out_shape,
        scratch_shapes=[
            pltpu.VMEM((PAIR, width), wide),
            pltpu.VMEM((width, PAIR), wide),
            pltpu.VMEM((width, width), wide),
        ],
        work=1e8,
        name="outer_qkv",
    )
    if len(result) == 2:
        return result
    (full,) = result
    rows = width // batch
    start = 3 * width
    spread = [full[:, : start + 4]]
    for first, share in ((4, 4), (8, 3)):
        part = full[:, start + first : start + first + share].T.reshape(batch, share, rows)
        spread.append(part.transpose(0, 2, 1).reshape(width, share))
    spread.append(full[:, start + 11 :])
    return split_shards(jnp.concatenate(spread, axis=1), place, core[0])


def project_far_back_kernel(cuts, noisy_ref, x_ref, *rest):
    far, clean = rest[:HALVES], rest[HALVES : HALVES + cuts]
    wk_ref, wv_ref, gain1_ref, dfar_ref = rest[HALVES + cuts :]
    steps = pl.num_programs(0) // HALVES
    source = x_ref[...].astype(wide)
    for i, ref in enumerate(far):
        chosen = (noisy_ref[0] == 1) & (pl.program_id(0) // steps == i)
        source = jnp.where(chosen, ref[...].astype(wide), source)
    normed, factor = normalize(source)
    dh = jnp.zeros_like(source)
    for part, w_ref in enumerate((wk_ref, wv_ref)):
        grads = jnp.concatenate([c[part] for c in clean], axis=1)
        dh = dh + dot_nt(grads, w_ref[...])
    dfar_ref[...] = norm_back(dh * row_of(gain1_ref), normed, factor).astype(low)


def project_far_back(noisy, x, far, clean, weight, gain1, after):
    count, width = x.shape
    return ordered_call(
        partial(project_far_back_kernel, len(clean)),
        after,
        (count // ROWS,),
        [pl.BlockSpec(memory_space=pltpu.SMEM)]
        + [row_spec(width)]
        + [
            pl.BlockSpec(
                (ROWS, width),
                lambda i, first=n * f.shape[0] // ROWS, last=f.shape[0] // ROWS - 1: (
                    jnp.clip(i - first, 0, last),
                    0,
                ),
            )
            for n, f in enumerate(far)
        ]
        + [pl.BlockSpec((2, ROWS, c.shape[2]), lambda i: (0, i, 0)) for c in clean]
        + [
            pl.BlockSpec((width, width), lambda i, part=part: (0, part), pipeline_mode=pl.Buffered(1))
            for part in (1, 2)
        ]
        + [whole_spec(gain1.shape)],
        (noisy, x, *far, *clean, weight, weight, gain1),
        out_specs=row_spec(width),
        out_shape=jax.ShapeDtypeStruct((count, width), low),
        work=1e8,
        name="project_far_back",
    )


def project_back_kernel(cuts, noisy_ref, x_ref, dy_ref, dfar_ref, *rest):
    own = rest[:cuts]
    w_ref, gain1_ref, dx_ref = rest[cuts:]
    width = x_ref.shape[1]
    normed, factor = normalize(x_ref[...].astype(wide))
    dh = jnp.zeros_like(dy_ref)
    for part in range(3):
        grads = jnp.concatenate([c[part] for c in own], axis=1)
        dh = dh + dot_nt(grads, w_ref[:, part * width : (part + 1) * width])
    dx = dy_ref[...] + norm_back(dh * row_of(gain1_ref), normed, factor)
    dx_ref[...] = dx + jnp.where(noisy_ref[0] == 0, dfar_ref[...].astype(wide), 0.0)


def project_back(noisy, x, dy, dfar, own, weight, gain1, after):
    count, width = x.shape
    return ordered_call(
        partial(project_back_kernel, len(own)),
        after,
        (count // ROWS,),
        [pl.BlockSpec(memory_space=pltpu.SMEM)]
        + [row_spec(width)] * 3
        + [pl.BlockSpec((3, ROWS, c.shape[2]), lambda i: (0, i, 0)) for c in own]
        + [whole_spec(weight.shape), whole_spec(gain1.shape)],
        (noisy, x, dy, dfar, *own, weight, gain1),
        out_specs=row_spec(width),
        out_shape=jax.ShapeDtypeStruct((count, width), wide),
        work=1.5e10,
        name="project_back",
    )


def flip(values, mask):
    batch = lax.axis_size("batch")
    return lax.ppermute(values, "batch", [(i, i ^ mask) for i in range(batch)])


def flip_stream(values):
    return lax.ppermute(values, "stream", [(0, 1), (1, 0)])


def total(terms):
    result = terms[0].astype(wide)
    for term in terms[1:]:
        result = result + term.astype(wide)
    return result


class Reduction:
    def __init__(self, name, shards):
        keep, send = shards
        self.name = name
        self.terms = [keep, flip(send, 1)]
        self.stages = stages_of(2 * keep.shape[0])
        self.size = keep.shape[0]

    def wait_for(self, others):
        self.terms, _ = lax.optimization_barrier((self.terms, list(others)))

    def step(self):
        bits = self.stages.pop(0)
        parts = 2 ** len(bits)
        size = self.size // parts
        pieces = [
            total([t[j * size : (j + 1) * size] for t in self.terms]).astype(low)
            for j in range(1, parts)
        ]
        arrived = [flip(p, mask_of(bits, j + 1)) for j, p in enumerate(pieces)]
        self.terms = self.terms + arrived
        self.arrived = arrived
        self.size = size
        return pieces

    def last(self):
        while self.stages:
            self.step()
        self.mine = total([t[:1] for t in self.terms]).astype(low)
        self.other = flip_stream(self.mine)
        return [self.mine]

    def result(self, first, count):
        at = slice(first, first + count)
        return self.mine[0][:, at].astype(wide) + self.other[0][:, at].astype(wide)


def local(
    layer_input,
    out_cotangent,
    block_size,
    norm1_gain,
    norm1_bias,
    qkv_weight,
    qkv_bias,
    proj_weight,
    proj_bias,
    norm2_gain,
    norm2_bias,
    up_weight,
    up_bias,
    down_weight,
    down_bias,
):
    length, width = layer_input.shape[2:]
    batch = lax.axis_size("batch")
    noisy = lax.axis_index("stream").astype(jnp.int32).reshape(1)
    x = layer_input.reshape(length, width)
    g = out_cotangent.reshape(length, width)
    half = length // HALVES
    far_x, source = [], x
    for i in range(HALVES):
        piece = source[i * half : (i + 1) * half]
        far_x.append(lax.ppermute(piece, "stream", [(0, 1)]))
        source, _ = lax.optimization_barrier((source, piece))
    tables = rotary_tables(length)
    me = lax.axis_index("batch").astype(jnp.int32)
    place, core = places_of(batch, me), (me % 2).reshape(1)
    h, q, k, v = project(x, qkv_weight, qkv_bias, norm1_gain, norm1_bias, tables)
    da = early_part(g, down_weight, EARLY)
    fars, attended = [], []
    for i in range(HALVES):
        fars = project_far(
            noisy, x, far_x[i], qkv_weight, qkv_bias, norm1_gain, norm1_bias, tables, i, fars,
            [] if i else [da, h],
        )
        hf, kf, vf = fars
        attended = attend(block_size, q, k, v, kf, vf, i, HALVES, attended)
    o, lse = attended
    (out, dy, do, early), downw, upw = middle(
        place,
        core,
        x,
        o,
        g,
        da,
        proj_weight,
        proj_bias,
        norm2_gain,
        norm2_bias,
        up_weight,
        up_bias,
        down_weight,
        down_bias,
    )
    down, up = Reduction("down", downw), Reduction("up", upw)
    backs, after = [], []
    for i, (first, pairs) in enumerate(CUTS):
        if i == 1:
            down.wait_for(backs[0])
            after = down.step()
        after = after + [b[0] for b in backs[-1:]]
        backs.append(
            attend_back(
                block_size, q, k, v, kf, vf, do, o, lse, tables, first, pairs, after, 2e10
            )
        )
    own, clean, sums = ([b[i] for b in backs] for i in range(3))
    up.wait_for(backs[-1])
    down.wait_for(backs[-1])
    after = up.step() + down.step()
    dfar = project_far_back(noisy, x, far_x, clean, qkv_weight, norm1_gain, after)
    qkvw = outer_qkv(
        h,
        hf,
        qkv_weight,
        norm1_gain,
        norm1_bias,
        early,
        own,
        clean,
        sums,
        place,
        core,
        [dfar],
    )
    qkvw, _ = lax.optimization_barrier((list(qkvw), up.arrived + down.arrived))
    qkv = Reduction("qkv", qkvw)
    after = up.step()
    leaving, _ = lax.optimization_barrier((dfar, after))
    back_x = lax.ppermute(leaving, "stream", [(1, 0)])
    qkv.wait_for(after)
    after = qkv.step()
    dx = project_back(noisy, x, dy, dfar, own, qkv_weight, norm1_gain, after)
    down.wait_for([dx])
    qkv.wait_for(down.last())
    after = qkv.step()
    up.wait_for(after)
    up.last()
    arriving, down.other, _ = lax.optimization_barrier((back_x, down.other, up.mine))
    input_grad = (dx + arriving.astype(wide)).reshape(layer_input.shape)
    downw_grad = down.result(0, width)
    qkv.wait_for([input_grad, downw_grad])
    qkv.last()
    ff = up_weight.shape[1]
    upw_grad, projw_grad = up.result(0, ff), up.result(ff, width)
    qkvw_grad = qkv.result(0, 3 * width)
    vectors = qkv.result(3 * width, PAIR).T
    downb_grad, gain2_grad, bias2_grad, projb_grad = (vectors[i] for i in range(4))
    upb_grad = jnp.concatenate([vectors[i] for i in range(4, 8)])
    qkvb_grad = jnp.concatenate([vectors[i] for i in range(8, 11)])
    gain1_grad, bias1_grad = vectors[11], vectors[12]
    return (
        out.reshape(layer_input.shape),
        input_grad,
        gain1_grad,
        bias1_grad,
        qkvw_grad,
        qkvb_grad,
        projw_grad,
        projb_grad,
        gain2_grad,
        bias2_grad,
        upw_grad,
        upb_grad,
        downw_grad,
        downb_grad,
    )


def solution(mesh):
    rows = P("stream", "batch", None, None)
    return jax.shard_map(
        local,
        mesh=mesh,
        in_specs=(rows, rows, P("batch")) + (P(),) * 12,
        out_specs=(
            rows,
            rows,
            P("batch"),
            P("batch"),
            P("batch", None),
            P("batch"),
            P("batch", None),
            P("batch"),
            P("batch"),
            P("batch"),
            P("batch", None),
            P("batch"),
            P("batch", None),
            P("batch"),
        ),
        check_vma=False,
    )
```
